32 devices in a mesh: section: 2 (over core), dp: 4 (over y, x), seq: 4 (over z).
Axes of the slice: x: 2, y: 2, z: 4, core: 2. Of those that a mesh axis runs over, the one named last changes fastest.
Arguments:
- inputs: bfloat16 [2, 4, 1280, 1024], P(None, 'dp', 'seq'), may hold values from -6 to 6
- cotangent: bfloat16 [2, 4, 1280, 1024], P(None, 'dp', 'seq'), may hold values from -6 to 6
- view_tokens: int32 [2, 4, 6], P(None, 'dp'), may hold values from 0 to 128, as said below
- ln1_gain: bfloat16 [2, 1024], P('section'), may hold values from 0.099609375 to 1.8984375
- ln1_bias: bfloat16 [2, 1024], P('section'), may hold values from -3 to 3
- w_qkv: bfloat16 [2, 1024, 3072], P('section'), may hold values from -0.1875 to 0.1875
- b_query: bfloat16 [2, 1024], P('section'), may hold values from -3 to 3
- b_value: bfloat16 [2, 1024], P('section'), may hold values from -0.29882812 to 0.29882812
- w_out: bfloat16 [2, 1024, 1024], P('section'), may hold values from -3 to 3
- b_out: bfloat16 [2, 1024], P('section'), may hold values from -3 to 3
- ln2_gain: bfloat16 [2, 1024], P('section'), may hold values from 0.099609375 to 1.8984375
- ln2_bias: bfloat16 [2, 1024], P('section'), may hold values from -3 to 3
- w_up: bfloat16 [2, 1024, 4096], P('section'), may hold values from -0.1875 to 0.1875
- b_up: bfloat16 [2, 4096], P('section'), may hold values from -3 to 3
- w_down: bfloat16 [2, 4096, 1024], P('section'), may hold values from -0.09375 to 0.09375
- b_down: bfloat16 [2, 1024], P('section'), may hold values from -3 to 3
Outputs:
- activations: bfloat16 [2, 2, 4, 1280, 1024], P('section', None, 'dp', 'seq')
- input_grad: bfloat16 [2, 2, 4, 1280, 1024], P('section', None, 'dp', 'seq')
- g_ln1_gain: float32 [2, 1024], P('section', ('dp', 'seq'))
- g_ln1_bias: float32 [2, 1024], P('section', ('dp', 'seq'))
- g_w_qkv: float32 [2, 1024, 3072], P('section', None, ('dp', 'seq'))
- g_b_query: float32 [2, 1024], P('section', ('dp', 'seq'))
- g_b_value: float32 [2, 1024], P('section', ('dp', 'seq'))
- g_w_out: float32 [2, 1024, 1024], P('section', None, ('dp', 'seq'))
- g_b_out: float32 [2, 1024], P('section', ('dp', 'seq'))
- g_ln2_gain: float32 [2, 1024], P('section', ('dp', 'seq'))
- g_ln2_bias: float32 [2, 1024], P('section', ('dp', 'seq'))
- g_w_up: float32 [2, 1024, 4096], P('section', None, ('dp', 'seq'))
- g_b_up: float32 [2, 4096], P('section', ('dp', 'seq'))
- g_w_down: float32 [2, 4096, 1024], P('section', None, ('dp', 'seq'))
- g_b_down: float32 [2, 1024], P('section', ('dp', 'seq'))
The draws below stay inside these ranges and needn't reach their ends.
Inputs may be any that keep to these rules, and one draw needn't show every extreme that they name: view_tokens[m, s, i] counts the valid tokens of view i of scene s in micro-batch m; its 128 slots follow the 512 triplane tokens and the slots of earlier views, and its valid tokens come first. A scene has 2 to 6 views, which take the first slots; a present view has 32 to 128 valid tokens, the first view of each scene exactly 128; absent views hold 0.
All inputs are finite; a program needn't handle non-finite values.
Results may differ from the reference program's by a relative error of at most 0.015.
Values may be sent and summed in bfloat16 or wider, within the bound.
A program may use at most 448 MiB of HBM per device.

```python
import math
import jax
import jax.numpy as jnp
from jax import lax

D = 1024
H = 16
DH = 64
FF = 4096
VIEWS = 6
TRI = 512
VSLOT = 128
MICRO = 2
LEN = 1280
SCENES = 4


def draw_view_tokens(key, part):
    first_key, second_key = jax.random.split(key)
    present = jax.random.randint(first_key, (MICRO, SCENES, 1), 2, VIEWS + 1)
    counts = jax.random.randint(second_key, (MICRO, SCENES, VIEWS), VSLOT // 4, VSLOT + 1)
    slots = jnp.arange(VIEWS, dtype=jnp.int32)[None, None, :]
    counts = jnp.where(slots == 0, VSLOT, counts)
    return jnp.where(slots < present, counts, 0).astype(jnp.int32)


def block_scale(key, extent, cuts, smallest, largest):
    level = 1.0
    for dim, parts in cuts:
        steps = jax.random.uniform(jax.random.fold_in(jax.random.fold_in(key, 6), dim), (parts,), jnp.float32, smallest / len(cuts), largest / len(cuts))
        level = level * jnp.repeat(jnp.exp(steps), extent[dim] // parts).reshape((-1,) + (1,) * (len(extent) - 1 - dim))
    return level


def noise(stream_key, dims, scale, limit, cuts=(), kind=jnp.bfloat16):
    array = scale * jax.random.normal(stream_key, dims, jnp.float32)
    if cuts:
        array = array * block_scale(stream_key, dims, cuts, -0.22, 0.18)
    return jnp.clip(array, -limit, limit).astype(kind)


def setup_inputs(seed: int = 0) -> dict:
    key_of = jax.random.split(jax.random.key(seed), 17)
    inputs = noise(key_of[0], (MICRO, SCENES, LEN, D), 1.0, 6.0, ((1, 4), (2, 4)))
    cotangent = noise(key_of[1], (MICRO, SCENES, LEN, D), 1.0, 6.0, ((1, 4), (2, 4)))
    view_tokens = draw_view_tokens(jax.random.fold_in(key_of[16], 71), 0)
    ln1_gain = jnp.clip(1.0 + 0.18 * jax.random.normal(key_of[3], (2, D), jnp.float32), 0.099609375, 1.8984375).astype(jnp.bfloat16)
    ln1_bias = noise(key_of[4], (2, D), 0.5, 3.0, ((0, 2),))
    w_qkv = noise(key_of[5], (2, D, 3 * D), D ** -0.5, 0.1875, ((0, 2),))
    b_query = noise(key_of[6], (2, D), 0.5, 3.0, ((0, 2),))
    b_value = noise(key_of[7], (2, D), 0.05, 0.29882812, ((0, 2),))
    w_out = noise(key_of[8], (2, D, D), 4 ** -0.5, 3.0, ((0, 2),))
    b_out = noise(key_of[9], (2, D), 0.5, 3.0, ((0, 2),))
    ln2_gain = jnp.clip(1.0 + 0.18 * jax.random.normal(key_of[10], (2, D), jnp.float32), 0.099609375, 1.8984375).astype(jnp.bfloat16)
    ln2_bias = noise(key_of[11], (2, D), 0.5, 3.0, ((0, 2),))
    w_up = noise(key_of[12], (2, D, FF), D ** -0.5, 0.1875, ((0, 2),))
    b_up = noise(key_of[13], (2, FF), 0.5, 3.0, ((0, 2),))
    w_down = noise(key_of[14], (2, FF, D), FF ** -0.5, 0.09375, ((0, 2),))
    b_down = noise(key_of[15], (2, D), 0.5, 3.0, ((0, 2),))
    return dict(inputs=inputs, cotangent=cotangent, view_tokens=view_tokens, ln1_gain=ln1_gain, ln1_bias=ln1_bias, w_qkv=w_qkv, b_query=b_query, b_value=b_value, w_out=w_out, b_out=b_out, ln2_gain=ln2_gain, ln2_bias=ln2_bias, w_up=w_up, b_up=b_up, w_down=w_down, b_down=b_down)


@jax.custom_vjp
def low(v):
    return lax.optimization_barrier(v.astype(jnp.bfloat16)).astype(jnp.float32)

@jax.custom_vjp
def low_back(v):
    return v

def low_keep(v):
    return (low(v), None)

def low_pass(kept, grad):
    return (grad,)

def back_keep(v):
    return (v, None)

def back_low(kept, grad):
    return (low(grad),)
low.defvjp(low_keep, low_pass)
low_back.defvjp(back_keep, back_low)

def layer_norm(values, norm_gain, norm_bias):
    average = lax.optimization_barrier(jnp.mean(values, axis=-1, keepdims=True))
    centered = values - average
    variance = lax.optimization_barrier(jnp.mean(centered * centered, axis=-1, keepdims=True))
    return centered * lax.rsqrt(variance + 1e-05) * norm_gain + norm_bias

def key_valid(counts):
    places = jnp.arange(LEN, dtype=jnp.int32)
    offset = jnp.maximum(places - TRI, 0)
    view_index = offset // VSLOT
    inside = offset - view_index * VSLOT
    match = view_index[:, None] == jnp.arange(VIEWS, dtype=jnp.int32)[None, :]
    limits = lax.optimization_barrier(jnp.sum(jnp.where(match, counts[None, :], 0), axis=1))
    return (places < TRI) | (inside < limits)

def layer(layer_in, weights, valid):
    ln1_gain, ln1_bias, w_qkv, b_query, b_value, w_out, b_out, ln2_gain, ln2_bias, w_up, b_up, w_down, b_down = weights
    highest = lax.Precision.HIGHEST
    normed = low(layer_norm(layer_in, ln1_gain, ln1_bias))
    joined = jnp.dot(normed, w_qkv, precision=highest)
    queries = low_back(low(joined[:, :D] + b_query))
    keys_all = low_back(low(joined[:, D:2 * D])).reshape(LEN, H, DH)
    values_all = low_back(low(joined[:, 2 * D:] + b_value)).reshape(LEN, H, DH)
    scale = DH ** (-0.5)
    block_rows = math.gcd(LEN, 512)

    def attend(block):
        scores = low_back(jnp.einsum('qhd,khd->hqk', block, keys_all, precision=highest) * scale)
        scores = jnp.where(valid[None, None, :], scores, -1e+30)
        probs = low(jax.nn.softmax(scores, axis=-1))
        return jnp.einsum('hqk,khd->qhd', probs, values_all, precision=highest)
    blocks = queries.reshape(LEN // block_rows, block_rows, H, DH)
    mixed = lax.map(jax.checkpoint(attend), blocks).reshape(LEN, D)
    mixed = low_back(low(mixed))
    branch = low_back(jnp.dot(mixed, w_out, precision=highest) + b_out)
    hidden = layer_in + branch
    normed_two = low(layer_norm(hidden, ln2_gain, ln2_bias))
    upper = low_back(jnp.dot(normed_two, w_up, precision=highest) + b_up)
    gated = low(jax.nn.gelu(upper, approximate=True))
    return hidden + jnp.dot(gated, w_down, precision=highest) + b_down

def reference(inputs, cotangent, view_tokens, ln1_gain, ln1_bias, w_qkv, b_query, b_value, w_out, b_out, ln2_gain, ln2_bias, w_up, b_up, w_down, b_down):
    weights = tuple((w.astype(jnp.float32) for w in (ln1_gain, ln1_bias, w_qkv, b_query, b_value, w_out, b_out, ln2_gain, ln2_bias, w_up, b_up, w_down, b_down)))
    flat_in = inputs.reshape(MICRO * SCENES, LEN, D)
    flat_cot = cotangent.reshape(MICRO * SCENES, LEN, D)
    flat_counts = view_tokens.reshape(MICRO * SCENES, VIEWS)

    def scene(totals, item):
        scene_in, scene_cot, counts = item
        valid = key_valid(counts)

        def whole(first, params, dummy):
            lower = layer(first, tuple((p[0] for p in params)), valid)
            middle = low(lower)
            final = layer(low_back(middle + dummy), tuple((p[1] for p in params)), valid)
            return (final, middle)
        start = scene_in.astype(jnp.float32)
        dummy = jnp.zeros((LEN, D), jnp.float32)
        final, pull, middle = jax.vjp(whole, start, weights, dummy, has_aux=True)
        grad_in, grad_weights, grad_middle = pull(scene_cot.astype(jnp.float32))
        totals = jax.tree.map(jnp.add, totals, grad_weights)
        return (totals, (middle.astype(jnp.bfloat16), final.astype(jnp.bfloat16), grad_in.astype(jnp.bfloat16), grad_middle.astype(jnp.bfloat16)))
    zeros = tuple((jnp.zeros_like(w) for w in weights))
    totals, outs = lax.scan(scene, zeros, (flat_in, flat_cot, flat_counts))
    middles, finals, grad_ins, grad_middles = outs
    shape = (MICRO, SCENES, LEN, D)
    activations = jnp.stack([middles.reshape(shape), finals.reshape(shape)])
    input_grad = jnp.stack([grad_ins.reshape(shape), grad_middles.reshape(shape)])
    return (activations, input_grad, totals[0], totals[1], totals[2], totals[3], totals[4], totals[5], totals[6], totals[7], totals[8], totals[9], totals[10], totals[11], totals[12])
```

```python
import functools
import math

import jax
import jax.numpy as jnp
from jax import lax
from jax.experimental import pallas as pl
from jax.experimental.pallas import tpu as pltpu
from jax.sharding import PartitionSpec as P

D = 1024
H = 16
DH = 64
FF = 4096
VIEWS = 6
TRI = 512
VSLOT = 128
MICRO = 2
LEN = 1280
BQ = 256
NCH = 8
FC = FF // NCH
SCALE2 = DH ** (-0.5) * math.log2(math.e)
F32 = jnp.float32
BF16 = jnp.bfloat16
VMEM_LIMIT = 56 * 2**20


def params():
    return pltpu.CompilerParams(vmem_limit_bytes=VMEM_LIMIT)


def mm(a, b):
    return lax.dot_general(a, b, (((1,), (0,)), ((), ())), preferred_element_type=F32)


def mm_nt(a, b):
    return lax.dot_general(a, b, (((1,), (1,)), ((), ())), preferred_element_type=F32)


def mm_tn(a, b):
    return lax.dot_general(a, b, (((0,), (0,)), ((), ())), preferred_element_type=F32)


def norm_stats(values):
    average = jnp.mean(values, axis=-1, keepdims=True)
    centered = values - average
    variance = jnp.mean(centered * centered, axis=-1, keepdims=True)
    inverse = lax.rsqrt(variance + 1e-05)
    return centered * inverse, inverse


def qkv_kernel(x_ref, w_ref, bias_ref, gain_ref, shift_ref, a_ref, q_ref, k_ref, v_ref):
    width = q_ref.shape[1]
    normal, _ = norm_stats(x_ref[...].astype(F32))
    a = (normal * gain_ref[...] + shift_ref[...]).astype(BF16)
    a_ref[...] = a
    joined = mm(a, w_ref[...]) + bias_ref[...]
    q_ref[...] = joined[:, :width].astype(BF16)
    k_ref[...] = joined[:, width : 2 * width].astype(BF16)
    v_ref[...] = joined[:, 2 * width :].astype(BF16)


def qkv_call(x_all, weights, bias, gain, shift):
    length = x_all.shape[0]
    width = weights.shape[1] // 3
    row = lambda i: (i, 0)
    whole = lambda i: (0, 0)
    return pl.pallas_call(
        qkv_kernel,
        grid=(length // BQ,),
        in_specs=[
            pl.BlockSpec((BQ, D), row),
            pl.BlockSpec((D, 3 * width), whole),
            pl.BlockSpec((1, 3 * width), whole),
            pl.BlockSpec((1, D), whole),
            pl.BlockSpec((1, D), whole),
        ],
        out_specs=[pl.BlockSpec((BQ, D), row)] + [pl.BlockSpec((BQ, width), row)] * 3,
        out_shape=[jax.ShapeDtypeStruct((length, D), BF16)]
        + [jax.ShapeDtypeStruct((length, width), BF16)] * 3,
        compiler_params=params(),
        cost_estimate=pl.CostEstimate(
            flops=2 * length * D * 3 * width, bytes_accessed=8 * 2**20, transcendentals=0
        ),
    )(x_all, weights, bias, gain, shift)


def head_lanes(shape, head):
    lane = lax.broadcasted_iota(jnp.int32, shape, 1)
    return (lane >= head * DH) & (lane < (head + 1) * DH)


def attend_kernel(q_ref, k_ref, v_ref, mask_ref, o_ref, lse_ref):
    width = q_ref.shape[1]
    heads = width // DH
    q = q_ref[...]
    keys = k_ref[...]
    values = v_ref[...]
    mask = mask_ref[...]
    mixed = jnp.zeros((BQ, width), F32)
    totals = jnp.zeros((BQ, 128), F32)
    lane = lax.broadcasted_iota(jnp.int32, (BQ, 128), 1)
    for head in range(heads):
        mine = head_lanes((BQ, width), head)
        scores = mm_nt(jnp.where(mine, q, jnp.zeros_like(q)), keys) * SCALE2 + mask
        top = jnp.max(scores, axis=-1, keepdims=True)
        weights = jnp.exp2(scores - top)
        total = jnp.sum(weights, axis=-1, keepdims=True)
        part = mm(weights.astype(BF16), values) / total
        mixed = jnp.where(mine, part, mixed)
        totals = jnp.where(lane == head, top + jnp.log2(total), totals)
    o_ref[...] = mixed.astype(BF16)
    lse_ref[...] = totals


def attend_call(q, k, v, mask):
    length, width = q.shape
    row = lambda i: (i, 0)
    whole = lambda i: (0, 0)
    return pl.pallas_call(
        attend_kernel,
        grid=(length // BQ,),
        in_specs=[
            pl.BlockSpec((BQ, width), row),
            pl.BlockSpec((length, width), whole),
            pl.BlockSpec((length, width), whole),
            pl.BlockSpec((1, length), whole),
        ],
        out_specs=[pl.BlockSpec((BQ, width), row), pl.BlockSpec((BQ, 128), row)],
        out_shape=[
            jax.ShapeDtypeStruct((length, width), BF16),
            jax.ShapeDtypeStruct((length, 128), F32),
        ],
        compiler_params=params(),
        cost_estimate=pl.CostEstimate(
            flops=16 * length * length * width,
            bytes_accessed=4 * 2**20,
            transcendentals=length * length * width // DH,
        ),
    )(q, k, v, mask)


def attend_back_kernel(
    q_ref, do_ref, k_ref, v_ref, lse_ref, mask_ref, dj_ref, sums_ref, dk_acc, dv_acc
):
    step = pl.program_id(0)
    width = q_ref.shape[1]
    heads = width // DH
    scale = DH ** (-0.5)

    @pl.when(step == 0)
    def _():
        dk_acc[...] = jnp.zeros_like(dk_acc)
        dv_acc[...] = jnp.zeros_like(dv_acc)
        sums_ref[...] = jnp.zeros_like(sums_ref)

    q = q_ref[...]
    grad = do_ref[...]
    keys = k_ref[...]
    values = v_ref[...]
    mask = mask_ref[...]
    totals = lse_ref[...]
    d_q = jnp.zeros((BQ, width), F32)
    for head in range(heads):
        mine = head_lanes((BQ, width), head)
        q_head = jnp.where(mine, q, jnp.zeros_like(q))
        grad_head = jnp.where(mine, grad, jnp.zeros_like(grad))
        scores = mm_nt(q_head, keys) * SCALE2 + mask
        probs = jnp.exp2(scores - totals[:, head : head + 1])
        d_probs = mm_nt(grad_head, values)
        term = jnp.sum(probs * d_probs, axis=-1, keepdims=True)
        d_scores = (probs * (d_probs - term)).astype(BF16)
        dv_acc[...] += mm_tn(probs.astype(BF16), grad_head)
        dk_acc[...] += mm_tn(d_scores, q_head)
        d_q = jnp.where(mine, mm(d_scores, keys), d_q)
    low = (d_q * scale).astype(BF16)
    dj_ref[pl.ds(pl.multiple_of(step * BQ, BQ), BQ), :width] = low
    sums_ref[0:1, :] += jnp.sum(low.astype(F32), axis=0, keepdims=True)

    @pl.when(step == pl.num_programs(0) - 1)
    def _():
        dj_ref[:, width : 2 * width] = (dk_acc[...] * scale).astype(BF16)
        low_v = dv_acc[...].astype(BF16)
        dj_ref[:, 2 * width :] = low_v
        sums_ref[1:2, :] = jnp.sum(low_v.astype(F32), axis=0, keepdims=True)


def attend_back_call(q, d_o, k, v, lse, mask):
    length, width = q.shape
    row = lambda i: (i, 0)
    whole = lambda i: (0, 0)
    return pl.pallas_call(
        attend_back_kernel,
        grid=(length // BQ,),
        in_specs=[
            pl.BlockSpec((BQ, width), row),
            pl.BlockSpec((BQ, width), row),
            pl.BlockSpec((length, width), whole),
            pl.BlockSpec((length, width), whole),
            pl.BlockSpec((BQ, 128), row),
            pl.BlockSpec((1, length), whole),
        ],
        out_specs=[
            pl.BlockSpec((length, 3 * width), whole),
            pl.BlockSpec((8, width), whole),
        ],
        out_shape=[
            jax.ShapeDtypeStruct((length, 3 * width), BF16),
            jax.ShapeDtypeStruct((8, width), F32),
        ],
        scratch_shapes=[pltpu.VMEM((length, width), F32), pltpu.VMEM((length, width), F32)],
        compiler_params=params(),
        cost_estimate=pl.CostEstimate(
            flops=40 * length * length * width,
            bytes_accessed=6 * 2**20,
            transcendentals=length * length * width // DH,
        ),
    )(q, d_o, k, v, lse, mask)


GELU_A = math.sqrt(2.0 / math.pi)
GELU_B = 0.044715


def mlp_kernel(
    sel_ref,
    o_ref,
    x_ref,
    wo_ref,
    vec_ref,
    bup_ref,
    up0_ref,
    up1_ref,
    down0_ref,
    down1_ref,
    h_ref,
    a_ref,
    u_ref,
    g_ref,
    y_ref,
    acc,
):
    step = pl.program_id(0)
    groups, _, width = o_ref.shape

    @pl.when(step == 0)
    def _():
        hidden = x_ref[...].astype(F32) + vec_ref[0:1, :]
        for group in range(groups):
            hidden += mm(o_ref[group], wo_ref[group * width : (group + 1) * width, :])
        h_ref[...] = hidden
        normal, _ = norm_stats(hidden)
        a_ref[...] = (normal * vec_ref[1:2, :] + vec_ref[2:3, :]).astype(BF16)
        acc[...] = hidden + vec_ref[3:4, :]

    def part(up_ref, down_ref):
        upper = mm(a_ref[...], up_ref[...]) + bup_ref[...]
        u_ref[...] = upper
        inner = GELU_A * (upper + GELU_B * upper * upper * upper)
        gated = (0.5 * upper * (1.0 + jnp.tanh(inner))).astype(BF16)
        g_ref[...] = gated
        acc[...] += mm(gated, down_ref[...])

    pl.when(sel_ref[0] == 0)(lambda: part(up0_ref, down0_ref))
    pl.when(sel_ref[0] == 1)(lambda: part(up1_ref, down1_ref))

    @pl.when(step == pl.num_programs(0) - 1)
    def _():
        y_ref[...] = acc[...].astype(BF16)


def mlp_call(sel, o_all, x_own, wo, vecs, bup, ups, downs):
    rows = x_own.shape[0]
    groups, _, width = o_all.shape
    whole = lambda i, s: (0, 0)
    col = lambda which: (lambda i, s: (0, jnp.where(s[0] == which, i, 0)))
    line = lambda which: (lambda i, s: (jnp.where(s[0] == which, i, 0), 0))
    chunk = lambda i, s: (0, i)
    return pl.pallas_call(
        mlp_kernel,
        grid_spec=pltpu.PrefetchScalarGridSpec(
            num_scalar_prefetch=1,
            grid=(NCH,),
            in_specs=[
                pl.BlockSpec((groups, rows, width), lambda i, s: (0, 0, 0)),
                pl.BlockSpec((rows, D), whole),
                pl.BlockSpec((D, D), whole),
                pl.BlockSpec((8, D), whole),
                pl.BlockSpec((1, FC), chunk),
                pl.BlockSpec((D, FC), col(0)),
                pl.BlockSpec((D, FC), col(1)),
                pl.BlockSpec((FC, D), line(0)),
                pl.BlockSpec((FC, D), line(1)),
            ],
            out_specs=[
                pl.BlockSpec((rows, D), whole),
                pl.BlockSpec((rows, D), whole),
                pl.BlockSpec((rows, FC), chunk),
                pl.BlockSpec((rows, FC), chunk),
                pl.BlockSpec((rows, D), whole),
            ],
            scratch_shapes=[pltpu.VMEM((rows, D), F32)],
        ),
        out_shape=[
            jax.ShapeDtypeStruct((rows, D), F32),
            jax.ShapeDtypeStruct((rows, D), BF16),
            jax.ShapeDtypeStruct((rows, FF), F32),
            jax.ShapeDtypeStruct((rows, FF), BF16),
            jax.ShapeDtypeStruct((rows, D), BF16),
        ],
        compiler_params=params(),
        cost_estimate=pl.CostEstimate(
            flops=2 * rows * D * (D + 2 * FF), bytes_accessed=30 * 2**20, transcendentals=rows * FF
        ),
    )(sel, o_all, x_own, wo, vecs, bup, ups[0], ups[1], downs[0], downs[1])


def mlp_back_kernel(
    sel_ref,
    dy_ref,
    h_ref,
    wo_ref,
    vec_ref,
    u_ref,
    up0_ref,
    up1_ref,
    down0_ref,
    down1_ref,
    du_ref,
    gbup_ref,
    dh_ref,
    dr_ref,
    do_ref,
    sums_ref,
    acc,
):
    step = pl.program_id(0)
    groups, _, width = do_ref.shape

    @pl.when(step == 0)
    def _():
        acc[...] = jnp.zeros_like(acc)

    def part(up_ref, down_ref):
        d_gated = mm_nt(dy_ref[...], down_ref[...])
        upper = u_ref[...]
        square = upper * upper
        turn = jnp.tanh(GELU_A * upper * (1.0 + GELU_B * square))
        slope = 0.5 * (1.0 + turn) + (0.5 * GELU_A) * upper * (1.0 - turn * turn) * (
            1.0 + (3.0 * GELU_B) * square
        )
        d_upper = (d_gated * slope).astype(BF16)
        du_ref[...] = d_upper
        gbup_ref[...] = jnp.sum(d_upper.astype(F32), axis=0, keepdims=True)
        acc[...] += mm_nt(d_upper, up_ref[...])

    pl.when(sel_ref[0] == 0)(lambda: part(up0_ref, down0_ref))
    pl.when(sel_ref[0] == 1)(lambda: part(up1_ref, down1_ref))

    @pl.when(step == pl.num_programs(0) - 1)
    def _():
        normal, inverse = norm_stats(h_ref[...])
        d_out = dy_ref[...].astype(F32)
        d_normed = acc[...]
        sums_ref[...] = jnp.zeros_like(sums_ref)
        sums_ref[0:1, :] = jnp.sum(d_normed * normal, axis=0, keepdims=True)
        sums_ref[1:2, :] = jnp.sum(d_normed, axis=0, keepdims=True)
        d_normal = d_normed * vec_ref[1:2, :]
        d_hidden = d_out + inverse * (
            d_normal
            - jnp.mean(d_normal, axis=-1, keepdims=True)
            - normal * jnp.mean(d_normal * normal, axis=-1, keepdims=True)
        )
        dh_ref[...] = d_hidden
        d_branch = d_hidden.astype(BF16)
        dr_ref[...] = d_branch
        sums_ref[2:3, :] = jnp.sum(d_branch.astype(F32), axis=0, keepdims=True)
        sums_ref[3:4, :] = jnp.sum(d_out, axis=0, keepdims=True)
        for group in range(groups):
            do_ref[group] = mm_nt(
                d_branch, wo_ref[group * width : (group + 1) * width, :]
            ).astype(BF16)


def mlp_back_call(sel, dy, hidden, wo, vecs, upper, ups, downs, groups):
    rows = dy.shape[0]
    width = D // groups
    whole = lambda i, s: (0, 0)
    col = lambda which: (lambda i, s: (0, jnp.where(s[0] == which, i, 0)))
    line = lambda which: (lambda i, s: (jnp.where(s[0] == which, i, 0), 0))
    chunk = lambda i, s: (0, i)
    return pl.pallas_call(
        mlp_back_kernel,
        grid_spec=pltpu.PrefetchScalarGridSpec(
            num_scalar_prefetch=1,
            grid=(NCH,),
            in_specs=[
                pl.BlockSpec((rows, D), whole),
                pl.BlockSpec((rows, D), whole),
                pl.BlockSpec((D, D), whole),
                pl.BlockSpec((8, D), whole),
                pl.BlockSpec((rows, FC), chunk),
                pl.BlockSpec((D, FC), col(0)),
                pl.BlockSpec((D, FC), col(1)),
                pl.BlockSpec((FC, D), line(0)),
                pl.BlockSpec((FC, D), line(1)),
            ],
            out_specs=[
                pl.BlockSpec((rows, FC), chunk),
                pl.BlockSpec((1, FC), chunk),
                pl.BlockSpec((rows, D), whole),
                pl.BlockSpec((rows, D), whole),
                pl.BlockSpec((groups, rows, width), lambda i, s: (0, 0, 0)),
                pl.BlockSpec((8, D), whole),
            ],
            scratch_shapes=[pltpu.VMEM((rows, D), F32)],
        ),
        out_shape=[
            jax.ShapeDtypeStruct((rows, FF), BF16),
            jax.ShapeDtypeStruct((1, FF), F32),
            jax.ShapeDtypeStruct((rows, D), F32),
            jax.ShapeDtypeStruct((rows, D), BF16),
            jax.ShapeDtypeStruct((groups, rows, width), BF16),
            jax.ShapeDtypeStruct((8, D), F32),
        ],
        compiler_params=params(),
        cost_estimate=pl.CostEstimate(
            flops=2 * rows * D * (D + 2 * FF), bytes_accessed=30 * 2**20, transcendentals=rows * FF
        ),
    )(sel, dy, hidden, wo, vecs, upper, ups[0], ups[1], downs[0], downs[1])


def norm_back_kernel(mine_ref, other_ref, x_ref, dh_ref, gain_ref, dx_ref, sums_ref):
    d_normed = mine_ref[...].astype(F32) + other_ref[...].astype(F32)
    normal, inverse = norm_stats(x_ref[...].astype(F32))
    sums_ref[...] = jnp.zeros_like(sums_ref)
    sums_ref[0:1, :] = jnp.sum(d_normed * normal, axis=0, keepdims=True)
    sums_ref[1:2, :] = jnp.sum(d_normed, axis=0, keepdims=True)
    d_normal = d_normed * gain_ref[...]
    dx_ref[...] = (
        dh_ref[...]
        + inverse
        * (
            d_normal
            - jnp.mean(d_normal, axis=-1, keepdims=True)
            - normal * jnp.mean(d_normal * normal, axis=-1, keepdims=True)
        )
    ).astype(BF16)


def norm_back_call(mine, other, x_own, d_hidden, gain):
    return pl.pallas_call(
        norm_back_kernel,
        out_shape=[
            jax.ShapeDtypeStruct(x_own.shape, BF16),
            jax.ShapeDtypeStruct((8, D), F32),
        ],
        compiler_params=params(),
        cost_estimate=pl.CostEstimate(
            flops=20 * x_own.size, bytes_accessed=10 * x_own.size, transcendentals=0
        ),
    )(mine, other, x_own, d_hidden, gain)


def swap(value, axis, mask):
    count = lax.axis_size(axis)
    return lax.ppermute(value, axis, [(i, i ^ mask) for i in range(count)])


def take(value, index, dim):
    return lax.dynamic_index_in_dim(value, index, dim, keepdims=False)


def ordered(bit, mine, other, dim):
    return jnp.where(
        bit == 0,
        jnp.stack([mine, other], axis=dim),
        jnp.stack([other, mine], axis=dim),
    )


def key_bias(counts, rotate):
    places = jnp.arange(LEN, dtype=jnp.int32)
    places = jnp.where(rotate, (places + LEN // 2) % LEN, places)
    offset = jnp.maximum(places - TRI, 0)
    view_index = offset // VSLOT
    inside = offset - view_index * VSLOT
    match = view_index[:, None] == jnp.arange(VIEWS, dtype=jnp.int32)[None, :]
    limits = jnp.sum(jnp.where(match, counts[None, :], 0), axis=1)
    valid = (places < TRI) | (inside < limits)
    return jnp.where(valid, 0.0, -1e30).astype(F32)[None, :]


def shards(
    inputs,
    cotangent,
    view_tokens,
    ln1_gain,
    ln1_bias,
    w_qkv,
    b_query,
    b_value,
    w_out,
    b_out,
    ln2_gain,
    ln2_bias,
    w_up,
    b_up,
    w_down,
    b_down,
):
    core = lax.axis_index("section")
    place = lax.axis_index("seq")
    dp_index = lax.axis_index("dp")
    count = lax.axis_size("seq")
    dp_count = lax.axis_size("dp")
    groups = dp_count * count
    half = count // 2
    micro = place // half
    low = place % half
    low_bits = half.bit_length() - 1
    rows = inputs.shape[2]
    width = D // count
    rank = core * half + low

    def swap_core(value):
        return swap(value, "section", 1)

    def swap_seq(value, bit):
        return swap(value, "seq", 1 << bit)

    def low_bit(bit):
        return (place >> bit) & 1

    def own_rows(local):
        chunks = local[:, 0]
        far = lax.ppermute(
            take(chunks, 1 - micro, 0),
            ("section", "seq"),
            [(count + z, count + (z ^ half)) for z in range(count)],
        )
        return jnp.where(core == 0, take(chunks, micro, 0), far)

    def gather_rows(own):
        value = own[None]
        for bit in range(low_bits):
            other = swap_seq(value, bit)
            value = ordered(low_bit(bit), value, other, 0).reshape((-1,) + own.shape)
        value = ordered(core, value, swap_core(value), 0)
        return value.reshape((-1,) + own.shape[1:])

    def exchange(value):
        tail = value.shape[1:]
        value = value.reshape((2,) * (low_bits + 1) + tail)
        for bit in range(low_bits):
            dim = low_bits - bit
            mine = take(value, low_bit(bit), dim)
            other = swap_seq(take(value, 1 - low_bit(bit), dim), bit)
            value = ordered(low_bit(bit), mine, other, dim)
        mine = take(value, core, 0)
        other = swap_core(take(value, 1 - core, 0))
        return ordered(core, mine, other, 0).reshape((count,) + tail)

    def to_section(own, layer):
        first = own
        if layer == 1:
            first = lax.ppermute(
                own, ("section", "seq"), [(z, count + z) for z in range(count)]
            )
        second = lax.ppermute(
            own,
            ("section", "seq"),
            [(count + z, layer * count + (z ^ half)) for z in range(count)],
        )
        return ordered(micro, first, second, 0)

    def both_vectors(value):
        return jnp.stack([value, value])

    vectors = jnp.concatenate(
        [v[0].astype(F32) for v in (ln1_gain, ln1_bias, b_query, b_value, b_out, ln2_gain, ln2_bias, b_down, b_up)]
    )
    vector_pair = ordered(core, vectors, swap_core(vectors), 0)

    def vector(layer, index):
        size = FF if index == 8 else D
        return vector_pair[layer, index * D : index * D + size]

    joint = w_qkv[0].reshape(D, 3, count, width)
    joint_mine = take(joint, rank, 2).reshape(D, 3 * width)
    joint_other = swap_core(take(joint, (1 - core) * half + low, 2).reshape(D, 3 * width))
    out_other = swap_core(w_out[0])
    up_other = swap_core(w_up[0])
    down_other = swap_core(w_down[0])
    ups = (w_up[0], up_other)
    downs = (w_down[0], down_other)

    bias_mask = key_bias(take(view_tokens[:, 0], micro, 0), micro == 1)

    saved = []
    layer_in = own_rows(inputs)
    acts = []
    for layer in range(2):
        sel = jnp.where(core == layer, 0, 1).astype(jnp.int32)[None]
        w_joint = jnp.where(core == layer, joint_mine, joint_other)
        w_proj = jnp.where(core == layer, w_out[0], out_other)
        zero = jnp.zeros((width,), F32)
        slice_of = lambda v: lax.dynamic_slice_in_dim(v, rank * width, width)
        bias = jnp.concatenate([slice_of(vector(layer, 2)), zero, slice_of(vector(layer, 3))])
        vecs = jnp.concatenate(
            [
                jnp.stack([vector(layer, 4), vector(layer, 5), vector(layer, 6), vector(layer, 7)]),
                jnp.zeros((4, D), F32),
            ]
        )
        x_all = gather_rows(layer_in)
        a1, q, k, v = qkv_call(
            x_all, w_joint, bias[None], vector(layer, 0)[None], vector(layer, 1)[None]
        )
        mixed, lse = attend_call(q, k, v, bias_mask)
        o_own = exchange(mixed.reshape(count, rows, width))
        hidden, a2, upper, gated, output = mlp_call(
            sel, o_own, layer_in, w_proj, vecs, vector(layer, 8)[None], ups, downs
        )
        acts.append(output)
        saved.append(
            (sel, w_joint, w_proj, vecs, layer_in, a1, q, k, v, lse, o_own, hidden, a2, upper, gated)
        )
        layer_in = output

    dp_bits = dp_count.bit_length() - 1
    seq_bits = count.bit_length() - 1
    bits = [("dp", dp_bits - 1 - i) for i in range(dp_bits)]
    bits += [("seq", seq_bits - 1 - i) for i in range(seq_bits)]
    dp_dims = list(range(dp_bits))
    seq_dims = list(range(dp_bits, dp_bits + seq_bits))[::-1]
    orders = (
        dp_dims[::-1] + seq_dims,
        dp_dims + seq_dims,
        seq_dims[:1] + dp_dims + seq_dims[1:],
        seq_dims[:1] + dp_dims[::-1] + seq_dims[1:],
    )

    def reduce_one(value, order):
        tail = value.shape[1:]
        value = value.reshape((2,) * len(bits) + tail)
        left = list(range(len(bits)))
        for dim in order:
            axis, bit = bits[dim]
            index = (lax.axis_index(axis) >> bit) & 1
            at = left.index(dim)
            left.remove(dim)
            other = swap(take(value, 1 - index, at), axis, 1 << bit)
            total = take(value, index, at).astype(F32) + other.astype(F32)
            value = total.astype(value.dtype) if left else total
        return value

    def reduce_parts(value, cuts):
        outs = []
        start = 0
        for order, size in zip(orders, cuts):
            if size:
                outs.append(reduce_one(value[..., start : start + size], order))
            start += size
        return jnp.concatenate(outs, axis=-1)

    def halves(value):
        split = value.reshape(rows, groups, 2, FF // groups // 2)
        mine = take(split, core, 2).reshape(rows, FF // 2)
        return mine, take(split, 1 - core, 2).reshape(rows, FF // 2)

    def joined(mine, other):
        return jnp.concatenate([mine, other], axis=0)

    def give(value, layer):
        return lax.ppermute(value, "section", [(1 - layer, layer)])

    smalls = []
    results = []
    grads_in = []
    d_out = own_rows(cotangent)
    for layer in (1, 0):
        sel, w_joint, w_proj, vecs, x_own, a1, q, k, v, lse, o_own, hidden, a2, upper, gated = saved[layer]
        gated_mine, gated_send = halves(gated)
        gated_all = joined(gated_mine, swap_core(gated_send))
        a2_all = joined(a2, swap_core(a2))
        d_out_all = joined(d_out, swap_core(d_out))
        g_down = mm_tn(d_out_all, gated_all).astype(BF16).reshape(groups, D // groups, FF // 2)
        r_down = reduce_parts(g_down, (640, 640, 384, 384))
        d_upper, g_bup, d_hidden, d_branch, d_heads, sums_two = mlp_back_call(
            sel, d_out, hidden, w_proj, vecs, upper, ups, downs, count
        )
        upper_mine, upper_send = halves(d_upper)
        upper_all = joined(upper_mine, swap_core(upper_send))
        g_up = mm_tn(upper_all, a2_all).astype(BF16).reshape(groups, FF // groups // 2, D)
        r_up = reduce_parts(g_up, (384, 384, 128, 128))
        d_mixed = exchange(d_heads).reshape(LEN, width)
        o_split = o_own.reshape(2, half, rows, width)
        flat = lambda t: jnp.swapaxes(t, 0, 1).reshape(rows, half * width)
        o_all = joined(flat(take(o_split, core, 0)), swap_core(flat(take(o_split, 1 - core, 0))))
        branch_all = joined(d_branch, swap_core(d_branch))
        g_out = mm_tn(branch_all, o_all).astype(BF16).reshape(groups, D // groups, D // 2)
        r_out = reduce_parts(g_out, (128, 128, 128, 128))
        d_joint, sums_qv = attend_back_call(q, d_mixed, k, v, lse, bias_mask)
        d_normed = mm_nt(d_joint, w_joint).astype(BF16).reshape((2,) * (low_bits + 1) + (rows, D))
        other = swap_core(take(d_normed, 1 - core, 0))
        mine = take(d_normed, core, 0)
        for bit in range(low_bits):
            total = (mine.astype(F32) + other.astype(F32)).astype(BF16)
            dim = low_bits - 1 - bit
            other = swap_seq(take(total, 1 - low_bit(bit), dim), bit)
            mine = take(total, low_bit(bit), dim)
        d_in, sums_one = norm_back_call(mine, other, x_own, d_hidden, vector(layer, 0)[None])
        g_joint = mm_tn(d_joint, a1).astype(BF16).reshape(3, width, 2, D // 2)
        g_joint = ordered(core, take(g_joint, core, 2), swap_core(take(g_joint, 1 - core, 2)), 1)
        spread = jnp.stack(
            [jnp.where(low == i, g_joint, jnp.zeros_like(g_joint)) for i in range(half)], axis=2
        )
        r_joint = reduce_parts(spread.reshape(groups, 3 * D // groups, D // 2), (128, 128, 128, 128))
        mine_at = jnp.zeros((2, count, width), F32)
        mine_at = lax.dynamic_update_slice(mine_at, sums_qv[0:2, None, :], (0, rank, 0))
        smalls.append(
            jnp.concatenate(
                [
                    piece.reshape(groups, -1)
                    for piece in (
                        sums_one[0],
                        sums_one[1],
                        mine_at[0].reshape(-1),
                        mine_at[1].reshape(-1),
                        sums_two[2],
                        sums_two[0],
                        sums_two[1],
                        g_bup[0],
                        sums_two[3],
                    )
                ],
                axis=1,
            )
        )
        parts = []
        for piece in (r_down, r_out, r_joint, r_up):
            parts.append((piece, give(piece, layer)))
        results.append(parts)
        grads_in.append(d_in)
        d_out = d_in

    results = results[::-1]
    grads_in = grads_in[::-1]
    small_pair = jnp.stack(smalls[::-1])
    small = take(small_pair, core, 0) + swap_core(take(small_pair, 1 - core, 0))
    small = reduce_one(small, orders[0])

    acts_rows = jnp.where(core == 0, to_section(acts[0], 0), to_section(acts[1], 1))
    grad_rows = jnp.where(core == 0, to_section(grads_in[0], 0), to_section(grads_in[1], 1))

    def choose(index):
        first = jnp.where(core == 0, results[0][index][0], results[1][index][1])
        second = jnp.where(core == 0, results[0][index][1], results[1][index][0])
        return first, second

    down_0, down_1 = choose(0)
    d_down = jnp.stack([down_0.reshape(-1, groups, FF // groups // 2), down_1.reshape(-1, groups, FF // groups // 2)], axis=2)
    g_w_down = d_down.reshape(-1, FF).T
    out_0, out_1 = choose(1)
    g_w_out = jnp.concatenate([out_0, out_1], axis=1).T
    joint_0, joint_1 = choose(2)
    g_w_qkv = jnp.concatenate([joint_0, joint_1], axis=1).T
    up_0, up_1 = choose(3)
    g_w_up = jnp.concatenate([up_0, up_1], axis=0).T

    unit = D // groups
    pieces = []
    start = 0
    for size in (unit, unit, unit, unit, unit, unit, unit, FF // groups, unit):
        pieces.append(small[start : start + size])
        start += size
    g_ln1g, g_ln1b, g_bq, g_bv, g_bo, g_ln2g, g_ln2b, g_bup, g_bd = pieces
    outs = (
        g_ln1g,
        g_ln1b,
        g_w_qkv,
        g_bq,
        g_bv,
        g_w_out,
        g_bo,
        g_ln2g,
        g_ln2b,
        g_w_up,
        g_bup,
        g_w_down,
        g_bd,
    )
    return (acts_rows[None, :, None], grad_rows[None, :, None]) + tuple(g[None] for g in outs)


def solution(mesh):
    rows = P(None, "dp", "seq", None)
    vector = P("section", None)
    matrix = P("section", None, None)
    placed = (
        rows,
        rows,
        P(None, "dp", None),
        vector,
        vector,
        matrix,
        vector,
        vector,
        matrix,
        vector,
        vector,
        vector,
        matrix,
        vector,
        matrix,
        vector,
    )
    both = P("section", None, "dp", "seq", None)
    line = P("section", ("dp", "seq"))
    table = P("section", None, ("dp", "seq"))
    return jax.shard_map(
        shards,
        mesh=mesh,
        in_specs=placed,
        out_specs=(
            both,
            both,
            line,
            line,
            table,
            line,
            line,
            table,
            line,
            line,
            line,
            table,
            line,
            table,
            line,
        ),
        check_vma=False,
    )
```

```python
import functools
import math

import jax
import jax.numpy as jnp
from jax import lax
from jax.experimental import pallas as pl
from jax.experimental.pallas import tpu as pltpu
from jax.sharding import PartitionSpec as P

D = 1024
H = 16
DH = 64
FF = 4096
VIEWS = 6
TRI = 512
VSLOT = 128
MICRO = 2
LEN = 1280
BQ = 256
NCH = 8
FC = FF // NCH
SCALE2 = DH ** (-0.5) * math.log2(math.e)
F32 = jnp.float32
BF16 = jnp.bfloat16
VMEM_LIMIT = 56 * 2**20


def params():
    return pltpu.CompilerParams(vmem_limit_bytes=VMEM_LIMIT)


def mm(a, b):
    return lax.dot_general(a, b, (((1,), (0,)), ((), ())), preferred_element_type=F32)


def mm_nt(a, b):
    return lax.dot_general(a, b, (((1,), (1,)), ((), ())), preferred_element_type=F32)


def mm_tn(a, b):
    return lax.dot_general(a, b, (((0,), (0,)), ((), ())), preferred_element_type=F32)


def norm_stats(values):
    average = jnp.mean(values, axis=-1, keepdims=True)
    centered = values - average
    variance = jnp.mean(centered * centered, axis=-1, keepdims=True)
    inverse = lax.rsqrt(variance + 1e-05)
    return centered * inverse, inverse


def qkv_kernel(x_ref, w_ref, bias_ref, gain_ref, shift_ref, a_ref, q_ref, k_ref, v_ref):
    width = q_ref.shape[1]
    normal, _ = norm_stats(x_ref[...].astype(F32))
    a = (normal * gain_ref[...] + shift_ref[...]).astype(BF16)
    a_ref[...] = a
    joined = mm(a, w_ref[...]) + bias_ref[...]
    q_ref[...] = joined[:, :width].astype(BF16)
    k_ref[...] = joined[:, width : 2 * width].astype(BF16)
    v_ref[...] = joined[:, 2 * width :].astype(BF16)


def qkv_call(x_all, weights, bias, gain, shift):
    length = x_all.shape[0]
    width = weights.shape[1] // 3
    row = lambda i: (i, 0)
    whole = lambda i: (0, 0)
    return pl.pallas_call(
        qkv_kernel,
        grid=(length // BQ,),
        in_specs=[
            pl.BlockSpec((BQ, D), row),
            pl.BlockSpec((D, 3 * width), whole),
            pl.BlockSpec((1, 3 * width), whole),
            pl.BlockSpec((1, D), whole),
            pl.BlockSpec((1, D), whole),
        ],
        out_specs=[pl.BlockSpec((BQ, D), row)] + [pl.BlockSpec((BQ, width), row)] * 3,
        out_shape=[jax.ShapeDtypeStruct((length, D), BF16)]
        + [jax.ShapeDtypeStruct((length, width), BF16)] * 3,
        compiler_params=params(),
        cost_estimate=pl.CostEstimate(
            flops=2 * length * D * 3 * width, bytes_accessed=8 * 2**20, transcendentals=0
        ),
    )(x_all, weights, bias, gain, shift)


def head_lanes(shape, head):
    lane = lax.broadcasted_iota(jnp.int32, shape, 1)
    return (lane >= head * DH) & (lane < (head + 1) * DH)


def attend_kernel(q_ref, k_ref, v_ref, mask_ref, o_ref, lse_ref):
    width = q_ref.shape[1]
    heads = width // DH
    q = q_ref[...]
    keys = k_ref[...]
    values = v_ref[...]
    mask = mask_ref[...]
    mixed = jnp.zeros((BQ, width), F32)
    totals = jnp.zeros((BQ, 128), F32)
    lane = lax.broadcasted_iota(jnp.int32, (BQ, 128), 1)
    for head in range(heads):
        mine = head_lanes((BQ, width), head)
        scores = mm_nt(jnp.where(mine, q, jnp.zeros_like(q)), keys) * SCALE2 + mask
        top = jnp.max(scores, axis=-1, keepdims=True)
        weights = jnp.exp2(scores - top)
        total = jnp.sum(weights, axis=-1, keepdims=True)
        part = mm(weights.astype(BF16), values) / total
        mixed = jnp.where(mine, part, mixed)
        totals = jnp.where(lane == head, top + jnp.log2(total), totals)
    o_ref[...] = mixed.astype(BF16)
    lse_ref[...] = totals


def attend_call(q, k, v, mask):
    length, width = q.shape
    row = lambda i: (i, 0)
    whole = lambda i: (0, 0)
    return pl.pallas_call(
        attend_kernel,
        grid=(length // BQ,),
        in_specs=[
            pl.BlockSpec((BQ, width), row),
            pl.BlockSpec((length, width), whole),
            pl.BlockSpec((length, width), whole),
            pl.BlockSpec((1, length), whole),
        ],
        out_specs=[pl.BlockSpec((BQ, width), row), pl.BlockSpec((BQ, 128), row)],
        out_shape=[
            jax.ShapeDtypeStruct((length, width), BF16),
            jax.ShapeDtypeStruct((length, 128), F32),
        ],
        compiler_params=params(),
        cost_estimate=pl.CostEstimate(
            flops=16 * length * length * width,
            bytes_accessed=4 * 2**20,
            transcendentals=length * length * width // DH,
        ),
    )(q, k, v, mask)


def shards_of():
    return lax.axis_size("dp") * lax.axis_size("seq")


def put_halves(ref, value, unit):
    for at in range(value.shape[1] // unit):
        ref[at % 2, :, at // 2 * unit : (at // 2 + 1) * unit] = value[:, at * unit : (at + 1) * unit]


GELU_A = math.sqrt(2.0 / math.pi)
GELU_B = 0.044715


def mlp_kernel(
    sel_ref,
    o_ref,
    x_ref,
    wo_ref,
    vec_ref,
    bup_ref,
    up0_ref,
    up1_ref,
    down0_ref,
    down1_ref,
    h_ref,
    a_ref,
    u_ref,
    g_ref,
    y_ref,
    acc,
):
    step = pl.program_id(0)
    groups, _, width = o_ref.shape
    unit = FF // shards_of() // 2

    @pl.when(step == 0)
    def _():
        hidden = x_ref[...].astype(F32) + vec_ref[0:1, :]
        for group in range(groups):
            hidden += mm(o_ref[group], wo_ref[group * width : (group + 1) * width, :])
        h_ref[...] = hidden
        normal, _ = norm_stats(hidden)
        a_ref[...] = (normal * vec_ref[1:2, :] + vec_ref[2:3, :]).astype(BF16)
        acc[...] = hidden + vec_ref[3:4, :]

    def part(up_ref, down_ref):
        upper = mm(a_ref[...], up_ref[...]) + bup_ref[...]
        u_ref[...] = upper
        inner = GELU_A * (upper + GELU_B * upper * upper * upper)
        gated = (0.5 * upper * (1.0 + jnp.tanh(inner))).astype(BF16)
        put_halves(g_ref, gated, unit)
        acc[...] += mm(gated, down_ref[...])

    pl.when(sel_ref[0] == 0)(lambda: part(up0_ref, down0_ref))
    pl.when(sel_ref[0] == 1)(lambda: part(up1_ref, down1_ref))

    @pl.when(step == pl.num_programs(0) - 1)
    def _():
        y_ref[...] = acc[...].astype(BF16)


def mlp_call(sel, o_all, x_own, wo, vecs, bup, ups, downs):
    rows = x_own.shape[0]
    groups, _, width = o_all.shape
    whole = lambda i, s: (0, 0)
    col = lambda which: (lambda i, s: (0, jnp.where(s[0] == which, i, 0)))
    line = lambda which: (lambda i, s: (jnp.where(s[0] == which, i, 0), 0))
    chunk = lambda i, s: (0, i)
    return pl.pallas_call(
        mlp_kernel,
        grid_spec=pltpu.PrefetchScalarGridSpec(
            num_scalar_prefetch=1,
            grid=(NCH,),
            in_specs=[
                pl.BlockSpec((groups, rows, width), lambda i, s: (0, 0, 0)),
                pl.BlockSpec((rows, D), whole),
                pl.BlockSpec((D, D), whole),
                pl.BlockSpec((8, D), whole),
                pl.BlockSpec((1, FC), chunk),
                pl.BlockSpec((D, FC), col(0)),
                pl.BlockSpec((D, FC), col(1)),
                pl.BlockSpec((FC, D), line(0)),
                pl.BlockSpec((FC, D), line(1)),
            ],
            out_specs=[
                pl.BlockSpec((rows, D), whole),
                pl.BlockSpec((rows, D), whole),
                pl.BlockSpec((rows, FC), chunk),
                pl.BlockSpec((2, rows, FC // 2), lambda i, s: (0, 0, i)),
                pl.BlockSpec((rows, D), whole),
            ],
            scratch_shapes=[pltpu.VMEM((rows, D), F32)],
        ),
        out_shape=[
            jax.ShapeDtypeStruct((rows, D), F32),
            jax.ShapeDtypeStruct((rows, D), BF16),
            jax.ShapeDtypeStruct((rows, FF), F32),
            jax.ShapeDtypeStruct((2, rows, FF // 2), BF16),
            jax.ShapeDtypeStruct((rows, D), BF16),
        ],
        compiler_params=params(),
        cost_estimate=pl.CostEstimate(
            flops=2 * rows * D * (D + 2 * FF), bytes_accessed=30 * 2**20, transcendentals=rows * FF
        ),
    )(sel, o_all, x_own, wo, vecs, bup, ups[0], ups[1], downs[0], downs[1])


def norm_back_kernel(mine_ref, other_ref, x_ref, dh_ref, gain_ref, dx_ref, sums_ref):
    d_normed = mine_ref[...].astype(F32) + other_ref[...].astype(F32)
    normal, inverse = norm_stats(x_ref[...].astype(F32))
    sums_ref[...] = jnp.zeros_like(sums_ref)
    sums_ref[0:1, :] = jnp.sum(d_normed * normal, axis=0, keepdims=True)
    sums_ref[1:2, :] = jnp.sum(d_normed, axis=0, keepdims=True)
    d_normal = d_normed * gain_ref[...]
    dx_ref[...] = (
        dh_ref[...]
        + inverse
        * (
            d_normal
            - jnp.mean(d_normal, axis=-1, keepdims=True)
            - normal * jnp.mean(d_normal * normal, axis=-1, keepdims=True)
        )
    ).astype(BF16)


def norm_back_call(mine, other, x_own, d_hidden, gain):
    return pl.pallas_call(
        norm_back_kernel,
        out_shape=[
            jax.ShapeDtypeStruct(x_own.shape, BF16),
            jax.ShapeDtypeStruct((8, D), F32),
        ],
        compiler_params=params(),
        cost_estimate=pl.CostEstimate(
            flops=20 * x_own.size, bytes_accessed=10 * x_own.size, transcendentals=0
        ),
    )(mine, other, x_own, d_hidden, gain)


MESH_AXES = ("dp", "seq")


def axis_bits(dp_count, count):
    bits = []
    for axis, size in (("dp", dp_count), ("seq", count)):
        mask = size // 2
        while mask:
            bits.append((axis, mask))
            mask //= 2
    return bits


def stream_orders(dp_count, count):
    dp_bits = dp_count.bit_length() - 1
    seq_bits = count.bit_length() - 1
    dp_dims = list(range(dp_bits))
    seq_dims = list(range(dp_bits, dp_bits + seq_bits))[::-1]
    return (
        dp_dims[::-1] + seq_dims,
        dp_dims + seq_dims,
        seq_dims[:1] + dp_dims + seq_dims[1:],
        seq_dims[:1] + dp_dims[::-1] + seq_dims[1:],
    )


def my_bit(axis, mask):
    return lax.rem(lax.div(lax.axis_index(axis), mask), 2)


def partner(axis, mask):
    return lax.axis_index(axis) + mask * (1 - 2 * my_bit(axis, mask))


def greet(bits):
    barrier = pltpu.get_barrier_semaphore()
    for axis, mask in bits:
        pl.semaphore_signal(
            barrier,
            inc=1,
            device_id={axis: partner(axis, mask)},
            device_id_type=pl.DeviceIdType.MESH,
        )
    pl.semaphore_wait(barrier, len(bits))


class Reducer:
    def __init__(self, bits, order, src, cols, out, rows, compact, buffers, sems):
        self.bits, self.order, self.src, self.cols = bits, order, src, cols
        self.out, self.out_cols, self.buffers, self.sems = out, cols, buffers, sems
        self.count, self.rows, self.compact = len(bits), rows, compact

    @staticmethod
    def scratch(count, rows, width):
        shapes = [pltpu.VMEM((2,) * (count - 1) + (rows, width), BF16)]
        for stage in range(count):
            shapes.append(pltpu.VMEM((2,) * (count - 1 - stage) + (rows, width), BF16))
        shapes += [
            pltpu.SemaphoreType.DMA((count + 2,)),
            pltpu.SemaphoreType.DMA((count + 2,)),
            pltpu.SemaphoreType.DMA,
        ]
        return shapes

    def place(self, stage):
        left = [d for d in range(self.count) if d not in self.order[:stage]]
        dim = self.order[stage]
        return left, left.index(dim), self.bits[dim]

    def cut(self, stage, index):
        left, at, _ = self.place(stage)
        where = [slice(None)] * len(left)
        where[at] = index
        return tuple(where)

    def source(self, stage):
        if stage == 0:
            return self.src
        return self.buffers[0] if stage == 1 else self.buffers[stage]

    def copy(self, stage):
        axis, mask = self.place(stage)[2]
        where = self.cut(stage, 1 - my_bit(axis, mask))
        if stage == 0:
            where = where + (slice(None), pl.ds(*self.cols))
        return pltpu.make_async_remote_copy(
            src_ref=self.source(stage).at[where],
            dst_ref=self.buffers[stage + 1],
            send_sem=self.sems[0].at[stage],
            recv_sem=self.sems[1].at[stage],
            device_id={axis: partner(axis, mask)},
            device_id_type=pl.DeviceIdType.MESH,
        )

    def load(self):
        axis, mask = self.place(0)[2]
        where = self.cut(0, my_bit(axis, mask)) + (slice(None), pl.ds(*self.cols))
        return pltpu.make_async_copy(self.src.at[where], self.buffers[0], self.sems[2])

    def share(self):
        core = lax.axis_index("section")
        return pltpu.make_async_remote_copy(
            src_ref=self.out.at[core, :, pl.ds(*self.out_cols)],
            dst_ref=self.out.at[core, :, pl.ds(*self.out_cols)],
            send_sem=self.sems[0].at[self.count],
            recv_sem=self.sems[1].at[self.count],
            device_id={"section": 1 - core},
            device_id_type=pl.DeviceIdType.MESH,
        )

    def trade(self):
        third = self.rows // 3
        core = lax.axis_index("section")
        bit = lax.rem(lax.axis_index("seq"), 2)
        row = pl.multiple_of((1 - bit) * 2 * third, third)
        return pltpu.make_async_remote_copy(
            src_ref=self.out.at[core, pl.ds(row, third), pl.ds(*self.out_cols)],
            dst_ref=self.out.at[core, pl.ds(self.rows, third), pl.ds(*self.out_cols)],
            send_sem=self.sems[0].at[self.count + 1],
            recv_sem=self.sems[1].at[self.count + 1],
            device_id={"seq": partner("seq", 1)},
            device_id_type=pl.DeviceIdType.MESH,
        )

    def begin(self):
        self.copy(0).start()
        self.load().start()

    def step(self, stage):
        left, at, (axis, mask) = self.place(stage)
        bit = my_bit(axis, mask)
        if stage == 0:
            self.load().wait()
        self.copy(stage).wait_recv()
        got = self.buffers[stage + 1]
        rows = got.shape[-2]
        chunk = 16
        per = rows // chunk
        last = stage == self.count - 1
        core = lax.axis_index("section")
        total = 2 ** (len(left) - 1)

        def body(i, carry):
            flat = lax.div(i, per)
            row = pl.multiple_of(lax.rem(i, per) * chunk, chunk)
            index = []
            for j in range(len(left) - 1):
                index.append(lax.rem(lax.div(flat, 2 ** (len(left) - 2 - j)), 2))
            there = tuple(index) + (pl.ds(row, chunk), slice(None))
            if stage == 0:
                mine = self.buffers[0][there]
            else:
                own = index[:at] + [bit] + index[at:]
                mine = self.source(stage)[tuple(own) + (pl.ds(row, chunk), slice(None))]
            value = mine.astype(F32) + got[there].astype(F32)
            if last:
                self.out[core, pl.ds(row, chunk), pl.ds(*self.out_cols)] = value
            elif stage == 0:
                self.buffers[0][there] = value.astype(BF16)
            else:
                got[there] = value.astype(BF16)
            return carry

        lax.fori_loop(0, total * per, body, 0)
        if not last:
            self.copy(stage + 1).start()
        elif self.compact:
            self.trade().start()
        else:
            self.share().start()

    def tail(self):
        if self.compact:
            self.trade().wait()
            self.share().start()

    def finish(self):
        for stage in range(self.count):
            self.copy(stage).wait_send()
        self.share().wait()


def part_widths(width):
    unit = 128 if width % 128 == 0 else width
    tiles = width // unit
    first = -(-tiles // 3)
    rest = tiles - 2 * first
    if rest <= 0:
        first = tiles // 2
        rest = tiles - 2 * first
    second = rest // 2
    return tuple(unit * n for n in (first, first, rest - second, second))


class Hosted:
    def __init__(self, dp_count, count, shapes):
        self.dp_count, self.count, self.shapes = dp_count, count, shapes
        self.all_bits = axis_bits(dp_count, count)
        self.plan = []
        for index, (rows, width, compact) in enumerate(shapes):
            bits = self.all_bits[:-1] if compact else self.all_bits
            orders = stream_orders(dp_count, count)
            widths = part_widths(width)
            if compact:
                last = len(bits)
                orders = [tuple(d for d in order if d != last) for order in orders[:2]]
                widths = (width // 2, width // 2)
            start = 0
            for order, size in zip(orders, widths):
                pieces = [size] if size else []
                if size >= 256 and not compact:
                    first = 128 * -(-size // 256)
                    pieces = [first, size - first]
                for k, piece in enumerate(pieces):
                    self.plan.append((index, tuple(order), bits, start, piece, rows, compact, k))
                    start += piece
        self.plan.sort(key=lambda p: (p[0], p[7]))
        self.arrays = len(shapes)
        self.events = []
        for k, part in enumerate(self.plan):
            for stage in range(len(part[2])):
                order = 1.0 - 0.5**stage + 0.25 * part[7] + 0.02 * part[0]
                self.events.append((order, k, stage))
        self.events.sort()

    def views(self, arrays):
        out = []
        for array, (_, _, compact) in zip(arrays, self.shapes):
            depth = len(self.all_bits) - (1 if compact else 0)
            out.append(array.reshape((2,) * depth + array.shape[1:]))
        return out

    def in_specs(self):
        return [pl.BlockSpec(memory_space=pl.ANY)] * self.arrays

    def out_shapes(self):
        return [
            jax.ShapeDtypeStruct((2, rows + (rows // 3 if compact else 0), width), F32)
            for rows, width, compact in self.shapes
        ]

    def out_specs(self):
        return [pl.BlockSpec(memory_space=pltpu.VMEM)] * self.arrays

    def scratch(self):
        shapes = [pltpu.VMEM(o.shape, F32) for o in self.out_shapes()]
        for _, _, bits, _, size, rows, _, _ in self.plan:
            shapes += Reducer.scratch(len(bits), rows, size)
        return shapes

    def bind(self, srcs, outs, scratch):
        self.parts = []
        self.outs, self.sums = outs, scratch[: self.arrays]
        at = self.arrays
        for index, order, bits, start, size, rows, compact, _ in self.plan:
            depth = len(bits) + 1
            mine = scratch[at : at + depth + 3]
            at += depth + 3
            self.parts.append(
                Reducer(
                    bits,
                    order,
                    srcs[index],
                    (start, size),
                    self.sums[index],
                    rows,
                    compact,
                    mine[:depth],
                    mine[depth:],
                )
            )
    def begin(self):
        greet(self.all_bits + [("section", 1)])
        for part in self.parts:
            part.begin()

    def run(self, first, last):
        for _, k, stage in self.events[first:last]:
            self.parts[k].step(stage)

    def slots(self, times, total):
        edges = []
        done = 0
        for time in times:
            while done < len(self.events) and self.expected(done) * total <= time:
                done += 1
            edges.append(done)
        edges[-1] = len(self.events)
        return list(zip([0] + edges[:-1], edges))

    def expected(self, event):
        _, k, stage = self.events[event]
        late = self.plan[k][7]
        return min(1.0, 0.3 + 0.25 * late + 0.5 * (1.0 - 0.5**stage))

    def finish(self):
        for part in self.parts:
            part.tail()
        for part in self.parts:
            part.finish()
        for out, value in zip(self.outs, self.sums):
            out[...] = value[...]


def reduce_kernel(host, *refs):
    n = host.arrays
    host.bind(refs[:n], refs[n : 2 * n], refs[2 * n :])
    host.begin()
    host.run(0, len(host.events))
    host.finish()


def reduce_call(host, arrays, collective_id):
    return pl.pallas_call(
        functools.partial(reduce_kernel, host),
        in_specs=host.in_specs(),
        out_specs=host.out_specs(),
        out_shape=host.out_shapes(),
        scratch_shapes=host.scratch(),
        compiler_params=pltpu.CompilerParams(
            vmem_limit_bytes=VMEM_LIMIT, collective_id=collective_id, has_side_effects=True
        ),
    )(*host.views(arrays))


MLP_SLOT = 2.4
ATT_SLOT = 1.4


def mlp_back_kernel(layer, host, ranges, *refs):
    n = host.arrays
    dy_ref, h_ref, wo_ref, vec_ref, u_ref, up0_ref, up1_ref, down0_ref, down1_ref = refs[:9]
    srcs = refs[9 : 9 + n]
    du_ref, gbup_ref, dh_ref, dr_ref, do_ref, sums_ref = refs[9 + n : 15 + n]
    outs = refs[15 + n : 15 + 2 * n]
    acc = refs[15 + 2 * n]
    host.bind(srcs, outs, refs[16 + 2 * n :])
    step = pl.program_id(0)
    groups, _, width = do_ref.shape
    unit = FF // shards_of() // 2
    own = lax.axis_index("section") == layer

    @pl.when(step == 0)
    def _():
        host.begin()
        acc[...] = jnp.zeros_like(acc)

    def part(up_ref, down_ref):
        d_gated = mm_nt(dy_ref[...], down_ref[...])
        upper = u_ref[...]
        square = upper * upper
        turn = jnp.tanh(GELU_A * upper * (1.0 + GELU_B * square))
        slope = 0.5 * (1.0 + turn) + (0.5 * GELU_A) * upper * (1.0 - turn * turn) * (
            1.0 + (3.0 * GELU_B) * square
        )
        d_upper = (d_gated * slope).astype(BF16)
        put_halves(du_ref, d_upper, unit)
        gbup_ref[...] = jnp.sum(d_upper.astype(F32), axis=0, keepdims=True)
        acc[...] += mm_nt(d_upper, up_ref[...])

    pl.when(own)(lambda: part(up0_ref, down0_ref))
    pl.when(jnp.logical_not(own))(lambda: part(up1_ref, down1_ref))

    for slot, (first, last) in enumerate(ranges[:-1]):
        if last > first:
            pl.when(step == slot)(functools.partial(host.run, first, last))

    @pl.when(step == pl.num_programs(0) - 1)
    def _():
        normal, inverse = norm_stats(h_ref[...])
        d_out = dy_ref[...].astype(F32)
        d_normed = acc[...]
        sums_ref[...] = jnp.zeros_like(sums_ref)
        sums_ref[0:1, :] = jnp.sum(d_normed * normal, axis=0, keepdims=True)
        sums_ref[1:2, :] = jnp.sum(d_normed, axis=0, keepdims=True)
        d_normal = d_normed * vec_ref[1:2, :]
        d_hidden = d_out + inverse * (
            d_normal
            - jnp.mean(d_normal, axis=-1, keepdims=True)
            - normal * jnp.mean(d_normal * normal, axis=-1, keepdims=True)
        )
        dh_ref[...] = d_hidden
        d_branch = d_hidden.astype(BF16)
        dr_ref[...] = d_branch
        sums_ref[2:3, :] = jnp.sum(d_branch.astype(F32), axis=0, keepdims=True)
        sums_ref[3:4, :] = jnp.sum(d_out, axis=0, keepdims=True)
        for group in range(groups):
            do_ref[group] = mm_nt(
                d_branch, wo_ref[group * width : (group + 1) * width, :]
            ).astype(BF16)
        host.run(*ranges[-1])
        host.finish()


def mlp_back_call(layer, dy, hidden, wo, vecs, upper, ups, downs, groups, host, arrays, total):
    rows = dy.shape[0]
    width = D // groups
    whole = lambda i: (0, 0)
    mine = lambda i, first: jnp.where((lax.axis_index("section") == layer) == first, i, 0)
    col = lambda first: (lambda i: (0, mine(i, first)))
    line = lambda first: (lambda i: (mine(i, first), 0))
    chunk = lambda i: (0, i)
    ranges = host.slots([MLP_SLOT * (i + 1) for i in range(NCH)], total)
    return pl.pallas_call(
        functools.partial(mlp_back_kernel, layer, host, ranges),
        grid=(NCH,),
        in_specs=[
            pl.BlockSpec((rows, D), whole),
            pl.BlockSpec((rows, D), whole),
            pl.BlockSpec((D, D), whole),
            pl.BlockSpec((8, D), whole),
            pl.BlockSpec((rows, FC), chunk),
            pl.BlockSpec((D, FC), col(True)),
            pl.BlockSpec((D, FC), col(False)),
            pl.BlockSpec((FC, D), line(True)),
            pl.BlockSpec((FC, D), line(False)),
        ]
        + host.in_specs(),
        out_specs=[
            pl.BlockSpec((2, rows, FC // 2), lambda i: (0, 0, i)),
            pl.BlockSpec((1, FC), chunk),
            pl.BlockSpec((rows, D), whole),
            pl.BlockSpec((rows, D), whole),
            pl.BlockSpec((groups, rows, width), lambda i: (0, 0, 0)),
            pl.BlockSpec((8, D), whole),
        ]
        + host.out_specs(),
        scratch_shapes=[pltpu.VMEM((rows, D), F32)] + host.scratch(),
        out_shape=[
            jax.ShapeDtypeStruct((2, rows, FF // 2), BF16),
            jax.ShapeDtypeStruct((1, FF), F32),
            jax.ShapeDtypeStruct((rows, D), F32),
            jax.ShapeDtypeStruct((rows, D), BF16),
            jax.ShapeDtypeStruct((groups, rows, width), BF16),
            jax.ShapeDtypeStruct((8, D), F32),
        ]
        + host.out_shapes(),
        compiler_params=pltpu.CompilerParams(
            vmem_limit_bytes=VMEM_LIMIT, collective_id=layer, has_side_effects=True
        ),
    )(dy, hidden, wo, vecs, upper, ups[0], ups[1], downs[0], downs[1], *host.views(arrays))


def attend_back_kernel(host, ranges, *refs):
    n = host.arrays
    q_ref, do_ref, k_ref, v_ref, lse_ref, mask_ref = refs[:6]
    srcs = refs[6 : 6 + n]
    dj_ref, sums_ref = refs[6 + n : 8 + n]
    outs = refs[8 + n : 8 + 2 * n]
    dk_acc, dv_acc = refs[8 + 2 * n : 10 + 2 * n]
    host.bind(srcs, outs, refs[10 + 2 * n :])
    step = pl.program_id(0)
    width = q_ref.shape[1]
    heads = width // DH
    scale = DH ** (-0.5)

    @pl.when(step == 0)
    def _():
        host.begin()
        dk_acc[...] = jnp.zeros_like(dk_acc)
        dv_acc[...] = jnp.zeros_like(dv_acc)
        sums_ref[...] = jnp.zeros_like(sums_ref)

    q = q_ref[...]
    grad = do_ref[...]
    keys = k_ref[...]
    values = v_ref[...]
    mask = mask_ref[...]
    totals = lse_ref[...]
    d_q = jnp.zeros((BQ, width), F32)
    for head in range(heads):
        mine = head_lanes((BQ, width), head)
        q_head = jnp.where(mine, q, jnp.zeros_like(q))
        grad_head = jnp.where(mine, grad, jnp.zeros_like(grad))
        scores = mm_nt(q_head, keys) * SCALE2 + mask
        probs = jnp.exp2(scores - totals[:, head : head + 1])
        d_probs = mm_nt(grad_head, values)
        term = jnp.sum(probs * d_probs, axis=-1, keepdims=True)
        d_scores = (probs * (d_probs - term)).astype(BF16)
        dv_acc[...] += mm_tn(probs.astype(BF16), grad_head)
        dk_acc[...] += mm_tn(d_scores, q_head)
        d_q = jnp.where(mine, mm(d_scores, keys), d_q)
        for slot, (first, last) in enumerate(ranges[:-1]):
            if last > first and slot % heads == head:
                pl.when(step == slot // heads)(functools.partial(host.run, first, last))
    low = (d_q * scale).astype(BF16)
    dj_ref[pl.ds(pl.multiple_of(step * BQ, BQ), BQ), :width] = low
    sums_ref[0:1, :] += jnp.sum(low.astype(F32), axis=0, keepdims=True)

    @pl.when(step == pl.num_programs(0) - 1)
    def _():
        dj_ref[:, width : 2 * width] = (dk_acc[...] * scale).astype(BF16)
        low_v = dv_acc[...].astype(BF16)
        dj_ref[:, 2 * width :] = low_v
        sums_ref[1:2, :] = jnp.sum(low_v.astype(F32), axis=0, keepdims=True)
        host.run(*ranges[-1])
        host.finish()


def attend_back_call(q, d_o, k, v, lse, mask, host, arrays, total, collective_id):
    length, width = q.shape
    row = lambda i: (i, 0)
    whole = lambda i: (0, 0)
    slots = length // BQ * (width // DH)
    ranges = host.slots([ATT_SLOT * (i + 1) for i in range(slots)], total)
    return pl.pallas_call(
        functools.partial(attend_back_kernel, host, ranges),
        grid=(length // BQ,),
        in_specs=[
            pl.BlockSpec((BQ, width), row),
            pl.BlockSpec((BQ, width), row),
            pl.BlockSpec((length, width), whole),
            pl.BlockSpec((length, width), whole),
            pl.BlockSpec((BQ, 128), row),
            pl.BlockSpec((1, length), whole),
        ]
        + host.in_specs(),
        out_specs=[
            pl.BlockSpec((length, 3 * width), whole),
            pl.BlockSpec((8, width), whole),
        ]
        + host.out_specs(),
        out_shape=[
            jax.ShapeDtypeStruct((length, 3 * width), BF16),
            jax.ShapeDtypeStruct((8, width), F32),
        ]
        + host.out_shapes(),
        scratch_shapes=[pltpu.VMEM((length, width), F32), pltpu.VMEM((length, width), F32)]
        + host.scratch(),
        compiler_params=pltpu.CompilerParams(
            vmem_limit_bytes=VMEM_LIMIT, collective_id=collective_id, has_side_effects=True
        ),
    )(q, d_o, k, v, lse, mask, *host.views(arrays))


def swap(value, axis, mask):
    count = lax.axis_size(axis)
    return lax.ppermute(value, axis, [(i, i ^ mask) for i in range(count)])


def take(value, index, dim):
    return lax.dynamic_index_in_dim(value, index, dim, keepdims=False)


def ordered(bit, mine, other, dim):
    return jnp.where(
        bit == 0,
        jnp.stack([mine, other], axis=dim),
        jnp.stack([other, mine], axis=dim),
    )


def key_bias(counts, rotate):
    places = jnp.arange(LEN, dtype=jnp.int32)
    places = jnp.where(rotate, (places + LEN // 2) % LEN, places)
    offset = jnp.maximum(places - TRI, 0)
    view_index = offset // VSLOT
    inside = offset - view_index * VSLOT
    match = view_index[:, None] == jnp.arange(VIEWS, dtype=jnp.int32)[None, :]
    limits = jnp.sum(jnp.where(match, counts[None, :], 0), axis=1)
    valid = (places < TRI) | (inside < limits)
    return jnp.where(valid, 0.0, -1e30).astype(F32)[None, :]


def shards(
    inputs,
    cotangent,
    view_tokens,
    ln1_gain,
    ln1_bias,
    w_qkv,
    b_query,
    b_value,
    w_out,
    b_out,
    ln2_gain,
    ln2_bias,
    w_up,
    b_up,
    w_down,
    b_down,
):
    core = lax.axis_index("section")
    place = lax.axis_index("seq")
    dp_index = lax.axis_index("dp")
    count = lax.axis_size("seq")
    dp_count = lax.axis_size("dp")
    groups = dp_count * count
    half = count // 2
    micro = place // half
    low = place % half
    low_bits = half.bit_length() - 1
    rows = inputs.shape[2]
    width = D // count
    rank = core * half + low

    def swap_core(value):
        return swap(value, "section", 1)

    def swap_seq(value, bit):
        return swap(value, "seq", 1 << bit)

    def low_bit(bit):
        return (place >> bit) & 1

    def own_rows(local):
        chunks = local[:, 0]
        far = lax.ppermute(
            take(chunks, 1 - micro, 0),
            ("section", "seq"),
            [(count + z, count + (z ^ half)) for z in range(count)],
        )
        return jnp.where(core == 0, take(chunks, micro, 0), far)

    def gather_rows(own):
        value = own[None]
        for bit in range(low_bits):
            other = swap_seq(value, bit)
            value = ordered(low_bit(bit), value, other, 0).reshape((-1,) + own.shape)
        value = ordered(core, value, swap_core(value), 0)
        return value.reshape((-1,) + own.shape[1:])

    def exchange(value):
        tail = value.shape[1:]
        value = value.reshape((2,) * (low_bits + 1) + tail)
        for bit in range(low_bits):
            dim = low_bits - bit
            mine = take(value, low_bit(bit), dim)
            other = swap_seq(take(value, 1 - low_bit(bit), dim), bit)
            value = ordered(low_bit(bit), mine, other, dim)
        mine = take(value, core, 0)
        other = swap_core(take(value, 1 - core, 0))
        return ordered(core, mine, other, 0).reshape((count,) + tail)

    def to_section(own, layer):
        first = own
        if layer == 1:
            first = lax.ppermute(
                own, ("section", "seq"), [(z, count + z) for z in range(count)]
            )
        second = lax.ppermute(
            own,
            ("section", "seq"),
            [(count + z, layer * count + (z ^ half)) for z in range(count)],
        )
        return ordered(micro, first, second, 0)

    def both_vectors(value):
        return jnp.stack([value, value])

    vectors = jnp.concatenate(
        [v[0].astype(F32) for v in (ln1_gain, ln1_bias, b_query, b_value, b_out, ln2_gain, ln2_bias, b_down, b_up)]
    )
    vector_pair = ordered(core, vectors, swap_core(vectors), 0)

    def vector(layer, index):
        size = FF if index == 8 else D
        return vector_pair[layer, index * D : index * D + size]

    compact = half == 2 and D // groups == DH
    span = half * width

    def joint_of(which):
        wide = lax.dynamic_slice_in_dim(
            w_qkv[0].reshape(D, 3, 2, span), which, 1, 2
        ).reshape(D, 3, span)
        source = jnp.arange(span)[:, None]
        target = jnp.arange(width)[None, :]
        if compact:
            wanted = (2 * (target // DH) + low) * DH + target % DH
        else:
            wanted = low * width + target
        pick = (source == wanted).astype(BF16)
        return lax.dot_general(
            wide, pick, (((2,), (0,)), ((), ())), preferred_element_type=F32
        ).astype(BF16).reshape(D, 3 * width)

    def vector_of(value):
        wide = lax.dynamic_slice_in_dim(value, core * span, span)
        if compact:
            return take(wide.reshape(-1, 2, DH), low, 1).reshape(width)
        return lax.dynamic_slice_in_dim(wide, low * width, width)

    def vector_to(value):
        if compact:
            wide = jnp.stack(
                [jnp.where(low == i, value.reshape(-1, DH), 0.0) for i in range(2)], axis=1
            )
        else:
            wide = jnp.stack([jnp.where(low == i, value, 0.0) for i in range(half)], axis=0)
        wide = wide.reshape(span)
        return jnp.concatenate([jnp.where(core == i, wide, 0.0) for i in range(2)])

    def rank_rows(value):
        if compact:
            value = value.reshape(2, width // DH, 2, DH, D)
            return jnp.swapaxes(value, 1, 2).reshape(D, D)
        return value

    joint_mine = joint_of(core)
    joint_other = swap_core(joint_of(1 - core))
    out_mine = rank_rows(w_out[0])
    out_other = swap_core(out_mine)
    up_other = swap_core(w_up[0])
    down_other = swap_core(w_down[0])
    ups = (w_up[0], up_other)
    downs = (w_down[0], down_other)

    bias_mask = key_bias(take(view_tokens[:, 0], micro, 0), micro == 1)

    saved = []
    layer_in = own_rows(inputs)
    acts = []
    for layer in range(2):
        sel = jnp.where(core == layer, 0, 1).astype(jnp.int32)[None]
        w_joint = jnp.where(core == layer, joint_mine, joint_other)
        w_proj = jnp.where(core == layer, out_mine, out_other)
        zero = jnp.zeros((width,), F32)
        bias = jnp.concatenate([vector_of(vector(layer, 2)), zero, vector_of(vector(layer, 3))])
        vecs = jnp.concatenate(
            [
                jnp.stack([vector(layer, 4), vector(layer, 5), vector(layer, 6), vector(layer, 7)]),
                jnp.zeros((4, D), F32),
            ]
        )
        x_all = gather_rows(layer_in)
        a1, q, k, v = qkv_call(
            x_all, w_joint, bias[None], vector(layer, 0)[None], vector(layer, 1)[None]
        )
        mixed, lse = attend_call(q, k, v, bias_mask)
        o_own = exchange(mixed.reshape(count, rows, width))
        hidden, a2, upper, gated, output = mlp_call(
            sel, o_own, layer_in, w_proj, vecs, vector(layer, 8)[None], ups, downs
        )
        acts.append(output)
        saved.append(
            (sel, w_joint, w_proj, vecs, layer_in, a1, q, k, v, lse, o_own, hidden, a2, upper, gated)
        )
        layer_in = output

    dp_bits = dp_count.bit_length() - 1
    seq_bits = count.bit_length() - 1
    bits = [("dp", dp_bits - 1 - i) for i in range(dp_bits)]
    bits += [("seq", seq_bits - 1 - i) for i in range(seq_bits)]
    dp_dims = list(range(dp_bits))
    seq_dims = list(range(dp_bits, dp_bits + seq_bits))[::-1]
    orders = (
        dp_dims[::-1] + seq_dims,
        dp_dims + seq_dims,
        seq_dims[:1] + dp_dims + seq_dims[1:],
        seq_dims[:1] + dp_dims[::-1] + seq_dims[1:],
    )

    def reduce_one(value, order):
        tail = value.shape[1:]
        value = value.reshape((2,) * len(bits) + tail)
        left = list(range(len(bits)))
        for dim in order:
            axis, bit = bits[dim]
            index = (lax.axis_index(axis) >> bit) & 1
            at = left.index(dim)
            left.remove(dim)
            other = swap(take(value, 1 - index, at), axis, 1 << bit)
            total = take(value, index, at).astype(F32) + other.astype(F32)
            value = total.astype(value.dtype) if left else total
        return value

    def both_halves(value):
        return jnp.concatenate([take(value, core, 0), swap_core(take(value, 1 - core, 0))], axis=0)

    def joined(mine, other):
        return jnp.concatenate([mine, other], axis=0)

    def hosted(*arrays):
        shapes = []
        for array in arrays:
            shapes.append((array.shape[1], array.shape[2], array.shape[0] != groups))
        return Hosted(dp_count, count, tuple(shapes)), arrays

    smalls = []
    results = [{}, {}]
    grads_in = []
    pending = None
    d_out = own_rows(cotangent)
    for layer in (1, 0):
        _, w_joint, w_proj, vecs, x_own, a1, q, k, v, lse, o_own, hidden, a2, upper, gated = saved[layer]
        gated_all = both_halves(gated)
        a2_all = joined(a2, swap_core(a2))
        d_out_all = joined(d_out, swap_core(d_out))
        g_down = mm_tn(d_out_all, gated_all).astype(BF16).reshape(groups, D // groups, FF // 2)
        host, arrays = hosted(g_down) if pending is None else hosted(*pending)
        d_upper, g_bup, d_hidden, d_branch, d_heads, sums_two, *reduced = mlp_back_call(
            layer, d_out, hidden, w_proj, vecs, upper, ups, downs, count, host, arrays, 32.0
        )
        if pending is None:
            results[layer]["down"] = reduced[0]
        else:
            results[1]["out"], results[1]["joint"] = reduced
        upper_all = both_halves(d_upper)
        g_up = mm_tn(upper_all, a2_all).astype(BF16).reshape(groups, FF // groups // 2, D)
        d_mixed = exchange(d_heads).reshape(LEN, width)
        host, arrays = hosted(g_up) if pending is None else hosted(g_down)
        d_joint, sums_qv, reduced = attend_back_call(
            q, d_mixed, k, v, lse, bias_mask, host, arrays, 32.0, 2 + layer
        )
        results[layer]["up" if pending is None else "down"] = reduced
        d_normed = mm_nt(d_joint, w_joint).astype(BF16).reshape((2,) * (low_bits + 1) + (rows, D))
        other = swap_core(take(d_normed, 1 - core, 0))
        mine = take(d_normed, core, 0)
        for bit in range(low_bits):
            total = (mine.astype(F32) + other.astype(F32)).astype(BF16)
            dim = low_bits - 1 - bit
            other = swap_seq(take(total, 1 - low_bit(bit), dim), bit)
            mine = take(total, low_bit(bit), dim)
        d_in, sums_one = norm_back_call(mine, other, x_own, d_hidden, vector(layer, 0)[None])
        o_split = o_own.reshape(2, half, rows, width)
        flat = lambda t: jnp.swapaxes(t, 0, 1).reshape(rows, half * width)
        o_all = joined(flat(take(o_split, core, 0)), swap_core(flat(take(o_split, 1 - core, 0))))
        branch_all = joined(d_branch, swap_core(d_branch))
        g_out = mm_tn(branch_all, o_all).astype(BF16).reshape(groups, D // groups, D // 2)
        g_joint = mm_tn(d_joint, a1).astype(BF16).reshape(3, width, 2, D // 2)
        g_joint = ordered(core, take(g_joint, core, 2), swap_core(take(g_joint, 1 - core, 2)), 1)
        if compact:
            g_joint = g_joint.reshape(groups // 2, 3 * D // groups, D // 2)
        else:
            spread = jnp.stack(
                [jnp.where(low == i, g_joint, jnp.zeros_like(g_joint)) for i in range(half)], axis=2
            )
            g_joint = spread.reshape(groups, 3 * D // groups, D // 2)
        if pending is None:
            pending = (g_out, g_joint)
        else:
            host, arrays = hosted(g_up, g_out, g_joint)
            results[layer]["up"], results[layer]["out"], results[layer]["joint"] = reduce_call(
                host, arrays, 4
            )
        smalls.append(
            jnp.concatenate(
                [
                    piece.reshape(groups, -1)
                    for piece in (
                        sums_one[0],
                        sums_one[1],
                        vector_to(sums_qv[0]),
                        vector_to(sums_qv[1]),
                        sums_two[2],
                        sums_two[0],
                        sums_two[1],
                        g_bup[0],
                        sums_two[3],
                    )
                ],
                axis=1,
            )
        )
        grads_in.append(d_in)
        d_out = d_in

    grads_in = grads_in[::-1]
    small_pair = jnp.stack(smalls[::-1])
    small = take(small_pair, core, 0) + swap_core(take(small_pair, 1 - core, 0))
    small = reduce_one(small, orders[0])

    acts_rows = jnp.where(core == 0, to_section(acts[0], 0), to_section(acts[1], 1))
    grad_rows = jnp.where(core == 0, to_section(grads_in[0], 0), to_section(grads_in[1], 1))

    def choose(name):
        return jnp.where(core == 0, results[0][name], results[1][name])

    r_down = choose("down").reshape(2, D // groups, groups, FF // groups // 2)
    g_w_down = jnp.transpose(r_down, (2, 0, 3, 1)).reshape(FF, D // groups)
    r_out = choose("out")
    if compact:
        r_out = r_out.reshape(2, D // groups, 2, width // DH, DH)
        g_w_out = jnp.transpose(r_out, (0, 3, 2, 4, 1)).reshape(D, D // groups)
    else:
        g_w_out = jnp.swapaxes(r_out, 1, 2).reshape(D, D // groups)
    r_joint = choose("joint")
    if compact:
        r_joint = r_joint.reshape(2, 4, DH, D // 2)
        r_joint = jnp.where(
            low == 0,
            jnp.stack([r_joint[:, 0], r_joint[:, 3], r_joint[:, 1]], axis=1),
            jnp.stack([r_joint[:, 1], r_joint[:, 3], r_joint[:, 2]], axis=1),
        ).reshape(2, 3 * DH, D // 2)
    g_w_qkv = jnp.swapaxes(r_joint, 1, 2).reshape(D, 3 * D // groups)
    r_up = choose("up")
    g_w_up = jnp.transpose(r_up, (2, 0, 1)).reshape(D, FF // groups)

    unit = D // groups
    pieces = []
    start = 0
    for size in (unit, unit, unit, unit, unit, unit, unit, FF // groups, unit):
        pieces.append(small[start : start + size])
        start += size
    g_ln1g, g_ln1b, g_bq, g_bv, g_bo, g_ln2g, g_ln2b, g_bup, g_bd = pieces
    outs = (
        g_ln1g,
        g_ln1b,
        g_w_qkv,
        g_bq,
        g_bv,
        g_w_out,
        g_bo,
        g_ln2g,
        g_ln2b,
        g_w_up,
        g_bup,
        g_w_down,
        g_bd,
    )
    return (acts_rows[None, :, None], grad_rows[None, :, None]) + tuple(g[None] for g in outs)


def solution(mesh):
    rows = P(None, "dp", "seq", None)
    vector = P("section", None)
    matrix = P("section", None, None)
    placed = (
        rows,
        rows,
        P(None, "dp", None),
        vector,
        vector,
        matrix,
        vector,
        vector,
        matrix,
        vector,
        vector,
        vector,
        matrix,
        vector,
        matrix,
        vector,
    )
    both = P("section", None, "dp", "seq", None)
    line = P("section", ("dp", "seq"))
    table = P("section", None, ("dp", "seq"))
    return jax.shard_map(
        shards,
        mesh=mesh,
        in_specs=placed,
        out_specs=(
            both,
            both,
            line,
            line,
            table,
            line,
            line,
            table,
            line,
            line,
            line,
            table,
            line,
            table,
            line,
        ),
        check_vma=False,
    )
```

```python
import functools
import math

import jax
import jax.numpy as jnp
from jax import lax
from jax.experimental import pallas as pl
from jax.experimental.pallas import tpu as pltpu
from jax.sharding import PartitionSpec as P

D = 1024
H = 16
DH = 64
FF = 4096
VIEWS = 6
TRI = 512
VSLOT = 128
MICRO = 2
LEN = 1280
BQ = 256
NCH = 8
FC = FF // NCH
SCALE2 = DH ** (-0.5) * math.log2(math.e)
F32 = jnp.float32
BF16 = jnp.bfloat16
VMEM_LIMIT = 56 * 2**20


def params():
    return pltpu.CompilerParams(vmem_limit_bytes=VMEM_LIMIT)


def mm(a, b):
    return lax.dot_general(a, b, (((1,), (0,)), ((), ())), preferred_element_type=F32)


def mm_nt(a, b):
    return lax.dot_general(a, b, (((1,), (1,)), ((), ())), preferred_element_type=F32)


def mm_tn(a, b):
    return lax.dot_general(a, b, (((0,), (0,)), ((), ())), preferred_element_type=F32)


def norm_stats(values):
    average = jnp.mean(values, axis=-1, keepdims=True)
    centered = values - average
    variance = jnp.mean(centered * centered, axis=-1, keepdims=True)
    inverse = lax.rsqrt(variance + 1e-05)
    return centered * inverse, inverse


def head_lanes(shape, head):
    lane = lax.broadcasted_iota(jnp.int32, shape, 1)
    return (lane >= head * DH) & (lane < (head + 1) * DH)


def shards_of():
    return lax.axis_size("dp") * lax.axis_size("seq")


def put_halves(ref, value, unit):
    for at in range(value.shape[1] // unit):
        ref[at % 2, :, at // 2 * unit : (at // 2 + 1) * unit] = value[:, at * unit : (at + 1) * unit]


GELU_A = math.sqrt(2.0 / math.pi)
GELU_B = 0.044715


MESH_AXES = ("dp", "seq")


def axis_bits(dp_count, count):
    bits = []
    for axis, size in (("dp", dp_count), ("seq", count)):
        mask = size // 2
        while mask:
            bits.append((axis, mask))
            mask //= 2
    return bits


def stream_orders(dp_count, count):
    dp_bits = dp_count.bit_length() - 1
    seq_bits = count.bit_length() - 1
    dp_dims = list(range(dp_bits))
    seq_dims = list(range(dp_bits, dp_bits + seq_bits))[::-1]
    return (
        dp_dims[::-1] + seq_dims,
        dp_dims + seq_dims,
        seq_dims[:1] + dp_dims + seq_dims[1:],
        seq_dims[:1] + dp_dims[::-1] + seq_dims[1:],
    )


def my_bit(axis, mask):
    return lax.rem(lax.div(lax.axis_index(axis), mask), 2)


def partner(axis, mask):
    return lax.axis_index(axis) + mask * (1 - 2 * my_bit(axis, mask))


def greet(bits):
    barrier = pltpu.get_barrier_semaphore()
    for axis, mask in bits:
        pl.semaphore_signal(
            barrier,
            inc=1,
            device_id={axis: partner(axis, mask)},
            device_id_type=pl.DeviceIdType.MESH,
        )
    pl.semaphore_wait(barrier, len(bits))


class Reducer:
    def __init__(self, bits, order, src, cols, out, rows, compact, buffers, sems):
        self.bits, self.order, self.src, self.cols = bits, order, src, cols
        self.out, self.out_cols, self.buffers, self.sems = out, cols, buffers, sems
        self.count, self.rows, self.compact = len(bits), rows, compact

    @staticmethod
    def scratch(count, rows, width):
        shapes = [pltpu.VMEM((2,) * (count - 1) + (rows, width), BF16)]
        for stage in range(count):
            shapes.append(pltpu.VMEM((2,) * (count - 1 - stage) + (rows, width), BF16))
        shapes += [
            pltpu.SemaphoreType.DMA((count + 2,)),
            pltpu.SemaphoreType.DMA((count + 2,)),
            pltpu.SemaphoreType.DMA,
        ]
        return shapes

    def place(self, stage):
        left = [d for d in range(self.count) if d not in self.order[:stage]]
        dim = self.order[stage]
        return left, left.index(dim), self.bits[dim]

    def cut(self, stage, index):
        left, at, _ = self.place(stage)
        where = [slice(None)] * len(left)
        where[at] = index
        return tuple(where)

    def source(self, stage):
        if stage == 0:
            return self.src
        return self.buffers[0] if stage == 1 else self.buffers[stage]

    def copy(self, stage):
        axis, mask = self.place(stage)[2]
        where = self.cut(stage, 1 - my_bit(axis, mask))
        if stage == 0:
            where = where + (slice(None), pl.ds(*self.cols))
        return pltpu.make_async_remote_copy(
            src_ref=self.source(stage).at[where],
            dst_ref=self.buffers[stage + 1],
            send_sem=self.sems[0].at[stage],
            recv_sem=self.sems[1].at[stage],
            device_id={axis: partner(axis, mask)},
            device_id_type=pl.DeviceIdType.MESH,
        )

    def load(self):
        axis, mask = self.place(0)[2]
        where = self.cut(0, my_bit(axis, mask)) + (slice(None), pl.ds(*self.cols))
        return pltpu.make_async_copy(self.src.at[where], self.buffers[0], self.sems[2])

    def share(self):
        core = lax.axis_index("section")
        return pltpu.make_async_remote_copy(
            src_ref=self.out.at[core, :, pl.ds(*self.out_cols)],
            dst_ref=self.out.at[core, :, pl.ds(*self.out_cols)],
            send_sem=self.sems[0].at[self.count],
            recv_sem=self.sems[1].at[self.count],
            device_id={"section": 1 - core},
            device_id_type=pl.DeviceIdType.MESH,
        )

    def trade(self):
        third = self.rows // 3
        core = lax.axis_index("section")
        bit = lax.rem(lax.axis_index("seq"), 2)
        row = pl.multiple_of((1 - bit) * 2 * third, third)
        return pltpu.make_async_remote_copy(
            src_ref=self.out.at[core, pl.ds(row, third), pl.ds(*self.out_cols)],
            dst_ref=self.out.at[core, pl.ds(self.rows, third), pl.ds(*self.out_cols)],
            send_sem=self.sems[0].at[self.count + 1],
            recv_sem=self.sems[1].at[self.count + 1],
            device_id={"seq": partner("seq", 1)},
            device_id_type=pl.DeviceIdType.MESH,
        )

    def begin(self):
        self.copy(0).start()
        self.load().start()

    def step(self, stage):
        left, at, (axis, mask) = self.place(stage)
        bit = my_bit(axis, mask)
        if stage == 0:
            self.load().wait()
        self.copy(stage).wait_recv()
        got = self.buffers[stage + 1]
        rows = got.shape[-2]
        chunk = rows
        while chunk * got.shape[-1] > 65536 and chunk % 32 == 0:
            chunk //= 2
        per = rows // chunk
        last = stage == self.count - 1
        core = lax.axis_index("section")
        total = 2 ** (len(left) - 1)

        def body(i, carry):
            flat = lax.div(i, per)
            row = pl.multiple_of(lax.rem(i, per) * chunk, chunk)
            index = []
            for j in range(len(left) - 1):
                index.append(lax.rem(lax.div(flat, 2 ** (len(left) - 2 - j)), 2))
            there = tuple(index) + (pl.ds(row, chunk), slice(None))
            if stage == 0:
                mine = self.buffers[0][there]
            else:
                own = index[:at] + [bit] + index[at:]
                mine = self.source(stage)[tuple(own) + (pl.ds(row, chunk), slice(None))]
            value = mine.astype(F32) + got[there].astype(F32)
            if last:
                self.out[core, pl.ds(row, chunk), pl.ds(*self.out_cols)] = value
            elif stage == 0:
                self.buffers[0][there] = value.astype(BF16)
            else:
                got[there] = value.astype(BF16)
            return carry

        lax.fori_loop(0, total * per, body, 0)
        if not last:
            self.copy(stage + 1).start()
        elif self.compact:
            self.trade().start()
        else:
            self.share().start()

    def tail(self):
        if self.compact:
            self.trade().wait()
            self.share().start()

    def finish(self):
        for stage in range(self.count):
            self.copy(stage).wait_send()
        self.share().wait()


def part_widths(width):
    unit = 128 if width % 128 == 0 else width
    tiles = width // unit
    first = -(-tiles // 3)
    rest = tiles - 2 * first
    if rest <= 0:
        first = tiles // 2
        rest = tiles - 2 * first
    second = rest // 2
    return tuple(unit * n for n in (first, first, rest - second, second))


SPLIT = True
DELAY = True


class Hosted:
    def __init__(self, dp_count, count, shapes):
        self.dp_count, self.count, self.shapes = dp_count, count, shapes
        self.all_bits = axis_bits(dp_count, count)
        self.plan = []
        for index, (rows, width, compact) in enumerate(shapes):
            bits = self.all_bits[:-1] if compact else self.all_bits
            orders = stream_orders(dp_count, count)
            widths = part_widths(width)
            if compact:
                last = len(bits)
                orders = [tuple(d for d in order if d != last) for order in orders[:2]]
                widths = (width // 2, width // 2)
            start = 0
            for order, size in zip(orders, widths):
                pieces = [size] if size else []
                if size >= 256 and not compact and SPLIT:
                    first = 128 * -(-size // 256)
                    pieces = [first, size - first]
                for k, piece in enumerate(pieces):
                    self.plan.append((index, tuple(order), bits, start, piece, rows, compact, k))
                    start += piece
        self.plan.sort(key=lambda p: (p[0], p[7]))
        self.arrays = len(shapes)
        self.events = []
        for k, part in enumerate(self.plan):
            for stage in range(len(part[2])):
                order = 1.0 - 0.5**stage + 0.25 * part[7] + 0.02 * part[0]
                self.events.append((order, k, stage))
        self.events.sort()

    def views(self, arrays):
        out = []
        for array, (_, _, compact) in zip(arrays, self.shapes):
            depth = len(self.all_bits) - (1 if compact else 0)
            out.append(array.reshape((2,) * depth + array.shape[1:]))
        return out

    def in_specs(self):
        return [pl.BlockSpec(memory_space=pl.ANY)] * self.arrays

    def out_shapes(self):
        return [
            jax.ShapeDtypeStruct((2, rows + (rows // 3 if compact else 0), width), F32)
            for rows, width, compact in self.shapes
        ]

    def out_specs(self):
        return [pl.BlockSpec(memory_space=pltpu.VMEM)] * self.arrays

    def scratch(self):
        shapes = [pltpu.VMEM(o.shape, F32) for o in self.out_shapes()]
        for _, _, bits, _, size, rows, _, _ in self.plan:
            shapes += Reducer.scratch(len(bits), rows, size)
        return shapes

    def bind(self, srcs, outs, scratch):
        self.parts = []
        self.outs, self.sums = outs, scratch[: self.arrays]
        at = self.arrays
        for index, order, bits, start, size, rows, compact, _ in self.plan:
            depth = len(bits) + 1
            mine = scratch[at : at + depth + 3]
            at += depth + 3
            self.parts.append(
                Reducer(
                    bits,
                    order,
                    srcs[index],
                    (start, size),
                    self.sums[index],
                    rows,
                    compact,
                    mine[:depth],
                    mine[depth:],
                )
            )
    def begin(self):
        for k, part in enumerate(self.parts):
            if not (DELAY and self.plan[k][7]):
                part.begin()

    def run(self, first, last):
        for _, k, stage in self.events[first:last]:
            self.parts[k].step(stage)
            if DELAY and stage == 0 and self.plan[k][7] == 0:
                for j, other in enumerate(self.plan):
                    if other[:2] == self.plan[k][:2] and other[7] == 1:
                        self.parts[j].begin()

    def slots(self, times, total):
        edges = []
        done = 0
        for time in times:
            while done < len(self.events) and self.expected(done) * total <= time:
                done += 1
            edges.append(done)
        edges[-1] = len(self.events)
        return list(zip([0] + edges[:-1], edges))

    def expected(self, event):
        _, k, stage = self.events[event]
        late = self.plan[k][7]
        return min(1.0, 0.3 + 0.25 * late + 0.5 * (1.0 - 0.5**stage))

    def finish(self):
        for part in self.parts:
            part.tail()
        for part in self.parts:
            part.finish()
        for out, value in zip(self.outs, self.sums):
            out[...] = value[...]


def reduce_kernel(host, *refs):
    n = host.arrays
    host.bind(refs[:n], refs[n : 2 * n], refs[2 * n :])
    greet(host.all_bits + [("section", 1)])
    host.begin()
    host.run(0, len(host.events))
    host.finish()


def reduce_call(host, arrays, collective_id):
    return pl.pallas_call(
        functools.partial(reduce_kernel, host),
        in_specs=host.in_specs(),
        out_specs=host.out_specs(),
        out_shape=host.out_shapes(),
        scratch_shapes=host.scratch(),
        compiler_params=pltpu.CompilerParams(
            vmem_limit_bytes=VMEM_LIMIT, collective_id=collective_id, has_side_effects=True
        ),
    )(*host.views(arrays))


MLP_SLOT = 2.9
ATT_SLOT = 1.4


class Group:
    def __init__(self):
        self.half = lax.axis_size("seq") // 2
        self.core = lax.axis_index("section")
        self.place = lax.axis_index("seq")
        self.low = lax.rem(self.place, self.half)
        self.base = self.place - self.low
        self.rank = self.core * self.half + self.low

    def others(self):
        pairs = [(dc, d) for d in range(1, self.half) for dc in (0, 1)]
        return pairs + [(1, 0)]

    def slot(self, dc, d):
        return dc * self.half + d

    def where(self, dc, d):
        core = lax.rem(self.core + dc, 2)
        low = lax.rem(self.low + d, self.half)
        return core, low

    def device(self, dc, d):
        core, low = self.where(dc, d)
        return {"section": core, "seq": self.base + low}

    def rank_of(self, dc, d):
        core, low = self.where(dc, d)
        return core * self.half + low

    def greet(self, dp_count):
        barrier = pltpu.get_barrier_semaphore()
        targets = [self.device(dc, d) for dc, d in self.others()]
        mask = dp_count // 2
        while mask:
            targets.append({"dp": partner("dp", mask)})
            mask //= 2
        targets.append({"seq": partner("seq", self.half)})
        for target in targets:
            pl.semaphore_signal(
                barrier, inc=1, device_id=target, device_id_type=pl.DeviceIdType.MESH
            )
        pl.semaphore_wait(barrier, len(targets))


def send(src, dst, sems, slot, device):
    return pltpu.make_async_remote_copy(
        src_ref=src,
        dst_ref=dst,
        send_sem=sems[0].at[slot],
        recv_sem=sems[1].at[slot],
        device_id=device,
        device_id_type=pl.DeviceIdType.MESH,
    )


def dma_pair(count):
    return [pltpu.SemaphoreType.DMA((count,)), pltpu.SemaphoreType.DMA((count,))]


VEC_ROWS = 16
LN1_GAIN, LN1_BIAS, B_QUERY, B_VALUE, B_OUT, LN2_GAIN, LN2_BIAS, B_DOWN, B_UP = range(9)


def attend_kernel(first, layer, dp_count, *refs):
    if first:
        x_ref, joint_ref, wout_ref, mask_ref = refs[:4]
        vectors = refs[4:13]
        o_out, lse_out, a_out, q_out, k_out, v_out = refs[13:19]
        x_out, joint_out, wout_out, vec_out = refs[19:23]
        rest = refs[23:]
    else:
        x_ref, joint_ref, mask_ref, vec_ref = refs[:4]
        o_out, lse_out, a_out, q_out, k_out, v_out = refs[4:10]
        rest = refs[10:]
    x_all, a_all, q_all, k_all, v_all, lse, o_send, o_recv = rest[:8]
    x_sems, o_sems = rest[8:10], rest[10:12]
    out_sems = rest[12]
    if first:
        joint_pair, wide_own, wide_other, vec_send, vec_recv, vec_pair = rest[13:19]
        wide_sems, vec_sems = rest[19:21], rest[21:23]
        load_sems = rest[23]
    else:
        joint_one = rest[13]
        load_sems = rest[14]
    group = Group()
    core, half, rank, low = group.core, group.half, group.rank, group.low
    ranks, rows, _ = x_all.shape
    width = q_all.shape[1]
    heads = width // DH
    span = half * width
    partner_core = group.device(1, 0)
    micro = lax.div(group.place, half)

    group.greet(dp_count)

    def x_copy(slot, from_rank, device):
        return send(x_all.at[from_rank], x_all.at[from_rank], x_sems, slot, device)

    far = {"seq": partner("seq", half)}

    if first:
        own_load = pltpu.make_async_copy(x_ref.at[micro, 0], x_all.at[rank], load_sems.at[0])
        far_copy = send(x_ref.at[1 - micro, 0], x_all.at[rank], x_sems, 2 * half - 1, far)
        pl.when(core == 1)(lambda: far_copy.start())
        pl.when(core == 0)(lambda: own_load.start())
        wide_copies = []
        own_loads = []
        for part in range(3):
            theirs = pl.ds(pl.multiple_of(part * D + (1 - core) * span, 128), span)
            ours = pl.ds(pl.multiple_of(part * D + core * span, 128), span)
            wide_copies.append(
                send(joint_ref.at[0, :, theirs], wide_other.at[part], wide_sems, part, partner_core)
            )
            own_loads.append(
                pltpu.make_async_copy(
                    joint_ref.at[0, :, ours], wide_own.at[part], load_sems.at[1 + part]
                )
            )
            wide_copies[-1].start()
            own_loads[-1].start()
        vec_send[...] = jnp.zeros_like(vec_send)
        for i, value in enumerate(vectors[:8]):
            vec_send[i : i + 1, :] = value[...].astype(F32)
        for i in range(FF // D):
            vec_send[8 + i : 9 + i, :] = vectors[8][:, i * D : (i + 1) * D].astype(F32)
        vec_copy = send(vec_send, vec_recv, vec_sems, 0, partner_core)
        vec_copy.start()
        wout_copy = send(wout_ref.at[0], wout_out, vec_sems, 1, partner_core)
        pl.when(core == 1)(lambda: far_copy.wait_recv())
        pl.when(core == 0)(lambda: own_load.wait())
    else:
        own_load = pltpu.make_async_copy(x_ref, x_all.at[rank], load_sems.at[0])
        joint_load = pltpu.make_async_copy(joint_ref, joint_one, load_sems.at[1])
        own_load.start()
        joint_load.start()
        own_load.wait()
    for d in range(1, half):
        x_copy(d - 1, rank, group.device(0, d)).start()
    x_copy(half - 1, rank, partner_core).start()

    source = lax.broadcasted_iota(jnp.int32, (span, width), 0)
    target = lax.broadcasted_iota(jnp.int32, (span, width), 1)
    if half == 2:
        wanted = (2 * lax.div(target, DH) + low) * DH + lax.rem(target, DH)
    else:
        wanted = low * width + target
    pick = (source == wanted).astype(F32).astype(BF16)
    if first:
        wout_copy.start()
        vec_copy.wait_recv()
        vec_pair[core] = vec_send[...]
        vec_pair[1 - core] = vec_recv[...]
        for load in own_loads:
            load.wait()
        for part in range(3):
            joint_pair[core, :, part * width : (part + 1) * width] = mm(
                wide_own[part], pick
            ).astype(BF16)
        for copy in wide_copies:
            copy.wait_recv()
        for part in range(3):
            joint_pair[1 - core, :, part * width : (part + 1) * width] = mm(
                wide_other[part], pick
            ).astype(BF16)
        vec = vec_pair[0]
        weights = lambda: joint_pair[0]
    else:
        joint_load.wait()
        vec = vec_ref[0]
        weights = lambda: joint_one[...]

    def of_heads(row):
        parts = vec[row : row + 1, :]
        mine = jnp.where(core == 0, parts[:, :span], parts[:, span:])
        wide = jnp.broadcast_to(mine, (16, span)).astype(BF16)
        return mm(wide, pick)[0:1, :]

    bias_q = of_heads(B_QUERY)
    bias_v = of_heads(B_VALUE)
    gain = vec[LN1_GAIN : LN1_GAIN + 1, :]
    shift = vec[LN1_BIAS : LN1_BIAS + 1, :]

    def project(at):
        normal, _ = norm_stats(x_all[at].astype(F32))
        a = (normal * gain + shift).astype(BF16)
        here = pl.ds(pl.multiple_of(at * rows, 16), rows)
        a_all[here, :] = a
        joined = mm(a, weights())
        q_all[here, :] = (joined[:, :width] + bias_q).astype(BF16)
        k_all[here, :] = joined[:, width : 2 * width].astype(BF16)
        v_all[here, :] = (joined[:, 2 * width :] + bias_v).astype(BF16)

    project(rank)
    x_copy(half - 1, rank, partner_core).wait_recv()
    project(group.rank_of(1, 0))
    for d in range(1, half):
        here = group.rank_of(0, half - d)
        x_copy(d - 1, here, partner_core).wait_recv()
        x_copy(half - 1 + d, here, partner_core).start()
        project(here)
    for d in range(1, half):
        there = group.rank_of(1, half - d)
        x_copy(half - 1 + d, there, partner_core).wait_recv()
        project(there)

    saves = [
        pltpu.make_async_copy(a_all, a_out, out_sems.at[0]),
        pltpu.make_async_copy(q_all, q_out, out_sems.at[1]),
        pltpu.make_async_copy(k_all, k_out, out_sems.at[2]),
        pltpu.make_async_copy(v_all, v_out, out_sems.at[3]),
    ]
    if first:
        saves.append(pltpu.make_async_copy(joint_pair, joint_out, out_sems.at[4]))
        saves.append(pltpu.make_async_copy(x_all.at[rank], x_out, out_sems.at[5]))
        saves.append(pltpu.make_async_copy(vec_pair, vec_out, out_sems.at[6]))
    for save in saves:
        save.start()

    lane = lax.broadcasted_iota(jnp.int32, (rows, 128), 1)
    mask = mask_ref[...]

    def attend(at):
        here = pl.ds(pl.multiple_of(at * rows, 16), rows)
        q = q_all[here, :]
        mixed = jnp.zeros((rows, width), F32)
        totals = jnp.zeros((rows, 128), F32)
        for head in range(heads):
            mine = head_lanes((rows, width), head)
            scores = mm_nt(jnp.where(mine, q, jnp.zeros_like(q)), k_all[...]) * SCALE2 + mask
            top = jnp.max(scores, axis=-1, keepdims=True)
            expo = jnp.exp2(scores - top)
            total = jnp.sum(expo, axis=-1, keepdims=True)
            part = mm(expo.astype(BF16), v_all[...]) / total
            mixed = jnp.where(mine, part, mixed)
            totals = jnp.where(lane == head, top + jnp.log2(total), totals)
        lse[here, :] = totals
        return mixed.astype(BF16)

    copies = []
    for dc, d in group.others():
        slot = group.slot(dc, d)
        o_send[slot] = attend(group.rank_of(dc, d))
        copies.append(send(o_send.at[slot], o_recv.at[rank], o_sems, slot, group.device(dc, d)))
        copies[-1].start()
    o_recv[rank] = attend(rank)
    lse_out[...] = lse[...]
    for copy in copies:
        copy.wait()
    o_out[...] = o_recv[...]
    for save in saves:
        save.wait()
    for d in range(1, half):
        x_copy(d - 1, rank, group.device(0, d)).wait_send()
        x_copy(half - 1 + d, group.rank_of(0, half - d), partner_core).wait_send()
    x_copy(half - 1, rank, partner_core).wait_send()
    if first:
        pl.when(core == 1)(lambda: far_copy.wait_send())
        for copy in wide_copies:
            copy.wait_send()
        vec_copy.wait_send()
        wout_copy.wait()


def attend_call(first, layer, mask, ranks, dp_count, *args):
    rows = args[0].shape[-2]
    width = D // ranks
    half = ranks // 2
    span = half * width
    anywhere = pl.BlockSpec(memory_space=pl.ANY)
    vmem = pl.BlockSpec(memory_space=pltpu.VMEM)
    out_shape = [
        jax.ShapeDtypeStruct((ranks, rows, width), BF16),
        jax.ShapeDtypeStruct((LEN, 128), F32),
        jax.ShapeDtypeStruct((LEN, D), BF16),
        jax.ShapeDtypeStruct((LEN, width), BF16),
        jax.ShapeDtypeStruct((LEN, width), BF16),
        jax.ShapeDtypeStruct((LEN, width), BF16),
    ]
    out_specs = [vmem, vmem] + [anywhere] * 4
    scratch = [
        pltpu.VMEM((ranks, rows, D), BF16),
        pltpu.VMEM((LEN, D), BF16),
        pltpu.VMEM((LEN, width), BF16),
        pltpu.VMEM((LEN, width), BF16),
        pltpu.VMEM((LEN, width), BF16),
        pltpu.VMEM((LEN, 128), F32),
        pltpu.VMEM((ranks, rows, width), BF16),
        pltpu.VMEM((ranks, rows, width), BF16),
    ]
    scratch += dma_pair(2 * half) + dma_pair(ranks) + [pltpu.SemaphoreType.DMA((7,))]
    if first:
        operands = args[:3] + (mask,) + args[3:]
        in_specs = [anywhere] * 3 + [vmem] * (1 + len(args[3:]))
        out_shape += [
            jax.ShapeDtypeStruct((rows, D), BF16),
            jax.ShapeDtypeStruct((2, D, 3 * width), BF16),
            jax.ShapeDtypeStruct((D, D), BF16),
            jax.ShapeDtypeStruct((2, VEC_ROWS, D), F32),
        ]
        out_specs += [anywhere] * 4
        scratch += [
            pltpu.VMEM((2, D, 3 * width), BF16),
            pltpu.VMEM((3, D, span), BF16),
            pltpu.VMEM((3, D, span), BF16),
            pltpu.VMEM((VEC_ROWS, D), F32),
            pltpu.VMEM((VEC_ROWS, D), F32),
            pltpu.VMEM((2, VEC_ROWS, D), F32),
        ]
        scratch += dma_pair(3) + dma_pair(2) + [pltpu.SemaphoreType.DMA((4,))]
    else:
        operands = args[:2] + (mask,) + args[2:]
        in_specs = [anywhere] * 2 + [vmem] * 2
        scratch += [pltpu.VMEM((D, 3 * width), BF16), pltpu.SemaphoreType.DMA((2,))]
    return pl.pallas_call(
        functools.partial(attend_kernel, first, layer, dp_count),
        in_specs=in_specs,
        out_specs=out_specs,
        out_shape=out_shape,
        scratch_shapes=scratch,
        compiler_params=pltpu.CompilerParams(
            vmem_limit_bytes=VMEM_LIMIT, collective_id=5 + layer, has_side_effects=True
        ),
        cost_estimate=pl.CostEstimate(
            flops=40 * 10**9, bytes_accessed=20 * 2**20, transcendentals=LEN * LEN * width // DH
        ),
    )(*operands)


def mlp_kernel(
    layer,
    o_ref,
    x_ref,
    wo0_ref,
    wo1_ref,
    vec_ref,
    up0_ref,
    up1_ref,
    down0_ref,
    down1_ref,
    h_ref,
    a_ref,
    u_ref,
    g_ref,
    y_ref,
    acc,
    wo,
    sem,
):
    step = pl.program_id(0)
    groups, _, width = o_ref.shape
    unit = FF // shards_of() // 2
    own = lax.axis_index("section") == layer

    @pl.when(step == 0)
    def _():
        first = pltpu.make_async_copy(wo0_ref, wo, sem)
        second = pltpu.make_async_copy(wo1_ref, wo, sem)

        @pl.when(own)
        def _():
            first.start()
            first.wait()

        @pl.when(jnp.logical_not(own))
        def _():
            second.start()
            second.wait()

        hidden = x_ref[...].astype(F32) + vec_ref[0, B_OUT : B_OUT + 1, :]
        for group in range(groups):
            hidden += mm(o_ref[group], wo[group * width : (group + 1) * width, :])
        h_ref[...] = hidden
        normal, _ = norm_stats(hidden)
        a_ref[...] = (
            normal * vec_ref[0, LN2_GAIN : LN2_GAIN + 1, :] + vec_ref[0, LN2_BIAS : LN2_BIAS + 1, :]
        ).astype(BF16)
        acc[...] = hidden + vec_ref[0, B_DOWN : B_DOWN + 1, :]

    def part(up_ref, down_ref):
        at = pl.multiple_of(lax.rem(step, D // FC) * FC, FC)
        bias = vec_ref[0, pl.ds(B_UP + lax.div(step, D // FC), 1), pl.ds(at, FC)]
        upper = mm(a_ref[...], up_ref[...]) + bias
        u_ref[...] = upper
        inner = GELU_A * (upper + GELU_B * upper * upper * upper)
        gated = (0.5 * upper * (1.0 + jnp.tanh(inner))).astype(BF16)
        put_halves(g_ref, gated, unit)
        acc[...] += mm(gated, down_ref[...])

    pl.when(own)(lambda: part(up0_ref, down0_ref))
    pl.when(jnp.logical_not(own))(lambda: part(up1_ref, down1_ref))

    @pl.when(step == pl.num_programs(0) - 1)
    def _():
        y_ref[...] = acc[...].astype(BF16)


def mlp_call(layer, o_all, x_own, outs, vec, ups, downs):
    rows = x_own.shape[0]
    groups, _, width = o_all.shape
    whole = lambda i: (0, 0)
    mine = lambda i, first: jnp.where((lax.axis_index("section") == layer) == first, i, 0)
    col = lambda first: (lambda i: (0, mine(i, first)))
    line = lambda first: (lambda i: (mine(i, first), 0))
    chunk = lambda i: (0, i)
    return pl.pallas_call(
        functools.partial(mlp_kernel, layer),
        grid=(NCH,),
        in_specs=[
            pl.BlockSpec((groups, rows, width), lambda i: (0, 0, 0)),
            pl.BlockSpec((rows, D), whole),
            pl.BlockSpec(memory_space=pl.ANY),
            pl.BlockSpec(memory_space=pl.ANY),
            pl.BlockSpec((1, VEC_ROWS, D), lambda i: (layer, 0, 0)),
            pl.BlockSpec((D, FC), col(True)),
            pl.BlockSpec((D, FC), col(False)),
            pl.BlockSpec((FC, D), line(True)),
            pl.BlockSpec((FC, D), line(False)),
        ],
        out_specs=[
            pl.BlockSpec((rows, D), whole),
            pl.BlockSpec((rows, D), whole),
            pl.BlockSpec((rows, FC), chunk),
            pl.BlockSpec((2, rows, FC // 2), lambda i: (0, 0, i)),
            pl.BlockSpec((rows, D), whole),
        ],
        scratch_shapes=[
            pltpu.VMEM((rows, D), F32),
            pltpu.VMEM((D, D), BF16),
            pltpu.SemaphoreType.DMA,
        ],
        out_shape=[
            jax.ShapeDtypeStruct((rows, D), F32),
            jax.ShapeDtypeStruct((rows, D), BF16),
            jax.ShapeDtypeStruct((rows, FF), F32),
            jax.ShapeDtypeStruct((2, rows, FF // 2), BF16),
            jax.ShapeDtypeStruct((rows, D), BF16),
        ],
        compiler_params=params(),
        cost_estimate=pl.CostEstimate(
            flops=2 * rows * D * (D + 2 * FF), bytes_accessed=30 * 2**20, transcendentals=rows * FF
        ),
    )(o_all, x_own, outs[0], outs[1], vec, ups[0], ups[1], downs[0], downs[1])


def mlp_back_kernel(layer, host, ranges, *refs):
    n = host.arrays
    dy_ref, h_ref, wo0_ref, wo1_ref, vec_ref, u_ref, a2_ref = refs[:7]
    up0_ref, up1_ref, down0_ref, down1_ref = refs[7:11]
    srcs = refs[11 : 11 + n]
    refs = refs[1:]
    gup_ref, gbup_ref, dh_ref, dr_ref, do_ref, sums_ref = refs[10 + n : 16 + n]
    outs = refs[16 + n : 16 + 2 * n]
    (acc, du_mine, du_send, du_recv, dr_send, dr_recv, do_send, do_recv) = refs[
        16 + 2 * n : 24 + 2 * n
    ]
    du_sems = refs[24 + 2 * n : 26 + 2 * n]
    do_sems = refs[26 + 2 * n : 28 + 2 * n]
    wo_ref, wo_sem = refs[28 + 2 * n : 30 + 2 * n]
    host.bind(srcs, outs, refs[30 + 2 * n :])
    group = Group()
    core = group.core
    step = pl.program_id(0)
    ranks, rows, width = do_ref.shape
    unit = FF // shards_of() // 2
    own = core == layer
    partner_core = group.device(1, 0)

    @pl.when(step == 0)
    def _():
        group.greet(host.dp_count)
        host.begin()
        pl.when(own)(lambda: pltpu.make_async_copy(wo0_ref, wo_ref, wo_sem).start())
        pl.when(jnp.logical_not(own))(
            lambda: pltpu.make_async_copy(wo1_ref, wo_ref, wo_sem).start()
        )
        acc[...] = jnp.zeros_like(acc)

    def du_copy(at):
        return send(du_send.at[at], du_recv.at[at], du_sems, at, partner_core)

    def part(up_ref, down_ref):
        d_gated = mm_nt(dy_ref[...], down_ref[...])
        upper = u_ref[...]
        square = upper * upper
        turn = jnp.tanh(GELU_A * upper * (1.0 + GELU_B * square))
        slope = 0.5 * (1.0 + turn) + (0.5 * GELU_A) * upper * (1.0 - turn * turn) * (
            1.0 + (3.0 * GELU_B) * square
        )
        d_upper = (d_gated * slope).astype(BF16)
        for at in range(0, FC // unit, 2):
            even = d_upper[:, at * unit : (at + 1) * unit]
            odd = d_upper[:, (at + 1) * unit : (at + 2) * unit]
            cols = slice(at // 2 * unit, (at // 2 + 1) * unit)
            du_mine[step, :, cols] = jnp.where(core == 0, even, odd)
            du_send[step, :, cols] = jnp.where(core == 0, odd, even)
        gbup_ref[...] = jnp.sum(d_upper.astype(F32), axis=0, keepdims=True)
        acc[...] += mm_nt(d_upper, up_ref[...])

    @pl.when(step < NCH)
    def _():
        pl.when(own)(lambda: part(up0_ref, down0_ref))
        pl.when(jnp.logical_not(own))(lambda: part(up1_ref, down1_ref))
        du_copy(step).start()

    @pl.when(step > 0)
    def _():
        at = step - 1
        du_copy(at).wait()
        value = mm_tn(du_mine[at], a2_ref[:rows, :]) + mm_tn(du_recv[at], a2_ref[rows:, :])
        gup_ref[...] = value.astype(BF16).reshape(gup_ref.shape)

    for slot, (first, last) in enumerate(ranges[:-1]):
        if last > first:
            pl.when(step == slot)(functools.partial(host.run, first, last))

    @pl.when(step == NCH)
    def _():
        normal, inverse = norm_stats(h_ref[...])
        d_out = dy_ref[...].astype(F32)
        d_normed = acc[...]
        sums_ref[...] = jnp.zeros_like(sums_ref)
        sums_ref[0:1, :] = jnp.sum(d_normed * normal, axis=0, keepdims=True)
        sums_ref[1:2, :] = jnp.sum(d_normed, axis=0, keepdims=True)
        d_normal = d_normed * vec_ref[0, LN2_GAIN : LN2_GAIN + 1, :]
        d_hidden = d_out + inverse * (
            d_normal
            - jnp.mean(d_normal, axis=-1, keepdims=True)
            - normal * jnp.mean(d_normal * normal, axis=-1, keepdims=True)
        )
        dh_ref[...] = d_hidden
        d_branch = d_hidden.astype(BF16)
        dr_ref[0] = d_branch
        dr_send[...] = d_branch
        branch_copy = send(dr_send, dr_recv, do_sems, ranks, partner_core)
        branch_copy.start()
        pltpu.make_async_copy(wo0_ref, wo_ref, wo_sem).wait()

        def heads_of(rank):
            at = pl.multiple_of(rank * width, width)
            return mm_nt(d_branch, wo_ref[pl.ds(at, width), :]).astype(BF16)

        copies = []
        for dc, d in group.others():
            slot = group.slot(dc, d)
            do_send[slot] = heads_of(group.rank_of(dc, d))
            copies.append(
                send(do_send.at[slot], do_recv.at[group.rank], do_sems, slot, group.device(dc, d))
            )
            copies[-1].start()
        do_recv[group.rank] = heads_of(group.rank)
        sums_ref[2:3, :] = jnp.sum(d_branch.astype(F32), axis=0, keepdims=True)
        sums_ref[3:4, :] = jnp.sum(d_out, axis=0, keepdims=True)
        host.run(*ranges[-1])
        branch_copy.wait()
        dr_ref[1] = dr_recv[...]
        for copy in copies:
            copy.wait()
        do_ref[...] = do_recv[...]
        host.finish()


def mlp_back_call(layer, dy, hidden, wos, vec, upper, a2_all, ups, downs, ranks, host, arrays, total):
    rows = dy.shape[0]
    width = D // ranks
    shards = host.dp_count * host.count
    per = shards // NCH if shards >= NCH else 1
    unit = FF // shards // 2
    whole = lambda i: (0, 0)
    now = lambda i: jnp.minimum(i, NCH - 1)
    mine = lambda i, first: jnp.where((lax.axis_index("section") == layer) == first, now(i), 0)
    col = lambda first: (lambda i: (0, mine(i, first)))
    line = lambda first: (lambda i: (mine(i, first), 0))
    chunk = lambda i: (0, now(i))
    ranges = host.slots([MLP_SLOT * (i + 1) for i in range(NCH + 1)], total)
    return pl.pallas_call(
        functools.partial(mlp_back_kernel, layer, host, ranges),
        grid=(NCH + 1,),
        in_specs=[
            pl.BlockSpec((rows, D), whole),
            pl.BlockSpec((rows, D), whole),
            pl.BlockSpec(memory_space=pl.ANY),
            pl.BlockSpec(memory_space=pl.ANY),
            pl.BlockSpec((1, VEC_ROWS, D), lambda i: (layer, 0, 0)),
            pl.BlockSpec((rows, FC), chunk),
            pl.BlockSpec((2 * rows, D), whole),
            pl.BlockSpec((D, FC), col(True)),
            pl.BlockSpec((D, FC), col(False)),
            pl.BlockSpec((FC, D), line(True)),
            pl.BlockSpec((FC, D), line(False)),
        ]
        + host.in_specs(),
        out_specs=[
            pl.BlockSpec((per, unit, D), lambda i: (jnp.maximum(i - 1, 0), 0, 0)),
            pl.BlockSpec((1, FC), chunk),
            pl.BlockSpec((rows, D), whole),
            pl.BlockSpec((2, rows, D), lambda i: (0, 0, 0)),
            pl.BlockSpec((ranks, rows, width), lambda i: (0, 0, 0)),
            pl.BlockSpec((8, D), whole),
        ]
        + host.out_specs(),
        scratch_shapes=[
            pltpu.VMEM((rows, D), F32),
            pltpu.VMEM((NCH, rows, FC // 2), BF16),
            pltpu.VMEM((NCH, rows, FC // 2), BF16),
            pltpu.VMEM((NCH, rows, FC // 2), BF16),
            pltpu.VMEM((rows, D), BF16),
            pltpu.VMEM((rows, D), BF16),
            pltpu.VMEM((ranks, rows, width), BF16),
            pltpu.VMEM((ranks, rows, width), BF16),
        ]
        + dma_pair(NCH)
        + dma_pair(ranks + 1)
        + [pltpu.VMEM((D, D), BF16), pltpu.SemaphoreType.DMA]
        + host.scratch(),
        out_shape=[
            jax.ShapeDtypeStruct((shards, unit, D), BF16),
            jax.ShapeDtypeStruct((1, FF), F32),
            jax.ShapeDtypeStruct((rows, D), F32),
            jax.ShapeDtypeStruct((2, rows, D), BF16),
            jax.ShapeDtypeStruct((ranks, rows, width), BF16),
            jax.ShapeDtypeStruct((8, D), F32),
        ]
        + host.out_shapes(),
        compiler_params=pltpu.CompilerParams(
            vmem_limit_bytes=VMEM_LIMIT, collective_id=layer, has_side_effects=True
        ),
    )(dy, hidden, wos[0], wos[1], vec, upper, a2_all, ups[0], ups[1], downs[0], downs[1], *host.views(arrays))


def attend_back_kernel(host, ranges, *refs):
    n = host.arrays
    (q_ref, do_ref, k_ref, v_ref, lse_ref, mask_ref, gain_ref) = refs[:7]
    late = refs[7:13]
    srcs = refs[13 : 13 + n]
    dx_ref, sums_ref, sums_qv_ref, gjoint_ref, gout_ref = refs[13 + n : 18 + n]
    outs = refs[18 + n : 18 + 2 * n]
    rest = refs[18 + 2 * n :]
    dk_acc, dv_acc, dj, da_acc, core_send, core_recv, far_send, far_recv = rest[:8]
    g_send, g_recv, dx_send, dx_recv = rest[8:12]
    a1, w_joint, x_own, dh, branch, mixed = rest[12:18]
    load_sems = rest[18]
    core_sems, far_sems, pair_sems = rest[19:21], rest[21:23], rest[23:25]
    host.bind(srcs, outs, rest[25:])
    group = Group()
    core, half = group.core, group.half
    partner_core = group.device(1, 0)
    width = q_ref.shape[1]
    length = q_ref.shape[0]
    rows = x_own.shape[0]
    heads = width // DH
    scale = DH ** (-0.5)

    group.greet(host.dp_count)
    host.begin()
    loads = []
    for i, (source, target) in enumerate(zip(late, (a1, w_joint, x_own, dh, branch, mixed))):
        loads.append(pltpu.make_async_copy(source, target, load_sems.at[i]))
        loads[-1].start()
    dk_acc[...] = jnp.zeros_like(dk_acc)
    dv_acc[...] = jnp.zeros_like(dv_acc)
    sums_qv_ref[...] = jnp.zeros_like(sums_qv_ref)
    sums_ref[...] = jnp.zeros_like(sums_ref)

    def block(step, carry):
        here = pl.ds(pl.multiple_of(step * BQ, BQ), BQ)
        q = q_ref[here, :]
        grad = do_ref[here, :]
        totals = lse_ref[here, :]
        d_q = jnp.zeros((BQ, width), F32)
        for head in range(heads):
            mine = head_lanes((BQ, width), head)
            q_head = jnp.where(mine, q, jnp.zeros_like(q))
            grad_head = jnp.where(mine, grad, jnp.zeros_like(grad))
            scores = mm_nt(q_head, k_ref[...]) * SCALE2 + mask_ref[...]
            probs = jnp.exp2(scores - totals[:, head : head + 1])
            d_probs = mm_nt(grad_head, v_ref[...])
            term = jnp.sum(probs * d_probs, axis=-1, keepdims=True)
            d_scores = (probs * (d_probs - term)).astype(BF16)
            dv_acc[...] += mm_tn(probs.astype(BF16), grad_head)
            dk_acc[...] += mm_tn(d_scores, q_head)
            d_q = jnp.where(mine, mm(d_scores, k_ref[...]), d_q)
            for slot, (first, last) in enumerate(ranges[: length // BQ * heads]):
                if last > first and slot % heads == head:
                    pl.when(step == slot // heads)(functools.partial(host.run, first, last))
        low = (d_q * scale).astype(BF16)
        dj[here, :width] = low
        sums_qv_ref[0:1, :] += jnp.sum(low.astype(F32), axis=0, keepdims=True)
        return carry

    lax.fori_loop(0, length // BQ, block, 0)
    dj[:, width : 2 * width] = (dk_acc[...] * scale).astype(BF16)
    low_v = dv_acc[...].astype(BF16)
    dj[:, 2 * width :] = low_v
    sums_qv_ref[1:2, :] = jnp.sum(low_v.astype(F32), axis=0, keepdims=True)

    for load in loads:
        load.wait()

    def partial_rows(rank):
        here = pl.ds(pl.multiple_of(rank * rows, 16), rows)
        return mm_nt(dj[here, :], w_joint[...])

    def core_copy(d):
        return send(core_send.at[d], core_recv.at[d], core_sems, d, partner_core)

    def far_copy(d):
        return send(far_send.at[d - 1], far_recv.at[d - 1], far_sems, d - 1, group.device(0, d))

    for d in [d for d in range(1, half)] + [0]:
        core_send[d] = partial_rows(group.rank_of(1, d)).astype(BF16)
        core_copy(d).start()
    for d in range(1, half):
        value = partial_rows(group.rank_of(0, d))
        core_copy(d).wait_recv()
        far_send[d - 1] = (value + core_recv[d].astype(F32)).astype(BF16)
        far_copy(d).start()
    value = partial_rows(group.rank)
    core_copy(0).wait_recv()
    da_acc[...] = value + core_recv[0].astype(F32)
    tail = ranges[length // BQ * heads :]
    host.run(*tail[0])

    half_cols = D // 2
    mine_cols = pl.ds(pl.multiple_of(core * half_cols, half_cols), half_cols)
    other_cols = pl.ds(pl.multiple_of((1 - core) * half_cols, half_cols), half_cols)
    g_send[...] = mm_tn(dj[...], a1[:, other_cols]).astype(BF16)
    g_copy = send(g_send, g_recv, pair_sems, 0, partner_core)
    g_copy.start()
    gjoint_ref[:, core] = mm_tn(dj[...], a1[:, mine_cols]).astype(BF16).reshape(3, width, half_cols)
    host.run(*tail[1])
    gout_ref[...] = mm_tn(branch[...], mixed[...]).astype(BF16)
    host.run(*tail[2])

    for d in range(1, half):
        far_copy(d).wait_recv()
        da_acc[...] += far_recv[d - 1].astype(F32)
    d_normed = da_acc[...]
    normal, inverse = norm_stats(x_own[...].astype(F32))
    sums_ref[0:1, :] = jnp.sum(d_normed * normal, axis=0, keepdims=True)
    sums_ref[1:2, :] = jnp.sum(d_normed, axis=0, keepdims=True)
    d_normal = d_normed * gain_ref[LN1_GAIN : LN1_GAIN + 1, :]
    d_in = (
        dh[...]
        + inverse
        * (
            d_normal
            - jnp.mean(d_normal, axis=-1, keepdims=True)
            - normal * jnp.mean(d_normal * normal, axis=-1, keepdims=True)
        )
    ).astype(BF16)
    dx_send[...] = d_in
    dx_copy = send(dx_send, dx_recv, pair_sems, 1, partner_core)
    dx_copy.start()
    dx_ref[0] = d_in
    host.run(*tail[3])
    g_copy.wait()
    gjoint_ref[:, 1 - core] = g_recv[...].reshape(3, width, half_cols)
    dx_copy.wait()
    dx_ref[1] = dx_recv[...]
    for d in range(half):
        core_copy(d).wait_send()
    for d in range(1, half):
        far_copy(d).wait_send()
    host.finish()


def attend_back_call(
    q, d_o, k, v, lse, mask, gain, a1, w_joint, x_own, d_hidden, branch, mixed, host, arrays, total, collective_id
):
    length, width = q.shape
    rows = x_own.shape[0]
    half = host.count // 2
    blocks = length // BQ * (width // DH)
    times = [ATT_SLOT * (i + 1) for i in range(blocks)]
    times += [times[-1] + extra for extra in (5.0, 10.0, 13.0, 18.0)]
    ranges = host.slots(times, total)
    vmem = pl.BlockSpec(memory_space=pltpu.VMEM)
    late = (a1, w_joint, x_own, d_hidden, branch, mixed)
    return pl.pallas_call(
        functools.partial(attend_back_kernel, host, ranges),
        in_specs=[vmem] * 7 + [pl.BlockSpec(memory_space=pl.ANY)] * 6 + host.in_specs(),
        out_specs=[vmem] * 5 + host.out_specs(),
        out_shape=[
            jax.ShapeDtypeStruct((2, rows, D), BF16),
            jax.ShapeDtypeStruct((8, D), F32),
            jax.ShapeDtypeStruct((8, width), F32),
            jax.ShapeDtypeStruct((3, 2, width, D // 2), BF16),
            jax.ShapeDtypeStruct((D, D // 2), BF16),
        ]
        + host.out_shapes(),
        scratch_shapes=[
            pltpu.VMEM((length, width), F32),
            pltpu.VMEM((length, width), F32),
            pltpu.VMEM((length, 3 * width), BF16),
            pltpu.VMEM((rows, D), F32),
            pltpu.VMEM((half, rows, D), BF16),
            pltpu.VMEM((half, rows, D), BF16),
            pltpu.VMEM((half - 1, rows, D), BF16),
            pltpu.VMEM((half - 1, rows, D), BF16),
            pltpu.VMEM((3 * width, D // 2), BF16),
            pltpu.VMEM((3 * width, D // 2), BF16),
            pltpu.VMEM((rows, D), BF16),
            pltpu.VMEM((rows, D), BF16),
        ]
        + [pltpu.VMEM(t.shape, t.dtype) for t in late]
        + [pltpu.SemaphoreType.DMA((len(late),))]
        + dma_pair(half)
        + dma_pair(half - 1)
        + dma_pair(2)
        + host.scratch(),
        compiler_params=pltpu.CompilerParams(
            vmem_limit_bytes=VMEM_LIMIT, collective_id=collective_id, has_side_effects=True
        ),
    )(q, d_o, k, v, lse, mask, gain, *late, *host.views(arrays))


def swap(value, axis, mask):
    count = lax.axis_size(axis)
    return lax.ppermute(value, axis, [(i, i ^ mask) for i in range(count)])


def take(value, index, dim):
    return lax.dynamic_index_in_dim(value, index, dim, keepdims=False)


def ordered(bit, mine, other, dim):
    return jnp.where(
        bit == 0,
        jnp.stack([mine, other], axis=dim),
        jnp.stack([other, mine], axis=dim),
    )


def key_bias(counts, rotate):
    places = jnp.arange(LEN, dtype=jnp.int32)
    places = jnp.where(rotate, (places + LEN // 2) % LEN, places)
    offset = jnp.maximum(places - TRI, 0)
    view_index = offset // VSLOT
    inside = offset - view_index * VSLOT
    match = view_index[:, None] == jnp.arange(VIEWS, dtype=jnp.int32)[None, :]
    limits = jnp.sum(jnp.where(match, counts[None, :], 0), axis=1)
    valid = (places < TRI) | (inside < limits)
    return jnp.where(valid, 0.0, -1e30).astype(F32)[None, :]


def shards(
    inputs,
    cotangent,
    view_tokens,
    ln1_gain,
    ln1_bias,
    w_qkv,
    b_query,
    b_value,
    w_out,
    b_out,
    ln2_gain,
    ln2_bias,
    w_up,
    b_up,
    w_down,
    b_down,
):
    core = lax.axis_index("section")
    place = lax.axis_index("seq")
    dp_index = lax.axis_index("dp")
    count = lax.axis_size("seq")
    dp_count = lax.axis_size("dp")
    groups = dp_count * count
    half = count // 2
    micro = place // half
    low = place % half
    low_bits = half.bit_length() - 1
    rows = inputs.shape[2]
    width = D // count
    rank = core * half + low

    def swap_core(value):
        return swap(value, "section", 1)

    def swap_seq(value, bit):
        return swap(value, "seq", 1 << bit)

    def low_bit(bit):
        return (place >> bit) & 1

    def own_rows(local):
        chunks = local[:, 0]
        far = lax.ppermute(
            take(chunks, 1 - micro, 0),
            ("section", "seq"),
            [(count + z, count + (z ^ half)) for z in range(count)],
        )
        return jnp.where(core == 0, take(chunks, micro, 0), far)

    def gather_rows(own):
        value = own[None]
        for bit in range(low_bits):
            other = swap_seq(value, bit)
            value = ordered(low_bit(bit), value, other, 0).reshape((-1,) + own.shape)
        value = ordered(core, value, swap_core(value), 0)
        return value.reshape((-1,) + own.shape[1:])

    def exchange(value):
        tail = value.shape[1:]
        value = value.reshape((2,) * (low_bits + 1) + tail)
        for bit in range(low_bits):
            dim = low_bits - bit
            mine = take(value, low_bit(bit), dim)
            other = swap_seq(take(value, 1 - low_bit(bit), dim), bit)
            value = ordered(low_bit(bit), mine, other, dim)
        mine = take(value, core, 0)
        other = swap_core(take(value, 1 - core, 0))
        return ordered(core, mine, other, 0).reshape((count,) + tail)

    def to_section(own, layer):
        first = own
        if layer == 1:
            first = lax.ppermute(
                own, ("section", "seq"), [(z, count + z) for z in range(count)]
            )
        second = lax.ppermute(
            own,
            ("section", "seq"),
            [(count + z, layer * count + (z ^ half)) for z in range(count)],
        )
        return ordered(micro, first, second, 0)

    compact = half == 2
    span = half * width

    def vector_to(value):
        if compact:
            wide = jnp.stack(
                [jnp.where(low == i, value.reshape(-1, DH), 0.0) for i in range(2)], axis=1
            )
        else:
            wide = jnp.stack([jnp.where(low == i, value, 0.0) for i in range(half)], axis=0)
        wide = wide.reshape(span)
        return jnp.concatenate([jnp.where(core == i, wide, 0.0) for i in range(2)])

    def rank_rows(value):
        if compact:
            value = value.reshape(2, width // DH, 2, DH, D)
            return jnp.swapaxes(value, 1, 2).reshape(D, D)
        return value

    out_mine = rank_rows(w_out[0])
    ups = (w_up[0], swap_core(w_up[0]))
    downs = (w_down[0], swap_core(w_down[0]))
    bias_mask = key_bias(take(view_tokens[:, 0], micro, 0), micro == 1)

    saved = []
    acts = []
    for layer in range(2):
        if layer == 0:
            o_own, lse, a1, q, k, v, layer_in, joint_pair, out_other, vec = attend_call(
                True,
                0,
                bias_mask,
                count,
                dp_count,
                inputs,
                w_qkv,
                out_mine[None],
                ln1_gain,
                ln1_bias,
                b_query,
                b_value,
                b_out,
                ln2_gain,
                ln2_bias,
                b_down,
                b_up,
            )
            outs_pair = (out_mine, out_other)
        else:
            o_own, lse, a1, q, k, v = attend_call(
                False, 1, bias_mask, count, dp_count, layer_in, joint_pair[1], vec[1:2]
            )
        hidden, a2, upper, gated, output = mlp_call(
            layer, o_own, layer_in, outs_pair, vec, ups, downs
        )
        acts.append(output)
        saved.append((layer_in, a1, q, k, v, lse, o_own, hidden, a2, upper, gated))
        layer_in = output

    dp_bits = dp_count.bit_length() - 1
    seq_bits = count.bit_length() - 1
    bits = [("dp", dp_bits - 1 - i) for i in range(dp_bits)]
    bits += [("seq", seq_bits - 1 - i) for i in range(seq_bits)]
    dp_dims = list(range(dp_bits))
    seq_dims = list(range(dp_bits, dp_bits + seq_bits))[::-1]
    orders = (
        dp_dims[::-1] + seq_dims,
        dp_dims + seq_dims,
        seq_dims[:1] + dp_dims + seq_dims[1:],
        seq_dims[:1] + dp_dims[::-1] + seq_dims[1:],
    )

    def reduce_one(value, order):
        tail = value.shape[1:]
        value = value.reshape((2,) * len(bits) + tail)
        left = list(range(len(bits)))
        for dim in order:
            axis, bit = bits[dim]
            index = (lax.axis_index(axis) >> bit) & 1
            at = left.index(dim)
            left.remove(dim)
            other = swap(take(value, 1 - index, at), axis, 1 << bit)
            total = take(value, index, at).astype(F32) + other.astype(F32)
            value = total.astype(value.dtype) if left else total
        return value

    def both_halves(value):
        return jnp.concatenate([take(value, core, 0), swap_core(take(value, 1 - core, 0))], axis=0)

    def joined(mine, other):
        return jnp.concatenate([mine, other], axis=0)

    def hosted(*arrays):
        shapes = []
        for array in arrays:
            shapes.append((array.shape[1], array.shape[2], array.shape[0] != groups))
        return Hosted(dp_count, count, tuple(shapes)), arrays

    smalls = []
    results = [{}, {}]
    grads_in = []
    pending = None
    d_out = own_rows(cotangent)
    d_out_all = joined(d_out, swap_core(d_out))
    for layer in (1, 0):
        x_own, a1, q, k, v, lse, o_own, hidden, a2, upper, gated = saved[layer]
        gated_all = both_halves(gated)
        a2_all = joined(a2, swap_core(a2))
        o_split = o_own.reshape(2, half, rows, width)
        flat = lambda t: jnp.swapaxes(t, 0, 1).reshape(rows, half * width)
        o_all = joined(flat(take(o_split, core, 0)), swap_core(flat(take(o_split, 1 - core, 0))))
        g_down = mm_tn(d_out_all, gated_all).astype(BF16).reshape(groups, D // groups, FF // 2)
        host, arrays = hosted(g_down) if pending is None else hosted(*pending)
        g_up, g_bup, d_hidden, branch, d_heads, sums_two, *reduced = mlp_back_call(
            layer, d_out, hidden, outs_pair, vec, upper, a2_all, ups, downs, count, host, arrays, 40.0
        )
        if pending is None:
            results[layer]["down"] = reduced[0]
        else:
            results[1]["out"], results[1]["joint"] = reduced
        host, arrays = hosted(g_up) if pending is None else hosted(g_down, g_up)
        d_in, sums_one, sums_qv, g_joint, g_out, *reduced = attend_back_call(
            q,
            d_heads.reshape(LEN, width),
            k,
            v,
            lse,
            bias_mask,
            vec[layer],
            a1,
            joint_pair[layer],
            x_own,
            d_hidden,
            branch.reshape(2 * rows, D),
            o_all,
            host,
            arrays,
            42.0 if pending is None else 80.0,
            2 + layer,
        )
        if pending is None:
            results[layer]["up"] = reduced[0]
        else:
            results[layer]["down"], results[layer]["up"] = reduced
        g_out = g_out.reshape(groups, D // groups, D // 2)
        if compact:
            g_joint = g_joint.reshape(groups // 2, 3 * D // groups, D // 2)
        else:
            spread = jnp.stack(
                [jnp.where(low == i, g_joint, jnp.zeros_like(g_joint)) for i in range(half)], axis=2
            )
            g_joint = spread.reshape(groups, 3 * D // groups, D // 2)
        if pending is None:
            pending = (g_out, g_joint)
        else:
            host, arrays = hosted(g_out, g_joint)
            results[layer]["out"], results[layer]["joint"] = reduce_call(host, arrays, 4)
        d_out = d_in[0]
        d_out_all = d_in.reshape(2 * rows, D)
        smalls.append(
            jnp.concatenate(
                [
                    piece.reshape(groups, -1)
                    for piece in (
                        sums_one[0],
                        sums_one[1],
                        vector_to(sums_qv[0]),
                        vector_to(sums_qv[1]),
                        sums_two[2],
                        sums_two[0],
                        sums_two[1],
                        g_bup[0],
                        sums_two[3],
                    )
                ],
                axis=1,
            )
        )
        grads_in.append(d_out)

    grads_in = grads_in[::-1]
    small_pair = jnp.stack(smalls[::-1])
    small = take(small_pair, core, 0) + swap_core(take(small_pair, 1 - core, 0))
    small = reduce_one(small, orders[0])

    acts_rows = jnp.where(core == 0, to_section(acts[0], 0), to_section(acts[1], 1))
    grad_rows = jnp.where(core == 0, to_section(grads_in[0], 0), to_section(grads_in[1], 1))

    def choose(name):
        return jnp.where(core == 0, results[0][name], results[1][name])

    r_down = choose("down").reshape(2, D // groups, groups, FF // groups // 2)
    g_w_down = jnp.transpose(r_down, (2, 0, 3, 1)).reshape(FF, D // groups)
    r_out = choose("out")
    if compact:
        r_out = r_out.reshape(2, D // groups, 2, width // DH, DH)
        g_w_out = jnp.transpose(r_out, (0, 3, 2, 4, 1)).reshape(D, D // groups)
    else:
        g_w_out = jnp.swapaxes(r_out, 1, 2).reshape(D, D // groups)
    r_joint = choose("joint")
    if compact:
        r_joint = r_joint.reshape(2, 4, DH, D // 2)
        r_joint = jnp.where(
            low == 0,
            jnp.stack([r_joint[:, 0], r_joint[:, 3], r_joint[:, 1]], axis=1),
            jnp.stack([r_joint[:, 1], r_joint[:, 3], r_joint[:, 2]], axis=1),
        ).reshape(2, 3 * DH, D // 2)
    g_w_qkv = jnp.swapaxes(r_joint, 1, 2).reshape(D, 3 * D // groups)
    r_up = choose("up")
    g_w_up = jnp.transpose(r_up, (2, 0, 1)).reshape(D, FF // groups)

    unit = D // groups
    pieces = []
    start = 0
    for size in (unit, unit, unit, unit, unit, unit, unit, FF // groups, unit):
        pieces.append(small[start : start + size])
        start += size
    g_ln1g, g_ln1b, g_bq, g_bv, g_bo, g_ln2g, g_ln2b, g_bup, g_bd = pieces
    outs = (
        g_ln1g,
        g_ln1b,
        g_w_qkv,
        g_bq,
        g_bv,
        g_w_out,
        g_bo,
        g_ln2g,
        g_ln2b,
        g_w_up,
        g_bup,
        g_w_down,
        g_bd,
    )
    return (acts_rows[None, :, None], grad_rows[None, :, None]) + tuple(g[None] for g in outs)


def solution(mesh):
    rows = P(None, "dp", "seq", None)
    vector = P("section", None)
    matrix = P("section", None, None)
    placed = (
        rows,
        rows,
        P(None, "dp", None),
        vector,
        vector,
        matrix,
        vector,
        vector,
        matrix,
        vector,
        vector,
        vector,
        matrix,
        vector,
        matrix,
        vector,
    )
    both = P("section", None, "dp", "seq", None)
    line = P("section", ("dp", "seq"))
    table = P("section", None, ("dp", "seq"))
    return jax.shard_map(
        shards,
        mesh=mesh,
        in_specs=placed,
        out_specs=(
            both,
            both,
            line,
            line,
            table,
            line,
            line,
            table,
            line,
            line,
            line,
            table,
            line,
            table,
            line,
        ),
        check_vma=False,
    )
```

```python
import functools
import math

import jax
import jax.numpy as jnp
from jax import lax
from jax.experimental import pallas as pl
from jax.experimental.pallas import tpu as pltpu
from jax.sharding import PartitionSpec as P

D = 1024
H = 16
DH = 64
FF = 4096
VIEWS = 6
TRI = 512
VSLOT = 128
MICRO = 2
LEN = 1280
BQ = 256
NCH = 8
FC = FF // NCH
SCALE2 = DH ** (-0.5) * math.log2(math.e)
F32 = jnp.float32
BF16 = jnp.bfloat16
VMEM_LIMIT = 56 * 2**20


def params():
    return pltpu.CompilerParams(vmem_limit_bytes=VMEM_LIMIT)


def mm(a, b):
    return lax.dot_general(a, b, (((1,), (0,)), ((), ())), preferred_element_type=F32)


def mm_nt(a, b):
    return lax.dot_general(a, b, (((1,), (1,)), ((), ())), preferred_element_type=F32)


def mm_tn(a, b):
    return lax.dot_general(a, b, (((0,), (0,)), ((), ())), preferred_element_type=F32)


def norm_stats(values):
    average = jnp.mean(values, axis=-1, keepdims=True)
    centered = values - average
    variance = jnp.mean(centered * centered, axis=-1, keepdims=True)
    inverse = lax.rsqrt(variance + 1e-05)
    return centered * inverse, inverse


def head_lanes(shape, head):
    lane = lax.broadcasted_iota(jnp.int32, shape, 1)
    return (lane >= head * DH) & (lane < (head + 1) * DH)


def shards_of():
    return lax.axis_size("dp") * lax.axis_size("seq")


def split_halves(value, unit, core, mine, other, step):
    for at in range(0, value.shape[1] // unit, 2):
        even = value[:, at * unit : (at + 1) * unit]
        odd = value[:, (at + 1) * unit : (at + 2) * unit]
        cols = slice(at // 2 * unit, (at // 2 + 1) * unit)
        mine[step, :, cols] = jnp.where(core == 0, even, odd)
        other[step, :, cols] = jnp.where(core == 0, odd, even)


GELU_A = math.sqrt(2.0 / math.pi)
GELU_B = 0.044715


MESH_AXES = ("dp", "seq")


def axis_bits(dp_count, count):
    bits = []
    for axis, size in (("dp", dp_count), ("seq", count)):
        mask = size // 2
        while mask:
            bits.append((axis, mask))
            mask //= 2
    return bits


def stream_orders(dp_count, count):
    dp_bits = dp_count.bit_length() - 1
    seq_bits = count.bit_length() - 1
    dp_dims = list(range(dp_bits))
    seq_dims = list(range(dp_bits, dp_bits + seq_bits))[::-1]
    return (
        dp_dims[::-1] + seq_dims,
        dp_dims + seq_dims,
        seq_dims[:1] + dp_dims + seq_dims[1:],
        seq_dims[:1] + dp_dims[::-1] + seq_dims[1:],
    )


def my_bit(axis, mask):
    return lax.rem(lax.div(lax.axis_index(axis), mask), 2)


def partner(axis, mask):
    return lax.axis_index(axis) + mask * (1 - 2 * my_bit(axis, mask))


def greet(bits):
    barrier = pltpu.get_barrier_semaphore()
    for axis, mask in bits:
        pl.semaphore_signal(
            barrier,
            inc=1,
            device_id={axis: partner(axis, mask)},
            device_id_type=pl.DeviceIdType.MESH,
        )
    pl.semaphore_wait(barrier, len(bits))


class Reducer:
    def __init__(self, bits, order, src, cols, out, rows, compact, buffers, sems):
        self.bits, self.order, self.src, self.cols = bits, order, src, cols
        self.out, self.out_cols, self.buffers, self.sems = out, cols, buffers, sems
        self.count, self.rows, self.compact = len(bits), rows, compact

    @staticmethod
    def scratch(count, rows, width, dtype):
        shapes = [pltpu.VMEM((2,) * (count - 1) + (rows, width), dtype)]
        for stage in range(count):
            shapes.append(pltpu.VMEM((2,) * (count - 1 - stage) + (rows, width), dtype))
        shapes += [
            pltpu.SemaphoreType.DMA((count + 2,)),
            pltpu.SemaphoreType.DMA((count + 2,)),
            pltpu.SemaphoreType.DMA,
        ]
        return shapes

    def place(self, stage):
        left = [d for d in range(self.count) if d not in self.order[:stage]]
        dim = self.order[stage]
        return left, left.index(dim), self.bits[dim]

    def cut(self, stage, index):
        left, at, _ = self.place(stage)
        where = [slice(None)] * len(left)
        where[at] = index
        return tuple(where)

    def source(self, stage):
        if stage == 0:
            return self.src
        return self.buffers[0] if stage == 1 else self.buffers[stage]

    def copy(self, stage):
        axis, mask = self.place(stage)[2]
        where = self.cut(stage, 1 - my_bit(axis, mask))
        if stage == 0:
            where = where + (slice(None), pl.ds(*self.cols))
        return pltpu.make_async_remote_copy(
            src_ref=self.source(stage).at[where],
            dst_ref=self.buffers[stage + 1],
            send_sem=self.sems[0].at[stage],
            recv_sem=self.sems[1].at[stage],
            device_id={axis: partner(axis, mask)},
            device_id_type=pl.DeviceIdType.MESH,
        )

    def load(self):
        axis, mask = self.place(0)[2]
        where = self.cut(0, my_bit(axis, mask)) + (slice(None), pl.ds(*self.cols))
        return pltpu.make_async_copy(self.src.at[where], self.buffers[0], self.sems[2])

    def share(self):
        core = lax.axis_index("section")
        return pltpu.make_async_remote_copy(
            src_ref=self.out.at[core, :, pl.ds(*self.out_cols)],
            dst_ref=self.out.at[core, :, pl.ds(*self.out_cols)],
            send_sem=self.sems[0].at[self.count],
            recv_sem=self.sems[1].at[self.count],
            device_id={"section": 1 - core},
            device_id_type=pl.DeviceIdType.MESH,
        )

    def trade(self):
        third = self.rows // 3
        core = lax.axis_index("section")
        bit = lax.rem(lax.axis_index("seq"), 2)
        row = pl.multiple_of((1 - bit) * 2 * third, third)
        return pltpu.make_async_remote_copy(
            src_ref=self.out.at[core, pl.ds(row, third), pl.ds(*self.out_cols)],
            dst_ref=self.out.at[core, pl.ds(self.rows, third), pl.ds(*self.out_cols)],
            send_sem=self.sems[0].at[self.count + 1],
            recv_sem=self.sems[1].at[self.count + 1],
            device_id={"seq": partner("seq", 1)},
            device_id_type=pl.DeviceIdType.MESH,
        )

    def begin(self):
        self.copy(0).start()
        self.load().start()

    def step(self, stage):
        left, at, (axis, mask) = self.place(stage)
        bit = my_bit(axis, mask)
        if stage == 0:
            self.load().wait()
        self.copy(stage).wait_recv()
        got = self.buffers[stage + 1]
        rows = got.shape[-2]
        chunk = rows
        while chunk * got.shape[-1] > 65536 and chunk % 32 == 0:
            chunk //= 2
        per = rows // chunk
        last = stage == self.count - 1
        core = lax.axis_index("section")
        total = 2 ** (len(left) - 1)

        def body(i, carry):
            flat = lax.div(i, per)
            row = pl.multiple_of(lax.rem(i, per) * chunk, chunk)
            index = []
            for j in range(len(left) - 1):
                index.append(lax.rem(lax.div(flat, 2 ** (len(left) - 2 - j)), 2))
            there = tuple(index) + (pl.ds(row, chunk), slice(None))
            if stage == 0:
                mine = self.buffers[0][there]
            else:
                own = index[:at] + [bit] + index[at:]
                mine = self.source(stage)[tuple(own) + (pl.ds(row, chunk), slice(None))]
            value = mine.astype(F32) + got[there].astype(F32)
            if last:
                self.out[core, pl.ds(row, chunk), pl.ds(*self.out_cols)] = value
            elif stage == 0:
                self.buffers[0][there] = value.astype(got.dtype)
            else:
                got[there] = value.astype(got.dtype)
            return carry

        lax.fori_loop(0, total * per, body, 0)
        if not last:
            self.copy(stage + 1).start()
        elif self.compact:
            self.trade().start()
        else:
            self.share().start()

    def tail(self):
        if self.compact:
            self.trade().wait()
            self.share().start()

    def finish(self):
        for stage in range(self.count):
            self.copy(stage).wait_send()
        self.share().wait()


def part_widths(width):
    unit = 128 if width % 128 == 0 else width
    tiles = width // unit
    rest = tiles // 8
    first = -(-(tiles - rest) // 2)
    second = rest // 2
    return tuple(unit * n for n in (first, tiles - rest - first, rest - second, second))


STAGE_SHARES = (0.35, 0.6, 0.85, 1.0)


class Hosted:
    def __init__(self, dp_count, count, shapes, spans=None):
        self.dp_count, self.count, self.shapes = dp_count, count, shapes
        self.spans = spans or ((0, 0.0, 1.0),) * len(shapes)
        self.all_bits = axis_bits(dp_count, count)
        self.plan = []
        for index, (rows, width, compact, _) in enumerate(shapes):
            bits = self.all_bits[:-1] if compact else self.all_bits
            orders = stream_orders(dp_count, count)
            widths = part_widths(width)
            if compact:
                last = len(bits)
                orders = [tuple(d for d in order if d != last) for order in orders[:2]]
                widths = (width // 2, width // 2)
            start = 0
            for order, size in zip(orders, widths):
                pieces = [size] if size else []
                if size >= 256 and not compact:
                    first = 128 * -(-size // 256)
                    pieces = [first, size - first]
                for k, piece in enumerate(pieces):
                    self.plan.append((index, tuple(order), bits, start, piece, rows, compact, k))
                    start += piece
        self.plan.sort(key=lambda p: (p[0], p[7]))
        self.arrays = len(shapes)
        self.events = []
        for k, part in enumerate(self.plan):
            _, first, last = self.spans[part[0]]
            for stage in range(len(part[2])):
                share = STAGE_SHARES[min(stage, 3)]
                self.events.append((first + (last - first) * share + 0.01 * stage, k, stage))
        self.events.sort()

    def views(self, arrays):
        return [self.view(i, array) for i, array in enumerate(arrays)]

    def view_shape(self, index):
        rows, width, compact, _ = self.shapes[index]
        depth = len(self.all_bits) - (1 if compact else 0)
        return (2,) * depth + (rows, width)

    def view(self, index, array):
        return array.reshape(self.view_shape(index))

    def in_specs(self):
        return [pl.BlockSpec(memory_space=pl.ANY)] * self.arrays

    def out_shapes(self):
        return [
            jax.ShapeDtypeStruct((2, rows + (rows // 3 if compact else 0), width), F32)
            for rows, width, compact, _ in self.shapes
        ]

    def out_specs(self):
        return [pl.BlockSpec(memory_space=pl.ANY)] * self.arrays

    def scratch(self):
        shapes = [pltpu.VMEM(o.shape, F32) for o in self.out_shapes()]
        shapes.append(pltpu.SemaphoreType.DMA((max(1, self.arrays),)))
        for index, _, bits, _, size, rows, _, _ in self.plan:
            shapes += Reducer.scratch(len(bits), rows, size, self.shapes[index][3])
        return shapes

    def bind(self, srcs, outs, scratch):
        self.parts = []
        self.outs, self.sums = outs, scratch[: self.arrays]
        self.out_sems = scratch[self.arrays]
        at = self.arrays + 1
        for index, order, bits, start, size, rows, compact, _ in self.plan:
            depth = len(bits) + 1
            mine = scratch[at : at + depth + 3]
            at += depth + 3
            self.parts.append(
                Reducer(
                    bits,
                    order,
                    srcs[index],
                    (start, size),
                    self.sums[index],
                    rows,
                    compact,
                    mine[:depth],
                    mine[depth:],
                )
            )

    def begin(self, phase=0):
        for part, plan in zip(self.parts, self.plan):
            if self.spans[plan[0]][0] == phase:
                part.begin()

    def run(self, first, last):
        for _, k, stage in self.events[first:last]:
            self.parts[k].step(stage)

    def slots(self, times):
        edges = []
        done = 0
        for time in times:
            while done < len(self.events) and self.events[done][0] <= time:
                done += 1
            edges.append(done)
        edges[-1] = len(self.events)
        return list(zip([0] + edges[:-1], edges))

    def settle(self):
        for part in self.parts:
            part.tail()
        for part in self.parts:
            part.finish()

    def finish(self):
        self.settle()
        copies = []
        for i, (out, value) in enumerate(zip(self.outs, self.sums)):
            copies.append(pltpu.make_async_copy(value, out, self.out_sems.at[i]))
            copies[-1].start()
        for copy in copies:
            copy.wait()


BACK_LIMIT = 64 * 2**20 - 2**18


class Group:
    def __init__(self):
        self.half = lax.axis_size("seq") // 2
        self.core = lax.axis_index("section")
        self.place = lax.axis_index("seq")
        self.low = lax.rem(self.place, self.half)
        self.base = self.place - self.low
        self.rank = self.core * self.half + self.low

    def others(self):
        pairs = [(dc, d) for d in range(1, self.half) for dc in (0, 1)]
        return pairs + [(1, 0)]

    def slot(self, dc, d):
        return dc * self.half + d

    def where(self, dc, d):
        core = lax.rem(self.core + dc, 2)
        low = lax.rem(self.low + d, self.half)
        return core, low

    def device(self, dc, d):
        core, low = self.where(dc, d)
        return {"section": core, "seq": self.base + low}

    def rank_of(self, dc, d):
        core, low = self.where(dc, d)
        return core * self.half + low

    def greet(self, dp_count):
        barrier = pltpu.get_barrier_semaphore()
        targets = [self.device(dc, d) for dc, d in self.others()]
        mask = dp_count // 2
        while mask:
            targets.append({"dp": partner("dp", mask)})
            mask //= 2
        targets.append({"seq": partner("seq", self.half)})
        targets.append({"section": 1 - self.core, "seq": partner("seq", self.half)})
        for target in targets:
            pl.semaphore_signal(
                barrier, inc=1, device_id=target, device_id_type=pl.DeviceIdType.MESH
            )
        pl.semaphore_wait(barrier, len(targets))


def send(src, dst, sems, slot, device):
    return pltpu.make_async_remote_copy(
        src_ref=src,
        dst_ref=dst,
        send_sem=sems[0].at[slot],
        recv_sem=sems[1].at[slot],
        device_id=device,
        device_id_type=pl.DeviceIdType.MESH,
    )


class Deliver:
    def __init__(self, group, layer, src, out, sems):
        micro = lax.div(group.place, group.half)
        here, there = sems[0], sems[1]
        self.core, self.layer = group.core, layer
        self.local = pltpu.make_async_copy(src, out.at[micro], sems[2])
        self.chip = send(src, out.at[micro], (here, there), 0, {"section": 1 - group.core})
        self.far = send(
            src,
            out.at[micro],
            (here, there),
            1,
            {"section": layer, "seq": partner("seq", group.half)},
        )

    def start(self):
        first = self.local if self.layer == 0 else self.chip
        pl.when(self.core == 0)(lambda: first.start())
        pl.when(self.core == 1)(lambda: self.far.start())

    def wait(self):
        @pl.when(self.core == 0)
        def _():
            if self.layer == 0:
                self.local.wait()
                self.far.wait_recv()
            else:
                self.chip.wait_send()

        @pl.when(self.core == 1)
        def _():
            self.far.wait_send()
            if self.layer == 1:
                self.far.wait_recv()
                self.chip.wait_recv()


def deliver_sems():
    return dma_pair(2) + [pltpu.SemaphoreType.DMA]


def dma_pair(count):
    return [pltpu.SemaphoreType.DMA((count,)), pltpu.SemaphoreType.DMA((count,))]


VEC_ROWS = 16
LN1_GAIN, LN1_BIAS, B_QUERY, B_VALUE, B_OUT, LN2_GAIN, LN2_BIAS, B_DOWN, B_UP = range(9)


def attend_kernel(first, layer, dp_count, *refs):
    if first:
        x_ref, joint_ref, wout_ref, mask_ref = refs[:4]
        vectors = refs[4:13]
        o_out, lse_out, a_out, q_out, k_out, v_out = refs[13:19]
        x_out, joint_out, wout_out, vec_out = refs[19:23]
        rest = refs[23:]
    else:
        x_ref, joint_ref, mask_ref, vec_ref, cot_ref = refs[:5]
        o_out, lse_out, a_out, q_out, k_out, v_out, cot_out, rows_out = refs[5:13]
        rest = refs[13:]
    x_all, a_all, q_all, k_all, v_all, lse, o_send, o_recv = rest[:8]
    x_sems, o_sems = rest[8:10], rest[10:12]
    out_sems = rest[12]
    if first:
        joint_pair, wide_own, wide_other, vec_send, vec_recv, vec_pair = rest[13:19]
        wide_sems, vec_sems = rest[19:21], rest[21:23]
        load_sems = rest[23]
    else:
        joint_one, cot_own, cot_other = rest[13:16]
        cot_sems = rest[16:18]
        load_sems = rest[18]
        rows_sems = rest[19:22]
    group = Group()
    core, half, rank, low = group.core, group.half, group.rank, group.low
    ranks, rows, _ = x_all.shape
    width = q_all.shape[1]
    heads = width // DH
    span = half * width
    partner_core = group.device(1, 0)
    micro = lax.div(group.place, half)

    group.greet(dp_count)

    def x_copy(slot, from_rank, device):
        return send(x_all.at[from_rank], x_all.at[from_rank], x_sems, slot, device)

    far = {"seq": partner("seq", half)}

    if first:
        own_load = pltpu.make_async_copy(x_ref.at[micro, 0], x_all.at[rank], load_sems.at[0])
        far_copy = send(x_ref.at[1 - micro, 0], x_all.at[rank], x_sems, 2 * half - 1, far)
        pl.when(core == 1)(lambda: far_copy.start())
        pl.when(core == 0)(lambda: own_load.start())
        wide_copies = []
        own_loads = []
        for part in range(3):
            theirs = pl.ds(pl.multiple_of(part * D + (1 - core) * span, 128), span)
            ours = pl.ds(pl.multiple_of(part * D + core * span, 128), span)
            wide_copies.append(
                send(joint_ref.at[0, :, theirs], wide_other.at[part], wide_sems, part, partner_core)
            )
            own_loads.append(
                pltpu.make_async_copy(
                    joint_ref.at[0, :, ours], wide_own.at[part], load_sems.at[1 + part]
                )
            )
            wide_copies[-1].start()
            own_loads[-1].start()
        vec_send[...] = jnp.zeros_like(vec_send)
        for i, value in enumerate(vectors[:8]):
            vec_send[i : i + 1, :] = value[...].astype(F32)
        for i in range(FF // D):
            vec_send[8 + i : 9 + i, :] = vectors[8][:, i * D : (i + 1) * D].astype(F32)
        vec_copy = send(vec_send, vec_recv, vec_sems, 0, partner_core)
        vec_copy.start()
        wout_copy = send(wout_ref.at[0], wout_out, vec_sems, 1, partner_core)
        pl.when(core == 1)(lambda: far_copy.wait_recv())
        pl.when(core == 0)(lambda: own_load.wait())
    else:
        own_load = pltpu.make_async_copy(x_ref, x_all.at[rank], load_sems.at[0])
        joint_load = pltpu.make_async_copy(joint_ref, joint_one, load_sems.at[1])
        own_load.start()
        joint_load.start()
        cot_far = send(cot_ref.at[1 - micro, 0], cot_own, cot_sems, 0, far)
        cot_load = pltpu.make_async_copy(cot_ref.at[micro, 0], cot_own, load_sems.at[2])
        pl.when(core == 1)(lambda: cot_far.start())
        pl.when(core == 0)(lambda: cot_load.start())
        own_load.wait()
    for d in range(1, half):
        x_copy(d - 1, rank, group.device(0, d)).start()
    x_copy(half - 1, rank, partner_core).start()

    source = lax.broadcasted_iota(jnp.int32, (span, width), 0)
    target = lax.broadcasted_iota(jnp.int32, (span, width), 1)
    if half == 2:
        wanted = (2 * lax.div(target, DH) + low) * DH + lax.rem(target, DH)
    else:
        wanted = low * width + target
    pick = (source == wanted).astype(F32).astype(BF16)
    if first:
        wout_copy.start()
        vec_copy.wait_recv()
        vec_pair[core] = vec_send[...]
        vec_pair[1 - core] = vec_recv[...]
        for load in own_loads:
            load.wait()
        for part in range(3):
            joint_pair[core, :, part * width : (part + 1) * width] = mm(
                wide_own[part], pick
            ).astype(BF16)
        for copy in wide_copies:
            copy.wait_recv()
        for part in range(3):
            joint_pair[1 - core, :, part * width : (part + 1) * width] = mm(
                wide_other[part], pick
            ).astype(BF16)
        vec = vec_pair[0]
        weights = lambda: joint_pair[0]
    else:
        joint_load.wait()
        vec = vec_ref[0]
        weights = lambda: joint_one[...]

    def of_heads(row):
        parts = vec[row : row + 1, :]
        mine = jnp.where(core == 0, parts[:, :span], parts[:, span:])
        wide = jnp.broadcast_to(mine, (16, span)).astype(BF16)
        return mm(wide, pick)[0:1, :]

    bias_q = of_heads(B_QUERY)
    bias_v = of_heads(B_VALUE)
    gain = vec[LN1_GAIN : LN1_GAIN + 1, :]
    shift = vec[LN1_BIAS : LN1_BIAS + 1, :]

    def project(at):
        normal, _ = norm_stats(x_all[at].astype(F32))
        a = (normal * gain + shift).astype(BF16)
        here = pl.ds(pl.multiple_of(at * rows, 16), rows)
        a_all[here, :] = a
        joined = mm(a, weights())
        q_all[here, :] = (joined[:, :width] + bias_q).astype(BF16)
        k_all[here, :] = joined[:, width : 2 * width].astype(BF16)
        v_all[here, :] = (joined[:, 2 * width :] + bias_v).astype(BF16)

    project(rank)
    x_copy(half - 1, rank, partner_core).wait_recv()
    project(group.rank_of(1, 0))
    for d in range(1, half):
        here = group.rank_of(0, half - d)
        x_copy(d - 1, here, partner_core).wait_recv()
        x_copy(half - 1 + d, here, partner_core).start()
        project(here)
    for d in range(1, half):
        there = group.rank_of(1, half - d)
        x_copy(half - 1 + d, there, partner_core).wait_recv()
        project(there)

    saves = [
        pltpu.make_async_copy(a_all, a_out, out_sems.at[0]),
        pltpu.make_async_copy(q_all, q_out, out_sems.at[1]),
        pltpu.make_async_copy(k_all, k_out, out_sems.at[2]),
        pltpu.make_async_copy(v_all, v_out, out_sems.at[3]),
    ]
    if first:
        saves.append(pltpu.make_async_copy(joint_pair, joint_out, out_sems.at[4]))
        saves.append(pltpu.make_async_copy(x_all.at[rank], x_out, out_sems.at[5]))
        saves.append(pltpu.make_async_copy(vec_pair, vec_out, out_sems.at[6]))
    for save in saves:
        save.start()
    if not first:
        rows_copy = Deliver(group, 0, x_ref, rows_out, rows_sems)
        rows_copy.start()

    lane = lax.broadcasted_iota(jnp.int32, (rows, 128), 1)
    mask = mask_ref[...]

    def attend(at):
        here = pl.ds(pl.multiple_of(at * rows, 16), rows)
        q = q_all[here, :]
        mixed = jnp.zeros((rows, width), F32)
        totals = jnp.zeros((rows, 128), F32)
        for head in range(heads):
            mine = head_lanes((rows, width), head)
            scores = mm_nt(jnp.where(mine, q, jnp.zeros_like(q)), k_all[...]) * SCALE2 + mask
            top = jnp.max(scores, axis=-1, keepdims=True)
            expo = jnp.exp2(scores - top)
            total = jnp.sum(expo, axis=-1, keepdims=True)
            part = mm(expo.astype(BF16), v_all[...]) / total
            mixed = jnp.where(mine, part, mixed)
            totals = jnp.where(lane == head, top + jnp.log2(total), totals)
        lse[here, :] = totals
        return mixed.astype(BF16)

    copies = []
    for dc, d in group.others():
        slot = group.slot(dc, d)
        o_send[slot] = attend(group.rank_of(dc, d))
        copies.append(send(o_send.at[slot], o_recv.at[rank], o_sems, slot, group.device(dc, d)))
        copies[-1].start()
    if not first:
        pl.when(core == 1)(lambda: cot_far.wait())
        pl.when(core == 0)(lambda: cot_load.wait())
        cot_share = send(cot_own, cot_other, cot_sems, 1, partner_core)
        cot_share.start()
    o_recv[rank] = attend(rank)
    if not first:
        cot_share.wait()
        cot_out[0] = cot_own[...]
        cot_out[1] = cot_other[...]
    lse_out[...] = lse[...]
    for copy in copies:
        copy.wait()
    o_out[...] = o_recv[...]
    for save in saves:
        save.wait()
    if not first:
        rows_copy.wait()
    for d in range(1, half):
        x_copy(d - 1, rank, group.device(0, d)).wait_send()
        x_copy(half - 1 + d, group.rank_of(0, half - d), partner_core).wait_send()
    x_copy(half - 1, rank, partner_core).wait_send()
    if first:
        pl.when(core == 1)(lambda: far_copy.wait_send())
        for copy in wide_copies:
            copy.wait_send()
        vec_copy.wait_send()
        wout_copy.wait()


def attend_call(first, layer, mask, ranks, dp_count, *args):
    rows = args[0].shape[-2]
    width = D // ranks
    half = ranks // 2
    span = half * width
    anywhere = pl.BlockSpec(memory_space=pl.ANY)
    vmem = pl.BlockSpec(memory_space=pltpu.VMEM)
    out_shape = [
        jax.ShapeDtypeStruct((ranks, rows, width), BF16),
        jax.ShapeDtypeStruct((LEN, 128), F32),
        jax.ShapeDtypeStruct((LEN, D), BF16),
        jax.ShapeDtypeStruct((LEN, width), BF16),
        jax.ShapeDtypeStruct((LEN, width), BF16),
        jax.ShapeDtypeStruct((LEN, width), BF16),
    ]
    out_specs = [vmem, vmem] + [anywhere] * 4
    scratch = [
        pltpu.VMEM((ranks, rows, D), BF16),
        pltpu.VMEM((LEN, D), BF16),
        pltpu.VMEM((LEN, width), BF16),
        pltpu.VMEM((LEN, width), BF16),
        pltpu.VMEM((LEN, width), BF16),
        pltpu.VMEM((LEN, 128), F32),
        pltpu.VMEM((ranks, rows, width), BF16),
        pltpu.VMEM((ranks, rows, width), BF16),
    ]
    scratch += dma_pair(2 * half) + dma_pair(ranks) + [pltpu.SemaphoreType.DMA((7,))]
    if first:
        operands = args[:3] + (mask,) + args[3:]
        in_specs = [anywhere] * 3 + [vmem] * (1 + len(args[3:]))
        out_shape += [
            jax.ShapeDtypeStruct((rows, D), BF16),
            jax.ShapeDtypeStruct((2, D, 3 * width), BF16),
            jax.ShapeDtypeStruct((D, D), BF16),
            jax.ShapeDtypeStruct((2, VEC_ROWS, D), F32),
        ]
        out_specs += [anywhere] * 4
        scratch += [
            pltpu.VMEM((2, D, 3 * width), BF16),
            pltpu.VMEM((3, D, span), BF16),
            pltpu.VMEM((3, D, span), BF16),
            pltpu.VMEM((VEC_ROWS, D), F32),
            pltpu.VMEM((VEC_ROWS, D), F32),
            pltpu.VMEM((2, VEC_ROWS, D), F32),
        ]
        scratch += dma_pair(3) + dma_pair(2) + [pltpu.SemaphoreType.DMA((4,))]
    else:
        operands = args[:2] + (mask,) + args[2:]
        in_specs = [anywhere] * 2 + [vmem] * 2 + [anywhere]
        out_shape += [jax.ShapeDtypeStruct((2, rows, D), BF16)] * 2
        out_specs += [vmem, anywhere]
        scratch += [
            pltpu.VMEM((D, 3 * width), BF16),
            pltpu.VMEM((rows, D), BF16),
            pltpu.VMEM((rows, D), BF16),
        ]
        scratch += dma_pair(2) + [pltpu.SemaphoreType.DMA((3,))] + deliver_sems()
    return pl.pallas_call(
        functools.partial(attend_kernel, first, layer, dp_count),
        in_specs=in_specs,
        out_specs=out_specs,
        out_shape=out_shape,
        scratch_shapes=scratch,
        compiler_params=pltpu.CompilerParams(
            vmem_limit_bytes=VMEM_LIMIT, collective_id=5 + layer, has_side_effects=True
        ),
        cost_estimate=pl.CostEstimate(
            flops=40 * 10**9, bytes_accessed=20 * 2**20, transcendentals=LEN * LEN * width // DH
        ),
    )(*operands)


def mlp_kernel(
    layer,
    o_ref,
    x_ref,
    wo0_ref,
    wo1_ref,
    vec_ref,
    up0_ref,
    up1_ref,
    down0_ref,
    down1_ref,
    h_ref,
    u_ref,
    y_ref,
    a_all,
    o_all,
    g_all,
    acc,
    wo,
    a_mine,
    a_other,
    o_send,
    o_other,
    g_mine,
    g_send,
    g_other,
    send_sems,
    recv_sems,
    save_sems,
    wo_sem,
):
    step = pl.program_id(0)
    groups, rows, width = o_ref.shape
    half = groups // 2
    unit = FF // shards_of() // 2
    core = lax.axis_index("section")
    own = core == layer
    device = {"section": 1 - core}
    sems = (send_sems, recv_sems)
    a_copy = send(a_mine, a_other, sems, NCH, device)
    o_copy = send(o_send, o_other, sems, NCH + 1, device)

    def g_copy(at):
        return send(g_send.at[at], g_other.at[at], sems, at, device)

    def g_save(which, at):
        cols = pl.ds(pl.multiple_of(at * (FC // 2), FC // 2), FC // 2)
        source = g_other if which else g_mine
        return pltpu.make_async_copy(
            source.at[at], g_all.at[which, :, cols], save_sems.at[which, at]
        )

    @pl.when(step == 0)
    def _():
        barrier = pltpu.get_barrier_semaphore()
        pl.semaphore_signal(
            barrier, inc=1, device_id=device, device_id_type=pl.DeviceIdType.MESH
        )
        pl.semaphore_wait(barrier, 1)
        first = pltpu.make_async_copy(wo0_ref, wo, wo_sem)
        second = pltpu.make_async_copy(wo1_ref, wo, wo_sem)
        pl.when(own)(lambda: first.start())
        pl.when(jnp.logical_not(own))(lambda: second.start())
        for i in range(half):
            o_send[i] = o_ref[(1 - core) * half + i]
            o_all[0, :, i * width : (i + 1) * width] = o_ref[core * half + i]
        o_copy.start()
        first.wait()
        hidden = x_ref[...].astype(F32) + vec_ref[0, B_OUT : B_OUT + 1, :]
        for group in range(groups):
            hidden += mm(o_ref[group], wo[group * width : (group + 1) * width, :])
        h_ref[...] = hidden
        normal, _ = norm_stats(hidden)
        a_mine[...] = (
            normal * vec_ref[0, LN2_GAIN : LN2_GAIN + 1, :] + vec_ref[0, LN2_BIAS : LN2_BIAS + 1, :]
        ).astype(BF16)
        a_copy.start()
        acc[...] = hidden + vec_ref[0, B_DOWN : B_DOWN + 1, :]

    def part(up_ref, down_ref):
        at = pl.multiple_of(lax.rem(step, D // FC) * FC, FC)
        bias = vec_ref[0, pl.ds(B_UP + lax.div(step, D // FC), 1), pl.ds(at, FC)]
        upper = mm(a_mine[...], up_ref[...]) + bias
        u_ref[...] = upper
        inner = GELU_A * (upper + GELU_B * upper * upper * upper)
        gated = (0.5 * upper * (1.0 + jnp.tanh(inner))).astype(BF16)
        split_halves(gated, unit, core, g_mine, g_send, step)
        acc[...] += mm(gated, down_ref[...])

    @pl.when(step < NCH)
    def _():
        pl.when(own)(lambda: part(up0_ref, down0_ref))
        pl.when(jnp.logical_not(own))(lambda: part(up1_ref, down1_ref))
        g_copy(step).start()
        g_save(0, step).start()

    @pl.when(step > 0)
    def _():
        g_copy(step - 1).wait()
        g_save(1, step - 1).start()

    @pl.when(step == NCH)
    def _():
        y_ref[...] = acc[...].astype(BF16)
        a_copy.wait()
        a_all[0] = a_mine[...]
        a_all[1] = a_other[...]
        o_copy.wait()
        for i in range(half):
            o_all[1, :, i * width : (i + 1) * width] = o_other[i]

        def drain(at, carry):
            g_save(0, at).wait()
            g_save(1, at).wait()
            return carry

        lax.fori_loop(0, NCH, drain, 0)


def mlp_call(layer, o_all, x_own, outs, vec, ups, downs):
    rows = x_own.shape[0]
    groups, _, width = o_all.shape
    whole = lambda i: (0, 0)
    now = lambda i: jnp.minimum(i, NCH - 1)
    mine = lambda i, first: jnp.where((lax.axis_index("section") == layer) == first, now(i), 0)
    col = lambda first: (lambda i: (0, mine(i, first)))
    line = lambda first: (lambda i: (mine(i, first), 0))
    chunk = lambda i: (0, now(i))
    piece = pltpu.VMEM((NCH, rows, FC // 2), BF16)
    return pl.pallas_call(
        functools.partial(mlp_kernel, layer),
        grid=(NCH + 1,),
        in_specs=[
            pl.BlockSpec((groups, rows, width), lambda i: (0, 0, 0)),
            pl.BlockSpec((rows, D), whole),
            pl.BlockSpec(memory_space=pl.ANY),
            pl.BlockSpec(memory_space=pl.ANY),
            pl.BlockSpec((1, VEC_ROWS, D), lambda i: (layer, 0, 0)),
            pl.BlockSpec((D, FC), col(True)),
            pl.BlockSpec((D, FC), col(False)),
            pl.BlockSpec((FC, D), line(True)),
            pl.BlockSpec((FC, D), line(False)),
        ],
        out_specs=[
            pl.BlockSpec((rows, D), whole),
            pl.BlockSpec((rows, FC), chunk),
            pl.BlockSpec((rows, D), whole),
            pl.BlockSpec((2, rows, D), lambda i: (0, 0, 0)),
            pl.BlockSpec((2, rows, D // 2), lambda i: (0, 0, 0)),
            pl.BlockSpec(memory_space=pl.ANY),
        ],
        scratch_shapes=[
            pltpu.VMEM((rows, D), F32),
            pltpu.VMEM((D, D), BF16),
            pltpu.VMEM((rows, D), BF16),
            pltpu.VMEM((rows, D), BF16),
            pltpu.VMEM((groups // 2, rows, width), BF16),
            pltpu.VMEM((groups // 2, rows, width), BF16),
            piece,
            piece,
            piece,
        ]
        + dma_pair(NCH + 2)
        + [pltpu.SemaphoreType.DMA((2, NCH)), pltpu.SemaphoreType.DMA],
        out_shape=[
            jax.ShapeDtypeStruct((rows, D), F32),
            jax.ShapeDtypeStruct((rows, FF), F32),
            jax.ShapeDtypeStruct((rows, D), BF16),
            jax.ShapeDtypeStruct((2, rows, D), BF16),
            jax.ShapeDtypeStruct((2, rows, D // 2), BF16),
            jax.ShapeDtypeStruct((2, rows, FF // 2), BF16),
        ],
        compiler_params=pltpu.CompilerParams(
            vmem_limit_bytes=VMEM_LIMIT, collective_id=7 + layer, has_side_effects=True
        ),
        cost_estimate=pl.CostEstimate(
            flops=2 * rows * D * (D + 2 * FF), bytes_accessed=30 * 2**20, transcendentals=rows * FF
        ),
    )(o_all, x_own, outs[0], outs[1], vec, ups[0], ups[1], downs[0], downs[1])


def back_kernel(layer, host, ranges, *refs):
    n = host.arrays - 1
    refs = list(refs)

    def pop(count):
        taken = refs[:count]
        del refs[:count]
        return taken

    u_ref, mask_ref, vec_ref = pop(3)
    dy_src, h_src, a2_src, wo0_src, wo1_src, up0_src, up1_src, down0_src, down1_src = pop(9)
    rows_src = pop(1)[0]
    late = pop(8)
    srcs = pop(n)
    gbup_ref, sums_two_ref, sums_one_ref, sums_qv_ref = pop(4)
    gup_out, dx_out, gjoint_out, gout_out, rows_out = pop(5)
    outs = pop(n + 1)
    dy, h, a2, wo, ups, downs = pop(6)
    load_sems, weight_sems = pop(2)
    acc, du_mine, du_send, du_recv, gup, branch, dh, do_send, do_recv = pop(9)
    du_sems, do_sems = pop(2), pop(2)
    gup_sems, save_sems = pop(2)
    q_all, k_all, v_all, lse, a1, w_joint, x_own, mixed = pop(8)
    late_sems = pop(1)[0]
    dk_acc, dv_acc, dj, core_recv, far_send, far_recv = pop(6)
    core_send = a2 if lax.axis_size("seq") == 4 else pop(1)[0]
    g_own, g_send, g_recv, gout, dx_recv = pop(5)
    dx_own = dy
    core_sems, far_sems, pair_sems = pop(2), pop(2), pop(2)
    rows_sems = pop(3)
    host.bind(list(srcs) + [gup_out], outs, refs)
    group = Group()
    core, half, rank = group.core, group.half, group.rank
    step = pl.program_id(0)
    ranks, rows, width = do_send.shape
    length = q_all.shape[0]
    heads = width // DH
    scale = DH ** (-0.5)
    unit = FF // shards_of() // 2
    own = core == layer
    partner_core = group.device(1, 0)
    ranges = list(ranges)
    lead, middle = ranges[: 2 * NCH], ranges[2 * NCH : 2 * NCH + 3]
    blocks = length // BQ * heads
    inner = ranges[2 * NCH + 3 : 2 * NCH + 3 + blocks]
    tail = ranges[2 * NCH + 3 + blocks :]

    def weight_copies(at, second):
        slot = lax.rem(at, 2)
        cols = pl.ds(pl.multiple_of(at * FC, FC), FC)
        up, down = (up1_src, down1_src) if second else (up0_src, down0_src)
        return (
            pltpu.make_async_copy(up.at[:, cols], ups.at[slot], weight_sems.at[0, slot]),
            pltpu.make_async_copy(down.at[cols, :], downs.at[slot], weight_sems.at[1, slot]),
        )

    def fetch(at):
        @pl.when(own)
        def _():
            for copy in weight_copies(at, False):
                copy.start()

        @pl.when(jnp.logical_not(own))
        def _():
            for copy in weight_copies(at, True):
                copy.start()

    rows_copy = Deliver(group, 1, rows_src, rows_out, rows_sems)
    dy_load = pltpu.make_async_copy(dy_src, dy, load_sems.at[0])
    h_load = pltpu.make_async_copy(h_src, h, load_sems.at[1])
    a2_load = pltpu.make_async_copy(a2_src, a2, load_sems.at[2])
    wo_load = pltpu.make_async_copy(wo0_src, wo, load_sems.at[3])
    wo_load_other = pltpu.make_async_copy(wo1_src, wo, load_sems.at[3])
    late_loads = [
        pltpu.make_async_copy(source, target, late_sems.at[i])
        for i, (source, target) in enumerate(
            zip(late, (q_all, k_all, v_all, lse, a1, w_joint, x_own, mixed))
        )
    ]

    def du_copy(at):
        return send(du_send.at[at], du_recv.at[at], du_sems, at, partner_core)

    def gup_save(at):
        per = gup.shape[1]
        lead_bits = NCH.bit_length() - 1
        index = tuple(
            lax.rem(lax.div(at, 2 ** (lead_bits - 1 - j)), 2) for j in range(lead_bits)
        )
        return pltpu.make_async_copy(
            gup.at[lax.rem(at, 2)].reshape(gup_out.shape[lead_bits:]),
            gup_out.at[index],
            gup_sems.at[lax.rem(at, 2)],
        )

    @pl.when(step == 0)
    def _():
        group.greet(host.dp_count)
        rows_copy.start()
        dy_load.start()
        fetch(0)
        host.begin()
        a2_load.start()
        h_load.start()
        pl.when(own)(lambda: wo_load.start())
        pl.when(jnp.logical_not(own))(lambda: wo_load_other.start())
        for load in late_loads:
            load.start()
        acc[...] = jnp.zeros_like(acc)
        dy_load.wait()
        a2_load.wait()

    @pl.when(step < NCH - 1)
    def _():
        fetch(step + 1)

    @pl.when(step < NCH)
    def _():
        slot = lax.rem(step, 2)
        for copy in weight_copies(step, False):
            copy.wait()
        d_gated = mm_nt(dy[...], downs[slot])
        upper = u_ref[...]
        square = upper * upper
        turn = jnp.tanh(GELU_A * upper * (1.0 + GELU_B * square))
        slope = 0.5 * (1.0 + turn) + (0.5 * GELU_A) * upper * (1.0 - turn * turn) * (
            1.0 + (3.0 * GELU_B) * square
        )
        d_upper = (d_gated * slope).astype(BF16)
        split_halves(d_upper, unit, core, du_mine, du_send, step)
        du_copy(step).start()
        gbup_ref[...] = jnp.sum(d_upper.astype(F32), axis=0, keepdims=True)
        acc[...] += mm_nt(d_upper, ups[slot])

    for at, (first, last) in enumerate(lead):
        if last > first and at % 2 == 0:
            pl.when(step == at // 2)(functools.partial(host.run, first, last))

    @pl.when(step > 0)
    def _():
        at = step - 1
        du_copy(at).wait()
        pl.when(at >= 2)(lambda: gup_save(at - 2).wait())
        value = mm_tn(du_mine[at], a2[0]) + mm_tn(du_recv[at], a2[1])
        gup[lax.rem(at, 2)] = value.astype(BF16).reshape(gup.shape[1:])
        gup_save(at).start()

    for at, (first, last) in enumerate(lead):
        if last > first and at % 2 == 1:
            pl.when(step == at // 2)(functools.partial(host.run, first, last))

    @pl.when(step == NCH)
    def _():
        h_load.wait()
        gup_save(NCH - 2).wait()
        gup_save(NCH - 1).wait()
        host.begin(1)
        normal, inverse = norm_stats(h[...])
        d_out = dy[...].astype(F32)
        d_normed = acc[...]
        sums_two_ref[...] = jnp.zeros_like(sums_two_ref)
        sums_two_ref[0:1, :] = jnp.sum(d_normed * normal, axis=0, keepdims=True)
        sums_two_ref[1:2, :] = jnp.sum(d_normed, axis=0, keepdims=True)
        d_normal = d_normed * vec_ref[0, LN2_GAIN : LN2_GAIN + 1, :]
        d_hidden = d_out + inverse * (
            d_normal
            - jnp.mean(d_normal, axis=-1, keepdims=True)
            - normal * jnp.mean(d_normal * normal, axis=-1, keepdims=True)
        )
        dh[...] = d_hidden
        d_branch = d_hidden.astype(BF16)
        branch[0] = d_branch
        branch_copy = send(branch.at[0], branch.at[1], do_sems, ranks, partner_core)
        branch_copy.start()
        wo_load.wait()

        def heads_of(to_rank):
            at = pl.multiple_of(to_rank * width, width)
            return mm_nt(d_branch, wo[pl.ds(at, width), :]).astype(BF16)

        copies = []
        for dc, d in group.others():
            slot = group.slot(dc, d)
            do_send[slot] = heads_of(group.rank_of(dc, d))
            copies.append(
                send(do_send.at[slot], do_recv.at[pl.ds(pl.multiple_of(rank * rows, 16), rows)], do_sems, slot, group.device(dc, d))
            )
            copies[-1].start()
        do_recv[pl.ds(pl.multiple_of(rank * rows, 16), rows), :] = heads_of(rank)
        host.run(*middle[0])
        sums_two_ref[2:3, :] = jnp.sum(d_branch.astype(F32), axis=0, keepdims=True)
        sums_two_ref[3:4, :] = jnp.sum(d_out, axis=0, keepdims=True)
        dk_acc[...] = jnp.zeros_like(dk_acc)
        dv_acc[...] = jnp.zeros_like(dv_acc)
        sums_qv_ref[...] = jnp.zeros_like(sums_qv_ref)
        sums_one_ref[...] = jnp.zeros_like(sums_one_ref)
        for load in late_loads:
            load.wait()
        branch_copy.wait()
        gout[...] = (mm_tn(branch[0], mixed[0]) + mm_tn(branch[1], mixed[1])).astype(BF16)
        gout_save = pltpu.make_async_copy(gout, gout_out, save_sems.at[0])
        gout_save.start()
        host.run(*middle[1])
        for copy in copies:
            copy.wait()
        host.run(*middle[2])

        def block(at, carry):
            here = pl.ds(pl.multiple_of(at * BQ, BQ), BQ)
            q = q_all[here, :]
            grad = do_recv[here, :]
            totals = lse[here, :]
            d_q = jnp.zeros((BQ, width), F32)
            for head in range(heads):
                mine = head_lanes((BQ, width), head)
                q_head = jnp.where(mine, q, jnp.zeros_like(q))
                grad_head = jnp.where(mine, grad, jnp.zeros_like(grad))
                scores = mm_nt(q_head, k_all[...]) * SCALE2 + mask_ref[...]
                probs = jnp.exp2(scores - totals[:, head : head + 1])
                d_probs = mm_nt(grad_head, v_all[...])
                term = jnp.sum(probs * d_probs, axis=-1, keepdims=True)
                d_scores = (probs * (d_probs - term)).astype(BF16)
                dv_acc[...] += mm_tn(probs.astype(BF16), grad_head)
                dk_acc[...] += mm_tn(d_scores, q_head)
                d_q = jnp.where(mine, mm(d_scores, k_all[...]), d_q)
                for slot, (first, last) in enumerate(inner):
                    if last > first and slot % heads == head:
                        pl.when(at == slot // heads)(functools.partial(host.run, first, last))
            low = (d_q * scale).astype(BF16)
            dj[here, :width] = low
            sums_qv_ref[0:1, :] += jnp.sum(low.astype(F32), axis=0, keepdims=True)
            return carry

        lax.fori_loop(0, length // BQ, block, 0)
        dj[:, width : 2 * width] = (dk_acc[...] * scale).astype(BF16)
        low_v = dv_acc[...].astype(BF16)
        dj[:, 2 * width :] = low_v
        sums_qv_ref[1:2, :] = jnp.sum(low_v.astype(F32), axis=0, keepdims=True)

        def partial_rows(to_rank):
            here = pl.ds(pl.multiple_of(to_rank * rows, 16), rows)
            return mm_nt(dj[here, :], w_joint[...])

        def core_copy(d):
            return send(core_send.at[d], core_recv.at[d], core_sems, d, partner_core)

        def far_copy(d):
            return send(far_send.at[d - 1], far_recv.at[d - 1], far_sems, d - 1, group.device(0, d))

        for d in [d for d in range(1, half)] + [0]:
            core_send[d] = partial_rows(group.rank_of(1, d)).astype(BF16)
            core_copy(d).start()
        for d in range(1, half):
            value = partial_rows(group.rank_of(0, d))
            core_copy(d).wait_recv()
            far_send[d - 1] = (value + core_recv[d].astype(F32)).astype(BF16)
            far_copy(d).start()
        host.run(*tail[0])
        value = partial_rows(rank)
        core_copy(0).wait_recv()
        acc[...] = value + core_recv[0].astype(F32)

        half_cols = D // 2
        mine_cols = pl.ds(pl.multiple_of(core * half_cols, half_cols), half_cols)
        other_cols = pl.ds(pl.multiple_of((1 - core) * half_cols, half_cols), half_cols)
        g_send[...] = mm_tn(dj[...], a1[:, other_cols]).astype(BF16).reshape(g_send.shape)
        g_copy = send(g_send, g_recv, pair_sems, 0, partner_core)
        g_copy.start()
        host.run(*tail[1])
        g_own[...] = mm_tn(dj[...], a1[:, mine_cols]).astype(BF16).reshape(g_own.shape)
        g_save = pltpu.make_async_copy(g_own, gjoint_out.at[:, core], save_sems.at[1])
        g_save.start()
        host.run(*tail[2])

        for d in range(1, half):
            far_copy(d).wait_recv()
            acc[...] += far_recv[d - 1].astype(F32)
        d_normed = acc[...]
        normal, inverse = norm_stats(x_own[...].astype(F32))
        sums_one_ref[0:1, :] = jnp.sum(d_normed * normal, axis=0, keepdims=True)
        sums_one_ref[1:2, :] = jnp.sum(d_normed, axis=0, keepdims=True)
        d_normal = d_normed * vec_ref[0, LN1_GAIN : LN1_GAIN + 1, :]
        d_in = (
            dh[...]
            + inverse
            * (
                d_normal
                - jnp.mean(d_normal, axis=-1, keepdims=True)
                - normal * jnp.mean(d_normal * normal, axis=-1, keepdims=True)
            )
        ).astype(BF16)
        dx_own[...] = d_in
        dx_copy = send(dx_own, dx_recv, pair_sems, 1, partner_core)
        dx_copy.start()
        dx_save = pltpu.make_async_copy(dx_own, dx_out.at[0], save_sems.at[2])
        dx_save.start()
        host.run(*tail[3])
        g_copy.wait()
        g_save_other = pltpu.make_async_copy(g_recv, gjoint_out.at[:, 1 - core], save_sems.at[3])
        g_save_other.start()
        dx_copy.wait()
        dx_save_other = pltpu.make_async_copy(dx_recv, dx_out.at[1], save_sems.at[4])
        dx_save_other.start()
        for d in range(half):
            core_copy(d).wait_send()
        for d in range(1, half):
            far_copy(d).wait_send()
        for save in (gout_save, g_save, dx_save, g_save_other, dx_save_other):
            save.wait()
        rows_copy.wait()
        host.finish()


def back_call(layer, dy, hidden, wos, vec, upper, a2, ups, downs, given, late, mask, host, arrays):
    rows = dy.shape[0]
    ranks = host.count
    width = D // ranks
    half = ranks // 2
    shards = host.dp_count * ranks
    per = shards // NCH
    unit = FF // shards // 2
    heads = width // DH
    now = lambda i: (0, jnp.minimum(i, NCH - 1))
    whole = lambda i: (0, 0)
    anywhere = pl.BlockSpec(memory_space=pl.ANY)
    times = []
    for i in range(NCH):
        times += [2.9 * i + 1.6, 2.9 * i + 2.9]
    times += [29.0, 33.0, 36.0]
    for i in range(LEN // BQ * heads):
        times.append(36.0 + 28.0 / (LEN // BQ * heads) * (i + 1))
    times += [69.0, 73.0, 76.0, 84.0]
    ranges = host.slots(times)
    piece = pltpu.VMEM((NCH, rows, FC // 2), BF16)
    tokens = pltpu.VMEM((LEN, width), BF16)
    own = pltpu.VMEM((rows, D), BF16)
    view = host.view_shape(host.arrays - 1)
    return pl.pallas_call(
        functools.partial(back_kernel, layer, host, ranges),
        grid=(NCH + 1,),
        in_specs=[
            pl.BlockSpec((rows, FC), now),
            pl.BlockSpec((1, LEN), whole),
            pl.BlockSpec((1, VEC_ROWS, D), lambda i: (layer, 0, 0)),
        ]
        + [anywhere] * (10 + len(late) + len(arrays)),
        out_specs=[
            pl.BlockSpec((1, FC), now),
            pl.BlockSpec((8, D), whole),
            pl.BlockSpec((8, D), whole),
            pl.BlockSpec((8, width), whole),
        ]
        + [anywhere] * 5
        + host.out_specs(),
        out_shape=[
            jax.ShapeDtypeStruct((1, FF), F32),
            jax.ShapeDtypeStruct((8, D), F32),
            jax.ShapeDtypeStruct((8, D), F32),
            jax.ShapeDtypeStruct((8, width), F32),
            jax.ShapeDtypeStruct(view, BF16),
            jax.ShapeDtypeStruct((2, rows, D), BF16),
            jax.ShapeDtypeStruct((3, 2, width, D // 2), BF16),
            jax.ShapeDtypeStruct((D, D // 2), BF16),
            jax.ShapeDtypeStruct((2, rows, D), BF16),
        ]
        + host.out_shapes(),
        scratch_shapes=[
            own,
            pltpu.VMEM((rows, D), F32),
            pltpu.VMEM((2, rows, D), BF16),
            pltpu.VMEM((D, D), BF16),
            pltpu.VMEM((2, D, FC), BF16),
            pltpu.VMEM((2, FC, D), BF16),
            pltpu.SemaphoreType.DMA((4,)),
            pltpu.SemaphoreType.DMA((2, 2)),
            pltpu.VMEM((rows, D), F32),
            piece,
            piece,
            piece,
            pltpu.VMEM((2, per, unit, D), BF16),
            pltpu.VMEM((2, rows, D), BF16),
            pltpu.VMEM((rows, D), F32),
            pltpu.VMEM((ranks, rows, width), BF16),
            tokens,
        ]
        + dma_pair(NCH)
        + dma_pair(ranks + 1)
        + [pltpu.SemaphoreType.DMA((2,)), pltpu.SemaphoreType.DMA((5,))]
        + [pltpu.VMEM(t.shape, t.dtype) for t in late]
        + [pltpu.SemaphoreType.DMA((len(late),))]
        + [
            pltpu.VMEM((LEN, width), F32),
            pltpu.VMEM((LEN, width), F32),
            pltpu.VMEM((LEN, 3 * width), BF16),
            pltpu.VMEM((half, rows, D), BF16),
            pltpu.VMEM((half - 1, rows, D), BF16),
            pltpu.VMEM((half - 1, rows, D), BF16),
        ]
        + ([] if ranks == 4 else [pltpu.VMEM((half, rows, D), BF16)])
        + [
            pltpu.VMEM((3, width, D // 2), BF16),
            pltpu.VMEM((3, width, D // 2), BF16),
            pltpu.VMEM((3, width, D // 2), BF16),
            pltpu.VMEM((D, D // 2), BF16),
            own,
        ]
        + dma_pair(half)
        + dma_pair(half - 1)
        + dma_pair(2)
        + deliver_sems()
        + host.scratch(),
        compiler_params=pltpu.CompilerParams(
            vmem_limit_bytes=BACK_LIMIT, collective_id=layer, has_side_effects=True
        ),
        cost_estimate=pl.CostEstimate(
            flops=100 * 10**9, bytes_accessed=60 * 2**20, transcendentals=rows * FF
        ),
    )(
        upper,
        mask,
        vec,
        dy,
        hidden,
        a2,
        wos[0],
        wos[1],
        ups[0],
        ups[1],
        downs[0],
        downs[1],
        given,
        *late,
        *[host.view(i, array) for i, array in enumerate(arrays)],
    )


def final_kernel(host, *refs):
    refs = list(refs)

    def pop(count):
        taken = refs[:count]
        del refs[:count]
        return taken

    n = host.arrays
    srcs = pop(n)
    downs, ups = pop(2), pop(2)
    others = pop(3)
    rows_src = pop(1)[0]
    up_out, down_out, out_out, joint_out = pop(4)
    vec_outs = pop(9)
    rows_out = pop(1)[0]
    down, up = pop(2)
    held = pop(3)
    load_sems = pop(1)[0]
    rows_sems = pop(3)
    host.bind(srcs, [], refs)
    group = Group()
    core = group.core
    compact = group.half == 2
    group.greet(host.dp_count)
    host.begin()
    rows_copy = Deliver(group, 0, rows_src, rows_out, rows_sems)
    rows_copy.start()
    loads = []
    for i, (pair, target) in enumerate(((downs, down), (ups, up))):
        first = pltpu.make_async_copy(pair[0], target, load_sems.at[i])
        second = pltpu.make_async_copy(pair[1], target, load_sems.at[i])
        pl.when(core == 0)(functools.partial(first.start))
        pl.when(core == 1)(functools.partial(second.start))
        loads.append(first)
    for i, (source, target) in enumerate(zip(others, held)):
        loads.append(pltpu.make_async_copy(source, target, load_sems.at[2 + i]))
        loads[-1].start()
    for load in loads:
        load.wait()
    unit = up.shape[1]
    half_cols = D // 2
    for half in range(2):
        up_out[:, half * unit : (half + 1) * unit] = up[half].T
    for half in range(2):
        turned = down[half].T
        for g in range(FF // 2 // unit):
            at = (2 * g + half) * unit
            down_out[at : at + unit, :] = turned[g * unit : (g + 1) * unit, :]
    host.run(0, len(host.events))
    host.settle()

    def chosen(index, half):
        return jnp.where(core == 0, host.sums[index][half], held[index][half])

    for half in range(2):
        turned = chosen(0, half).T
        if compact:
            heads = half_cols // DH // 2
            for low in range(2):
                for i in range(heads):
                    to = (half * 2 * heads + 2 * i + low) * DH
                    at = (low * heads + i) * DH
                    out_out[to : to + DH, :] = turned[at : at + DH, :]
        else:
            out_out[half * half_cols : (half + 1) * half_cols, :] = turned
        value = chosen(1, half)
        if compact:
            low = group.low
            pieces = [value[i * DH : (i + 1) * DH, :] for i in range(4)]
            ordered_pieces = (
                jnp.where(low == 0, pieces[0], pieces[1]),
                pieces[3],
                jnp.where(low == 0, pieces[1], pieces[2]),
            )
            for i, piece in enumerate(ordered_pieces):
                joint_out[half * half_cols : (half + 1) * half_cols, i * DH : (i + 1) * DH] = piece.T
        else:
            joint_out[half * half_cols : (half + 1) * half_cols, :] = value.T
    small = chosen(2, 0) + chosen(2, 1)
    at = 0
    for out in vec_outs:
        size = out.shape[1]
        for start in range(0, size, 128):
            take_lanes = min(128, size - start)
            row, lane = (at + start) // 128, (at + start) % 128
            out[:, start : start + take_lanes] = small[row : row + 1, lane : lane + take_lanes]
        at += size
    rows_copy.wait()


def final_call(host, arrays, downs, ups, others, rows_src, collective_id):
    rows = rows_src.shape[0]
    groups = host.dp_count * host.count
    unit = D // groups
    anywhere = pl.BlockSpec(memory_space=pl.ANY)
    vmem = pl.BlockSpec(memory_space=pltpu.VMEM)
    sizes = [unit] * 8 + [FF // groups]
    return pl.pallas_call(
        functools.partial(final_kernel, host),
        in_specs=[anywhere] * (host.arrays + 8),
        out_specs=[vmem] * 13 + [anywhere],
        out_shape=[
            jax.ShapeDtypeStruct((D, FF // groups), F32),
            jax.ShapeDtypeStruct((FF, unit), F32),
            jax.ShapeDtypeStruct((D, unit), F32),
            jax.ShapeDtypeStruct((D, 3 * unit), F32),
        ]
        + [jax.ShapeDtypeStruct((1, size), F32) for size in sizes]
        + [jax.ShapeDtypeStruct((2, rows, D), BF16)],
        scratch_shapes=[
            pltpu.VMEM(downs[0].shape, F32),
            pltpu.VMEM(ups[0].shape, F32),
        ]
        + [pltpu.VMEM(o.shape, F32) for o in others]
        + [pltpu.SemaphoreType.DMA((5,))]
        + deliver_sems()
        + host.scratch(),
        compiler_params=pltpu.CompilerParams(
            vmem_limit_bytes=VMEM_LIMIT, collective_id=collective_id, has_side_effects=True
        ),
        cost_estimate=pl.CostEstimate(
            flops=10**9, bytes_accessed=60 * 2**20, transcendentals=0
        ),
    )(*host.views(arrays), *downs, *ups, *others, rows_src)


def swap(value, axis, mask):
    count = lax.axis_size(axis)
    return lax.ppermute(value, axis, [(i, i ^ mask) for i in range(count)])


def take(value, index, dim):
    return lax.dynamic_index_in_dim(value, index, dim, keepdims=False)


def ordered(bit, mine, other, dim):
    return jnp.where(
        bit == 0,
        jnp.stack([mine, other], axis=dim),
        jnp.stack([other, mine], axis=dim),
    )


def key_bias(counts, rotate):
    places = jnp.arange(LEN, dtype=jnp.int32)
    places = jnp.where(rotate, (places + LEN // 2) % LEN, places)
    offset = jnp.maximum(places - TRI, 0)
    view_index = offset // VSLOT
    inside = offset - view_index * VSLOT
    match = view_index[:, None] == jnp.arange(VIEWS, dtype=jnp.int32)[None, :]
    limits = jnp.sum(jnp.where(match, counts[None, :], 0), axis=1)
    valid = (places < TRI) | (inside < limits)
    return jnp.where(valid, 0.0, -1e30).astype(F32)[None, :]


def shards(
    inputs,
    cotangent,
    view_tokens,
    ln1_gain,
    ln1_bias,
    w_qkv,
    b_query,
    b_value,
    w_out,
    b_out,
    ln2_gain,
    ln2_bias,
    w_up,
    b_up,
    w_down,
    b_down,
):
    core = lax.axis_index("section")
    place = lax.axis_index("seq")
    dp_index = lax.axis_index("dp")
    count = lax.axis_size("seq")
    dp_count = lax.axis_size("dp")
    groups = dp_count * count
    half = count // 2
    micro = place // half
    low = place % half
    low_bits = half.bit_length() - 1
    rows = inputs.shape[2]
    width = D // count
    rank = core * half + low

    def swap_core(value):
        return swap(value, "section", 1)

    def swap_seq(value, bit):
        return swap(value, "seq", 1 << bit)

    def low_bit(bit):
        return (place >> bit) & 1

    def own_rows(local):
        chunks = local[:, 0]
        far = lax.ppermute(
            take(chunks, 1 - micro, 0),
            ("section", "seq"),
            [(count + z, count + (z ^ half)) for z in range(count)],
        )
        return jnp.where(core == 0, take(chunks, micro, 0), far)

    def gather_rows(own):
        value = own[None]
        for bit in range(low_bits):
            other = swap_seq(value, bit)
            value = ordered(low_bit(bit), value, other, 0).reshape((-1,) + own.shape)
        value = ordered(core, value, swap_core(value), 0)
        return value.reshape((-1,) + own.shape[1:])

    def exchange(value):
        tail = value.shape[1:]
        value = value.reshape((2,) * (low_bits + 1) + tail)
        for bit in range(low_bits):
            dim = low_bits - bit
            mine = take(value, low_bit(bit), dim)
            other = swap_seq(take(value, 1 - low_bit(bit), dim), bit)
            value = ordered(low_bit(bit), mine, other, dim)
        mine = take(value, core, 0)
        other = swap_core(take(value, 1 - core, 0))
        return ordered(core, mine, other, 0).reshape((count,) + tail)

    compact = half == 2
    span = half * width

    def vector_to(value):
        if compact:
            wide = jnp.stack(
                [jnp.where(low == i, value.reshape(2, -1, DH), 0.0) for i in range(2)], axis=2
            )
        else:
            wide = jnp.stack([jnp.where(low == i, value, 0.0) for i in range(half)], axis=1)
        wide = wide.reshape(2, span)
        return jnp.concatenate([jnp.where(core == i, wide, 0.0) for i in range(2)], axis=1)

    def rank_rows(value):
        if compact:
            value = value.reshape(2, width // DH, 2, DH, D)
            return jnp.swapaxes(value, 1, 2).reshape(D, D)
        return value

    out_mine = rank_rows(w_out[0])
    ups = (w_up[0], swap_core(w_up[0]))
    downs = (w_down[0], swap_core(w_down[0]))
    bias_mask = key_bias(take(view_tokens[:, 0], micro, 0), micro == 1)

    saved = []
    acts = []
    for layer in range(2):
        if layer == 0:
            o_own, lse, a1, q, k, v, layer_in, joint_pair, out_other, vec = attend_call(
                True,
                0,
                bias_mask,
                count,
                dp_count,
                inputs,
                w_qkv,
                out_mine[None],
                ln1_gain,
                ln1_bias,
                b_query,
                b_value,
                b_out,
                ln2_gain,
                ln2_bias,
                b_down,
                b_up,
            )
            outs_pair = (out_mine, out_other)
        else:
            o_own, lse, a1, q, k, v, d_out_all, first_rows = attend_call(
                False, 1, bias_mask, count, dp_count, layer_in, joint_pair[1], vec[1:2], cotangent
            )
        hidden, upper, output, a2_all, o_all, gated_all = mlp_call(
            layer, o_own, layer_in, outs_pair, vec, ups, downs
        )
        acts.append(output)
        saved.append((layer_in, a1, q, k, v, lse, hidden, upper, a2_all, o_all, gated_all))
        layer_in = output

    def hosted(arrays, spans=None):
        shapes = []
        for array in arrays:
            shapes.append((array.shape[1], array.shape[2], array.shape[0] != groups, array.dtype))
        return Hosted(dp_count, count, tuple(shapes), spans)

    results = [{}, {}]
    pending = None
    d_out = d_out_all[0]
    for layer in (1, 0):
        x_own, a1, q, k, v, lse, hidden, upper, a2_all, o_all, gated_all = saved[layer]
        g_down = mm_tn(d_out_all.reshape(2 * rows, D), gated_all.reshape(2 * rows, FF // 2))
        g_down = g_down.astype(BF16).reshape(groups, D // groups, FF // 2)
        up_like = jax.ShapeDtypeStruct((groups, FF // groups // 2, D), BF16)
        if pending is None:
            arrays = [g_down]
            host = hosted(arrays + [up_like], ((0, 0.0, 52.0), (1, 28.0, 84.0)))
        else:
            arrays = list(pending) + [g_down]
            host = hosted(
                arrays + [up_like],
                ((0, 0.0, 30.0), (0, 0.0, 30.0), (0, 0.0, 30.0), (0, 5.0, 68.0), (1, 40.0, 105.0)),
            )
        (g_bup, sums_two, sums_one, sums_qv, g_up, d_in, g_joint, g_out, given, *reduced) = back_call(
            layer,
            d_out,
            hidden,
            outs_pair,
            vec,
            upper,
            a2_all,
            ups,
            downs,
            acts[1] if pending is None else d_out,
            (q, k, v, lse, a1, joint_pair[layer], x_own, o_all),
            bias_mask,
            host,
            arrays,
        )
        if pending is None:
            second_rows = given
        else:
            second_grads = given
            for name in ("out", "joint", "small"):
                results[1][name] = reduced.pop(0)
        results[layer]["down"], results[layer]["up"] = reduced
        g_out = g_out.reshape(groups, D // groups, D // 2)
        if compact:
            g_joint = g_joint.reshape(groups // 2, 3 * D // groups, D // 2)
        else:
            spread = jnp.stack(
                [jnp.where(low == i, g_joint, jnp.zeros_like(g_joint)) for i in range(half)], axis=2
            )
            g_joint = spread.reshape(groups, 3 * D // groups, D // 2)
        wide = vector_to(sums_qv[0:2])
        rows_of = jnp.concatenate([sums_one[0:2], wide, sums_two[2:3], sums_two[0:2], sums_two[3:4]])
        small = jnp.concatenate(
            [
                jnp.swapaxes(rows_of.reshape(8, groups, D // groups), 0, 1).reshape(groups, -1),
                g_bup.reshape(groups, FF // groups),
            ],
            axis=1,
        )
        lines = -(-small.shape[1] // 128)
        lines += -lines % 8
        small = jnp.pad(small, ((0, 0), (0, lines * 128 - small.shape[1])))
        small = small.reshape(groups, lines, 128)
        if pending is None:
            pending = (g_out, g_joint, small)
        else:
            arrays = (g_out, g_joint, small)
            results[0]["last"] = final_call(
                hosted(arrays),
                arrays,
                (results[0]["down"], results[1]["down"]),
                (results[0]["up"], results[1]["up"]),
                [results[1][name] for name in ("out", "joint", "small")],
                d_in[0],
                4,
            )
        d_out = d_in[0]
        d_out_all = d_in

    g_w_up, g_w_down, g_w_out, g_w_qkv, *pieces, first_grads = results[0]["last"]
    acts_rows = jnp.where(core == 0, first_rows, second_rows)
    grad_rows = jnp.where(core == 0, first_grads, second_grads)
    g_ln1g, g_ln1b, g_bq, g_bv, g_bo, g_ln2g, g_ln2b, g_bd, g_bup = pieces
    return (
        acts_rows[None, :, None],
        grad_rows[None, :, None],
        g_ln1g,
        g_ln1b,
        g_w_qkv[None],
        g_bq,
        g_bv,
        g_w_out[None],
        g_bo,
        g_ln2g,
        g_ln2b,
        g_w_up[None],
        g_bup,
        g_w_down[None],
        g_bd,
    )


def solution(mesh):
    rows = P(None, "dp", "seq", None)
    vector = P("section", None)
    matrix = P("section", None, None)
    placed = (
        rows,
        rows,
        P(None, "dp", None),
        vector,
        vector,
        matrix,
        vector,
        vector,
        matrix,
        vector,
        vector,
        vector,
        matrix,
        vector,
        matrix,
        vector,
    )
    both = P("section", None, "dp", "seq", None)
    line = P("section", ("dp", "seq"))
    table = P("section", None, ("dp", "seq"))
    return jax.shard_map(
        shards,
        mesh=mesh,
        in_specs=placed,
        out_specs=(
            both,
            both,
            line,
            line,
            table,
            line,
            line,
            table,
            line,
            line,
            line,
            table,
            line,
            table,
            line,
        ),
        check_vma=False,
    )
```

```python
import functools
import math

import jax
import jax.numpy as jnp
from jax import lax
from jax.experimental import pallas as pl
from jax.experimental.pallas import tpu as pltpu
from jax.sharding import PartitionSpec as P

D = 1024
H = 16
DH = 64
FF = 4096
VIEWS = 6
TRI = 512
VSLOT = 128
MICRO = 2
LEN = 1280
BQ = 256
NCH = 8
FC = FF // NCH
SCALE2 = DH ** (-0.5) * math.log2(math.e)
F32 = jnp.float32
BF16 = jnp.bfloat16
VMEM_LIMIT = 56 * 2**20


def params():
    return pltpu.CompilerParams(vmem_limit_bytes=VMEM_LIMIT)


def mm(a, b):
    return lax.dot_general(a, b, (((1,), (0,)), ((), ())), preferred_element_type=F32)


def mm_nt(a, b):
    return lax.dot_general(a, b, (((1,), (1,)), ((), ())), preferred_element_type=F32)


def mm_tn(a, b):
    return lax.dot_general(a, b, (((0,), (0,)), ((), ())), preferred_element_type=F32)


def norm_stats(values):
    average = jnp.mean(values, axis=-1, keepdims=True)
    centered = values - average
    variance = jnp.mean(centered * centered, axis=-1, keepdims=True)
    inverse = lax.rsqrt(variance + 1e-05)
    return centered * inverse, inverse


def head_lanes(shape, head):
    lane = lax.broadcasted_iota(jnp.int32, shape, 1)
    return (lane >= head * DH) & (lane < (head + 1) * DH)


def shards_of():
    return lax.axis_size("dp") * lax.axis_size("seq")


def split_halves(value, unit, core, mine, other, step):
    for at in range(0, value.shape[1] // unit, 2):
        even = value[:, at * unit : (at + 1) * unit]
        odd = value[:, (at + 1) * unit : (at + 2) * unit]
        cols = slice(at // 2 * unit, (at // 2 + 1) * unit)
        mine[step, :, cols] = jnp.where(core == 0, even, odd)
        other[step, :, cols] = jnp.where(core == 0, odd, even)


GELU_A = math.sqrt(2.0 / math.pi)
GELU_B = 0.044715


MESH_AXES = ("dp", "seq")


def axis_bits(dp_count, count):
    bits = []
    for axis, size in (("dp", dp_count), ("seq", count)):
        mask = size // 2
        while mask:
            bits.append((axis, mask))
            mask //= 2
    return bits


def stream_orders(dp_count, count):
    dp_bits = dp_count.bit_length() - 1
    seq_bits = count.bit_length() - 1
    dp_dims = list(range(dp_bits))
    seq_dims = list(range(dp_bits, dp_bits + seq_bits))[::-1]
    return (
        dp_dims[::-1] + seq_dims,
        dp_dims + seq_dims,
        seq_dims[:1] + dp_dims + seq_dims[1:],
        seq_dims[:1] + dp_dims[::-1] + seq_dims[1:],
    )


def my_bit(axis, mask):
    return lax.rem(lax.div(lax.axis_index(axis), mask), 2)


def partner(axis, mask):
    return lax.axis_index(axis) + mask * (1 - 2 * my_bit(axis, mask))


def greet(bits):
    barrier = pltpu.get_barrier_semaphore()
    for axis, mask in bits:
        pl.semaphore_signal(
            barrier,
            inc=1,
            device_id={axis: partner(axis, mask)},
            device_id_type=pl.DeviceIdType.MESH,
        )
    pl.semaphore_wait(barrier, len(bits))


class Reducer:
    def __init__(self, bits, order, src, cols, out, rows, compact, buffers, sems):
        self.bits, self.order, self.src, self.cols = bits, order, src, cols
        self.out, self.out_cols, self.buffers, self.sems = out, cols, buffers, sems
        self.count, self.rows, self.compact = len(bits), rows, compact

    @staticmethod
    def scratch(count, rows, width, dtype):
        shapes = [pltpu.VMEM((2,) * (count - 1) + (rows, width), dtype)]
        for stage in range(count):
            shapes.append(pltpu.VMEM((2,) * (count - 1 - stage) + (rows, width), dtype))
        shapes += [
            pltpu.SemaphoreType.DMA((count + 2,)),
            pltpu.SemaphoreType.DMA((count + 2,)),
            pltpu.SemaphoreType.DMA,
        ]
        return shapes

    def place(self, stage):
        left = [d for d in range(self.count) if d not in self.order[:stage]]
        dim = self.order[stage]
        return left, left.index(dim), self.bits[dim]

    def cut(self, stage, index):
        left, at, _ = self.place(stage)
        where = [slice(None)] * len(left)
        where[at] = index
        return tuple(where)

    def source(self, stage):
        if stage == 0:
            return self.src
        return self.buffers[0] if stage == 1 else self.buffers[stage]

    def copy(self, stage):
        axis, mask = self.place(stage)[2]
        where = self.cut(stage, 1 - my_bit(axis, mask))
        if stage == 0:
            where = where + (slice(None), pl.ds(*self.cols))
        return pltpu.make_async_remote_copy(
            src_ref=self.source(stage).at[where],
            dst_ref=self.buffers[stage + 1],
            send_sem=self.sems[0].at[stage],
            recv_sem=self.sems[1].at[stage],
            device_id={axis: partner(axis, mask)},
            device_id_type=pl.DeviceIdType.MESH,
        )

    def load(self):
        axis, mask = self.place(0)[2]
        where = self.cut(0, my_bit(axis, mask)) + (slice(None), pl.ds(*self.cols))
        return pltpu.make_async_copy(self.src.at[where], self.buffers[0], self.sems[2])

    def share(self):
        core = lax.axis_index("section")
        return pltpu.make_async_remote_copy(
            src_ref=self.out.at[core, :, pl.ds(*self.out_cols)],
            dst_ref=self.out.at[core, :, pl.ds(*self.out_cols)],
            send_sem=self.sems[0].at[self.count],
            recv_sem=self.sems[1].at[self.count],
            device_id={"section": 1 - core},
            device_id_type=pl.DeviceIdType.MESH,
        )

    def trade(self):
        third = self.rows // 3
        core = lax.axis_index("section")
        bit = lax.rem(lax.axis_index("seq"), 2)
        row = pl.multiple_of((1 - bit) * 2 * third, third)
        return pltpu.make_async_remote_copy(
            src_ref=self.out.at[core, pl.ds(row, third), pl.ds(*self.out_cols)],
            dst_ref=self.out.at[core, pl.ds(self.rows, third), pl.ds(*self.out_cols)],
            send_sem=self.sems[0].at[self.count + 1],
            recv_sem=self.sems[1].at[self.count + 1],
            device_id={"seq": partner("seq", 1)},
            device_id_type=pl.DeviceIdType.MESH,
        )

    def begin(self):
        self.copy(0).start()
        self.load().start()

    def step(self, stage):
        left, at, (axis, mask) = self.place(stage)
        bit = my_bit(axis, mask)
        if stage == 0:
            self.load().wait()
        self.copy(stage).wait_recv()
        got = self.buffers[stage + 1]
        rows = got.shape[-2]
        chunk = rows
        while chunk * got.shape[-1] > 65536 and chunk % 32 == 0:
            chunk //= 2
        per = rows // chunk
        last = stage == self.count - 1
        core = lax.axis_index("section")
        total = 2 ** (len(left) - 1)

        def body(i, carry):
            flat = lax.div(i, per)
            row = pl.multiple_of(lax.rem(i, per) * chunk, chunk)
            index = []
            for j in range(len(left) - 1):
                index.append(lax.rem(lax.div(flat, 2 ** (len(left) - 2 - j)), 2))
            there = tuple(index) + (pl.ds(row, chunk), slice(None))
            if stage == 0:
                mine = self.buffers[0][there]
            else:
                own = index[:at] + [bit] + index[at:]
                mine = self.source(stage)[tuple(own) + (pl.ds(row, chunk), slice(None))]
            value = mine.astype(F32) + got[there].astype(F32)
            if last:
                self.out[core, pl.ds(row, chunk), pl.ds(*self.out_cols)] = value
            elif stage == 0:
                self.buffers[0][there] = value.astype(got.dtype)
            else:
                got[there] = value.astype(got.dtype)
            return carry

        lax.fori_loop(0, total * per, body, 0)
        if not last:
            self.copy(stage + 1).start()
        elif self.compact:
            self.trade().start()
        else:
            self.share().start()

    def tail(self):
        if self.compact:
            self.trade().wait()
            self.share().start()

    def finish(self):
        for stage in range(self.count):
            self.copy(stage).wait_send()
        self.share().wait()


def part_widths(width):
    unit = 128 if width % 128 == 0 else width
    tiles = width // unit
    rest = tiles // 8
    first = -(-(tiles - rest) // 2)
    second = rest // 2
    return tuple(unit * n for n in (first, tiles - rest - first, rest - second, second))


STAGE_SHARES = (0.45, 0.7, 0.9, 1.0)


class Hosted:
    def __init__(self, dp_count, count, shapes, spans=None, shares=STAGE_SHARES):
        self.dp_count, self.count, self.shapes = dp_count, count, shapes
        self.spans = spans or ((0, 0.0, 1.0),) * len(shapes)
        self.all_bits = axis_bits(dp_count, count)
        self.plan = []
        for index, (rows, width, compact, _) in enumerate(shapes):
            bits = self.all_bits[:-1] if compact else self.all_bits
            orders = stream_orders(dp_count, count)
            widths = part_widths(width)
            if compact:
                last = len(bits)
                orders = [tuple(d for d in order if d != last) for order in orders[:2]]
                widths = (width // 2, width // 2)
            start = 0
            for order, size in zip(orders, widths):
                pieces = [size] if size else []
                if size >= 256 and not compact:
                    first = 128 * -(-size // 256)
                    pieces = [first, size - first]
                for k, piece in enumerate(pieces):
                    self.plan.append((index, tuple(order), bits, start, piece, rows, compact, k))
                    start += piece
        self.plan.sort(key=lambda p: (p[0], p[7]))
        self.arrays = len(shapes)
        self.events = []
        for k, part in enumerate(self.plan):
            phase, first, last = self.spans[part[0]]
            if phase == 0 and first > 0.0:
                self.events.append((first, k, -1))
            for stage in range(len(part[2])):
                share = shares[min(stage, 3)]
                self.events.append((first + (last - first) * share + 0.01 * stage, k, stage))
        self.events.sort()

    def views(self, arrays):
        return [self.view(i, array) for i, array in enumerate(arrays)]

    def view_shape(self, index):
        rows, width, compact, _ = self.shapes[index]
        depth = len(self.all_bits) - (1 if compact else 0)
        return (2,) * depth + (rows, width)

    def view(self, index, array):
        return array.reshape(self.view_shape(index))

    def in_specs(self):
        return [pl.BlockSpec(memory_space=pl.ANY)] * self.arrays

    def out_shapes(self):
        return [
            jax.ShapeDtypeStruct((2, rows + (rows // 3 if compact else 0), width), F32)
            for rows, width, compact, _ in self.shapes
        ]

    def out_specs(self):
        return [pl.BlockSpec(memory_space=pl.ANY)] * self.arrays

    def scratch(self):
        shapes = [pltpu.VMEM(o.shape, F32) for o in self.out_shapes()]
        shapes.append(pltpu.SemaphoreType.DMA((max(1, self.arrays),)))
        for index, _, bits, _, size, rows, _, _ in self.plan:
            shapes += Reducer.scratch(len(bits), rows, size, self.shapes[index][3])
        return shapes

    def bind(self, srcs, outs, scratch):
        self.parts = []
        self.outs, self.sums = outs, scratch[: self.arrays]
        self.out_sems = scratch[self.arrays]
        at = self.arrays + 1
        for index, order, bits, start, size, rows, compact, _ in self.plan:
            depth = len(bits) + 1
            mine = scratch[at : at + depth + 3]
            at += depth + 3
            self.parts.append(
                Reducer(
                    bits,
                    order,
                    srcs[index],
                    (start, size),
                    self.sums[index],
                    rows,
                    compact,
                    mine[:depth],
                    mine[depth:],
                )
            )

    def begin(self, phase=0):
        for part, plan in zip(self.parts, self.plan):
            span = self.spans[plan[0]]
            if span[0] == phase and (phase or span[1] == 0.0):
                part.begin()

    def run(self, first, last):
        for _, k, stage in self.events[first:last]:
            if stage < 0:
                self.parts[k].begin()
            else:
                self.parts[k].step(stage)

    def slots(self, times):
        edges = []
        done = 0
        for time in times:
            while done < len(self.events) and self.events[done][0] <= time:
                done += 1
            edges.append(done)
        edges[-1] = len(self.events)
        return list(zip([0] + edges[:-1], edges))

    def settle(self):
        for part in self.parts:
            part.tail()
        for part in self.parts:
            part.finish()

    def finish(self):
        self.settle()
        copies = []
        for i, (out, value) in enumerate(zip(self.outs, self.sums)):
            copies.append(pltpu.make_async_copy(value, out, self.out_sems.at[i]))
            copies[-1].start()
        for copy in copies:
            copy.wait()


BACK_LIMIT = 64 * 2**20 - 2**18


class Group:
    def __init__(self):
        self.half = lax.axis_size("seq") // 2
        self.core = lax.axis_index("section")
        self.place = lax.axis_index("seq")
        self.low = lax.rem(self.place, self.half)
        self.base = self.place - self.low
        self.rank = self.core * self.half + self.low

    def others(self):
        pairs = [(dc, d) for d in range(1, self.half) for dc in (0, 1)]
        return pairs + [(1, 0)]

    def slot(self, dc, d):
        return dc * self.half + d

    def where(self, dc, d):
        core = lax.rem(self.core + dc, 2)
        low = lax.rem(self.low + d, self.half)
        return core, low

    def device(self, dc, d):
        core, low = self.where(dc, d)
        return {"section": core, "seq": self.base + low}

    def rank_of(self, dc, d):
        core, low = self.where(dc, d)
        return core * self.half + low

    def greet(self, dp_count):
        barrier = pltpu.get_barrier_semaphore()
        targets = [self.device(dc, d) for dc, d in self.others()]
        mask = dp_count // 2
        while mask:
            targets.append({"dp": partner("dp", mask)})
            mask //= 2
        targets.append({"seq": partner("seq", self.half)})
        targets.append({"section": 1 - self.core, "seq": partner("seq", self.half)})
        for target in targets:
            pl.semaphore_signal(
                barrier, inc=1, device_id=target, device_id_type=pl.DeviceIdType.MESH
            )
        pl.semaphore_wait(barrier, len(targets))


def send(src, dst, sems, slot, device):
    return pltpu.make_async_remote_copy(
        src_ref=src,
        dst_ref=dst,
        send_sem=sems[0].at[slot],
        recv_sem=sems[1].at[slot],
        device_id=device,
        device_id_type=pl.DeviceIdType.MESH,
    )


class Deliver:
    def __init__(self, group, layer, src, out, sems):
        micro = lax.div(group.place, group.half)
        here, there = sems[0], sems[1]
        self.core, self.layer = group.core, layer
        self.local = pltpu.make_async_copy(src, out.at[micro], sems[2])
        self.chip = send(src, out.at[micro], (here, there), 0, {"section": 1 - group.core})
        self.far = send(
            src,
            out.at[micro],
            (here, there),
            1,
            {"section": layer, "seq": partner("seq", group.half)},
        )

    def start(self):
        first = self.local if self.layer == 0 else self.chip
        pl.when(self.core == 0)(lambda: first.start())
        pl.when(self.core == 1)(lambda: self.far.start())

    def wait(self):
        @pl.when(self.core == 0)
        def _():
            if self.layer == 0:
                self.local.wait()
                self.far.wait_recv()
            else:
                self.chip.wait_send()

        @pl.when(self.core == 1)
        def _():
            self.far.wait_send()
            if self.layer == 1:
                self.far.wait_recv()
                self.chip.wait_recv()


def deliver_sems():
    return dma_pair(2) + [pltpu.SemaphoreType.DMA]


def dma_pair(count):
    return [pltpu.SemaphoreType.DMA((count,)), pltpu.SemaphoreType.DMA((count,))]


VEC_ROWS = 16
LN1_GAIN, LN1_BIAS, B_QUERY, B_VALUE, B_OUT, LN2_GAIN, LN2_BIAS, B_DOWN, B_UP = range(9)


def attend_kernel(first, layer, dp_count, *refs):
    if first:
        x_ref, joint_ref, wout_ref, mask_ref = refs[:4]
        vectors = refs[4:13]
        o_out, lse_out, a_out, q_out, k_out, v_out = refs[13:19]
        x_out, joint_out, wout_out, vec_out = refs[19:23]
        rest = refs[23:]
    else:
        x_ref, joint_ref, mask_ref, vec_ref, cot_ref = refs[:5]
        o_out, lse_out, a_out, q_out, k_out, v_out, cot_out = refs[5:12]
        rest = refs[12:]
    x_all, a_all, q_all, k_all, v_all, lse, o_send, o_recv = rest[:8]
    x_sems, o_sems = rest[8:10], rest[10:12]
    out_sems = rest[12]
    if first:
        joint_pair, wide_own, wide_other, vec_send, vec_recv, vec_pair = rest[13:19]
        wide_sems, vec_sems = rest[19:21], rest[21:23]
        load_sems = rest[23]
    else:
        joint_one, cot_own, cot_other = rest[13:16]
        cot_sems = rest[16:18]
        load_sems = rest[18]
    group = Group()
    core, half, rank, low = group.core, group.half, group.rank, group.low
    ranks, rows, _ = x_all.shape
    width = q_all.shape[1]
    heads = width // DH
    span = half * width
    partner_core = group.device(1, 0)
    micro = lax.div(group.place, half)

    group.greet(dp_count)

    def x_copy(slot, from_rank, device):
        return send(x_all.at[from_rank], x_all.at[from_rank], x_sems, slot, device)

    far = {"seq": partner("seq", half)}

    if first:
        own_load = pltpu.make_async_copy(x_ref.at[micro, 0], x_all.at[rank], load_sems.at[0])
        far_copy = send(x_ref.at[1 - micro, 0], x_all.at[rank], x_sems, 2 * half - 1, far)
        pl.when(core == 1)(lambda: far_copy.start())
        pl.when(core == 0)(lambda: own_load.start())
        wide_copies = []
        own_loads = []
        for part in range(3):
            theirs = pl.ds(pl.multiple_of(part * D + (1 - core) * span, 128), span)
            ours = pl.ds(pl.multiple_of(part * D + core * span, 128), span)
            wide_copies.append(
                send(joint_ref.at[0, :, theirs], wide_other.at[part], wide_sems, part, partner_core)
            )
            own_loads.append(
                pltpu.make_async_copy(
                    joint_ref.at[0, :, ours], wide_own.at[part], load_sems.at[1 + part]
                )
            )
            wide_copies[-1].start()
            own_loads[-1].start()
        vec_send[...] = jnp.zeros_like(vec_send)
        for i, value in enumerate(vectors[:8]):
            vec_send[i : i + 1, :] = value[...].astype(F32)
        for i in range(FF // D):
            vec_send[8 + i : 9 + i, :] = vectors[8][:, i * D : (i + 1) * D].astype(F32)
        vec_copy = send(vec_send, vec_recv, vec_sems, 0, partner_core)
        vec_copy.start()
        wout_copy = send(wout_ref.at[0], wout_out, vec_sems, 1, partner_core)
        pl.when(core == 1)(lambda: far_copy.wait_recv())
        pl.when(core == 0)(lambda: own_load.wait())
    else:
        own_load = pltpu.make_async_copy(x_ref, x_all.at[rank], load_sems.at[0])
        joint_load = pltpu.make_async_copy(joint_ref.at[1], joint_one, load_sems.at[1])
        own_load.start()
        joint_load.start()
        cot_far = send(cot_ref.at[1 - micro, 0], cot_own, cot_sems, 0, far)
        cot_load = pltpu.make_async_copy(cot_ref.at[micro, 0], cot_own, load_sems.at[2])
        pl.when(core == 1)(lambda: cot_far.start())
        pl.when(core == 0)(lambda: cot_load.start())
        own_load.wait()
    for d in range(1, half):
        x_copy(d - 1, rank, group.device(0, d)).start()
    x_copy(half - 1, rank, partner_core).start()

    source = lax.broadcasted_iota(jnp.int32, (span, width), 0)
    target = lax.broadcasted_iota(jnp.int32, (span, width), 1)
    if half == 2:
        wanted = (2 * lax.div(target, DH) + low) * DH + lax.rem(target, DH)
    else:
        wanted = low * width + target
    pick = (source == wanted).astype(F32).astype(BF16)
    if first:
        wout_copy.start()
        vec_copy.wait_recv()
        vec_pair[core] = vec_send[...]
        vec_pair[1 - core] = vec_recv[...]
        for load in own_loads:
            load.wait()
        for part in range(3):
            joint_pair[core, :, part * width : (part + 1) * width] = mm(
                wide_own[part], pick
            ).astype(BF16)
        for copy in wide_copies:
            copy.wait_recv()
        for part in range(3):
            joint_pair[1 - core, :, part * width : (part + 1) * width] = mm(
                wide_other[part], pick
            ).astype(BF16)
        vec = vec_pair[0]
        weights = lambda: joint_pair[0]
    else:
        joint_load.wait()
        vec = vec_ref[1]
        weights = lambda: joint_one[...]

    def of_heads(row):
        parts = vec[row : row + 1, :]
        mine = jnp.where(core == 0, parts[:, :span], parts[:, span:])
        wide = jnp.broadcast_to(mine, (16, span)).astype(BF16)
        return mm(wide, pick)[0:1, :]

    bias_q = of_heads(B_QUERY)
    bias_v = of_heads(B_VALUE)
    gain = vec[LN1_GAIN : LN1_GAIN + 1, :]
    shift = vec[LN1_BIAS : LN1_BIAS + 1, :]

    def project(at):
        normal, _ = norm_stats(x_all[at].astype(F32))
        a = (normal * gain + shift).astype(BF16)
        here = pl.ds(pl.multiple_of(at * rows, 16), rows)
        a_all[here, :] = a
        joined = mm(a, weights())
        q_all[here, :] = (joined[:, :width] + bias_q).astype(BF16)
        k_all[here, :] = joined[:, width : 2 * width].astype(BF16)
        v_all[here, :] = (joined[:, 2 * width :] + bias_v).astype(BF16)

    project(rank)
    x_copy(half - 1, rank, partner_core).wait_recv()
    project(group.rank_of(1, 0))
    for d in range(1, half):
        here = group.rank_of(0, half - d)
        x_copy(d - 1, here, partner_core).wait_recv()
        x_copy(half - 1 + d, here, partner_core).start()
        project(here)
    for d in range(1, half):
        there = group.rank_of(1, half - d)
        x_copy(half - 1 + d, there, partner_core).wait_recv()
        project(there)

    saves = [
        pltpu.make_async_copy(a_all, a_out, out_sems.at[0]),
        pltpu.make_async_copy(q_all, q_out, out_sems.at[1]),
        pltpu.make_async_copy(k_all, k_out, out_sems.at[2]),
        pltpu.make_async_copy(v_all, v_out, out_sems.at[3]),
    ]
    if first:
        saves.append(pltpu.make_async_copy(joint_pair, joint_out, out_sems.at[4]))
        saves.append(pltpu.make_async_copy(x_all.at[rank], x_out, out_sems.at[5]))
        saves.append(pltpu.make_async_copy(vec_pair, vec_out, out_sems.at[6]))
    for save in saves:
        save.start()
    lane = lax.broadcasted_iota(jnp.int32, (rows, 128), 1)
    mask = mask_ref[...]

    def attend(at):
        here = pl.ds(pl.multiple_of(at * rows, 16), rows)
        q = q_all[here, :]
        mixed = jnp.zeros((rows, width), F32)
        totals = jnp.zeros((rows, 128), F32)
        for head in range(heads):
            mine = head_lanes((rows, width), head)
            scores = mm_nt(jnp.where(mine, q, jnp.zeros_like(q)), k_all[...]) * SCALE2 + mask
            top = jnp.max(scores, axis=-1, keepdims=True)
            expo = jnp.exp2(scores - top)
            total = jnp.sum(expo, axis=-1, keepdims=True)
            part = mm(expo.astype(BF16), v_all[...]) / total
            mixed = jnp.where(mine, part, mixed)
            totals = jnp.where(lane == head, top + jnp.log2(total), totals)
        lse[here, :] = totals
        return mixed.astype(BF16)

    copies = []
    for dc, d in group.others():
        slot = group.slot(dc, d)
        o_send[slot] = attend(group.rank_of(dc, d))
        copies.append(send(o_send.at[slot], o_recv.at[rank], o_sems, slot, group.device(dc, d)))
        copies[-1].start()
    if not first:
        pl.when(core == 1)(lambda: cot_far.wait())
        pl.when(core == 0)(lambda: cot_load.wait())
        cot_share = send(cot_own, cot_other, cot_sems, 1, partner_core)
        cot_share.start()
    o_recv[rank] = attend(rank)
    if not first:
        cot_share.wait()
        cot_out[0] = cot_own[...]
        cot_out[1] = cot_other[...]
    lse_out[...] = lse[...]
    for copy in copies:
        copy.wait()
    o_out[...] = o_recv[...]
    for save in saves:
        save.wait()
    for d in range(1, half):
        x_copy(d - 1, rank, group.device(0, d)).wait_send()
        x_copy(half - 1 + d, group.rank_of(0, half - d), partner_core).wait_send()
    x_copy(half - 1, rank, partner_core).wait_send()
    if first:
        pl.when(core == 1)(lambda: far_copy.wait_send())
        for copy in wide_copies:
            copy.wait_send()
        vec_copy.wait_send()
        wout_copy.wait()


def attend_call(first, layer, mask, ranks, dp_count, *args):
    rows = args[0].shape[-2]
    width = D // ranks
    half = ranks // 2
    span = half * width
    anywhere = pl.BlockSpec(memory_space=pl.ANY)
    vmem = pl.BlockSpec(memory_space=pltpu.VMEM)
    out_shape = [
        jax.ShapeDtypeStruct((ranks, rows, width), BF16),
        jax.ShapeDtypeStruct((LEN, 128), F32),
        jax.ShapeDtypeStruct((LEN, D), BF16),
        jax.ShapeDtypeStruct((LEN, width), BF16),
        jax.ShapeDtypeStruct((LEN, width), BF16),
        jax.ShapeDtypeStruct((LEN, width), BF16),
    ]
    out_specs = [vmem, vmem] + [anywhere] * 4
    scratch = [
        pltpu.VMEM((ranks, rows, D), BF16),
        pltpu.VMEM((LEN, D), BF16),
        pltpu.VMEM((LEN, width), BF16),
        pltpu.VMEM((LEN, width), BF16),
        pltpu.VMEM((LEN, width), BF16),
        pltpu.VMEM((LEN, 128), F32),
        pltpu.VMEM((ranks, rows, width), BF16),
        pltpu.VMEM((ranks, rows, width), BF16),
    ]
    scratch += dma_pair(2 * half) + dma_pair(ranks) + [pltpu.SemaphoreType.DMA((7,))]
    if first:
        operands = args[:3] + (mask,) + args[3:]
        in_specs = [anywhere] * 3 + [vmem] * (1 + len(args[3:]))
        out_shape += [
            jax.ShapeDtypeStruct((rows, D), BF16),
            jax.ShapeDtypeStruct((2, D, 3 * width), BF16),
            jax.ShapeDtypeStruct((D, D), BF16),
            jax.ShapeDtypeStruct((2, VEC_ROWS, D), F32),
        ]
        out_specs += [anywhere] * 4
        scratch += [
            pltpu.VMEM((2, D, 3 * width), BF16),
            pltpu.VMEM((3, D, span), BF16),
            pltpu.VMEM((3, D, span), BF16),
            pltpu.VMEM((VEC_ROWS, D), F32),
            pltpu.VMEM((VEC_ROWS, D), F32),
            pltpu.VMEM((2, VEC_ROWS, D), F32),
        ]
        scratch += dma_pair(3) + dma_pair(2) + [pltpu.SemaphoreType.DMA((4,))]
    else:
        operands = args[:2] + (mask,) + args[2:]
        in_specs = [anywhere] * 2 + [vmem] * 2 + [anywhere]
        out_shape += [jax.ShapeDtypeStruct((2, rows, D), BF16)]
        out_specs += [vmem]
        scratch += [
            pltpu.VMEM((D, 3 * width), BF16),
            pltpu.VMEM((rows, D), BF16),
            pltpu.VMEM((rows, D), BF16),
        ]
        scratch += dma_pair(2) + [pltpu.SemaphoreType.DMA((3,))]
    return pl.pallas_call(
        functools.partial(attend_kernel, first, layer, dp_count),
        in_specs=in_specs,
        out_specs=out_specs,
        out_shape=out_shape,
        scratch_shapes=scratch,
        compiler_params=pltpu.CompilerParams(
            vmem_limit_bytes=VMEM_LIMIT, collective_id=5 + layer, has_side_effects=True
        ),
        cost_estimate=pl.CostEstimate(
            flops=40 * 10**9, bytes_accessed=20 * 2**20, transcendentals=LEN * LEN * width // DH
        ),
    )(*operands)


def mlp_kernel(
    layer,
    dp_count,
    o_ref,
    x_ref,
    wo0_ref,
    wo1_ref,
    vec_ref,
    up0_ref,
    up1_ref,
    down0_ref,
    down1_ref,
    h_ref,
    u_ref,
    y_ref,
    a_all,
    o_all,
    g_all,
    rows_out,
    acc,
    wo,
    a_mine,
    a_other,
    o_send,
    o_other,
    g_mine,
    g_send,
    g_other,
    send_sems,
    recv_sems,
    save_sems,
    wo_sem,
    rows_mine,
    *rows_sems,
):
    step = pl.program_id(0)
    groups, rows, width = o_ref.shape
    half = groups // 2
    unit = FF // shards_of() // 2
    core = lax.axis_index("section")
    own = core == layer
    device = {"section": 1 - core}
    sems = (send_sems, recv_sems)
    if layer == 1:
        rows_copy = Deliver(Group(), 0, rows_mine, rows_out, rows_sems)
    a_copy = send(a_mine, a_other, sems, NCH, device)
    o_copy = send(o_send, o_other, sems, NCH + 1, device)

    def g_copy(at):
        return send(g_send.at[at], g_other.at[at], sems, at, device)

    def g_save(which, at):
        cols = pl.ds(pl.multiple_of(at * (FC // 2), FC // 2), FC // 2)
        source = g_other if which else g_mine
        return pltpu.make_async_copy(
            source.at[at], g_all.at[which, :, cols], save_sems.at[which, at]
        )

    @pl.when(step == 0)
    def _():
        Group().greet(dp_count)
        if layer == 1:
            rows_mine[...] = x_ref[...]
            rows_copy.start()
        first = pltpu.make_async_copy(wo0_ref, wo, wo_sem)
        second = pltpu.make_async_copy(wo1_ref, wo, wo_sem)
        pl.when(own)(lambda: first.start())
        pl.when(jnp.logical_not(own))(lambda: second.start())
        for i in range(half):
            o_send[i] = o_ref[(1 - core) * half + i]
            o_all[0, :, i * width : (i + 1) * width] = o_ref[core * half + i]
        o_copy.start()
        first.wait()
        hidden = x_ref[...].astype(F32) + vec_ref[0, B_OUT : B_OUT + 1, :]
        for group in range(groups):
            hidden += mm(o_ref[group], wo[group * width : (group + 1) * width, :])
        h_ref[...] = hidden
        normal, _ = norm_stats(hidden)
        a_mine[...] = (
            normal * vec_ref[0, LN2_GAIN : LN2_GAIN + 1, :] + vec_ref[0, LN2_BIAS : LN2_BIAS + 1, :]
        ).astype(BF16)
        a_copy.start()
        acc[...] = hidden + vec_ref[0, B_DOWN : B_DOWN + 1, :]

    def part(up_ref, down_ref):
        at = pl.multiple_of(lax.rem(step, D // FC) * FC, FC)
        bias = vec_ref[0, pl.ds(B_UP + lax.div(step, D // FC), 1), pl.ds(at, FC)]
        upper = mm(a_mine[...], up_ref[...]) + bias
        u_ref[...] = upper
        inner = GELU_A * (upper + GELU_B * upper * upper * upper)
        gated = (0.5 * upper * (1.0 + jnp.tanh(inner))).astype(BF16)
        split_halves(gated, unit, core, g_mine, g_send, step)
        acc[...] += mm(gated, down_ref[...])

    @pl.when(step < NCH)
    def _():
        pl.when(own)(lambda: part(up0_ref, down0_ref))
        pl.when(jnp.logical_not(own))(lambda: part(up1_ref, down1_ref))
        g_copy(step).start()
        g_save(0, step).start()

    @pl.when(step > 0)
    def _():
        g_copy(step - 1).wait()
        g_save(1, step - 1).start()

    @pl.when(step == NCH)
    def _():
        y_ref[...] = acc[...].astype(BF16)
        a_copy.wait()
        a_all[0] = a_mine[...]
        a_all[1] = a_other[...]
        o_copy.wait()
        for i in range(half):
            o_all[1, :, i * width : (i + 1) * width] = o_other[i]

        def drain(at, carry):
            g_save(0, at).wait()
            g_save(1, at).wait()
            return carry

        lax.fori_loop(0, NCH, drain, 0)
        if layer == 1:
            rows_copy.wait()


def mlp_call(layer, dp_count, o_all, x_own, outs, vec, ups, downs):
    rows = x_own.shape[0]
    groups, _, width = o_all.shape
    whole = lambda i: (0, 0)
    now = lambda i: jnp.minimum(i, NCH - 1)
    mine = lambda i, first: jnp.where((lax.axis_index("section") == layer) == first, now(i), 0)
    col = lambda first: (lambda i: (0, mine(i, first)))
    line = lambda first: (lambda i: (mine(i, first), 0))
    chunk = lambda i: (0, now(i))
    piece = pltpu.VMEM((NCH, rows, FC // 2), BF16)
    return pl.pallas_call(
        functools.partial(mlp_kernel, layer, dp_count),
        grid=(NCH + 1,),
        in_specs=[
            pl.BlockSpec((groups, rows, width), lambda i: (0, 0, 0)),
            pl.BlockSpec((rows, D), whole),
            pl.BlockSpec(memory_space=pl.ANY),
            pl.BlockSpec(memory_space=pl.ANY),
            pl.BlockSpec((1, VEC_ROWS, D), lambda i: (layer, 0, 0)),
            pl.BlockSpec((D, FC), col(True)),
            pl.BlockSpec((D, FC), col(False)),
            pl.BlockSpec((FC, D), line(True)),
            pl.BlockSpec((FC, D), line(False)),
        ],
        out_specs=[
            pl.BlockSpec((rows, D), whole),
            pl.BlockSpec((rows, FC), chunk),
            pl.BlockSpec((rows, D), whole),
            pl.BlockSpec((2, rows, D), lambda i: (0, 0, 0)),
            pl.BlockSpec((2, rows, D // 2), lambda i: (0, 0, 0)),
            pl.BlockSpec(memory_space=pl.ANY),
            pl.BlockSpec(memory_space=pl.ANY),
        ],
        scratch_shapes=[
            pltpu.VMEM((rows, D), F32),
            pltpu.VMEM((D, D), BF16),
            pltpu.VMEM((rows, D), BF16),
            pltpu.VMEM((rows, D), BF16),
            pltpu.VMEM((groups // 2, rows, width), BF16),
            pltpu.VMEM((groups // 2, rows, width), BF16),
            piece,
            piece,
            piece,
        ]
        + dma_pair(NCH + 2)
        + [pltpu.SemaphoreType.DMA((2, NCH)), pltpu.SemaphoreType.DMA]
        + [pltpu.VMEM((rows, D), BF16)]
        + deliver_sems(),
        out_shape=[
            jax.ShapeDtypeStruct((rows, D), F32),
            jax.ShapeDtypeStruct((rows, FF), F32),
            jax.ShapeDtypeStruct((rows, D), BF16),
            jax.ShapeDtypeStruct((2, rows, D), BF16),
            jax.ShapeDtypeStruct((2, rows, D // 2), BF16),
            jax.ShapeDtypeStruct((2, rows, FF // 2), BF16),
            jax.ShapeDtypeStruct((2, rows, D), BF16),
        ],
        compiler_params=pltpu.CompilerParams(
            vmem_limit_bytes=VMEM_LIMIT, collective_id=7 + layer, has_side_effects=True
        ),
        cost_estimate=pl.CostEstimate(
            flops=2 * rows * D * (D + 2 * FF), bytes_accessed=30 * 2**20, transcendentals=rows * FF
        ),
    )(o_all, x_own, outs[0], outs[1], vec, ups[0], ups[1], downs[0], downs[1])


def back_kernel(layer, host, ranges, *refs):
    n = host.arrays - 1
    refs = list(refs)

    def pop(count):
        taken = refs[:count]
        del refs[:count]
        return taken

    u_ref, mask_ref, vec_ref = pop(3)
    dy_src, h_src, a2_src, wo0_src, wo1_src, up0_src, up1_src, down0_src, down1_src = pop(9)
    rows_src = pop(1)[0]
    late = pop(8)
    srcs = pop(n)
    gbup_ref, sums_two_ref, sums_one_ref, sums_qv_ref = pop(4)
    gup_out, dx_out, gjoint_out, gout_out, rows_out = pop(5)
    outs = pop(n + 1)
    dy, h, a2, wo, ups, downs = pop(6)
    load_sems, weight_sems = pop(2)
    acc, du_mine, du_send, du_recv, gup, branch, dh, do_send, do_recv = pop(9)
    du_sems, do_sems = pop(2), pop(2)
    gup_sems, save_sems = pop(2)
    q_all, k_all, v_all, lse, a1, w_joint, x_own, mixed = pop(8)
    late_sems = pop(1)[0]
    dk_acc, dv_acc, dj, core_recv, far_send, far_recv = pop(6)
    core_send = a2 if lax.axis_size("seq") == 4 else pop(1)[0]
    g_own, g_send, g_recv, gout, dx_recv = pop(5)
    dx_own = dy
    core_sems, far_sems, pair_sems = pop(2), pop(2), pop(2)
    rows_sems = pop(3)
    host.bind(list(srcs) + [gup_out], outs, refs)
    group = Group()
    core, half, rank = group.core, group.half, group.rank
    step = pl.program_id(0)
    ranks, rows, width = do_send.shape
    length = q_all.shape[0]
    heads = width // DH
    scale = DH ** (-0.5)
    unit = FF // shards_of() // 2
    own = core == layer
    partner_core = group.device(1, 0)
    ranges = list(ranges)
    lead, middle = ranges[: 2 * NCH], ranges[2 * NCH : 2 * NCH + 3]
    blocks = length // BQ * heads
    inner = ranges[2 * NCH + 3 : 2 * NCH + 3 + blocks]
    tail = ranges[2 * NCH + 3 + blocks :]

    def weight_copies(at, second):
        slot = lax.rem(at, 2)
        cols = pl.ds(pl.multiple_of(at * FC, FC), FC)
        up, down = (up1_src, down1_src) if second else (up0_src, down0_src)
        return (
            pltpu.make_async_copy(up.at[:, cols], ups.at[slot], weight_sems.at[0, slot]),
            pltpu.make_async_copy(down.at[cols, :], downs.at[slot], weight_sems.at[1, slot]),
        )

    def fetch(at):
        @pl.when(own)
        def _():
            for copy in weight_copies(at, False):
                copy.start()

        @pl.when(jnp.logical_not(own))
        def _():
            for copy in weight_copies(at, True):
                copy.start()

    rows_copy = Deliver(group, 1, rows_src.at[0], rows_out, rows_sems)
    dy_load = pltpu.make_async_copy(dy_src.at[0], dy, load_sems.at[0])
    h_load = pltpu.make_async_copy(h_src, h, load_sems.at[1])
    a2_load = pltpu.make_async_copy(a2_src, a2, load_sems.at[2])
    wo_load = pltpu.make_async_copy(wo0_src, wo, load_sems.at[3])
    wo_load_other = pltpu.make_async_copy(wo1_src, wo, load_sems.at[3])
    late_loads = [
        pltpu.make_async_copy(source.at[layer] if i == 5 else source, target, late_sems.at[i])
        for i, (source, target) in enumerate(
            zip(late, (q_all, k_all, v_all, lse, a1, w_joint, x_own, mixed))
        )
    ]

    def du_copy(at):
        return send(du_send.at[at], du_recv.at[at], du_sems, at, partner_core)

    def gup_save(at):
        per = gup.shape[1]
        lead_bits = NCH.bit_length() - 1
        index = tuple(
            lax.rem(lax.div(at, 2 ** (lead_bits - 1 - j)), 2) for j in range(lead_bits)
        )
        return pltpu.make_async_copy(
            gup.at[lax.rem(at, 2)].reshape(gup_out.shape[lead_bits:]),
            gup_out.at[index],
            gup_sems.at[lax.rem(at, 2)],
        )

    @pl.when(step == 0)
    def _():
        group.greet(host.dp_count)
        rows_copy.start()
        dy_load.start()
        fetch(0)
        host.begin()
        a2_load.start()
        h_load.start()
        pl.when(own)(lambda: wo_load.start())
        pl.when(jnp.logical_not(own))(lambda: wo_load_other.start())
        for load in late_loads:
            load.start()
        acc[...] = jnp.zeros_like(acc)
        dy_load.wait()
        a2_load.wait()

    @pl.when(step < NCH - 1)
    def _():
        fetch(step + 1)

    @pl.when(step < NCH)
    def _():
        slot = lax.rem(step, 2)
        for copy in weight_copies(step, False):
            copy.wait()
        d_gated = mm_nt(dy[...], downs[slot])
        upper = u_ref[...]
        square = upper * upper
        turn = jnp.tanh(GELU_A * upper * (1.0 + GELU_B * square))
        slope = 0.5 * (1.0 + turn) + (0.5 * GELU_A) * upper * (1.0 - turn * turn) * (
            1.0 + (3.0 * GELU_B) * square
        )
        d_upper = (d_gated * slope).astype(BF16)
        split_halves(d_upper, unit, core, du_mine, du_send, step)
        du_copy(step).start()
        gbup_ref[...] = jnp.sum(d_upper.astype(F32), axis=0, keepdims=True)
        acc[...] += mm_nt(d_upper, ups[slot])

    for at, (first, last) in enumerate(lead):
        if last > first and at % 2 == 0:
            pl.when(step == at // 2)(functools.partial(host.run, first, last))

    @pl.when(step > 0)
    def _():
        at = step - 1
        du_copy(at).wait()
        pl.when(at >= 2)(lambda: gup_save(at - 2).wait())
        value = mm_tn(du_mine[at], a2[0]) + mm_tn(du_recv[at], a2[1])
        gup[lax.rem(at, 2)] = value.astype(BF16).reshape(gup.shape[1:])
        gup_save(at).start()

    for at, (first, last) in enumerate(lead):
        if last > first and at % 2 == 1:
            pl.when(step == at // 2)(functools.partial(host.run, first, last))

    @pl.when(step == NCH)
    def _():
        h_load.wait()
        gup_save(NCH - 2).wait()
        gup_save(NCH - 1).wait()
        host.begin(1)
        normal, inverse = norm_stats(h[...])
        d_out = dy[...].astype(F32)
        d_normed = acc[...]
        sums_two_ref[...] = jnp.zeros_like(sums_two_ref)
        sums_two_ref[0:1, :] = jnp.sum(d_normed * normal, axis=0, keepdims=True)
        sums_two_ref[1:2, :] = jnp.sum(d_normed, axis=0, keepdims=True)
        d_normal = d_normed * vec_ref[0, LN2_GAIN : LN2_GAIN + 1, :]
        d_hidden = d_out + inverse * (
            d_normal
            - jnp.mean(d_normal, axis=-1, keepdims=True)
            - normal * jnp.mean(d_normal * normal, axis=-1, keepdims=True)
        )
        dh[...] = d_hidden
        d_branch = d_hidden.astype(BF16)
        branch[0] = d_branch
        branch_copy = send(branch.at[0], branch.at[1], do_sems, ranks, partner_core)
        branch_copy.start()
        wo_load.wait()

        def heads_of(to_rank):
            at = pl.multiple_of(to_rank * width, width)
            return mm_nt(d_branch, wo[pl.ds(at, width), :]).astype(BF16)

        copies = []
        for dc, d in group.others():
            slot = group.slot(dc, d)
            do_send[slot] = heads_of(group.rank_of(dc, d))
            copies.append(
                send(do_send.at[slot], do_recv.at[pl.ds(pl.multiple_of(rank * rows, 16), rows)], do_sems, slot, group.device(dc, d))
            )
            copies[-1].start()
        do_recv[pl.ds(pl.multiple_of(rank * rows, 16), rows), :] = heads_of(rank)
        host.run(*middle[0])
        sums_two_ref[2:3, :] = jnp.sum(d_branch.astype(F32), axis=0, keepdims=True)
        sums_two_ref[3:4, :] = jnp.sum(d_out, axis=0, keepdims=True)
        dk_acc[...] = jnp.zeros_like(dk_acc)
        dv_acc[...] = jnp.zeros_like(dv_acc)
        sums_qv_ref[...] = jnp.zeros_like(sums_qv_ref)
        sums_one_ref[...] = jnp.zeros_like(sums_one_ref)
        for load in late_loads:
            load.wait()
        branch_copy.wait()
        gout[...] = (mm_tn(branch[0], mixed[0]) + mm_tn(branch[1], mixed[1])).astype(BF16)
        gout_save = pltpu.make_async_copy(gout, gout_out, save_sems.at[0])
        gout_save.start()
        host.run(*middle[1])
        for copy in copies:
            copy.wait()
        host.run(*middle[2])

        def block(at, carry):
            here = pl.ds(pl.multiple_of(at * BQ, BQ), BQ)
            q = q_all[here, :]
            grad = do_recv[here, :]
            totals = lse[here, :]
            d_q = jnp.zeros((BQ, width), F32)
            for head in range(heads):
                mine = head_lanes((BQ, width), head)
                q_head = jnp.where(mine, q, jnp.zeros_like(q))
                grad_head = jnp.where(mine, grad, jnp.zeros_like(grad))
                scores = mm_nt(q_head, k_all[...]) * SCALE2 + mask_ref[...]
                probs = jnp.exp2(scores - totals[:, head : head + 1])
                d_probs = mm_nt(grad_head, v_all[...])
                term = jnp.sum(probs * d_probs, axis=-1, keepdims=True)
                d_scores = (probs * (d_probs - term)).astype(BF16)
                dv_acc[...] += mm_tn(probs.astype(BF16), grad_head)
                dk_acc[...] += mm_tn(d_scores, q_head)
                d_q = jnp.where(mine, mm(d_scores, k_all[...]), d_q)
                for slot, (first, last) in enumerate(inner):
                    if last > first and slot % heads == head:
                        pl.when(at == slot // heads)(functools.partial(host.run, first, last))
            low = (d_q * scale).astype(BF16)
            dj[here, :width] = low
            sums_qv_ref[0:1, :] += jnp.sum(low.astype(F32), axis=0, keepdims=True)
            return carry

        lax.fori_loop(0, length // BQ, block, 0)
        dj[:, width : 2 * width] = (dk_acc[...] * scale).astype(BF16)
        low_v = dv_acc[...].astype(BF16)
        dj[:, 2 * width :] = low_v
        sums_qv_ref[1:2, :] = jnp.sum(low_v.astype(F32), axis=0, keepdims=True)

        def partial_rows(to_rank):
            here = pl.ds(pl.multiple_of(to_rank * rows, 16), rows)
            return mm_nt(dj[here, :], w_joint[...])

        def core_copy(d):
            return send(core_send.at[d], core_recv.at[d], core_sems, d, partner_core)

        def far_copy(d):
            return send(far_send.at[d - 1], far_recv.at[d - 1], far_sems, d - 1, group.device(0, d))

        for d in [d for d in range(1, half)] + [0]:
            core_send[d] = partial_rows(group.rank_of(1, d)).astype(BF16)
            core_copy(d).start()
        for d in range(1, half):
            value = partial_rows(group.rank_of(0, d))
            core_copy(d).wait_recv()
            far_send[d - 1] = (value + core_recv[d].astype(F32)).astype(BF16)
            far_copy(d).start()
        host.run(*tail[0])
        value = partial_rows(rank)
        core_copy(0).wait_recv()
        acc[...] = value + core_recv[0].astype(F32)

        half_cols = D // 2
        mine_cols = pl.ds(pl.multiple_of(core * half_cols, half_cols), half_cols)
        other_cols = pl.ds(pl.multiple_of((1 - core) * half_cols, half_cols), half_cols)
        g_send[...] = mm_tn(dj[...], a1[:, other_cols]).astype(BF16).reshape(g_send.shape)
        g_copy = send(g_send, g_recv, pair_sems, 0, partner_core)
        g_copy.start()
        host.run(*tail[1])
        g_own[...] = mm_tn(dj[...], a1[:, mine_cols]).astype(BF16).reshape(g_own.shape)
        g_save = pltpu.make_async_copy(g_own, gjoint_out.at[:, core], save_sems.at[1])
        g_save.start()
        host.run(*tail[2])

        for d in range(1, half):
            far_copy(d).wait_recv()
            acc[...] += far_recv[d - 1].astype(F32)
        d_normed = acc[...]
        normal, inverse = norm_stats(x_own[...].astype(F32))
        sums_one_ref[0:1, :] = jnp.sum(d_normed * normal, axis=0, keepdims=True)
        sums_one_ref[1:2, :] = jnp.sum(d_normed, axis=0, keepdims=True)
        d_normal = d_normed * vec_ref[0, LN1_GAIN : LN1_GAIN + 1, :]
        d_in = (
            dh[...]
            + inverse
            * (
                d_normal
                - jnp.mean(d_normal, axis=-1, keepdims=True)
                - normal * jnp.mean(d_normal * normal, axis=-1, keepdims=True)
            )
        ).astype(BF16)
        dx_own[...] = d_in
        dx_copy = send(dx_own, dx_recv, pair_sems, 1, partner_core)
        dx_copy.start()
        dx_save = pltpu.make_async_copy(dx_own, dx_out.at[0], save_sems.at[2])
        dx_save.start()
        host.run(*tail[3])
        g_copy.wait()
        g_save_other = pltpu.make_async_copy(g_recv, gjoint_out.at[:, 1 - core], save_sems.at[3])
        g_save_other.start()
        dx_copy.wait()
        dx_save_other = pltpu.make_async_copy(dx_recv, dx_out.at[1], save_sems.at[4])
        dx_save_other.start()
        for d in range(half):
            core_copy(d).wait_send()
        for d in range(1, half):
            far_copy(d).wait_send()
        for save in (gout_save, g_save, dx_save, g_save_other, dx_save_other):
            save.wait()
        rows_copy.wait()
        host.finish()


def back_call(layer, dy, hidden, wos, vec, upper, a2, ups, downs, given, late, mask, host, arrays):
    rows = dy.shape[1]
    ranks = host.count
    width = D // ranks
    half = ranks // 2
    shards = host.dp_count * ranks
    per = shards // NCH
    unit = FF // shards // 2
    heads = width // DH
    now = lambda i: (0, jnp.minimum(i, NCH - 1))
    whole = lambda i: (0, 0)
    anywhere = pl.BlockSpec(memory_space=pl.ANY)
    times = []
    for i in range(NCH):
        times += [2.9 * i + 1.6, 2.9 * i + 2.9]
    times += [29.0, 33.0, 36.0]
    for i in range(LEN // BQ * heads):
        times.append(36.0 + 28.0 / (LEN // BQ * heads) * (i + 1))
    times += [69.0, 73.0, 76.0, 84.0]
    ranges = host.slots(times)
    piece = pltpu.VMEM((NCH, rows, FC // 2), BF16)
    tokens = pltpu.VMEM((LEN, width), BF16)
    own = pltpu.VMEM((rows, D), BF16)
    view = host.view_shape(host.arrays - 1)
    return pl.pallas_call(
        functools.partial(back_kernel, layer, host, ranges),
        grid=(NCH + 1,),
        in_specs=[
            pl.BlockSpec((rows, FC), now),
            pl.BlockSpec((1, LEN), whole),
            pl.BlockSpec((1, VEC_ROWS, D), lambda i: (layer, 0, 0)),
        ]
        + [anywhere] * (10 + len(late) + len(arrays)),
        out_specs=[
            pl.BlockSpec((1, FC), now),
            pl.BlockSpec((8, D), whole),
            pl.BlockSpec((8, D), whole),
            pl.BlockSpec((8, width), whole),
        ]
        + [anywhere] * 5
        + host.out_specs(),
        out_shape=[
            jax.ShapeDtypeStruct((1, FF), F32),
            jax.ShapeDtypeStruct((8, D), F32),
            jax.ShapeDtypeStruct((8, D), F32),
            jax.ShapeDtypeStruct((8, width), F32),
            jax.ShapeDtypeStruct(view, BF16),
            jax.ShapeDtypeStruct((2, rows, D), BF16),
            jax.ShapeDtypeStruct((3, 2, width, D // 2), BF16),
            jax.ShapeDtypeStruct((D, D // 2), BF16),
            jax.ShapeDtypeStruct((2, rows, D), BF16),
        ]
        + host.out_shapes(),
        scratch_shapes=[
            own,
            pltpu.VMEM((rows, D), F32),
            pltpu.VMEM((2, rows, D), BF16),
            pltpu.VMEM((D, D), BF16),
            pltpu.VMEM((2, D, FC), BF16),
            pltpu.VMEM((2, FC, D), BF16),
            pltpu.SemaphoreType.DMA((4,)),
            pltpu.SemaphoreType.DMA((2, 2)),
            pltpu.VMEM((rows, D), F32),
            piece,
            piece,
            piece,
            pltpu.VMEM((2, per, unit, D), BF16),
            pltpu.VMEM((2, rows, D), BF16),
            pltpu.VMEM((rows, D), F32),
            pltpu.VMEM((ranks, rows, width), BF16),
            tokens,
        ]
        + dma_pair(NCH)
        + dma_pair(ranks + 1)
        + [pltpu.SemaphoreType.DMA((2,)), pltpu.SemaphoreType.DMA((5,))]
        + [pltpu.VMEM(t.shape[1:] if i == 5 else t.shape, t.dtype) for i, t in enumerate(late)]
        + [pltpu.SemaphoreType.DMA((len(late),))]
        + [
            pltpu.VMEM((LEN, width), F32),
            pltpu.VMEM((LEN, width), F32),
            pltpu.VMEM((LEN, 3 * width), BF16),
            pltpu.VMEM((half, rows, D), BF16),
            pltpu.VMEM((half - 1, rows, D), BF16),
            pltpu.VMEM((half - 1, rows, D), BF16),
        ]
        + ([] if ranks == 4 else [pltpu.VMEM((half, rows, D), BF16)])
        + [
            pltpu.VMEM((3, width, D // 2), BF16),
            pltpu.VMEM((3, width, D // 2), BF16),
            pltpu.VMEM((3, width, D // 2), BF16),
            pltpu.VMEM((D, D // 2), BF16),
            own,
        ]
        + dma_pair(half)
        + dma_pair(half - 1)
        + dma_pair(2)
        + deliver_sems()
        + host.scratch(),
        compiler_params=pltpu.CompilerParams(
            vmem_limit_bytes=BACK_LIMIT, collective_id=layer, has_side_effects=True
        ),
        cost_estimate=pl.CostEstimate(
            flops=100 * 10**9, bytes_accessed=60 * 2**20, transcendentals=rows * FF
        ),
    )(
        upper,
        mask,
        vec,
        dy,
        hidden,
        a2,
        wos[0],
        wos[1],
        ups[0],
        ups[1],
        downs[0],
        downs[1],
        given,
        *late,
        *[host.view(i, array) for i, array in enumerate(arrays)],
    )


def final_kernel(host, *refs):
    n = host.arrays
    srcs, rows_src = refs[:n], refs[n]
    outs, rows_out = refs[n + 1 : 2 * n + 1], refs[2 * n + 1]
    rows_sems = refs[2 * n + 2 : 2 * n + 5]
    rows_mine, rows_sem = refs[2 * n + 5 : 2 * n + 7]
    host.bind(srcs, outs, refs[2 * n + 7 :])
    rows_load = pltpu.make_async_copy(rows_src.at[0], rows_mine, rows_sem)
    rows_load.start()
    group = Group()
    group.greet(host.dp_count)
    host.begin()
    rows_copy = Deliver(group, 0, rows_mine, rows_out, rows_sems)
    rows_load.wait()
    rows_copy.start()
    host.run(0, len(host.events))
    host.finish()
    rows_copy.wait()


def final_call(host, arrays, rows_src, collective_id):
    anywhere = pl.BlockSpec(memory_space=pl.ANY)
    return pl.pallas_call(
        functools.partial(final_kernel, host),
        in_specs=[anywhere] * (host.arrays + 1),
        out_specs=[anywhere] * (host.arrays + 1),
        out_shape=host.out_shapes() + [jax.ShapeDtypeStruct(rows_src.shape, BF16)],
        scratch_shapes=deliver_sems()
        + [pltpu.VMEM(rows_src.shape[1:], BF16), pltpu.SemaphoreType.DMA]
        + host.scratch(),
        compiler_params=pltpu.CompilerParams(
            vmem_limit_bytes=VMEM_LIMIT, collective_id=collective_id, has_side_effects=True
        ),
    )(*host.views(arrays), rows_src)


def assemble_kernel(count, *refs):
    refs = list(refs)

    def pop(number):
        taken = refs[:number]
        del refs[:number]
        return taken

    sources = [pop(2) for _ in range(7)]
    row_outs = pop(2)
    up_out, down_out, out_out, joint_out = pop(4)
    vec_outs = pop(9)
    up, down, mixed, joint, little = pop(5)
    sems = pop(1)[0]
    core = lax.axis_index("section")
    half_ranks = count // 2
    compact = half_ranks == 2
    low = lax.rem(lax.axis_index("seq"), half_ranks)
    loads = []
    for i, (pair, target) in enumerate(zip(sources, [up, down, mixed, joint, little] + row_outs)):
        first = pltpu.make_async_copy(pair[0], target, sems.at[i])
        second = pltpu.make_async_copy(pair[1], target, sems.at[i])
        pl.when(core == 0)(first.start)
        pl.when(core == 1)(second.start)
        loads.append(first)
    unit = up.shape[1]
    half_cols = D // 2
    loads[1].wait()
    for half in range(2):
        for g in range(FF // 2 // unit):
            at = (2 * g + half) * unit
            down_out[:, at : at + unit] = down[half, :, g * unit : (g + 1) * unit]
    loads[0].wait()
    for half in range(2):
        up_out[:, half * unit : (half + 1) * unit] = up[half].T
    for load in loads[2:5]:
        load.wait()
    for half in range(2):
        cols = slice(half * half_cols, (half + 1) * half_cols)
        value = mixed[half]
        if compact:
            heads = half_cols // DH // 2
            pieces = []
            for i in range(heads):
                for j in range(2):
                    at = (j * heads + i) * DH
                    pieces.append(value[:, at : at + DH])
            value = jnp.concatenate(pieces, axis=1)
        out_out[:, cols] = value
        value = joint[half]
        if compact:
            pieces = [value[i * DH : (i + 1) * DH, :] for i in range(4)]
            joint_out[0:DH, cols] = jnp.where(low == 0, pieces[0], pieces[1])
            joint_out[DH : 2 * DH, cols] = pieces[3]
            joint_out[2 * DH : 3 * DH, cols] = jnp.where(low == 0, pieces[1], pieces[2])
        else:
            joint_out[:, cols] = value
    total = little[0] + little[1]
    at = 0
    for out in vec_outs:
        size = out.shape[1]
        for start in range(0, size, 128):
            wide = min(128, size - start)
            row, lane = (at + start) // 128, (at + start) % 128
            out[:, start : start + wide] = total[row : row + 1, lane : lane + wide]
        at += size
    for load in loads[5:]:
        load.wait()


def assemble_call(count, groups, pairs):
    unit = D // groups
    anywhere = pl.BlockSpec(memory_space=pl.ANY)
    vmem = pl.BlockSpec(memory_space=pltpu.VMEM)
    sizes = [unit] * 8 + [FF // groups]
    flat = [array for pair in pairs for array in pair]
    return pl.pallas_call(
        functools.partial(assemble_kernel, count),
        in_specs=[anywhere] * len(flat),
        out_specs=[vmem] * 15,
        out_shape=[jax.ShapeDtypeStruct(pair[0].shape, BF16) for pair in pairs[5:]]
        + [
            jax.ShapeDtypeStruct((D, FF // groups), F32),
            jax.ShapeDtypeStruct((unit, FF), F32),
            jax.ShapeDtypeStruct((unit, D), F32),
            jax.ShapeDtypeStruct((3 * unit, D), F32),
        ]
        + [jax.ShapeDtypeStruct((1, size), F32) for size in sizes],
        scratch_shapes=[pltpu.VMEM(pair[0].shape, F32) for pair in pairs[:5]]
        + [pltpu.SemaphoreType.DMA((7,))],
        compiler_params=params(),
    )(*flat)


def swap(value, axis, mask):
    count = lax.axis_size(axis)
    return lax.ppermute(value, axis, [(i, i ^ mask) for i in range(count)])


def take(value, index, dim):
    return lax.dynamic_index_in_dim(value, index, dim, keepdims=False)


def ordered(bit, mine, other, dim):
    return jnp.where(
        bit == 0,
        jnp.stack([mine, other], axis=dim),
        jnp.stack([other, mine], axis=dim),
    )


def key_bias(counts, rotate):
    places = jnp.arange(LEN, dtype=jnp.int32)
    places = jnp.where(rotate, (places + LEN // 2) % LEN, places)
    offset = jnp.maximum(places - TRI, 0)
    view_index = offset // VSLOT
    inside = offset - view_index * VSLOT
    match = view_index[:, None] == jnp.arange(VIEWS, dtype=jnp.int32)[None, :]
    limits = jnp.sum(jnp.where(match, counts[None, :], 0), axis=1)
    valid = (places < TRI) | (inside < limits)
    return jnp.where(valid, 0.0, -1e30).astype(F32)[None, :]


def shards(
    inputs,
    cotangent,
    view_tokens,
    ln1_gain,
    ln1_bias,
    w_qkv,
    b_query,
    b_value,
    w_out,
    b_out,
    ln2_gain,
    ln2_bias,
    w_up,
    b_up,
    w_down,
    b_down,
):
    core = lax.axis_index("section")
    place = lax.axis_index("seq")
    dp_index = lax.axis_index("dp")
    count = lax.axis_size("seq")
    dp_count = lax.axis_size("dp")
    groups = dp_count * count
    half = count // 2
    micro = place // half
    low = place % half
    low_bits = half.bit_length() - 1
    rows = inputs.shape[2]
    width = D // count
    rank = core * half + low

    def swap_core(value):
        return swap(value, "section", 1)

    def swap_seq(value, bit):
        return swap(value, "seq", 1 << bit)

    def low_bit(bit):
        return (place >> bit) & 1

    def own_rows(local):
        chunks = local[:, 0]
        far = lax.ppermute(
            take(chunks, 1 - micro, 0),
            ("section", "seq"),
            [(count + z, count + (z ^ half)) for z in range(count)],
        )
        return jnp.where(core == 0, take(chunks, micro, 0), far)

    def gather_rows(own):
        value = own[None]
        for bit in range(low_bits):
            other = swap_seq(value, bit)
            value = ordered(low_bit(bit), value, other, 0).reshape((-1,) + own.shape)
        value = ordered(core, value, swap_core(value), 0)
        return value.reshape((-1,) + own.shape[1:])

    def exchange(value):
        tail = value.shape[1:]
        value = value.reshape((2,) * (low_bits + 1) + tail)
        for bit in range(low_bits):
            dim = low_bits - bit
            mine = take(value, low_bit(bit), dim)
            other = swap_seq(take(value, 1 - low_bit(bit), dim), bit)
            value = ordered(low_bit(bit), mine, other, dim)
        mine = take(value, core, 0)
        other = swap_core(take(value, 1 - core, 0))
        return ordered(core, mine, other, 0).reshape((count,) + tail)

    compact = half == 2
    span = half * width

    def vector_to(value):
        if compact:
            wide = jnp.stack(
                [jnp.where(low == i, value.reshape(2, -1, DH), 0.0) for i in range(2)], axis=2
            )
        else:
            wide = jnp.stack([jnp.where(low == i, value, 0.0) for i in range(half)], axis=1)
        wide = wide.reshape(2, span)
        return jnp.concatenate([jnp.where(core == i, wide, 0.0) for i in range(2)], axis=1)

    def rank_rows(value):
        if compact:
            value = value.reshape(2, width // DH, 2, DH, D)
            return jnp.swapaxes(value, 1, 2).reshape(D, D)
        return value

    out_mine = rank_rows(w_out[0])
    ups = (w_up[0], swap_core(w_up[0]))
    downs = (w_down[0], swap_core(w_down[0]))
    bias_mask = key_bias(take(view_tokens[:, 0], micro, 0), micro == 1)

    saved = []
    acts = []
    for layer in range(2):
        if layer == 0:
            o_own, lse, a1, q, k, v, layer_in, joint_pair, out_other, vec = attend_call(
                True,
                0,
                bias_mask,
                count,
                dp_count,
                inputs,
                w_qkv,
                out_mine[None],
                ln1_gain,
                ln1_bias,
                b_query,
                b_value,
                b_out,
                ln2_gain,
                ln2_bias,
                b_down,
                b_up,
            )
            outs_pair = (out_mine, out_other)
        else:
            o_own, lse, a1, q, k, v, d_out_all = attend_call(
                False, 1, bias_mask, count, dp_count, layer_in, joint_pair, vec, cotangent
            )
        hidden, upper, output, a2_all, o_all, gated_all, first_rows = mlp_call(
            layer, dp_count, o_own, layer_in, outs_pair, vec, ups, downs
        )
        acts.append(output)
        saved.append((layer_in, a1, q, k, v, lse, hidden, upper, a2_all, o_all, gated_all))
        layer_in = output

    def hosted(arrays, spans=None, shares=STAGE_SHARES):
        shapes = []
        for array in arrays:
            shapes.append((array.shape[1], array.shape[2], array.shape[0] != groups, array.dtype))
        return Hosted(dp_count, count, tuple(shapes), spans, shares)

    results = [{}, {}]
    pending = None
    for layer in (1, 0):
        x_own, a1, q, k, v, lse, hidden, upper, a2_all, o_all, gated_all = saved[layer]
        g_down = mm_tn(d_out_all.reshape(2 * rows, D), gated_all.reshape(2 * rows, FF // 2))
        g_down = g_down.astype(BF16).reshape(groups, D // groups, FF // 2)
        up_like = jax.ShapeDtypeStruct((groups, FF // groups // 2, D), BF16)
        if pending is None:
            arrays = [g_down]
            host = hosted(
                arrays + [up_like], ((0, 0.0, 52.0), (1, 28.0, 84.0)), (0.35, 0.6, 0.85, 1.0)
            )
        else:
            arrays = list(pending) + [g_down]
            host = hosted(
                arrays + [up_like],
                ((0, 0.0, 36.0), (0, 0.0, 36.0), (0, 0.0, 36.0), (0, 12.0, 80.0), (1, 40.0, 120.0)),
            )
        (g_bup, sums_two, sums_one, sums_qv, g_up, d_in, g_joint, g_out, given, *reduced) = back_call(
            layer,
            d_out_all,
            hidden,
            outs_pair,
            vec,
            upper,
            a2_all,
            ups,
            downs,
            acts[1][None] if pending is None else d_out_all,
            (q, k, v, lse, a1, joint_pair, x_own, o_all),
            bias_mask,
            host,
            arrays,
        )
        if pending is None:
            second_rows = given
        else:
            second_grads = given
            for name in ("out", "joint", "small"):
                results[1][name] = reduced.pop(0)
        results[layer]["down"], results[layer]["up"] = reduced
        g_out = g_out.reshape(groups, D // groups, D // 2)
        if compact:
            g_joint = g_joint.reshape(groups // 2, 3 * D // groups, D // 2)
        else:
            spread = jnp.stack(
                [jnp.where(low == i, g_joint, jnp.zeros_like(g_joint)) for i in range(half)], axis=2
            )
            g_joint = spread.reshape(groups, 3 * D // groups, D // 2)
        wide = vector_to(sums_qv[0:2])
        rows_of = jnp.concatenate([sums_one[0:2], wide, sums_two[2:3], sums_two[0:2], sums_two[3:4]])
        small = jnp.concatenate(
            [
                jnp.swapaxes(rows_of.reshape(8, groups, D // groups), 0, 1).reshape(groups, -1),
                g_bup.reshape(groups, FF // groups),
            ],
            axis=1,
        )
        lines = -(-small.shape[1] // 128)
        lines += -lines % 8
        small = jnp.pad(small, ((0, 0), (0, lines * 128 - small.shape[1])))
        small = small.reshape(groups, lines, 128)
        if pending is None:
            pending = (g_out, g_joint, small)
        else:
            arrays = (g_out, g_joint, small)
            out_0, joint_0, small_0, first_grads = final_call(hosted(arrays), arrays, d_in, 4)
            results[0]["out"], results[0]["joint"], results[0]["small"] = out_0, joint_0, small_0
        d_out_all = d_in

    pairs = [
        (results[0][name], results[1][name]) for name in ("up", "down", "out", "joint", "small")
    ]
    pairs += [(first_rows, second_rows), (first_grads, second_grads)]
    acts_rows, grad_rows, g_w_up, g_w_down, g_w_out, g_w_qkv, *pieces = assemble_call(
        count, groups, pairs
    )
    g_ln1g, g_ln1b, g_bq, g_bv, g_bo, g_ln2g, g_ln2b, g_bd, g_bup = pieces
    return (
        acts_rows[None, :, None],
        grad_rows[None, :, None],
        g_ln1g,
        g_ln1b,
        g_w_qkv.T[None],
        g_bq,
        g_bv,
        g_w_out.T[None],
        g_bo,
        g_ln2g,
        g_ln2b,
        g_w_up[None],
        g_bup,
        g_w_down.T[None],
        g_bd,
    )


def solution(mesh):
    rows = P(None, "dp", "seq", None)
    vector = P("section", None)
    matrix = P("section", None, None)
    placed = (
        rows,
        rows,
        P(None, "dp", None),
        vector,
        vector,
        matrix,
        vector,
        vector,
        matrix,
        vector,
        vector,
        vector,
        matrix,
        vector,
        matrix,
        vector,
    )
    both = P("section", None, "dp", "seq", None)
    line = P("section", ("dp", "seq"))
    table = P("section", None, ("dp", "seq"))
    return jax.shard_map(
        shards,
        mesh=mesh,
        in_specs=placed,
        out_specs=(
            both,
            both,
            line,
            line,
            table,
            line,
            line,
            table,
            line,
            line,
            line,
            table,
            line,
            table,
            line,
        ),
        check_vma=False,
    )
```

```python
import functools
import math

import jax
import jax.numpy as jnp
from jax import lax
from jax.experimental import pallas as pl
from jax.experimental.pallas import tpu as pltpu
from jax.sharding import PartitionSpec as P

D = 1024
H = 16
DH = 64
FF = 4096
VIEWS = 6
TRI = 512
VSLOT = 128
MICRO = 2
LEN = 1280
BQ = 256
NCH = 8
FC = FF // NCH
NCHF = 4
FCF = FF // NCHF
SCALE2 = DH ** (-0.5) * math.log2(math.e)
F32 = jnp.float32
BF16 = jnp.bfloat16
VMEM_LIMIT = 56 * 2**20


def params():
    return pltpu.CompilerParams(vmem_limit_bytes=VMEM_LIMIT)


def mm(a, b):
    return lax.dot_general(a, b, (((1,), (0,)), ((), ())), preferred_element_type=F32)


def mm_nt(a, b):
    return lax.dot_general(a, b, (((1,), (1,)), ((), ())), preferred_element_type=F32)


def mm_tn(a, b):
    return lax.dot_general(a, b, (((0,), (0,)), ((), ())), preferred_element_type=F32)


def norm_stats(values):
    average = jnp.mean(values, axis=-1, keepdims=True)
    centered = values - average
    variance = jnp.mean(centered * centered, axis=-1, keepdims=True)
    inverse = lax.rsqrt(variance + 1e-05)
    return centered * inverse, inverse


def head_lanes(shape, head):
    lane = lax.broadcasted_iota(jnp.int32, shape, 1)
    return (lane >= head * DH) & (lane < (head + 1) * DH)


def shards_of():
    return lax.axis_size("dp") * lax.axis_size("seq")


def split_halves(value, unit, core, mine, other, step):
    for at in range(0, value.shape[1] // unit, 2):
        even = value[:, at * unit : (at + 1) * unit]
        odd = value[:, (at + 1) * unit : (at + 2) * unit]
        cols = slice(at // 2 * unit, (at // 2 + 1) * unit)
        mine[step, :, cols] = jnp.where(core == 0, even, odd)
        other[step, :, cols] = jnp.where(core == 0, odd, even)


GELU_A = math.sqrt(2.0 / math.pi)
GELU_B = 0.044715


MESH_AXES = ("dp", "seq")


def axis_bits(dp_count, count):
    bits = []
    for axis, size in (("dp", dp_count), ("seq", count)):
        mask = size // 2
        while mask:
            bits.append((axis, mask))
            mask //= 2
    return bits


def stream_orders(dp_count, count):
    dp_bits = dp_count.bit_length() - 1
    seq_bits = count.bit_length() - 1
    dp_dims = list(range(dp_bits))
    seq_dims = list(range(dp_bits, dp_bits + seq_bits))[::-1]
    return (
        dp_dims[::-1] + seq_dims,
        dp_dims + seq_dims,
        seq_dims[:1] + dp_dims + seq_dims[1:],
        seq_dims[:1] + dp_dims[::-1] + seq_dims[1:],
    )


def my_bit(axis, mask):
    return lax.rem(lax.div(lax.axis_index(axis), mask), 2)


def partner(axis, mask):
    return lax.axis_index(axis) + mask * (1 - 2 * my_bit(axis, mask))


def greet(bits):
    barrier = pltpu.get_barrier_semaphore()
    for axis, mask in bits:
        pl.semaphore_signal(
            barrier,
            inc=1,
            device_id={axis: partner(axis, mask)},
            device_id_type=pl.DeviceIdType.MESH,
        )
    pl.semaphore_wait(barrier, len(bits))


class Reducer:
    def __init__(self, bits, order, src, cols, out, rows, compact, buffers, sems):
        self.bits, self.order, self.src, self.cols = bits, order, src, cols
        self.out, self.out_cols, self.buffers, self.sems = out, cols, buffers, sems
        self.count, self.rows, self.compact = len(bits), rows, compact

    @staticmethod
    def scratch(count, rows, width, dtype):
        shapes = [pltpu.VMEM((2,) * (count - 1) + (rows, width), dtype)]
        for stage in range(count):
            shapes.append(pltpu.VMEM((2,) * (count - 1 - stage) + (rows, width), dtype))
        shapes += [
            pltpu.SemaphoreType.DMA((count + 2,)),
            pltpu.SemaphoreType.DMA((count + 2,)),
            pltpu.SemaphoreType.DMA,
        ]
        return shapes

    def place(self, stage):
        left = [d for d in range(self.count) if d not in self.order[:stage]]
        dim = self.order[stage]
        return left, left.index(dim), self.bits[dim]

    def cut(self, stage, index):
        left, at, _ = self.place(stage)
        where = [slice(None)] * len(left)
        where[at] = index
        return tuple(where)

    def source(self, stage):
        if stage == 0:
            return self.src
        return self.buffers[0] if stage == 1 else self.buffers[stage]

    def copy(self, stage):
        axis, mask = self.place(stage)[2]
        where = self.cut(stage, 1 - my_bit(axis, mask))
        if stage == 0:
            where = where + (slice(None), pl.ds(*self.cols))
        return pltpu.make_async_remote_copy(
            src_ref=self.source(stage).at[where],
            dst_ref=self.buffers[stage + 1],
            send_sem=self.sems[0].at[stage],
            recv_sem=self.sems[1].at[stage],
            device_id={axis: partner(axis, mask)},
            device_id_type=pl.DeviceIdType.MESH,
        )

    def load(self):
        axis, mask = self.place(0)[2]
        where = self.cut(0, my_bit(axis, mask)) + (slice(None), pl.ds(*self.cols))
        return pltpu.make_async_copy(self.src.at[where], self.buffers[0], self.sems[2])

    def share(self):
        core = lax.axis_index("section")
        return pltpu.make_async_remote_copy(
            src_ref=self.out.at[core, :, pl.ds(*self.out_cols)],
            dst_ref=self.out.at[core, :, pl.ds(*self.out_cols)],
            send_sem=self.sems[0].at[self.count],
            recv_sem=self.sems[1].at[self.count],
            device_id={"section": 1 - core},
            device_id_type=pl.DeviceIdType.MESH,
        )

    def trade(self):
        third = self.rows // 3
        core = lax.axis_index("section")
        bit = lax.rem(lax.axis_index("seq"), 2)
        row = pl.multiple_of((1 - bit) * 2 * third, third)
        return pltpu.make_async_remote_copy(
            src_ref=self.out.at[core, pl.ds(row, third), pl.ds(*self.out_cols)],
            dst_ref=self.out.at[core, pl.ds(self.rows, third), pl.ds(*self.out_cols)],
            send_sem=self.sems[0].at[self.count + 1],
            recv_sem=self.sems[1].at[self.count + 1],
            device_id={"seq": partner("seq", 1)},
            device_id_type=pl.DeviceIdType.MESH,
        )

    def begin(self):
        self.copy(0).start()
        self.load().start()

    def step(self, stage):
        left, at, (axis, mask) = self.place(stage)
        bit = my_bit(axis, mask)
        if stage == 0:
            self.load().wait()
        self.copy(stage).wait_recv()
        got = self.buffers[stage + 1]
        rows = got.shape[-2]
        chunk = rows
        while chunk * got.shape[-1] > 65536 and chunk % 32 == 0:
            chunk //= 2
        per = rows // chunk
        last = stage == self.count - 1
        core = lax.axis_index("section")
        total = 2 ** (len(left) - 1)

        def body(i, carry):
            flat = lax.div(i, per)
            row = pl.multiple_of(lax.rem(i, per) * chunk, chunk)
            index = []
            for j in range(len(left) - 1):
                index.append(lax.rem(lax.div(flat, 2 ** (len(left) - 2 - j)), 2))
            there = tuple(index) + (pl.ds(row, chunk), slice(None))
            if stage == 0:
                mine = self.buffers[0][there]
            else:
                own = index[:at] + [bit] + index[at:]
                mine = self.source(stage)[tuple(own) + (pl.ds(row, chunk), slice(None))]
            value = mine.astype(F32) + got[there].astype(F32)
            if last:
                self.out[core, pl.ds(row, chunk), pl.ds(*self.out_cols)] = value
            elif stage == 0:
                self.buffers[0][there] = value.astype(got.dtype)
            else:
                got[there] = value.astype(got.dtype)
            return carry

        lax.fori_loop(0, total * per, body, 0)
        if not last:
            self.copy(stage + 1).start()
        elif self.compact:
            self.trade().start()
        else:
            self.share().start()

    def tail(self):
        if self.compact:
            self.trade().wait()
            self.share().start()

    def finish(self):
        for stage in range(self.count):
            self.copy(stage).wait_send()
        self.share().wait()


def part_widths(width):
    unit = 128 if width % 128 == 0 else width
    tiles = width // unit
    rest = tiles // 8
    first = -(-(tiles - rest) // 2)
    second = rest // 2
    return tuple(unit * n for n in (first, tiles - rest - first, rest - second, second))


STAGE_SHARES = (0.45, 0.7, 0.9, 1.0)


class Hosted:
    def __init__(self, dp_count, count, shapes, spans=None, shares=STAGE_SHARES, even=False):
        self.dp_count, self.count, self.shapes = dp_count, count, shapes
        self.spans = spans or ((0, 0.0, 1.0),) * len(shapes)
        self.all_bits = axis_bits(dp_count, count)
        self.plan = []
        for index, (rows, width, compact, _) in enumerate(shapes):
            bits = self.all_bits[:-1] if compact else self.all_bits
            orders = stream_orders(dp_count, count)
            widths = part_widths(width)
            if even and width % 256 == 0:
                widths = (width // 2, width // 2, 0, 0)
            if compact:
                last = len(bits)
                orders = [tuple(d for d in order if d != last) for order in orders[:2]]
                widths = (width // 2, width // 2)
            start = 0
            for order, size in zip(orders, widths):
                pieces = [size] if size else []
                if size >= 256 and not compact:
                    first = 128 * -(-size // 256)
                    pieces = [first, size - first]
                for k, piece in enumerate(pieces):
                    self.plan.append((index, tuple(order), bits, start, piece, rows, compact, k))
                    start += piece
        self.plan.sort(key=lambda p: (p[0], p[7]))
        self.arrays = len(shapes)
        self.events = []
        for k, part in enumerate(self.plan):
            phase, first, last = self.spans[part[0]]
            if phase == 0 and first > 0.0:
                self.events.append((first, k, -1))
            for stage in range(len(part[2])):
                share = shares[min(stage, 3)]
                self.events.append((first + (last - first) * share + 0.01 * stage, k, stage))
        self.events.sort()

    def views(self, arrays):
        return [self.view(i, array) for i, array in enumerate(arrays)]

    def view_shape(self, index):
        rows, width, compact, _ = self.shapes[index]
        depth = len(self.all_bits) - (1 if compact else 0)
        return (2,) * depth + (rows, width)

    def view(self, index, array):
        return array.reshape(self.view_shape(index))

    def in_specs(self):
        return [pl.BlockSpec(memory_space=pl.ANY)] * self.arrays

    def out_shapes(self):
        return [
            jax.ShapeDtypeStruct((2, rows + (rows // 3 if compact else 0), width), F32)
            for rows, width, compact, _ in self.shapes
        ]

    def out_specs(self):
        return [pl.BlockSpec(memory_space=pl.ANY)] * self.arrays

    def scratch(self):
        shapes = [pltpu.VMEM(o.shape, F32) for o in self.out_shapes()]
        shapes.append(pltpu.SemaphoreType.DMA((max(1, self.arrays),)))
        for index, _, bits, _, size, rows, _, _ in self.plan:
            shapes += Reducer.scratch(len(bits), rows, size, self.shapes[index][3])
        return shapes

    def bind(self, srcs, outs, scratch):
        self.parts = []
        self.outs, self.sums = outs, scratch[: self.arrays]
        self.out_sems = scratch[self.arrays]
        at = self.arrays + 1
        for index, order, bits, start, size, rows, compact, _ in self.plan:
            depth = len(bits) + 1
            mine = scratch[at : at + depth + 3]
            at += depth + 3
            self.parts.append(
                Reducer(
                    bits,
                    order,
                    srcs[index],
                    (start, size),
                    self.sums[index],
                    rows,
                    compact,
                    mine[:depth],
                    mine[depth:],
                )
            )

    def begin(self, phase=0):
        for part, plan in zip(self.parts, self.plan):
            span = self.spans[plan[0]]
            if span[0] == phase and (phase or span[1] == 0.0):
                part.begin()

    def run(self, first, last):
        for _, k, stage in self.events[first:last]:
            if stage < 0:
                self.parts[k].begin()
            else:
                self.parts[k].step(stage)

    def slots(self, times):
        edges = []
        done = 0
        for time in times:
            while done < len(self.events) and self.events[done][0] <= time:
                done += 1
            edges.append(done)
        edges[-1] = len(self.events)
        return list(zip([0] + edges[:-1], edges))

    def settle(self):
        for part in self.parts:
            part.tail()
        for part in self.parts:
            part.finish()

    def finish(self):
        self.settle()
        copies = []
        for i, (out, value) in enumerate(zip(self.outs, self.sums)):
            copies.append(pltpu.make_async_copy(value, out, self.out_sems.at[i]))
            copies[-1].start()
        for copy in copies:
            copy.wait()


BACK_LIMIT = 64 * 2**20 - 2**18


class Group:
    def __init__(self):
        self.half = lax.axis_size("seq") // 2
        self.core = lax.axis_index("section")
        self.place = lax.axis_index("seq")
        self.low = lax.rem(self.place, self.half)
        self.base = self.place - self.low
        self.rank = self.core * self.half + self.low

    def others(self):
        pairs = [(dc, d) for d in range(1, self.half) for dc in (0, 1)]
        return pairs + [(1, 0)]

    def slot(self, dc, d):
        return dc * self.half + d

    def where(self, dc, d):
        core = lax.rem(self.core + dc, 2)
        low = lax.rem(self.low + d, self.half)
        return core, low

    def device(self, dc, d):
        core, low = self.where(dc, d)
        return {"section": core, "seq": self.base + low}

    def rank_of(self, dc, d):
        core, low = self.where(dc, d)
        return core * self.half + low

    def greet(self, dp_count):
        barrier = pltpu.get_barrier_semaphore()
        targets = [self.device(dc, d) for dc, d in self.others()]
        mask = dp_count // 2
        while mask:
            targets.append({"dp": partner("dp", mask)})
            mask //= 2
        targets.append({"seq": partner("seq", self.half)})
        targets.append({"section": 1 - self.core, "seq": partner("seq", self.half)})
        for target in targets:
            pl.semaphore_signal(
                barrier, inc=1, device_id=target, device_id_type=pl.DeviceIdType.MESH
            )
        pl.semaphore_wait(barrier, len(targets))


def send(src, dst, sems, slot, device):
    return pltpu.make_async_remote_copy(
        src_ref=src,
        dst_ref=dst,
        send_sem=sems[0].at[slot],
        recv_sem=sems[1].at[slot],
        device_id=device,
        device_id_type=pl.DeviceIdType.MESH,
    )


class Deliver:
    def __init__(self, group, layer, src, out, sems):
        micro = lax.div(group.place, group.half)
        here, there = sems[0], sems[1]
        self.core, self.layer = group.core, layer
        self.local = pltpu.make_async_copy(src, out.at[micro], sems[2])
        self.chip = send(src, out.at[micro], (here, there), 0, {"section": 1 - group.core})
        self.far = send(
            src,
            out.at[micro],
            (here, there),
            1,
            {"section": layer, "seq": partner("seq", group.half)},
        )

    def start(self):
        first = self.local if self.layer == 0 else self.chip
        pl.when(self.core == 0)(lambda: first.start())
        pl.when(self.core == 1)(lambda: self.far.start())

    def wait(self):
        @pl.when(self.core == 0)
        def _():
            if self.layer == 0:
                self.local.wait()
                self.far.wait_recv()
            else:
                self.chip.wait_send()

        @pl.when(self.core == 1)
        def _():
            self.far.wait_send()
            if self.layer == 1:
                self.far.wait_recv()
                self.chip.wait_recv()


def deliver_sems():
    return dma_pair(2) + [pltpu.SemaphoreType.DMA]


def dma_pair(count):
    return [pltpu.SemaphoreType.DMA((count,)), pltpu.SemaphoreType.DMA((count,))]


VEC_ROWS = 16
LN1_GAIN, LN1_BIAS, B_QUERY, B_VALUE, B_OUT, LN2_GAIN, LN2_BIAS, B_DOWN, B_UP = range(9)


def attend_kernel(first, layer, dp_count, *refs):
    if first:
        x_ref, joint_ref, wout_ref, mask_ref = refs[:4]
        vectors = refs[4:13]
        o_out, lse_out, a_out, q_out, k_out, v_out = refs[13:19]
        x_out, joint_out, wout_out, vec_out = refs[19:23]
        rest = refs[23:]
    else:
        x_ref, joint_ref, mask_ref, vec_ref, cot_ref = refs[:5]
        o_out, lse_out, a_out, q_out, k_out, v_out, cot_out = refs[5:12]
        rest = refs[12:]
    x_all, a_all, q_all, k_all, v_all, lse, o_send, o_recv = rest[:8]
    x_sems, o_sems = rest[8:10], rest[10:12]
    out_sems = rest[12]
    if first:
        joint_pair, wide_own, wide_other, vec_send, vec_recv, vec_pair = rest[13:19]
        wide_sems, vec_sems = rest[19:21], rest[21:23]
        load_sems = rest[23]
    else:
        joint_one, cot_own, cot_other = rest[13:16]
        cot_sems = rest[16:18]
        load_sems = rest[18]
    group = Group()
    core, half, rank, low = group.core, group.half, group.rank, group.low
    ranks, rows, _ = x_all.shape
    width = q_all.shape[1]
    heads = width // DH
    span = half * width
    partner_core = group.device(1, 0)
    micro = lax.div(group.place, half)

    group.greet(dp_count)

    def x_copy(slot, from_rank, device):
        return send(x_all.at[from_rank], x_all.at[from_rank], x_sems, slot, device)

    far = {"seq": partner("seq", half)}

    if first:
        own_load = pltpu.make_async_copy(x_ref.at[micro, 0], x_all.at[rank], load_sems.at[0])
        far_copy = send(x_ref.at[1 - micro, 0], x_all.at[rank], x_sems, 2 * half - 1, far)
        pl.when(core == 1)(lambda: far_copy.start())
        pl.when(core == 0)(lambda: own_load.start())
        wide_copies = []
        own_loads = []
        for part in range(3):
            theirs = pl.ds(pl.multiple_of(part * D + (1 - core) * span, 128), span)
            ours = pl.ds(pl.multiple_of(part * D + core * span, 128), span)
            wide_copies.append(
                send(joint_ref.at[0, :, theirs], wide_other.at[part], wide_sems, part, partner_core)
            )
            own_loads.append(
                pltpu.make_async_copy(
                    joint_ref.at[0, :, ours], wide_own.at[part], load_sems.at[1 + part]
                )
            )
            wide_copies[-1].start()
            own_loads[-1].start()
        vec_send[...] = jnp.zeros_like(vec_send)
        for i, value in enumerate(vectors[:8]):
            vec_send[i : i + 1, :] = value[...].astype(F32)
        for i in range(FF // D):
            vec_send[8 + i : 9 + i, :] = vectors[8][:, i * D : (i + 1) * D].astype(F32)
        vec_copy = send(vec_send, vec_recv, vec_sems, 0, partner_core)
        vec_copy.start()
        wout_copy = send(wout_ref.at[0], wout_out, vec_sems, 1, partner_core)
        pl.when(core == 1)(lambda: far_copy.wait_recv())
        pl.when(core == 0)(lambda: own_load.wait())
    else:
        own_load = pltpu.make_async_copy(x_ref, x_all.at[rank], load_sems.at[0])
        joint_load = pltpu.make_async_copy(joint_ref.at[1], joint_one, load_sems.at[1])
        own_load.start()
        joint_load.start()
        cot_far = send(cot_ref.at[1 - micro, 0], cot_own, cot_sems, 0, far)
        cot_load = pltpu.make_async_copy(cot_ref.at[micro, 0], cot_own, load_sems.at[2])
        pl.when(core == 1)(lambda: cot_far.start())
        pl.when(core == 0)(lambda: cot_load.start())
        own_load.wait()
    for d in range(1, half):
        x_copy(d - 1, rank, group.device(0, d)).start()
    x_copy(half - 1, rank, partner_core).start()

    source = lax.broadcasted_iota(jnp.int32, (span, width), 0)
    target = lax.broadcasted_iota(jnp.int32, (span, width), 1)
    if half == 2:
        wanted = (2 * lax.div(target, DH) + low) * DH + lax.rem(target, DH)
    else:
        wanted = low * width + target
    pick = (source == wanted).astype(F32).astype(BF16)
    if first:
        wout_copy.start()
        vec_copy.wait_recv()
        vec_pair[core] = vec_send[...]
        vec_pair[1 - core] = vec_recv[...]
        for load in own_loads:
            load.wait()
        for part in range(3):
            joint_pair[core, :, part * width : (part + 1) * width] = mm(
                wide_own[part], pick
            ).astype(BF16)
        for copy in wide_copies:
            copy.wait_recv()
        for part in range(3):
            joint_pair[1 - core, :, part * width : (part + 1) * width] = mm(
                wide_other[part], pick
            ).astype(BF16)
        vec = vec_pair[0]
        weights = lambda: joint_pair[0]
    else:
        joint_load.wait()
        vec = vec_ref[1]
        weights = lambda: joint_one[...]

    def of_heads(row):
        parts = vec[row : row + 1, :]
        mine = jnp.where(core == 0, parts[:, :span], parts[:, span:])
        wide = jnp.broadcast_to(mine, (16, span)).astype(BF16)
        return mm(wide, pick)[0:1, :]

    bias_q = of_heads(B_QUERY)
    bias_v = of_heads(B_VALUE)
    gain = vec[LN1_GAIN : LN1_GAIN + 1, :]
    shift = vec[LN1_BIAS : LN1_BIAS + 1, :]

    def project(at):
        normal, _ = norm_stats(x_all[at].astype(F32))
        a = (normal * gain + shift).astype(BF16)
        here = pl.ds(pl.multiple_of(at * rows, 16), rows)
        a_all[here, :] = a
        joined = mm(a, weights())
        q_all[here, :] = (joined[:, :width] + bias_q).astype(BF16)
        k_all[here, :] = joined[:, width : 2 * width].astype(BF16)
        v_all[here, :] = (joined[:, 2 * width :] + bias_v).astype(BF16)

    project(rank)
    x_copy(half - 1, rank, partner_core).wait_recv()
    project(group.rank_of(1, 0))
    for d in range(1, half):
        here = group.rank_of(0, half - d)
        x_copy(d - 1, here, partner_core).wait_recv()
        x_copy(half - 1 + d, here, partner_core).start()
        project(here)
    for d in range(1, half):
        there = group.rank_of(1, half - d)
        x_copy(half - 1 + d, there, partner_core).wait_recv()
        project(there)

    saves = [
        pltpu.make_async_copy(a_all, a_out, out_sems.at[0]),
        pltpu.make_async_copy(q_all, q_out, out_sems.at[1]),
        pltpu.make_async_copy(k_all, k_out, out_sems.at[2]),
        pltpu.make_async_copy(v_all, v_out, out_sems.at[3]),
    ]
    if first:
        saves.append(pltpu.make_async_copy(joint_pair, joint_out, out_sems.at[4]))
        saves.append(pltpu.make_async_copy(x_all.at[rank], x_out, out_sems.at[5]))
        saves.append(pltpu.make_async_copy(vec_pair, vec_out, out_sems.at[6]))
    for save in saves:
        save.start()
    lane = lax.broadcasted_iota(jnp.int32, (rows, 128), 1)
    mask = mask_ref[...]

    def attend(at):
        here = pl.ds(pl.multiple_of(at * rows, 16), rows)
        q = q_all[here, :]
        mixed = jnp.zeros((rows, width), F32)
        totals = jnp.zeros((rows, 128), F32)
        for head in range(heads):
            mine = head_lanes((rows, width), head)
            scores = mm_nt(jnp.where(mine, q, jnp.zeros_like(q)), k_all[...]) * SCALE2 + mask
            top = jnp.max(scores, axis=-1, keepdims=True)
            expo = jnp.exp2(scores - top)
            total = jnp.sum(expo, axis=-1, keepdims=True)
            part = mm(expo.astype(BF16), v_all[...]) / total
            mixed = jnp.where(mine, part, mixed)
            totals = jnp.where(lane == head, top + jnp.log2(total), totals)
        lse[here, :] = totals
        return mixed.astype(BF16)

    copies = []
    for dc, d in group.others():
        slot = group.slot(dc, d)
        o_send[slot] = attend(group.rank_of(dc, d))
        copies.append(send(o_send.at[slot], o_recv.at[rank], o_sems, slot, group.device(dc, d)))
        copies[-1].start()
    if not first:
        pl.when(core == 1)(lambda: cot_far.wait())
        pl.when(core == 0)(lambda: cot_load.wait())
        cot_share = send(cot_own, cot_other, cot_sems, 1, partner_core)
        cot_share.start()
    o_recv[rank] = attend(rank)
    if not first:
        cot_share.wait()
        cot_out[0] = cot_own[...]
        cot_out[1] = cot_other[...]
    lse_out[...] = lse[...]
    for copy in copies:
        copy.wait()
    o_out[...] = o_recv[...]
    for save in saves:
        save.wait()
    for d in range(1, half):
        x_copy(d - 1, rank, group.device(0, d)).wait_send()
        x_copy(half - 1 + d, group.rank_of(0, half - d), partner_core).wait_send()
    x_copy(half - 1, rank, partner_core).wait_send()
    if first:
        pl.when(core == 1)(lambda: far_copy.wait_send())
        for copy in wide_copies:
            copy.wait_send()
        vec_copy.wait_send()
        wout_copy.wait()


def attend_call(first, layer, mask, ranks, dp_count, *args):
    rows = args[0].shape[-2]
    width = D // ranks
    half = ranks // 2
    span = half * width
    anywhere = pl.BlockSpec(memory_space=pl.ANY)
    vmem = pl.BlockSpec(memory_space=pltpu.VMEM)
    out_shape = [
        jax.ShapeDtypeStruct((ranks, rows, width), BF16),
        jax.ShapeDtypeStruct((LEN, 128), F32),
        jax.ShapeDtypeStruct((LEN, D), BF16),
        jax.ShapeDtypeStruct((LEN, width), BF16),
        jax.ShapeDtypeStruct((LEN, width), BF16),
        jax.ShapeDtypeStruct((LEN, width), BF16),
    ]
    out_specs = [vmem, vmem] + [anywhere] * 4
    scratch = [
        pltpu.VMEM((ranks, rows, D), BF16),
        pltpu.VMEM((LEN, D), BF16),
        pltpu.VMEM((LEN, width), BF16),
        pltpu.VMEM((LEN, width), BF16),
        pltpu.VMEM((LEN, width), BF16),
        pltpu.VMEM((LEN, 128), F32),
        pltpu.VMEM((ranks, rows, width), BF16),
        pltpu.VMEM((ranks, rows, width), BF16),
    ]
    scratch += dma_pair(2 * half) + dma_pair(ranks) + [pltpu.SemaphoreType.DMA((7,))]
    if first:
        operands = args[:3] + (mask,) + args[3:]
        in_specs = [anywhere] * 3 + [vmem] * (1 + len(args[3:]))
        out_shape += [
            jax.ShapeDtypeStruct((rows, D), BF16),
            jax.ShapeDtypeStruct((2, D, 3 * width), BF16),
            jax.ShapeDtypeStruct((D, D), BF16),
            jax.ShapeDtypeStruct((2, VEC_ROWS, D), F32),
        ]
        out_specs += [anywhere] * 4
        scratch += [
            pltpu.VMEM((2, D, 3 * width), BF16),
            pltpu.VMEM((3, D, span), BF16),
            pltpu.VMEM((3, D, span), BF16),
            pltpu.VMEM((VEC_ROWS, D), F32),
            pltpu.VMEM((VEC_ROWS, D), F32),
            pltpu.VMEM((2, VEC_ROWS, D), F32),
        ]
        scratch += dma_pair(3) + dma_pair(2) + [pltpu.SemaphoreType.DMA((4,))]
    else:
        operands = args[:2] + (mask,) + args[2:]
        in_specs = [anywhere] * 2 + [vmem] * 2 + [anywhere]
        out_shape += [jax.ShapeDtypeStruct((2, rows, D), BF16)]
        out_specs += [vmem]
        scratch += [
            pltpu.VMEM((D, 3 * width), BF16),
            pltpu.VMEM((rows, D), BF16),
            pltpu.VMEM((rows, D), BF16),
        ]
        scratch += dma_pair(2) + [pltpu.SemaphoreType.DMA((3,))]
    return pl.pallas_call(
        functools.partial(attend_kernel, first, layer, dp_count),
        in_specs=in_specs,
        out_specs=out_specs,
        out_shape=out_shape,
        scratch_shapes=scratch,
        compiler_params=pltpu.CompilerParams(
            vmem_limit_bytes=VMEM_LIMIT, collective_id=5 + layer, has_side_effects=True
        ),
        cost_estimate=pl.CostEstimate(
            flops=40 * 10**9, bytes_accessed=20 * 2**20, transcendentals=LEN * LEN * width // DH
        ),
    )(*operands)


def mlp_kernel(
    layer,
    dp_count,
    o_ref,
    x_ref,
    wo0_ref,
    wo1_ref,
    vec_ref,
    up0_ref,
    up1_ref,
    down0_ref,
    down1_ref,
    h_ref,
    u_ref,
    y_ref,
    a_all,
    o_all,
    g_all,
    rows_out,
    acc,
    wo,
    a_mine,
    a_other,
    o_send,
    o_other,
    g_mine,
    g_send,
    g_other,
    send_sems,
    recv_sems,
    save_sems,
    wo_sem,
    rows_mine,
    *rows_sems,
):
    step = pl.program_id(0)
    groups, rows, width = o_ref.shape
    half = groups // 2
    unit = FF // shards_of() // 2
    core = lax.axis_index("section")
    own = core == layer
    device = {"section": 1 - core}
    sems = (send_sems, recv_sems)
    if layer == 1:
        rows_copy = Deliver(Group(), 0, rows_mine, rows_out, rows_sems)
    a_copy = send(a_mine, a_other, sems, NCHF, device)
    o_copy = send(o_send, o_other, sems, NCHF + 1, device)

    def g_copy(at):
        return send(g_send.at[at], g_other.at[at], sems, at, device)

    def g_save(which, at):
        cols = pl.ds(pl.multiple_of(at * (FCF // 2), FCF // 2), FCF // 2)
        source = g_other if which else g_mine
        return pltpu.make_async_copy(
            source.at[at], g_all.at[which, :, cols], save_sems.at[which, at]
        )

    @pl.when(step == 0)
    def _():
        Group().greet(dp_count)
        if layer == 1:
            rows_mine[...] = x_ref[...]
            rows_copy.start()
        first = pltpu.make_async_copy(wo0_ref, wo, wo_sem)
        second = pltpu.make_async_copy(wo1_ref, wo, wo_sem)
        pl.when(own)(lambda: first.start())
        pl.when(jnp.logical_not(own))(lambda: second.start())
        for i in range(half):
            o_send[i] = o_ref[(1 - core) * half + i]
            o_all[0, :, i * width : (i + 1) * width] = o_ref[core * half + i]
        o_copy.start()
        first.wait()
        hidden = x_ref[...].astype(F32) + vec_ref[0, B_OUT : B_OUT + 1, :]
        for group in range(groups):
            hidden += mm(o_ref[group], wo[group * width : (group + 1) * width, :])
        h_ref[...] = hidden
        normal, _ = norm_stats(hidden)
        a_mine[...] = (
            normal * vec_ref[0, LN2_GAIN : LN2_GAIN + 1, :] + vec_ref[0, LN2_BIAS : LN2_BIAS + 1, :]
        ).astype(BF16)
        a_copy.start()
        acc[...] = hidden + vec_ref[0, B_DOWN : B_DOWN + 1, :]

    def part(up_ref, down_ref):
        at = pl.multiple_of(lax.rem(step, D // FCF) * FCF, FCF)
        bias = vec_ref[0, pl.ds(B_UP + lax.div(step, D // FCF), 1), pl.ds(at, FCF)]
        upper = mm(a_mine[...], up_ref[...]) + bias
        u_ref[...] = upper
        inner = GELU_A * (upper + GELU_B * upper * upper * upper)
        gated = (0.5 * upper * (1.0 + jnp.tanh(inner))).astype(BF16)
        split_halves(gated, unit, core, g_mine, g_send, step)
        acc[...] += mm(gated, down_ref[...])

    @pl.when(step < NCHF)
    def _():
        pl.when(own)(lambda: part(up0_ref, down0_ref))
        pl.when(jnp.logical_not(own))(lambda: part(up1_ref, down1_ref))
        g_copy(step).start()
        g_save(0, step).start()

    @pl.when(step > 0)
    def _():
        g_copy(step - 1).wait()
        g_save(1, step - 1).start()

    @pl.when(step == NCHF)
    def _():
        y_ref[...] = acc[...].astype(BF16)
        a_copy.wait()
        a_all[0] = a_mine[...]
        a_all[1] = a_other[...]
        o_copy.wait()
        for i in range(half):
            o_all[1, :, i * width : (i + 1) * width] = o_other[i]

        def drain(at, carry):
            g_save(0, at).wait()
            g_save(1, at).wait()
            return carry

        lax.fori_loop(0, NCHF, drain, 0)
        if layer == 1:
            rows_copy.wait()


def mlp_call(layer, dp_count, o_all, x_own, outs, vec, ups, downs):
    rows = x_own.shape[0]
    groups, _, width = o_all.shape
    whole = lambda i: (0, 0)
    now = lambda i: jnp.minimum(i, NCHF - 1)
    mine = lambda i, first: jnp.where((lax.axis_index("section") == layer) == first, now(i), 0)
    col = lambda first: (lambda i: (0, mine(i, first)))
    line = lambda first: (lambda i: (mine(i, first), 0))
    chunk = lambda i: (0, now(i))
    piece = pltpu.VMEM((NCHF, rows, FCF // 2), BF16)
    return pl.pallas_call(
        functools.partial(mlp_kernel, layer, dp_count),
        grid=(NCHF + 1,),
        in_specs=[
            pl.BlockSpec((groups, rows, width), lambda i: (0, 0, 0)),
            pl.BlockSpec((rows, D), whole),
            pl.BlockSpec(memory_space=pl.ANY),
            pl.BlockSpec(memory_space=pl.ANY),
            pl.BlockSpec((1, VEC_ROWS, D), lambda i: (layer, 0, 0)),
            pl.BlockSpec((D, FCF), col(True)),
            pl.BlockSpec((D, FCF), col(False)),
            pl.BlockSpec((FCF, D), line(True)),
            pl.BlockSpec((FCF, D), line(False)),
        ],
        out_specs=[
            pl.BlockSpec((rows, D), whole),
            pl.BlockSpec((rows, FCF), chunk),
            pl.BlockSpec((rows, D), whole),
            pl.BlockSpec((2, rows, D), lambda i: (0, 0, 0)),
            pl.BlockSpec((2, rows, D // 2), lambda i: (0, 0, 0)),
            pl.BlockSpec(memory_space=pl.ANY),
            pl.BlockSpec(memory_space=pl.ANY),
        ],
        scratch_shapes=[
            pltpu.VMEM((rows, D), F32),
            pltpu.VMEM((D, D), BF16),
            pltpu.VMEM((rows, D), BF16),
            pltpu.VMEM((rows, D), BF16),
            pltpu.VMEM((groups // 2, rows, width), BF16),
            pltpu.VMEM((groups // 2, rows, width), BF16),
            piece,
            piece,
            piece,
        ]
        + dma_pair(NCHF + 2)
        + [pltpu.SemaphoreType.DMA((2, NCHF)), pltpu.SemaphoreType.DMA]
        + [pltpu.VMEM((rows, D), BF16)]
        + deliver_sems(),
        out_shape=[
            jax.ShapeDtypeStruct((rows, D), F32),
            jax.ShapeDtypeStruct((rows, FF), F32),
            jax.ShapeDtypeStruct((rows, D), BF16),
            jax.ShapeDtypeStruct((2, rows, D), BF16),
            jax.ShapeDtypeStruct((2, rows, D // 2), BF16),
            jax.ShapeDtypeStruct((2, rows, FF // 2), BF16),
            jax.ShapeDtypeStruct((2, rows, D), BF16),
        ],
        compiler_params=pltpu.CompilerParams(
            vmem_limit_bytes=VMEM_LIMIT, collective_id=7 + layer, has_side_effects=True
        ),
        cost_estimate=pl.CostEstimate(
            flops=2 * rows * D * (D + 2 * FF), bytes_accessed=30 * 2**20, transcendentals=rows * FF
        ),
    )(o_all, x_own, outs[0], outs[1], vec, ups[0], ups[1], downs[0], downs[1])


def back_kernel(layer, host, ranges, *refs):
    n = host.arrays - 1
    refs = list(refs)

    def pop(count):
        taken = refs[:count]
        del refs[:count]
        return taken

    u_ref, mask_ref, vec_ref = pop(3)
    dy_src, h_src, a2_src, wo0_src, wo1_src, up0_src, up1_src, down0_src, down1_src = pop(9)
    rows_src = pop(1)[0]
    late = pop(8)
    srcs = pop(n)
    gbup_ref, sums_two_ref, sums_one_ref, sums_qv_ref = pop(4)
    gup_out, dx_out, gjoint_out, gout_out, rows_out = pop(5)
    outs = pop(n + 1)
    dy, h, a2, wo, ups, downs = pop(6)
    load_sems, weight_sems = pop(2)
    acc, du_mine, du_send, du_recv, gup, branch, dh, do_send, do_recv = pop(9)
    du_sems, do_sems = pop(2), pop(2)
    gup_sems, save_sems = pop(2)
    q_all, k_all, v_all, lse, a1, w_joint, x_own, mixed = pop(8)
    late_sems = pop(1)[0]
    dk_acc, dv_acc, dj, core_recv, far_send, far_recv = pop(6)
    core_send = a2 if lax.axis_size("seq") == 4 else pop(1)[0]
    g_own, g_send, g_recv, gout, dx_recv = pop(5)
    dx_own = dy
    core_sems, far_sems, pair_sems = pop(2), pop(2), pop(2)
    rows_sems = pop(3)
    host.bind(list(srcs) + [gup_out], outs, refs)
    group = Group()
    core, half, rank = group.core, group.half, group.rank
    step = pl.program_id(0)
    ranks, rows, width = do_send.shape
    length = q_all.shape[0]
    heads = width // DH
    scale = DH ** (-0.5)
    unit = FF // shards_of() // 2
    own = core == layer
    partner_core = group.device(1, 0)
    ranges = list(ranges)
    lead, middle = ranges[: 2 * NCH], ranges[2 * NCH : 2 * NCH + 3]
    blocks = length // BQ * heads
    inner = ranges[2 * NCH + 3 : 2 * NCH + 3 + blocks]
    tail = ranges[2 * NCH + 3 + blocks :]

    def weight_copies(at, second):
        slot = lax.rem(at, 2)
        cols = pl.ds(pl.multiple_of(at * FC, FC), FC)
        up, down = (up1_src, down1_src) if second else (up0_src, down0_src)
        return (
            pltpu.make_async_copy(up.at[:, cols], ups.at[slot], weight_sems.at[0, slot]),
            pltpu.make_async_copy(down.at[cols, :], downs.at[slot], weight_sems.at[1, slot]),
        )

    def fetch(at):
        @pl.when(own)
        def _():
            for copy in weight_copies(at, False):
                copy.start()

        @pl.when(jnp.logical_not(own))
        def _():
            for copy in weight_copies(at, True):
                copy.start()

    rows_copy = Deliver(group, 1, rows_src.at[0], rows_out, rows_sems)
    dy_load = pltpu.make_async_copy(dy_src.at[0], dy, load_sems.at[0])
    h_load = pltpu.make_async_copy(h_src, h, load_sems.at[1])
    a2_load = pltpu.make_async_copy(a2_src, a2, load_sems.at[2])
    wo_load = pltpu.make_async_copy(wo0_src, wo, load_sems.at[3])
    wo_load_other = pltpu.make_async_copy(wo1_src, wo, load_sems.at[3])
    late_loads = [
        pltpu.make_async_copy(source.at[layer] if i == 5 else source, target, late_sems.at[i])
        for i, (source, target) in enumerate(
            zip(late, (q_all, k_all, v_all, lse, a1, w_joint, x_own, mixed))
        )
    ]

    def du_copy(at):
        return send(du_send.at[at], du_recv.at[at], du_sems, at, partner_core)

    def gup_save(at):
        per = gup.shape[1]
        lead_bits = NCH.bit_length() - 1
        index = tuple(
            lax.rem(lax.div(at, 2 ** (lead_bits - 1 - j)), 2) for j in range(lead_bits)
        )
        return pltpu.make_async_copy(
            gup.at[lax.rem(at, 2)].reshape(gup_out.shape[lead_bits:]),
            gup_out.at[index],
            gup_sems.at[lax.rem(at, 2)],
        )

    @pl.when(step == 0)
    def _():
        group.greet(host.dp_count)
        rows_copy.start()
        dy_load.start()
        fetch(0)
        host.begin()
        a2_load.start()
        h_load.start()
        pl.when(own)(lambda: wo_load.start())
        pl.when(jnp.logical_not(own))(lambda: wo_load_other.start())
        for load in late_loads:
            load.start()
        acc[...] = jnp.zeros_like(acc)
        dy_load.wait()
        a2_load.wait()

    @pl.when(step < NCH - 1)
    def _():
        fetch(step + 1)

    @pl.when(step < NCH)
    def _():
        slot = lax.rem(step, 2)
        for copy in weight_copies(step, False):
            copy.wait()
        d_gated = mm_nt(dy[...], downs[slot])
        upper = u_ref[...]
        square = upper * upper
        turn = jnp.tanh(GELU_A * upper * (1.0 + GELU_B * square))
        slope = 0.5 * (1.0 + turn) + (0.5 * GELU_A) * upper * (1.0 - turn * turn) * (
            1.0 + (3.0 * GELU_B) * square
        )
        d_upper = (d_gated * slope).astype(BF16)
        split_halves(d_upper, unit, core, du_mine, du_send, step)
        du_copy(step).start()
        gbup_ref[...] = jnp.sum(d_upper.astype(F32), axis=0, keepdims=True)
        acc[...] += mm_nt(d_upper, ups[slot])

    for at, (first, last) in enumerate(lead):
        if last > first and at % 2 == 0:
            pl.when(step == at // 2)(functools.partial(host.run, first, last))

    @pl.when(step > 0)
    def _():
        at = step - 1
        du_copy(at).wait()
        pl.when(at >= 2)(lambda: gup_save(at - 2).wait())
        value = mm_tn(du_mine[at], a2[0]) + mm_tn(du_recv[at], a2[1])
        gup[lax.rem(at, 2)] = value.astype(BF16).reshape(gup.shape[1:])
        gup_save(at).start()

    for at, (first, last) in enumerate(lead):
        if last > first and at % 2 == 1:
            pl.when(step == at // 2)(functools.partial(host.run, first, last))

    @pl.when(step == NCH)
    def _():
        h_load.wait()
        gup_save(NCH - 2).wait()
        gup_save(NCH - 1).wait()
        host.begin(1)
        normal, inverse = norm_stats(h[...])
        d_out = dy[...].astype(F32)
        d_normed = acc[...]
        sums_two_ref[...] = jnp.zeros_like(sums_two_ref)
        sums_two_ref[0:1, :] = jnp.sum(d_normed * normal, axis=0, keepdims=True)
        sums_two_ref[1:2, :] = jnp.sum(d_normed, axis=0, keepdims=True)
        d_normal = d_normed * vec_ref[0, LN2_GAIN : LN2_GAIN + 1, :]
        d_hidden = d_out + inverse * (
            d_normal
            - jnp.mean(d_normal, axis=-1, keepdims=True)
            - normal * jnp.mean(d_normal * normal, axis=-1, keepdims=True)
        )
        dh[...] = d_hidden
        d_branch = d_hidden.astype(BF16)
        branch[0] = d_branch
        branch_copy = send(branch.at[0], branch.at[1], do_sems, ranks, partner_core)
        branch_copy.start()
        wo_load.wait()

        def heads_of(to_rank):
            at = pl.multiple_of(to_rank * width, width)
            return mm_nt(d_branch, wo[pl.ds(at, width), :]).astype(BF16)

        copies = []
        for dc, d in group.others():
            slot = group.slot(dc, d)
            do_send[slot] = heads_of(group.rank_of(dc, d))
            copies.append(
                send(do_send.at[slot], do_recv.at[pl.ds(pl.multiple_of(rank * rows, 16), rows)], do_sems, slot, group.device(dc, d))
            )
            copies[-1].start()
        do_recv[pl.ds(pl.multiple_of(rank * rows, 16), rows), :] = heads_of(rank)
        host.run(*middle[0])
        sums_two_ref[2:3, :] = jnp.sum(d_branch.astype(F32), axis=0, keepdims=True)
        sums_two_ref[3:4, :] = jnp.sum(d_out, axis=0, keepdims=True)
        dk_acc[...] = jnp.zeros_like(dk_acc)
        dv_acc[...] = jnp.zeros_like(dv_acc)
        sums_qv_ref[...] = jnp.zeros_like(sums_qv_ref)
        sums_one_ref[...] = jnp.zeros_like(sums_one_ref)
        for load in late_loads:
            load.wait()
        branch_copy.wait()
        gout[...] = (mm_tn(branch[0], mixed[0]) + mm_tn(branch[1], mixed[1])).astype(BF16)
        gout_save = pltpu.make_async_copy(gout, gout_out, save_sems.at[0])
        gout_save.start()
        host.run(*middle[1])
        for copy in copies:
            copy.wait()
        host.run(*middle[2])

        def block(at, carry):
            here = pl.ds(pl.multiple_of(at * BQ, BQ), BQ)
            q = q_all[here, :]
            grad = do_recv[here, :]
            totals = lse[here, :]
            d_q = jnp.zeros((BQ, width), F32)
            for head in range(heads):
                mine = head_lanes((BQ, width), head)
                q_head = jnp.where(mine, q, jnp.zeros_like(q))
                grad_head = jnp.where(mine, grad, jnp.zeros_like(grad))
                scores = mm_nt(q_head, k_all[...]) * SCALE2 + mask_ref[...]
                probs = jnp.exp2(scores - totals[:, head : head + 1])
                d_probs = mm_nt(grad_head, v_all[...])
                term = jnp.sum(probs * d_probs, axis=-1, keepdims=True)
                d_scores = (probs * (d_probs - term)).astype(BF16)
                dv_acc[...] += mm_tn(probs.astype(BF16), grad_head)
                dk_acc[...] += mm_tn(d_scores, q_head)
                d_q = jnp.where(mine, mm(d_scores, k_all[...]), d_q)
                for slot, (first, last) in enumerate(inner):
                    if last > first and slot % heads == head:
                        pl.when(at == slot // heads)(functools.partial(host.run, first, last))
            low = (d_q * scale).astype(BF16)
            dj[here, :width] = low
            sums_qv_ref[0:1, :] += jnp.sum(low.astype(F32), axis=0, keepdims=True)
            return carry

        lax.fori_loop(0, length // BQ, block, 0)
        dj[:, width : 2 * width] = (dk_acc[...] * scale).astype(BF16)
        low_v = dv_acc[...].astype(BF16)
        dj[:, 2 * width :] = low_v
        sums_qv_ref[1:2, :] = jnp.sum(low_v.astype(F32), axis=0, keepdims=True)

        def partial_rows(to_rank):
            here = pl.ds(pl.multiple_of(to_rank * rows, 16), rows)
            return mm_nt(dj[here, :], w_joint[...])

        def core_copy(d):
            return send(core_send.at[d], core_recv.at[d], core_sems, d, partner_core)

        def far_copy(d):
            return send(far_send.at[d - 1], far_recv.at[d - 1], far_sems, d - 1, group.device(0, d))

        for d in [d for d in range(1, half)] + [0]:
            core_send[d] = partial_rows(group.rank_of(1, d)).astype(BF16)
            core_copy(d).start()
        for d in range(1, half):
            value = partial_rows(group.rank_of(0, d))
            core_copy(d).wait_recv()
            far_send[d - 1] = (value + core_recv[d].astype(F32)).astype(BF16)
            far_copy(d).start()
        host.run(*tail[0])
        value = partial_rows(rank)
        core_copy(0).wait_recv()
        acc[...] = value + core_recv[0].astype(F32)

        half_cols = D // 2
        mine_cols = pl.ds(pl.multiple_of(core * half_cols, half_cols), half_cols)
        other_cols = pl.ds(pl.multiple_of((1 - core) * half_cols, half_cols), half_cols)
        g_send[...] = mm_tn(dj[...], a1[:, other_cols]).astype(BF16).reshape(g_send.shape)
        g_copy = send(g_send, g_recv, pair_sems, 0, partner_core)
        g_copy.start()
        host.run(*tail[1])
        g_own[...] = mm_tn(dj[...], a1[:, mine_cols]).astype(BF16).reshape(g_own.shape)
        g_save = pltpu.make_async_copy(g_own, gjoint_out.at[:, core], save_sems.at[1])
        g_save.start()
        host.run(*tail[2])

        for d in range(1, half):
            far_copy(d).wait_recv()
            acc[...] += far_recv[d - 1].astype(F32)
        d_normed = acc[...]
        normal, inverse = norm_stats(x_own[...].astype(F32))
        sums_one_ref[0:1, :] = jnp.sum(d_normed * normal, axis=0, keepdims=True)
        sums_one_ref[1:2, :] = jnp.sum(d_normed, axis=0, keepdims=True)
        d_normal = d_normed * vec_ref[0, LN1_GAIN : LN1_GAIN + 1, :]
        d_in = (
            dh[...]
            + inverse
            * (
                d_normal
                - jnp.mean(d_normal, axis=-1, keepdims=True)
                - normal * jnp.mean(d_normal * normal, axis=-1, keepdims=True)
            )
        ).astype(BF16)
        dx_own[...] = d_in
        dx_copy = send(dx_own, dx_recv, pair_sems, 1, partner_core)
        dx_copy.start()
        dx_save = pltpu.make_async_copy(dx_own, dx_out.at[0], save_sems.at[2])
        dx_save.start()
        host.run(*tail[3])
        g_copy.wait()
        g_save_other = pltpu.make_async_copy(g_recv, gjoint_out.at[:, 1 - core], save_sems.at[3])
        g_save_other.start()
        dx_copy.wait()
        dx_save_other = pltpu.make_async_copy(dx_recv, dx_out.at[1], save_sems.at[4])
        dx_save_other.start()
        for d in range(half):
            core_copy(d).wait_send()
        for d in range(1, half):
            far_copy(d).wait_send()
        for save in (gout_save, g_save, dx_save, g_save_other, dx_save_other):
            save.wait()
        rows_copy.wait()
        host.finish()


def back_call(layer, dy, hidden, wos, vec, upper, a2, ups, downs, given, late, mask, host, arrays):
    rows = dy.shape[1]
    ranks = host.count
    width = D // ranks
    half = ranks // 2
    shards = host.dp_count * ranks
    per = shards // NCH
    unit = FF // shards // 2
    heads = width // DH
    now = lambda i: (0, jnp.minimum(i, NCH - 1))
    whole = lambda i: (0, 0)
    anywhere = pl.BlockSpec(memory_space=pl.ANY)
    times = []
    for i in range(NCH):
        times += [2.9 * i + 1.6, 2.9 * i + 2.9]
    times += [29.0, 33.0, 36.0]
    for i in range(LEN // BQ * heads):
        times.append(36.0 + 28.0 / (LEN // BQ * heads) * (i + 1))
    times += [69.0, 73.0, 76.0, 84.0]
    ranges = host.slots(times)
    piece = pltpu.VMEM((NCH, rows, FC // 2), BF16)
    tokens = pltpu.VMEM((LEN, width), BF16)
    own = pltpu.VMEM((rows, D), BF16)
    view = host.view_shape(host.arrays - 1)
    return pl.pallas_call(
        functools.partial(back_kernel, layer, host, ranges),
        grid=(NCH + 1,),
        in_specs=[
            pl.BlockSpec((rows, FC), now),
            pl.BlockSpec((1, LEN), whole),
            pl.BlockSpec((1, VEC_ROWS, D), lambda i: (layer, 0, 0)),
        ]
        + [anywhere] * (10 + len(late) + len(arrays)),
        out_specs=[
            pl.BlockSpec((1, FC), now),
            pl.BlockSpec((8, D), whole),
            pl.BlockSpec((8, D), whole),
            pl.BlockSpec((8, width), whole),
        ]
        + [anywhere] * 5
        + host.out_specs(),
        out_shape=[
            jax.ShapeDtypeStruct((1, FF), F32),
            jax.ShapeDtypeStruct((8, D), F32),
            jax.ShapeDtypeStruct((8, D), F32),
            jax.ShapeDtypeStruct((8, width), F32),
            jax.ShapeDtypeStruct(view, BF16),
            jax.ShapeDtypeStruct((2, rows, D), BF16),
            jax.ShapeDtypeStruct((3, 2, width, D // 2), BF16),
            jax.ShapeDtypeStruct((D, D // 2), BF16),
            jax.ShapeDtypeStruct((2, rows, D), BF16),
        ]
        + host.out_shapes(),
        scratch_shapes=[
            own,
            pltpu.VMEM((rows, D), F32),
            pltpu.VMEM((2, rows, D), BF16),
            pltpu.VMEM((D, D), BF16),
            pltpu.VMEM((2, D, FC), BF16),
            pltpu.VMEM((2, FC, D), BF16),
            pltpu.SemaphoreType.DMA((4,)),
            pltpu.SemaphoreType.DMA((2, 2)),
            pltpu.VMEM((rows, D), F32),
            piece,
            piece,
            piece,
            pltpu.VMEM((2, per, unit, D), BF16),
            pltpu.VMEM((2, rows, D), BF16),
            pltpu.VMEM((rows, D), F32),
            pltpu.VMEM((ranks, rows, width), BF16),
            tokens,
        ]
        + dma_pair(NCH)
        + dma_pair(ranks + 1)
        + [pltpu.SemaphoreType.DMA((2,)), pltpu.SemaphoreType.DMA((5,))]
        + [pltpu.VMEM(t.shape[1:] if i == 5 else t.shape, t.dtype) for i, t in enumerate(late)]
        + [pltpu.SemaphoreType.DMA((len(late),))]
        + [
            pltpu.VMEM((LEN, width), F32),
            pltpu.VMEM((LEN, width), F32),
            pltpu.VMEM((LEN, 3 * width), BF16),
            pltpu.VMEM((half, rows, D), BF16),
            pltpu.VMEM((half - 1, rows, D), BF16),
            pltpu.VMEM((half - 1, rows, D), BF16),
        ]
        + ([] if ranks == 4 else [pltpu.VMEM((half, rows, D), BF16)])
        + [
            pltpu.VMEM((3, width, D // 2), BF16),
            pltpu.VMEM((3, width, D // 2), BF16),
            pltpu.VMEM((3, width, D // 2), BF16),
            pltpu.VMEM((D, D // 2), BF16),
            own,
        ]
        + dma_pair(half)
        + dma_pair(half - 1)
        + dma_pair(2)
        + deliver_sems()
        + host.scratch(),
        compiler_params=pltpu.CompilerParams(
            vmem_limit_bytes=BACK_LIMIT, collective_id=layer, has_side_effects=True
        ),
        cost_estimate=pl.CostEstimate(
            flops=100 * 10**9, bytes_accessed=60 * 2**20, transcendentals=rows * FF
        ),
    )(
        upper,
        mask,
        vec,
        dy,
        hidden,
        a2,
        wos[0],
        wos[1],
        ups[0],
        ups[1],
        downs[0],
        downs[1],
        given,
        *late,
        *[host.view(i, array) for i, array in enumerate(arrays)],
    )


def final_kernel(host, *refs):
    n = host.arrays
    srcs, rows_src = refs[:n], refs[n]
    outs, rows_out = refs[n + 1 : 2 * n + 1], refs[2 * n + 1]
    rows_sems = refs[2 * n + 2 : 2 * n + 5]
    rows_mine, rows_sem = refs[2 * n + 5 : 2 * n + 7]
    host.bind(srcs, outs, refs[2 * n + 7 :])
    rows_load = pltpu.make_async_copy(rows_src.at[0], rows_mine, rows_sem)
    rows_load.start()
    group = Group()
    group.greet(host.dp_count)
    host.begin()
    rows_copy = Deliver(group, 0, rows_mine, rows_out, rows_sems)
    rows_load.wait()
    rows_copy.start()
    host.run(0, len(host.events))
    host.finish()
    rows_copy.wait()


def final_call(host, arrays, rows_src, collective_id):
    anywhere = pl.BlockSpec(memory_space=pl.ANY)
    return pl.pallas_call(
        functools.partial(final_kernel, host),
        in_specs=[anywhere] * (host.arrays + 1),
        out_specs=[anywhere] * (host.arrays + 1),
        out_shape=host.out_shapes() + [jax.ShapeDtypeStruct(rows_src.shape, BF16)],
        scratch_shapes=deliver_sems()
        + [pltpu.VMEM(rows_src.shape[1:], BF16), pltpu.SemaphoreType.DMA]
        + host.scratch(),
        compiler_params=pltpu.CompilerParams(
            vmem_limit_bytes=VMEM_LIMIT, collective_id=collective_id, has_side_effects=True
        ),
    )(*host.views(arrays), rows_src)


def assemble_kernel(count, *refs):
    refs = list(refs)

    def pop(number):
        taken = refs[:number]
        del refs[:number]
        return taken

    sources = [pop(2) for _ in range(7)]
    row_outs = pop(2)
    up_out, down_out, out_out, joint_out = pop(4)
    vec_outs = pop(9)
    up, down, mixed, joint, little = pop(5)
    sems = pop(1)[0]
    core = lax.axis_index("section")
    half_ranks = count // 2
    compact = half_ranks == 2
    low = lax.rem(lax.axis_index("seq"), half_ranks)
    loads = []
    for i, (pair, target) in enumerate(zip(sources, [up, down, mixed, joint, little] + row_outs)):
        if i == 4:
            lines = little.shape[1]
            pair = [one.at[:, at * lines : (at + 1) * lines] for at, one in enumerate(pair)]
        first = pltpu.make_async_copy(pair[0], target, sems.at[i])
        second = pltpu.make_async_copy(pair[1], target, sems.at[i])
        pl.when(core == 0)(first.start)
        pl.when(core == 1)(second.start)
        loads.append(first)
    unit = up.shape[1]
    half_cols = D // 2
    loads[1].wait()
    for half in range(2):
        for g in range(FF // 2 // unit):
            at = (2 * g + half) * unit
            down_out[:, at : at + unit] = down[half, :, g * unit : (g + 1) * unit]
    loads[0].wait()
    for half in range(2):
        up_out[:, half * unit : (half + 1) * unit] = up[half].T
    for load in loads[2:5]:
        load.wait()
    for half in range(2):
        cols = slice(half * half_cols, (half + 1) * half_cols)
        value = mixed[half]
        if compact:
            heads = half_cols // DH // 2
            pieces = []
            for i in range(heads):
                for j in range(2):
                    at = (j * heads + i) * DH
                    pieces.append(value[:, at : at + DH])
            value = jnp.concatenate(pieces, axis=1)
        out_out[:, cols] = value
        value = joint[half]
        if compact:
            pieces = [value[i * DH : (i + 1) * DH, :] for i in range(4)]
            joint_out[0:DH, cols] = jnp.where(low == 0, pieces[0], pieces[1])
            joint_out[DH : 2 * DH, cols] = pieces[3]
            joint_out[2 * DH : 3 * DH, cols] = jnp.where(low == 0, pieces[1], pieces[2])
        else:
            joint_out[:, cols] = value
    total = little[0] + little[1]
    at = 0
    for out in vec_outs:
        size = out.shape[1]
        for start in range(0, size, 128):
            wide = min(128, size - start)
            row, lane = (at + start) // 128, (at + start) % 128
            out[:, start : start + wide] = total[row : row + 1, lane : lane + wide]
        at += size
    for load in loads[5:]:
        load.wait()


def assemble_call(count, groups, pairs):
    unit = D // groups
    anywhere = pl.BlockSpec(memory_space=pl.ANY)
    vmem = pl.BlockSpec(memory_space=pltpu.VMEM)
    sizes = [unit] * 8 + [FF // groups]
    flat = [array for pair in pairs for array in pair]
    return pl.pallas_call(
        functools.partial(assemble_kernel, count),
        in_specs=[anywhere] * len(flat),
        out_specs=[vmem] * 15,
        out_shape=[jax.ShapeDtypeStruct(pair[0].shape, BF16) for pair in pairs[5:]]
        + [
            jax.ShapeDtypeStruct((D, FF // groups), F32),
            jax.ShapeDtypeStruct((unit, FF), F32),
            jax.ShapeDtypeStruct((unit, D), F32),
            jax.ShapeDtypeStruct((3 * unit, D), F32),
        ]
        + [jax.ShapeDtypeStruct((1, size), F32) for size in sizes],
        scratch_shapes=[pltpu.VMEM(pair[0].shape, F32) for pair in pairs[:4]]
        + [pltpu.VMEM((2, pairs[4][0].shape[1] // 2, 128), F32)]
        + [pltpu.SemaphoreType.DMA((7,))],
        compiler_params=params(),
    )(*flat)


def swap(value, axis, mask):
    count = lax.axis_size(axis)
    return lax.ppermute(value, axis, [(i, i ^ mask) for i in range(count)])


def take(value, index, dim):
    return lax.dynamic_index_in_dim(value, index, dim, keepdims=False)


def ordered(bit, mine, other, dim):
    return jnp.where(
        bit == 0,
        jnp.stack([mine, other], axis=dim),
        jnp.stack([other, mine], axis=dim),
    )


def key_bias(counts, rotate):
    places = jnp.arange(LEN, dtype=jnp.int32)
    places = jnp.where(rotate, (places + LEN // 2) % LEN, places)
    offset = jnp.maximum(places - TRI, 0)
    view_index = offset // VSLOT
    inside = offset - view_index * VSLOT
    match = view_index[:, None] == jnp.arange(VIEWS, dtype=jnp.int32)[None, :]
    limits = jnp.sum(jnp.where(match, counts[None, :], 0), axis=1)
    valid = (places < TRI) | (inside < limits)
    return jnp.where(valid, 0.0, -1e30).astype(F32)[None, :]


def shards(
    inputs,
    cotangent,
    view_tokens,
    ln1_gain,
    ln1_bias,
    w_qkv,
    b_query,
    b_value,
    w_out,
    b_out,
    ln2_gain,
    ln2_bias,
    w_up,
    b_up,
    w_down,
    b_down,
):
    core = lax.axis_index("section")
    place = lax.axis_index("seq")
    dp_index = lax.axis_index("dp")
    count = lax.axis_size("seq")
    dp_count = lax.axis_size("dp")
    groups = dp_count * count
    half = count // 2
    micro = place // half
    low = place % half
    low_bits = half.bit_length() - 1
    rows = inputs.shape[2]
    width = D // count
    rank = core * half + low

    def swap_core(value):
        return swap(value, "section", 1)

    def swap_seq(value, bit):
        return swap(value, "seq", 1 << bit)

    def low_bit(bit):
        return (place >> bit) & 1

    def own_rows(local):
        chunks = local[:, 0]
        far = lax.ppermute(
            take(chunks, 1 - micro, 0),
            ("section", "seq"),
            [(count + z, count + (z ^ half)) for z in range(count)],
        )
        return jnp.where(core == 0, take(chunks, micro, 0), far)

    def gather_rows(own):
        value = own[None]
        for bit in range(low_bits):
            other = swap_seq(value, bit)
            value = ordered(low_bit(bit), value, other, 0).reshape((-1,) + own.shape)
        value = ordered(core, value, swap_core(value), 0)
        return value.reshape((-1,) + own.shape[1:])

    def exchange(value):
        tail = value.shape[1:]
        value = value.reshape((2,) * (low_bits + 1) + tail)
        for bit in range(low_bits):
            dim = low_bits - bit
            mine = take(value, low_bit(bit), dim)
            other = swap_seq(take(value, 1 - low_bit(bit), dim), bit)
            value = ordered(low_bit(bit), mine, other, dim)
        mine = take(value, core, 0)
        other = swap_core(take(value, 1 - core, 0))
        return ordered(core, mine, other, 0).reshape((count,) + tail)

    compact = half == 2
    span = half * width

    def vector_to(value):
        if compact:
            wide = jnp.stack(
                [jnp.where(low == i, value.reshape(len(value), -1, DH), 0.0) for i in range(2)], axis=2
            )
        else:
            wide = jnp.stack([jnp.where(low == i, value, 0.0) for i in range(half)], axis=1)
        wide = wide.reshape(len(value), span)
        return jnp.concatenate([jnp.where(core == i, wide, 0.0) for i in range(2)], axis=1)

    def rank_rows(value):
        if compact:
            value = value.reshape(2, width // DH, 2, DH, D)
            return jnp.swapaxes(value, 1, 2).reshape(D, D)
        return value

    out_mine = rank_rows(w_out[0])
    ups = (w_up[0], swap_core(w_up[0]))
    downs = (w_down[0], swap_core(w_down[0]))
    bias_mask = key_bias(take(view_tokens[:, 0], micro, 0), micro == 1)

    saved = []
    acts = []
    for layer in range(2):
        if layer == 0:
            o_own, lse, a1, q, k, v, layer_in, joint_pair, out_other, vec = attend_call(
                True,
                0,
                bias_mask,
                count,
                dp_count,
                inputs,
                w_qkv,
                out_mine[None],
                ln1_gain,
                ln1_bias,
                b_query,
                b_value,
                b_out,
                ln2_gain,
                ln2_bias,
                b_down,
                b_up,
            )
            outs_pair = (out_mine, out_other)
        else:
            o_own, lse, a1, q, k, v, d_out_all = attend_call(
                False, 1, bias_mask, count, dp_count, layer_in, joint_pair, vec, cotangent
            )
        hidden, upper, output, a2_all, o_all, gated_all, first_rows = mlp_call(
            layer, dp_count, o_own, layer_in, outs_pair, vec, ups, downs
        )
        acts.append(output)
        saved.append((layer_in, a1, q, k, v, lse, hidden, upper, a2_all, o_all, gated_all))
        layer_in = output

    def hosted(arrays, spans=None, shares=STAGE_SHARES, even=False):
        shapes = []
        for array in arrays:
            shapes.append((array.shape[1], array.shape[2], array.shape[0] != groups, array.dtype))
        return Hosted(dp_count, count, tuple(shapes), spans, shares, even)

    results = [{}, {}]
    pending = None
    sums = []
    for layer in (1, 0):
        x_own, a1, q, k, v, lse, hidden, upper, a2_all, o_all, gated_all = saved[layer]
        g_down = mm_tn(d_out_all.reshape(2 * rows, D), gated_all.reshape(2 * rows, FF // 2))
        g_down = g_down.astype(BF16).reshape(groups, D // groups, FF // 2)
        up_like = jax.ShapeDtypeStruct((groups, FF // groups // 2, D), BF16)
        if pending is None:
            arrays = [g_down]
            host = hosted(
                arrays + [up_like],
                ((0, 0.0, 48.0), (1, 28.0, 78.0)),
                (0.4, 0.6, 0.8, 1.0),
                True,
            )
        else:
            arrays = list(pending) + [g_down]
            host = hosted(
                arrays + [up_like],
                ((0, 0.0, 36.0), (0, 0.0, 36.0), (0, 12.0, 80.0), (1, 40.0, 120.0)),
            )
        (g_bup, sums_two, sums_one, sums_qv, g_up, d_in, g_joint, g_out, given, *reduced) = back_call(
            layer,
            d_out_all,
            hidden,
            outs_pair,
            vec,
            upper,
            a2_all,
            ups,
            downs,
            acts[1][None] if pending is None else d_out_all,
            (q, k, v, lse, a1, joint_pair, x_own, o_all),
            bias_mask,
            host,
            arrays,
        )
        if pending is None:
            second_rows = given
        else:
            second_grads = given
            for name in ("out", "joint"):
                results[1][name] = reduced.pop(0)
        results[layer]["down"], results[layer]["up"] = reduced
        g_out = g_out.reshape(groups, D // groups, D // 2)
        if compact:
            g_joint = g_joint.reshape(groups // 2, 3 * D // groups, D // 2)
        else:
            spread = jnp.stack(
                [jnp.where(low == i, g_joint, jnp.zeros_like(g_joint)) for i in range(half)], axis=2
            )
            g_joint = spread.reshape(groups, 3 * D // groups, D // 2)
        sums.append((sums_one, sums_qv, sums_two, g_bup))
        if pending is None:
            pending = (g_out, g_joint)
        else:
            one, qv, two, bup = (jnp.stack([sums[1][i], sums[0][i]]) for i in range(4))
            lines_of = jnp.concatenate(
                [
                    one[:, 0:2],
                    vector_to(qv[:, 0:2].reshape(4, width)).reshape(2, 2, D),
                    two[:, 2:3],
                    two[:, 0:2],
                    two[:, 3:4],
                ],
                axis=1,
            )
            small = jnp.concatenate(
                [
                    jnp.transpose(
                        lines_of.reshape(2, 8, groups, D // groups), (2, 0, 1, 3)
                    ).reshape(groups, 2, -1),
                    jnp.swapaxes(bup.reshape(2, groups, FF // groups), 0, 1),
                ],
                axis=2,
            )
            lines = -(-small.shape[2] // 128)
            lines += -lines % 8
            small = jnp.pad(small, ((0, 0), (0, 0), (0, lines * 128 - small.shape[2])))
            arrays = (g_out, g_joint, small.reshape(groups, 2 * lines, 128))
            out_0, joint_0, small_both, first_grads = final_call(hosted(arrays), arrays, d_in, 4)
            results[0]["out"], results[0]["joint"] = out_0, joint_0
            results[0]["small"] = results[1]["small"] = small_both
        d_out_all = d_in

    pairs = [
        (results[0][name], results[1][name]) for name in ("up", "down", "out", "joint", "small")
    ]
    pairs += [(first_rows, second_rows), (first_grads, second_grads)]
    acts_rows, grad_rows, g_w_up, g_w_down, g_w_out, g_w_qkv, *pieces = assemble_call(
        count, groups, pairs
    )
    g_ln1g, g_ln1b, g_bq, g_bv, g_bo, g_ln2g, g_ln2b, g_bd, g_bup = pieces
    return (
        acts_rows[None, :, None],
        grad_rows[None, :, None],
        g_ln1g,
        g_ln1b,
        g_w_qkv.T[None],
        g_bq,
        g_bv,
        g_w_out.T[None],
        g_bo,
        g_ln2g,
        g_ln2b,
        g_w_up[None],
        g_bup,
        g_w_down.T[None],
        g_bd,
    )


def solution(mesh):
    rows = P(None, "dp", "seq", None)
    vector = P("section", None)
    matrix = P("section", None, None)
    placed = (
        rows,
        rows,
        P(None, "dp", None),
        vector,
        vector,
        matrix,
        vector,
        vector,
        matrix,
        vector,
        vector,
        vector,
        matrix,
        vector,
        matrix,
        vector,
    )
    both = P("section", None, "dp", "seq", None)
    line = P("section", ("dp", "seq"))
    table = P("section", None, ("dp", "seq"))
    return jax.shard_map(
        shards,
        mesh=mesh,
        in_specs=placed,
        out_specs=(
            both,
            both,
            line,
            line,
            table,
            line,
            line,
            table,
            line,
            line,
            line,
            table,
            line,
            table,
            line,
        ),
        check_vma=False,
    )
```

```python
import functools
import math

import jax
import jax.numpy as jnp
from jax import lax
from jax.experimental import pallas as pl
from jax.experimental.pallas import tpu as pltpu
from jax.sharding import PartitionSpec as P

D = 1024
H = 16
DH = 64
FF = 4096
VIEWS = 6
TRI = 512
VSLOT = 128
MICRO = 2
LEN = 1280
BQ = 256
NCH = 8
FC = FF // NCH
NCHF = 4
FCF = FF // NCHF
SCALE2 = DH ** (-0.5) * math.log2(math.e)
F32 = jnp.float32
BF16 = jnp.bfloat16
VMEM_LIMIT = 56 * 2**20


def params():
    return pltpu.CompilerParams(vmem_limit_bytes=VMEM_LIMIT)


def mm(a, b):
    return lax.dot_general(a, b, (((1,), (0,)), ((), ())), preferred_element_type=F32)


def mm_nt(a, b):
    return lax.dot_general(a, b, (((1,), (1,)), ((), ())), preferred_element_type=F32)


def mm_tn(a, b):
    return lax.dot_general(a, b, (((0,), (0,)), ((), ())), preferred_element_type=F32)


def norm_stats(values):
    average = jnp.mean(values, axis=-1, keepdims=True)
    centered = values - average
    variance = jnp.mean(centered * centered, axis=-1, keepdims=True)
    inverse = lax.rsqrt(variance + 1e-05)
    return centered * inverse, inverse


def head_lanes(shape, head):
    lane = lax.broadcasted_iota(jnp.int32, shape, 1)
    return (lane >= head * DH) & (lane < (head + 1) * DH)


def shards_of():
    return lax.axis_size("dp") * lax.axis_size("seq")


def split_halves(value, unit, core, mine, other, step):
    for at in range(0, value.shape[1] // unit, 2):
        even = value[:, at * unit : (at + 1) * unit]
        odd = value[:, (at + 1) * unit : (at + 2) * unit]
        cols = slice(at // 2 * unit, (at // 2 + 1) * unit)
        mine[step, :, cols] = jnp.where(core == 0, even, odd)
        other[step, :, cols] = jnp.where(core == 0, odd, even)


GELU_A = math.sqrt(2.0 / math.pi)
GELU_B = 0.044715


MESH_AXES = ("dp", "seq")


def axis_bits(dp_count, count):
    bits = []
    for axis, size in (("dp", dp_count), ("seq", count)):
        mask = size // 2
        while mask:
            bits.append((axis, mask))
            mask //= 2
    return bits


def stream_orders(dp_count, count):
    dp_bits = dp_count.bit_length() - 1
    seq_bits = count.bit_length() - 1
    dp_dims = list(range(dp_bits))
    seq_dims = list(range(dp_bits, dp_bits + seq_bits))[::-1]
    return (
        dp_dims[::-1] + seq_dims,
        dp_dims + seq_dims,
        seq_dims[:1] + dp_dims + seq_dims[1:],
        seq_dims[:1] + dp_dims[::-1] + seq_dims[1:],
    )


def my_bit(axis, mask):
    return lax.rem(lax.div(lax.axis_index(axis), mask), 2)


def partner(axis, mask):
    return lax.axis_index(axis) + mask * (1 - 2 * my_bit(axis, mask))


def greet(bits):
    barrier = pltpu.get_barrier_semaphore()
    for axis, mask in bits:
        pl.semaphore_signal(
            barrier,
            inc=1,
            device_id={axis: partner(axis, mask)},
            device_id_type=pl.DeviceIdType.MESH,
        )
    pl.semaphore_wait(barrier, len(bits))


class Reducer:
    def __init__(self, bits, order, src, cols, out, rows, compact, buffers, sems):
        self.bits, self.order, self.src, self.cols = bits, order, src, cols
        self.out, self.out_cols, self.buffers, self.sems = out, cols, buffers, sems
        self.count, self.rows, self.compact = len(bits), rows, compact

    @staticmethod
    def scratch(count, rows, width, dtype):
        shapes = [pltpu.VMEM((2,) * (count - 1) + (rows, width), dtype)]
        for stage in range(count):
            shapes.append(pltpu.VMEM((2,) * (count - 1 - stage) + (rows, width), dtype))
        shapes += [
            pltpu.SemaphoreType.DMA((count + 2,)),
            pltpu.SemaphoreType.DMA((count + 2,)),
            pltpu.SemaphoreType.DMA,
        ]
        return shapes

    def place(self, stage):
        left = [d for d in range(self.count) if d not in self.order[:stage]]
        dim = self.order[stage]
        return left, left.index(dim), self.bits[dim]

    def cut(self, stage, index):
        left, at, _ = self.place(stage)
        where = [slice(None)] * len(left)
        where[at] = index
        return tuple(where)

    def source(self, stage):
        if stage == 0:
            return self.src
        return self.buffers[0] if stage == 1 else self.buffers[stage]

    def copy(self, stage):
        axis, mask = self.place(stage)[2]
        where = self.cut(stage, 1 - my_bit(axis, mask))
        if stage == 0:
            where = where + (slice(None), pl.ds(*self.cols))
        return pltpu.make_async_remote_copy(
            src_ref=self.source(stage).at[where],
            dst_ref=self.buffers[stage + 1],
            send_sem=self.sems[0].at[stage],
            recv_sem=self.sems[1].at[stage],
            device_id={axis: partner(axis, mask)},
            device_id_type=pl.DeviceIdType.MESH,
        )

    def load(self):
        axis, mask = self.place(0)[2]
        where = self.cut(0, my_bit(axis, mask)) + (slice(None), pl.ds(*self.cols))
        return pltpu.make_async_copy(self.src.at[where], self.buffers[0], self.sems[2])

    def share(self):
        core = lax.axis_index("section")
        return pltpu.make_async_remote_copy(
            src_ref=self.out.at[core, :, pl.ds(*self.out_cols)],
            dst_ref=self.out.at[core, :, pl.ds(*self.out_cols)],
            send_sem=self.sems[0].at[self.count],
            recv_sem=self.sems[1].at[self.count],
            device_id={"section": 1 - core},
            device_id_type=pl.DeviceIdType.MESH,
        )

    def trade(self):
        third = self.rows // 3
        core = lax.axis_index("section")
        bit = lax.rem(lax.axis_index("seq"), 2)
        row = pl.multiple_of((1 - bit) * 2 * third, third)
        return pltpu.make_async_remote_copy(
            src_ref=self.out.at[core, pl.ds(row, third), pl.ds(*self.out_cols)],
            dst_ref=self.out.at[core, pl.ds(self.rows, third), pl.ds(*self.out_cols)],
            send_sem=self.sems[0].at[self.count + 1],
            recv_sem=self.sems[1].at[self.count + 1],
            device_id={"seq": partner("seq", 1)},
            device_id_type=pl.DeviceIdType.MESH,
        )

    def begin(self):
        self.copy(0).start()
        self.load().start()

    def step(self, stage):
        left, at, (axis, mask) = self.place(stage)
        bit = my_bit(axis, mask)
        if stage == 0:
            self.load().wait()
        self.copy(stage).wait_recv()
        got = self.buffers[stage + 1]
        rows = got.shape[-2]
        chunk = rows
        while chunk * got.shape[-1] > 65536 and chunk % 32 == 0:
            chunk //= 2
        per = rows // chunk
        last = stage == self.count - 1
        core = lax.axis_index("section")
        total = 2 ** (len(left) - 1)

        def body(i, carry):
            flat = lax.div(i, per)
            row = pl.multiple_of(lax.rem(i, per) * chunk, chunk)
            index = []
            for j in range(len(left) - 1):
                index.append(lax.rem(lax.div(flat, 2 ** (len(left) - 2 - j)), 2))
            there = tuple(index) + (pl.ds(row, chunk), slice(None))
            if stage == 0:
                mine = self.buffers[0][there]
            else:
                own = index[:at] + [bit] + index[at:]
                mine = self.source(stage)[tuple(own) + (pl.ds(row, chunk), slice(None))]
            value = mine.astype(F32) + got[there].astype(F32)
            if last:
                self.out[core, pl.ds(row, chunk), pl.ds(*self.out_cols)] = value
            elif stage == 0:
                self.buffers[0][there] = value.astype(got.dtype)
            else:
                got[there] = value.astype(got.dtype)
            return carry

        lax.fori_loop(0, total * per, body, 0)
        if not last:
            self.copy(stage + 1).start()
        elif self.compact:
            self.trade().start()
        else:
            self.share().start()

    def tail(self):
        if self.compact:
            self.trade().wait()
            self.share().start()

    def finish(self):
        for stage in range(self.count):
            self.copy(stage).wait_send()
        self.share().wait()


def part_widths(width):
    unit = 128 if width % 128 == 0 else width
    tiles = width // unit
    rest = tiles // 8
    first = -(-(tiles - rest) // 2)
    second = rest // 2
    return tuple(unit * n for n in (first, tiles - rest - first, rest - second, second))


STAGE_SHARES = (0.45, 0.7, 0.9, 1.0)


class Hosted:
    def __init__(self, dp_count, count, shapes, spans=None, shares=STAGE_SHARES, even=False):
        self.dp_count, self.count, self.shapes = dp_count, count, shapes
        self.spans = spans or ((0, 0.0, 1.0),) * len(shapes)
        self.all_bits = axis_bits(dp_count, count)
        self.plan = []
        for index, (rows, width, compact, _) in enumerate(shapes):
            bits = self.all_bits[:-1] if compact else self.all_bits
            orders = stream_orders(dp_count, count)
            widths = part_widths(width)
            if even and width % 256 == 0:
                widths = (width // 2, width // 2, 0, 0)
            if compact:
                last = len(bits)
                orders = [tuple(d for d in order if d != last) for order in orders[:2]]
                widths = (width // 2, width // 2)
            start = 0
            for order, size in zip(orders, widths):
                pieces = [size] if size else []
                if size >= 256 and not compact:
                    first = 128 * -(-size // 256)
                    pieces = [first, size - first]
                for k, piece in enumerate(pieces):
                    self.plan.append((index, tuple(order), bits, start, piece, rows, compact, k))
                    start += piece
        self.plan.sort(key=lambda p: (p[0], p[7]))
        self.arrays = len(shapes)
        self.events = []
        for k, part in enumerate(self.plan):
            phase, first, last = self.spans[part[0]]
            if phase == 0 and first > 0.0:
                self.events.append((first, k, -1))
            for stage in range(len(part[2])):
                share = shares[min(stage, 3)]
                self.events.append((first + (last - first) * share + 0.01 * stage, k, stage))
        self.events.sort()

    def views(self, arrays):
        return [self.view(i, array) for i, array in enumerate(arrays)]

    def view_shape(self, index):
        rows, width, compact, _ = self.shapes[index]
        depth = len(self.all_bits) - (1 if compact else 0)
        return (2,) * depth + (rows, width)

    def view(self, index, array):
        return array.reshape(self.view_shape(index))

    def in_specs(self):
        return [pl.BlockSpec(memory_space=pl.ANY)] * self.arrays

    def out_shapes(self):
        return [
            jax.ShapeDtypeStruct((2, rows + (rows // 3 if compact else 0), width), F32)
            for rows, width, compact, _ in self.shapes
        ]

    def out_specs(self):
        return [pl.BlockSpec(memory_space=pl.ANY)] * self.arrays

    def scratch(self):
        shapes = [pltpu.VMEM(o.shape, F32) for o in self.out_shapes()]
        shapes.append(pltpu.SemaphoreType.DMA((max(1, self.arrays),)))
        for index, _, bits, _, size, rows, _, _ in self.plan:
            shapes += Reducer.scratch(len(bits), rows, size, self.shapes[index][3])
        return shapes

    def bind(self, srcs, outs, scratch):
        self.parts = []
        self.outs, self.sums = outs, scratch[: self.arrays]
        self.out_sems = scratch[self.arrays]
        at = self.arrays + 1
        for index, order, bits, start, size, rows, compact, _ in self.plan:
            depth = len(bits) + 1
            mine = scratch[at : at + depth + 3]
            at += depth + 3
            self.parts.append(
                Reducer(
                    bits,
                    order,
                    srcs[index],
                    (start, size),
                    self.sums[index],
                    rows,
                    compact,
                    mine[:depth],
                    mine[depth:],
                )
            )

    def begin(self, phase=0):
        for part, plan in zip(self.parts, self.plan):
            span = self.spans[plan[0]]
            if span[0] == phase and (phase or span[1] == 0.0):
                part.begin()

    def run(self, first, last):
        for _, k, stage in self.events[first:last]:
            if stage < 0:
                self.parts[k].begin()
            else:
                self.parts[k].step(stage)

    def slots(self, times):
        edges = []
        done = 0
        for time in times:
            while done < len(self.events) and self.events[done][0] <= time:
                done += 1
            edges.append(done)
        edges[-1] = len(self.events)
        return list(zip([0] + edges[:-1], edges))

    def settle(self):
        for part in self.parts:
            part.tail()
        for part in self.parts:
            part.finish()

    def finish(self):
        self.settle()
        copies = []
        for i, (out, value) in enumerate(zip(self.outs, self.sums)):
            copies.append(pltpu.make_async_copy(value, out, self.out_sems.at[i]))
            copies[-1].start()
        for copy in copies:
            copy.wait()


BACK_LIMIT = 64 * 2**20 - 2**18


class Group:
    def __init__(self):
        self.half = lax.axis_size("seq") // 2
        self.core = lax.axis_index("section")
        self.place = lax.axis_index("seq")
        self.low = lax.rem(self.place, self.half)
        self.base = self.place - self.low
        self.rank = self.core * self.half + self.low

    def others(self):
        pairs = [(dc, d) for d in range(1, self.half) for dc in (0, 1)]
        return pairs + [(1, 0)]

    def slot(self, dc, d):
        return dc * self.half + d

    def where(self, dc, d):
        core = lax.rem(self.core + dc, 2)
        low = lax.rem(self.low + d, self.half)
        return core, low

    def device(self, dc, d):
        core, low = self.where(dc, d)
        return {"section": core, "seq": self.base + low}

    def rank_of(self, dc, d):
        core, low = self.where(dc, d)
        return core * self.half + low

    def greet(self, dp_count):
        barrier = pltpu.get_barrier_semaphore()
        targets = [self.device(dc, d) for dc, d in self.others()]
        mask = dp_count // 2
        while mask:
            targets.append({"dp": partner("dp", mask)})
            mask //= 2
        targets.append({"seq": partner("seq", self.half)})
        targets.append({"section": 1 - self.core, "seq": partner("seq", self.half)})
        for target in targets:
            pl.semaphore_signal(
                barrier, inc=1, device_id=target, device_id_type=pl.DeviceIdType.MESH
            )
        pl.semaphore_wait(barrier, len(targets))


def send(src, dst, sems, slot, device):
    return pltpu.make_async_remote_copy(
        src_ref=src,
        dst_ref=dst,
        send_sem=sems[0].at[slot],
        recv_sem=sems[1].at[slot],
        device_id=device,
        device_id_type=pl.DeviceIdType.MESH,
    )


def rows_of_rank(weights, rank, width, half):
    if half != 2:
        return weights[pl.ds(rank * width, width), :]
    base = rank // 2 * (2 * width) + rank % 2 * DH if isinstance(rank, int) else (
        lax.div(rank, 2) * (2 * width) + lax.rem(rank, 2) * DH
    )
    pieces = []
    for i in range(width // DH):
        at = base + 2 * i * DH
        at = at if isinstance(at, int) else pl.multiple_of(at, DH)
        pieces.append(weights[pl.ds(at, DH), :])
    return jnp.concatenate(pieces, axis=0)


class Deliver:
    def __init__(self, group, layer, src, out, sems):
        micro = lax.div(group.place, group.half)
        here, there = sems[0], sems[1]
        self.core, self.layer = group.core, layer
        self.local = pltpu.make_async_copy(src, out.at[micro], sems[2])
        self.chip = send(src, out.at[micro], (here, there), 0, {"section": 1 - group.core})
        self.far = send(
            src,
            out.at[micro],
            (here, there),
            1,
            {"section": layer, "seq": partner("seq", group.half)},
        )

    def start(self):
        first = self.local if self.layer == 0 else self.chip
        pl.when(self.core == 0)(lambda: first.start())
        pl.when(self.core == 1)(lambda: self.far.start())

    def wait(self):
        @pl.when(self.core == 0)
        def _():
            if self.layer == 0:
                self.local.wait()
                self.far.wait_recv()
            else:
                self.chip.wait_send()

        @pl.when(self.core == 1)
        def _():
            self.far.wait_send()
            if self.layer == 1:
                self.far.wait_recv()
                self.chip.wait_recv()


def deliver_sems():
    return dma_pair(2) + [pltpu.SemaphoreType.DMA]


def dma_pair(count):
    return [pltpu.SemaphoreType.DMA((count,)), pltpu.SemaphoreType.DMA((count,))]


VEC_ROWS = 16
LN1_GAIN, LN1_BIAS, B_QUERY, B_VALUE, B_OUT, LN2_GAIN, LN2_BIAS, B_DOWN, B_UP = range(9)


def attend_kernel(first, layer, dp_count, *refs):
    if first:
        x_ref, joint_ref, wout_ref, mask_ref = refs[:4]
        vectors = refs[4:13]
        o_out, lse_out, a_out, q_out, k_out, v_out = refs[13:19]
        x_out, joint_out, wout_out, vec_out = refs[19:23]
        rest = refs[23:]
    else:
        x_ref, joint_ref, mask_ref, vec_ref, cot_ref = refs[:5]
        o_out, lse_out, a_out, q_out, k_out, v_out, cot_out = refs[5:12]
        rest = refs[12:]
    x_all, a_all, q_all, k_all, v_all, lse, o_send, o_recv = rest[:8]
    x_sems, o_sems = rest[8:10], rest[10:12]
    out_sems = rest[12]
    if first:
        joint_pair, wide_own, wide_other, vec_send, vec_recv, vec_pair = rest[13:19]
        wide_sems, vec_sems = rest[19:21], rest[21:23]
        load_sems = rest[23]
    else:
        joint_one, cot_own, cot_other = rest[13:16]
        cot_sems = rest[16:18]
        load_sems = rest[18]
    group = Group()
    core, half, rank, low = group.core, group.half, group.rank, group.low
    ranks, rows, _ = x_all.shape
    width = q_all.shape[1]
    heads = width // DH
    span = half * width
    partner_core = group.device(1, 0)
    micro = lax.div(group.place, half)

    group.greet(dp_count)

    def x_copy(slot, from_rank, device):
        return send(x_all.at[from_rank], x_all.at[from_rank], x_sems, slot, device)

    far = {"seq": partner("seq", half)}

    if first:
        own_load = pltpu.make_async_copy(x_ref.at[micro, 0], x_all.at[rank], load_sems.at[0])
        far_copy = send(x_ref.at[1 - micro, 0], x_all.at[rank], x_sems, 2 * half - 1, far)
        pl.when(core == 1)(lambda: far_copy.start())
        pl.when(core == 0)(lambda: own_load.start())
        wide_copies = []
        own_loads = []
        for part in range(3):
            theirs = pl.ds(pl.multiple_of(part * D + (1 - core) * span, 128), span)
            ours = pl.ds(pl.multiple_of(part * D + core * span, 128), span)
            wide_copies.append(
                send(joint_ref.at[0, :, theirs], wide_other.at[part], wide_sems, part, partner_core)
            )
            own_loads.append(
                pltpu.make_async_copy(
                    joint_ref.at[0, :, ours], wide_own.at[part], load_sems.at[1 + part]
                )
            )
            wide_copies[-1].start()
            own_loads[-1].start()
        vec_send[...] = jnp.zeros_like(vec_send)
        for i, value in enumerate(vectors[:8]):
            vec_send[i : i + 1, :] = value[...].astype(F32)
        for i in range(FF // D):
            vec_send[8 + i : 9 + i, :] = vectors[8][:, i * D : (i + 1) * D].astype(F32)
        vec_copy = send(vec_send, vec_recv, vec_sems, 0, partner_core)
        vec_copy.start()
        wout_copy = send(wout_ref.at[0], wout_out, vec_sems, 1, partner_core)
        pl.when(core == 1)(lambda: far_copy.wait_recv())
        pl.when(core == 0)(lambda: own_load.wait())
    else:
        own_load = pltpu.make_async_copy(x_ref, x_all.at[rank], load_sems.at[0])
        joint_load = pltpu.make_async_copy(joint_ref.at[1], joint_one, load_sems.at[1])
        own_load.start()
        joint_load.start()
        cot_far = send(cot_ref.at[1 - micro, 0], cot_own, cot_sems, 0, far)
        cot_load = pltpu.make_async_copy(cot_ref.at[micro, 0], cot_own, load_sems.at[2])
        pl.when(core == 1)(lambda: cot_far.start())
        pl.when(core == 0)(lambda: cot_load.start())
        own_load.wait()
    for d in range(1, half):
        x_copy(d - 1, rank, group.device(0, d)).start()
    x_copy(half - 1, rank, partner_core).start()

    source = lax.broadcasted_iota(jnp.int32, (span, width), 0)
    target = lax.broadcasted_iota(jnp.int32, (span, width), 1)
    if half == 2:
        wanted = (2 * lax.div(target, DH) + low) * DH + lax.rem(target, DH)
    else:
        wanted = low * width + target
    pick = (source == wanted).astype(F32).astype(BF16)
    if first:
        wout_copy.start()
        vec_copy.wait_recv()
        vec_pair[core] = vec_send[...]
        vec_pair[1 - core] = vec_recv[...]
        for load in own_loads:
            load.wait()
        for part in range(3):
            joint_pair[core, :, part * width : (part + 1) * width] = mm(
                wide_own[part], pick
            ).astype(BF16)
        for copy in wide_copies:
            copy.wait_recv()
        for part in range(3):
            joint_pair[1 - core, :, part * width : (part + 1) * width] = mm(
                wide_other[part], pick
            ).astype(BF16)
        vec = vec_pair[0]
        weights = lambda: joint_pair[0]
    else:
        joint_load.wait()
        vec = vec_ref[1]
        weights = lambda: joint_one[...]

    def of_heads(row):
        parts = vec[row : row + 1, :]
        mine = jnp.where(core == 0, parts[:, :span], parts[:, span:])
        wide = jnp.broadcast_to(mine, (16, span)).astype(BF16)
        return mm(wide, pick)[0:1, :]

    bias_q = of_heads(B_QUERY)
    bias_v = of_heads(B_VALUE)
    gain = vec[LN1_GAIN : LN1_GAIN + 1, :]
    shift = vec[LN1_BIAS : LN1_BIAS + 1, :]

    def project(at):
        normal, _ = norm_stats(x_all[at].astype(F32))
        a = (normal * gain + shift).astype(BF16)
        here = pl.ds(pl.multiple_of(at * rows, 16), rows)
        a_all[here, :] = a
        joined = mm(a, weights())
        q_all[here, :] = (joined[:, :width] + bias_q).astype(BF16)
        k_all[here, :] = joined[:, width : 2 * width].astype(BF16)
        v_all[here, :] = (joined[:, 2 * width :] + bias_v).astype(BF16)

    project(rank)
    x_copy(half - 1, rank, partner_core).wait_recv()
    project(group.rank_of(1, 0))
    for d in range(1, half):
        here = group.rank_of(0, half - d)
        x_copy(d - 1, here, partner_core).wait_recv()
        x_copy(half - 1 + d, here, partner_core).start()
        project(here)
    for d in range(1, half):
        there = group.rank_of(1, half - d)
        x_copy(half - 1 + d, there, partner_core).wait_recv()
        project(there)

    saves = [
        pltpu.make_async_copy(a_all, a_out, out_sems.at[0]),
        pltpu.make_async_copy(q_all, q_out, out_sems.at[1]),
        pltpu.make_async_copy(k_all, k_out, out_sems.at[2]),
        pltpu.make_async_copy(v_all, v_out, out_sems.at[3]),
    ]
    if first:
        saves.append(pltpu.make_async_copy(joint_pair, joint_out, out_sems.at[4]))
        saves.append(pltpu.make_async_copy(x_all.at[rank], x_out, out_sems.at[5]))
        saves.append(pltpu.make_async_copy(vec_pair, vec_out, out_sems.at[6]))
    for save in saves:
        save.start()
    lane = lax.broadcasted_iota(jnp.int32, (rows, 128), 1)
    mask = mask_ref[...]

    def attend(at):
        here = pl.ds(pl.multiple_of(at * rows, 16), rows)
        q = q_all[here, :]
        mixed = jnp.zeros((rows, width), F32)
        totals = jnp.zeros((rows, 128), F32)
        for head in range(heads):
            mine = head_lanes((rows, width), head)
            scores = mm_nt(jnp.where(mine, q, jnp.zeros_like(q)), k_all[...]) * SCALE2 + mask
            top = jnp.max(scores, axis=-1, keepdims=True)
            expo = jnp.exp2(scores - top)
            total = jnp.sum(expo, axis=-1, keepdims=True)
            part = mm(expo.astype(BF16), v_all[...]) / total
            mixed = jnp.where(mine, part, mixed)
            totals = jnp.where(lane == head, top + jnp.log2(total), totals)
        lse[here, :] = totals
        return mixed.astype(BF16)

    copies = []
    for dc, d in group.others():
        slot = group.slot(dc, d)
        o_send[slot] = attend(group.rank_of(dc, d))
        copies.append(send(o_send.at[slot], o_recv.at[rank], o_sems, slot, group.device(dc, d)))
        copies[-1].start()
    if not first:
        pl.when(core == 1)(lambda: cot_far.wait())
        pl.when(core == 0)(lambda: cot_load.wait())
        cot_share = send(cot_own, cot_other, cot_sems, 1, partner_core)
        cot_share.start()
    o_recv[rank] = attend(rank)
    if not first:
        cot_share.wait()
        cot_out[0] = cot_own[...]
        cot_out[1] = cot_other[...]
    lse_out[...] = lse[...]
    for copy in copies:
        copy.wait()
    o_out[...] = o_recv[...]
    for save in saves:
        save.wait()
    for d in range(1, half):
        x_copy(d - 1, rank, group.device(0, d)).wait_send()
        x_copy(half - 1 + d, group.rank_of(0, half - d), partner_core).wait_send()
    x_copy(half - 1, rank, partner_core).wait_send()
    if first:
        pl.when(core == 1)(lambda: far_copy.wait_send())
        for copy in wide_copies:
            copy.wait_send()
        vec_copy.wait_send()
        wout_copy.wait()


def attend_call(first, layer, mask, ranks, dp_count, *args):
    rows = args[0].shape[-2]
    width = D // ranks
    half = ranks // 2
    span = half * width
    anywhere = pl.BlockSpec(memory_space=pl.ANY)
    vmem = pl.BlockSpec(memory_space=pltpu.VMEM)
    out_shape = [
        jax.ShapeDtypeStruct((ranks, rows, width), BF16),
        jax.ShapeDtypeStruct((LEN, 128), F32),
        jax.ShapeDtypeStruct((LEN, D), BF16),
        jax.ShapeDtypeStruct((LEN, width), BF16),
        jax.ShapeDtypeStruct((LEN, width), BF16),
        jax.ShapeDtypeStruct((LEN, width), BF16),
    ]
    out_specs = [vmem, vmem] + [anywhere] * 4
    scratch = [
        pltpu.VMEM((ranks, rows, D), BF16),
        pltpu.VMEM((LEN, D), BF16),
        pltpu.VMEM((LEN, width), BF16),
        pltpu.VMEM((LEN, width), BF16),
        pltpu.VMEM((LEN, width), BF16),
        pltpu.VMEM((LEN, 128), F32),
        pltpu.VMEM((ranks, rows, width), BF16),
        pltpu.VMEM((ranks, rows, width), BF16),
    ]
    scratch += dma_pair(2 * half) + dma_pair(ranks) + [pltpu.SemaphoreType.DMA((7,))]
    if first:
        operands = args[:3] + (mask,) + args[3:]
        in_specs = [anywhere] * 3 + [vmem] * (1 + len(args[3:]))
        out_shape += [
            jax.ShapeDtypeStruct((rows, D), BF16),
            jax.ShapeDtypeStruct((2, D, 3 * width), BF16),
            jax.ShapeDtypeStruct((D, D), BF16),
            jax.ShapeDtypeStruct((2, VEC_ROWS, D), F32),
        ]
        out_specs += [anywhere] * 4
        scratch += [
            pltpu.VMEM((2, D, 3 * width), BF16),
            pltpu.VMEM((3, D, span), BF16),
            pltpu.VMEM((3, D, span), BF16),
            pltpu.VMEM((VEC_ROWS, D), F32),
            pltpu.VMEM((VEC_ROWS, D), F32),
            pltpu.VMEM((2, VEC_ROWS, D), F32),
        ]
        scratch += dma_pair(3) + dma_pair(2) + [pltpu.SemaphoreType.DMA((4,))]
    else:
        operands = args[:2] + (mask,) + args[2:]
        in_specs = [anywhere] * 2 + [vmem] * 2 + [anywhere]
        out_shape += [jax.ShapeDtypeStruct((2, rows, D), BF16)]
        out_specs += [vmem]
        scratch += [
            pltpu.VMEM((D, 3 * width), BF16),
            pltpu.VMEM((rows, D), BF16),
            pltpu.VMEM((rows, D), BF16),
        ]
        scratch += dma_pair(2) + [pltpu.SemaphoreType.DMA((3,))]
    return pl.pallas_call(
        functools.partial(attend_kernel, first, layer, dp_count),
        in_specs=in_specs,
        out_specs=out_specs,
        out_shape=out_shape,
        scratch_shapes=scratch,
        compiler_params=pltpu.CompilerParams(
            vmem_limit_bytes=VMEM_LIMIT, collective_id=5 + layer, has_side_effects=True
        ),
        cost_estimate=pl.CostEstimate(
            flops=40 * 10**9, bytes_accessed=20 * 2**20, transcendentals=LEN * LEN * width // DH
        ),
    )(*operands)


def mlp_kernel(
    layer,
    dp_count,
    o_ref,
    x_ref,
    wo0_ref,
    wo1_ref,
    vec_ref,
    up0_ref,
    up1_ref,
    down0_ref,
    down1_ref,
    h_ref,
    u_ref,
    y_ref,
    a_all,
    o_all,
    g_all,
    rows_out,
    acc,
    wo,
    a_mine,
    a_other,
    o_send,
    o_other,
    g_mine,
    g_send,
    g_other,
    send_sems,
    recv_sems,
    save_sems,
    wo_sem,
    rows_mine,
    *rows_sems,
):
    step = pl.program_id(0)
    groups, rows, width = o_ref.shape
    half = groups // 2
    unit = FF // shards_of() // 2
    core = lax.axis_index("section")
    own = core == layer
    device = {"section": 1 - core}
    sems = (send_sems, recv_sems)
    if layer == 1:
        rows_copy = Deliver(Group(), 0, rows_mine, rows_out, rows_sems)
    a_copy = send(a_mine, a_other, sems, NCHF, device)
    o_copy = send(o_send, o_other, sems, NCHF + 1, device)

    def g_copy(at):
        return send(g_send.at[at], g_other.at[at], sems, at, device)

    def g_save(which, at):
        cols = pl.ds(pl.multiple_of(at * (FCF // 2), FCF // 2), FCF // 2)
        source = g_other if which else g_mine
        return pltpu.make_async_copy(
            source.at[at], g_all.at[which, :, cols], save_sems.at[which, at]
        )

    @pl.when(step == 0)
    def _():
        Group().greet(dp_count)
        if layer == 1:
            rows_mine[...] = x_ref[...]
            rows_copy.start()
        first = pltpu.make_async_copy(wo0_ref, wo, wo_sem)
        second = pltpu.make_async_copy(wo1_ref, wo, wo_sem)
        pl.when(own)(lambda: first.start())
        pl.when(jnp.logical_not(own))(lambda: second.start())
        for i in range(half):
            o_send[i] = o_ref[(1 - core) * half + i]
            o_all[0, :, i * width : (i + 1) * width] = o_ref[core * half + i]
        o_copy.start()
        first.wait()
        hidden = x_ref[...].astype(F32) + vec_ref[0, B_OUT : B_OUT + 1, :]
        for group in range(groups):
            hidden += mm(o_ref[group], rows_of_rank(wo, group, width, half))
        h_ref[...] = hidden
        normal, _ = norm_stats(hidden)
        a_mine[...] = (
            normal * vec_ref[0, LN2_GAIN : LN2_GAIN + 1, :] + vec_ref[0, LN2_BIAS : LN2_BIAS + 1, :]
        ).astype(BF16)
        a_copy.start()
        acc[...] = hidden + vec_ref[0, B_DOWN : B_DOWN + 1, :]

    def part(up_ref, down_ref):
        at = pl.multiple_of(lax.rem(step, D // FCF) * FCF, FCF)
        bias = vec_ref[0, pl.ds(B_UP + lax.div(step, D // FCF), 1), pl.ds(at, FCF)]
        upper = mm(a_mine[...], up_ref[...]) + bias
        u_ref[...] = upper
        inner = GELU_A * (upper + GELU_B * upper * upper * upper)
        gated = (0.5 * upper * (1.0 + jnp.tanh(inner))).astype(BF16)
        split_halves(gated, unit, core, g_mine, g_send, step)
        acc[...] += mm(gated, down_ref[...])

    @pl.when(step < NCHF)
    def _():
        pl.when(own)(lambda: part(up0_ref, down0_ref))
        pl.when(jnp.logical_not(own))(lambda: part(up1_ref, down1_ref))
        g_copy(step).start()
        g_save(0, step).start()

    @pl.when(step > 0)
    def _():
        g_copy(step - 1).wait()
        g_save(1, step - 1).start()

    @pl.when(step == NCHF)
    def _():
        y_ref[...] = acc[...].astype(BF16)
        a_copy.wait()
        a_all[0] = a_mine[...]
        a_all[1] = a_other[...]
        o_copy.wait()
        for i in range(half):
            o_all[1, :, i * width : (i + 1) * width] = o_other[i]

        def drain(at, carry):
            g_save(0, at).wait()
            g_save(1, at).wait()
            return carry

        lax.fori_loop(0, NCHF, drain, 0)
        if layer == 1:
            rows_copy.wait()


def mlp_call(layer, dp_count, o_all, x_own, outs, vec, ups, downs):
    rows = x_own.shape[0]
    groups, _, width = o_all.shape
    whole = lambda i: (0, 0)
    now = lambda i: jnp.minimum(i, NCHF - 1)
    mine = lambda i, first: jnp.where((lax.axis_index("section") == layer) == first, now(i), 0)
    col = lambda first: (lambda i: (0, mine(i, first)))
    line = lambda first: (lambda i: (mine(i, first), 0))
    chunk = lambda i: (0, now(i))
    piece = pltpu.VMEM((NCHF, rows, FCF // 2), BF16)
    return pl.pallas_call(
        functools.partial(mlp_kernel, layer, dp_count),
        grid=(NCHF + 1,),
        in_specs=[
            pl.BlockSpec((groups, rows, width), lambda i: (0, 0, 0)),
            pl.BlockSpec((rows, D), whole),
            pl.BlockSpec(memory_space=pl.ANY),
            pl.BlockSpec(memory_space=pl.ANY),
            pl.BlockSpec((1, VEC_ROWS, D), lambda i: (layer, 0, 0)),
            pl.BlockSpec((D, FCF), col(True)),
            pl.BlockSpec((D, FCF), col(False)),
            pl.BlockSpec((FCF, D), line(True)),
            pl.BlockSpec((FCF, D), line(False)),
        ],
        out_specs=[
            pl.BlockSpec((rows, D), whole),
            pl.BlockSpec((rows, FCF), chunk),
            pl.BlockSpec((rows, D), whole),
            pl.BlockSpec((2, rows, D), lambda i: (0, 0, 0)),
            pl.BlockSpec((2, rows, D // 2), lambda i: (0, 0, 0)),
            pl.BlockSpec(memory_space=pl.ANY),
            pl.BlockSpec(memory_space=pl.ANY),
        ],
        scratch_shapes=[
            pltpu.VMEM((rows, D), F32),
            pltpu.VMEM((D, D), BF16),
            pltpu.VMEM((rows, D), BF16),
            pltpu.VMEM((rows, D), BF16),
            pltpu.VMEM((groups // 2, rows, width), BF16),
            pltpu.VMEM((groups // 2, rows, width), BF16),
            piece,
            piece,
            piece,
        ]
        + dma_pair(NCHF + 2)
        + [pltpu.SemaphoreType.DMA((2, NCHF)), pltpu.SemaphoreType.DMA]
        + [pltpu.VMEM((rows, D), BF16)]
        + deliver_sems(),
        out_shape=[
            jax.ShapeDtypeStruct((rows, D), F32),
            jax.ShapeDtypeStruct((rows, FF), F32),
            jax.ShapeDtypeStruct((rows, D), BF16),
            jax.ShapeDtypeStruct((2, rows, D), BF16),
            jax.ShapeDtypeStruct((2, rows, D // 2), BF16),
            jax.ShapeDtypeStruct((2, rows, FF // 2), BF16),
            jax.ShapeDtypeStruct((2, rows, D), BF16),
        ],
        compiler_params=pltpu.CompilerParams(
            vmem_limit_bytes=VMEM_LIMIT, collective_id=7 + layer, has_side_effects=True
        ),
        cost_estimate=pl.CostEstimate(
            flops=2 * rows * D * (D + 2 * FF), bytes_accessed=30 * 2**20, transcendentals=rows * FF
        ),
    )(o_all, x_own, outs[0], outs[1], vec, ups[0], ups[1], downs[0], downs[1])


def back_kernel(layer, host, ranges, *refs):
    n = host.arrays - 1
    refs = list(refs)

    def pop(count):
        taken = refs[:count]
        del refs[:count]
        return taken

    u_ref, mask_ref, vec_ref = pop(3)
    dy_src, h_src, a2_src, wo0_src, wo1_src, up0_src, up1_src, down0_src, down1_src = pop(9)
    rows_src = pop(1)[0]
    late = pop(8)
    srcs = pop(n)
    gbup_ref, sums_two_ref, sums_one_ref, sums_qv_ref = pop(4)
    gup_out, dx_out, gjoint_out, gout_out, rows_out = pop(5)
    outs = pop(n + 1)
    dy, h, a2, wo, ups, downs = pop(6)
    load_sems, weight_sems = pop(2)
    acc, du_mine, du_send, du_recv, gup, branch, dh, do_send, do_recv = pop(9)
    du_sems, do_sems = pop(2), pop(2)
    gup_sems, save_sems = pop(2)
    q_all, k_all, v_all, lse, a1, w_joint, x_own, mixed = pop(8)
    late_sems = pop(1)[0]
    dk_acc, dv_acc, dj, core_recv, far_send, far_recv = pop(6)
    core_send = a2 if lax.axis_size("seq") == 4 else pop(1)[0]
    g_own, g_send, g_recv, gout, dx_recv = pop(5)
    dx_own = dy
    core_sems, far_sems, pair_sems = pop(2), pop(2), pop(2)
    rows_sems = pop(3)
    host.bind(list(srcs) + [gup_out], outs, refs)
    group = Group()
    core, half, rank = group.core, group.half, group.rank
    step = pl.program_id(0)
    ranks, rows, width = do_send.shape
    length = q_all.shape[0]
    heads = width // DH
    scale = DH ** (-0.5)
    unit = FF // shards_of() // 2
    own = core == layer
    partner_core = group.device(1, 0)
    ranges = list(ranges)
    lead, middle = ranges[: 2 * NCH], ranges[2 * NCH : 2 * NCH + 3]
    blocks = length // BQ * heads
    inner = ranges[2 * NCH + 3 : 2 * NCH + 3 + blocks]
    tail = ranges[2 * NCH + 3 + blocks :]

    def weight_copies(at, second):
        slot = lax.rem(at, 2)
        cols = pl.ds(pl.multiple_of(at * FC, FC), FC)
        up, down = (up1_src, down1_src) if second else (up0_src, down0_src)
        return (
            pltpu.make_async_copy(up.at[:, cols], ups.at[slot], weight_sems.at[0, slot]),
            pltpu.make_async_copy(down.at[cols, :], downs.at[slot], weight_sems.at[1, slot]),
        )

    def fetch(at):
        @pl.when(own)
        def _():
            for copy in weight_copies(at, False):
                copy.start()

        @pl.when(jnp.logical_not(own))
        def _():
            for copy in weight_copies(at, True):
                copy.start()

    rows_copy = Deliver(group, 1, rows_src.at[0], rows_out, rows_sems)
    dy_load = pltpu.make_async_copy(dy_src.at[0], dy, load_sems.at[0])
    h_load = pltpu.make_async_copy(h_src, h, load_sems.at[1])
    a2_load = pltpu.make_async_copy(a2_src, a2, load_sems.at[2])
    wo_load = pltpu.make_async_copy(wo0_src, wo, load_sems.at[3])
    wo_load_other = pltpu.make_async_copy(wo1_src, wo, load_sems.at[3])
    late_loads = [
        pltpu.make_async_copy(source.at[layer] if i == 5 else source, target, late_sems.at[i])
        for i, (source, target) in enumerate(
            zip(late, (q_all, k_all, v_all, lse, a1, w_joint, x_own, mixed))
        )
    ]

    def du_copy(at):
        return send(du_send.at[at], du_recv.at[at], du_sems, at, partner_core)

    def gup_save(at):
        per = gup.shape[1]
        lead_bits = NCH.bit_length() - 1
        index = tuple(
            lax.rem(lax.div(at, 2 ** (lead_bits - 1 - j)), 2) for j in range(lead_bits)
        )
        return pltpu.make_async_copy(
            gup.at[lax.rem(at, 2)].reshape(gup_out.shape[lead_bits:]),
            gup_out.at[index],
            gup_sems.at[lax.rem(at, 2)],
        )

    @pl.when(step == 0)
    def _():
        group.greet(host.dp_count)
        rows_copy.start()
        dy_load.start()
        fetch(0)
        host.begin()
        a2_load.start()
        h_load.start()
        pl.when(own)(lambda: wo_load.start())
        pl.when(jnp.logical_not(own))(lambda: wo_load_other.start())
        for load in late_loads:
            load.start()
        acc[...] = jnp.zeros_like(acc)
        dy_load.wait()
        a2_load.wait()

    @pl.when(step < NCH - 1)
    def _():
        fetch(step + 1)

    @pl.when(step < NCH)
    def _():
        slot = lax.rem(step, 2)
        for copy in weight_copies(step, False):
            copy.wait()
        d_gated = mm_nt(dy[...], downs[slot])
        upper = u_ref[...]
        square = upper * upper
        turn = jnp.tanh(GELU_A * upper * (1.0 + GELU_B * square))
        slope = 0.5 * (1.0 + turn) + (0.5 * GELU_A) * upper * (1.0 - turn * turn) * (
            1.0 + (3.0 * GELU_B) * square
        )
        d_upper = (d_gated * slope).astype(BF16)
        split_halves(d_upper, unit, core, du_mine, du_send, step)
        du_copy(step).start()
        gbup_ref[...] = jnp.sum(d_upper.astype(F32), axis=0, keepdims=True)
        acc[...] += mm_nt(d_upper, ups[slot])

    for at, (first, last) in enumerate(lead):
        if last > first and at % 2 == 0:
            pl.when(step == at // 2)(functools.partial(host.run, first, last))

    @pl.when(step > 0)
    def _():
        at = step - 1
        du_copy(at).wait()
        pl.when(at >= 2)(lambda: gup_save(at - 2).wait())
        value = mm_tn(du_mine[at], a2[0]) + mm_tn(du_recv[at], a2[1])
        gup[lax.rem(at, 2)] = value.astype(BF16).reshape(gup.shape[1:])
        gup_save(at).start()

    for at, (first, last) in enumerate(lead):
        if last > first and at % 2 == 1:
            pl.when(step == at // 2)(functools.partial(host.run, first, last))

    @pl.when(step == NCH)
    def _():
        h_load.wait()
        gup_save(NCH - 2).wait()
        gup_save(NCH - 1).wait()
        host.begin(1)
        normal, inverse = norm_stats(h[...])
        d_out = dy[...].astype(F32)
        d_normed = acc[...]
        sums_two_ref[...] = jnp.zeros_like(sums_two_ref)
        sums_two_ref[0:1, :] = jnp.sum(d_normed * normal, axis=0, keepdims=True)
        sums_two_ref[1:2, :] = jnp.sum(d_normed, axis=0, keepdims=True)
        d_normal = d_normed * vec_ref[0, LN2_GAIN : LN2_GAIN + 1, :]
        d_hidden = d_out + inverse * (
            d_normal
            - jnp.mean(d_normal, axis=-1, keepdims=True)
            - normal * jnp.mean(d_normal * normal, axis=-1, keepdims=True)
        )
        dh[...] = d_hidden
        d_branch = d_hidden.astype(BF16)
        branch[0] = d_branch
        branch_copy = send(branch.at[0], branch.at[1], do_sems, ranks, partner_core)
        branch_copy.start()
        wo_load.wait()

        def heads_of(to_rank):
            return mm_nt(d_branch, rows_of_rank(wo, to_rank, width, half)).astype(BF16)

        copies = []
        for dc, d in group.others():
            slot = group.slot(dc, d)
            do_send[slot] = heads_of(group.rank_of(dc, d))
            copies.append(
                send(do_send.at[slot], do_recv.at[pl.ds(pl.multiple_of(rank * rows, 16), rows)], do_sems, slot, group.device(dc, d))
            )
            copies[-1].start()
        do_recv[pl.ds(pl.multiple_of(rank * rows, 16), rows), :] = heads_of(rank)
        host.run(*middle[0])
        sums_two_ref[2:3, :] = jnp.sum(d_branch.astype(F32), axis=0, keepdims=True)
        sums_two_ref[3:4, :] = jnp.sum(d_out, axis=0, keepdims=True)
        dk_acc[...] = jnp.zeros_like(dk_acc)
        dv_acc[...] = jnp.zeros_like(dv_acc)
        sums_qv_ref[...] = jnp.zeros_like(sums_qv_ref)
        sums_one_ref[...] = jnp.zeros_like(sums_one_ref)
        for load in late_loads:
            load.wait()
        branch_copy.wait()
        gout[...] = (mm_tn(branch[0], mixed[0]) + mm_tn(branch[1], mixed[1])).astype(BF16)
        gout_save = pltpu.make_async_copy(gout, gout_out, save_sems.at[0])
        gout_save.start()
        host.run(*middle[1])
        for copy in copies:
            copy.wait()
        host.run(*middle[2])

        def block(at, carry):
            here = pl.ds(pl.multiple_of(at * BQ, BQ), BQ)
            q = q_all[here, :]
            grad = do_recv[here, :]
            totals = lse[here, :]
            d_q = jnp.zeros((BQ, width), F32)
            for head in range(heads):
                mine = head_lanes((BQ, width), head)
                q_head = jnp.where(mine, q, jnp.zeros_like(q))
                grad_head = jnp.where(mine, grad, jnp.zeros_like(grad))
                scores = mm_nt(q_head, k_all[...]) * SCALE2 + mask_ref[...]
                probs = jnp.exp2(scores - totals[:, head : head + 1])
                d_probs = mm_nt(grad_head, v_all[...])
                term = jnp.sum(probs * d_probs, axis=-1, keepdims=True)
                d_scores = (probs * (d_probs - term)).astype(BF16)
                dv_acc[...] += mm_tn(probs.astype(BF16), grad_head)
                dk_acc[...] += mm_tn(d_scores, q_head)
                d_q = jnp.where(mine, mm(d_scores, k_all[...]), d_q)
                for slot, (first, last) in enumerate(inner):
                    if last > first and slot % heads == head:
                        pl.when(at == slot // heads)(functools.partial(host.run, first, last))
            low = (d_q * scale).astype(BF16)
            dj[here, :width] = low
            sums_qv_ref[0:1, :] += jnp.sum(low.astype(F32), axis=0, keepdims=True)
            return carry

        lax.fori_loop(0, length // BQ, block, 0)
        dj[:, width : 2 * width] = (dk_acc[...] * scale).astype(BF16)
        low_v = dv_acc[...].astype(BF16)
        dj[:, 2 * width :] = low_v
        sums_qv_ref[1:2, :] = jnp.sum(low_v.astype(F32), axis=0, keepdims=True)

        def partial_rows(to_rank):
            here = pl.ds(pl.multiple_of(to_rank * rows, 16), rows)
            return mm_nt(dj[here, :], w_joint[...])

        def core_copy(d):
            return send(core_send.at[d], core_recv.at[d], core_sems, d, partner_core)

        def far_copy(d):
            return send(far_send.at[d - 1], far_recv.at[d - 1], far_sems, d - 1, group.device(0, d))

        for d in [d for d in range(1, half)] + [0]:
            core_send[d] = partial_rows(group.rank_of(1, d)).astype(BF16)
            core_copy(d).start()
        for d in range(1, half):
            value = partial_rows(group.rank_of(0, d))
            core_copy(d).wait_recv()
            far_send[d - 1] = (value + core_recv[d].astype(F32)).astype(BF16)
            far_copy(d).start()
        host.run(*tail[0])
        value = partial_rows(rank)
        core_copy(0).wait_recv()
        acc[...] = value + core_recv[0].astype(F32)

        half_cols = D // 2
        mine_cols = pl.ds(pl.multiple_of(core * half_cols, half_cols), half_cols)
        other_cols = pl.ds(pl.multiple_of((1 - core) * half_cols, half_cols), half_cols)
        g_send[...] = mm_tn(dj[...], a1[:, other_cols]).astype(BF16).reshape(g_send.shape)
        g_copy = send(g_send, g_recv, pair_sems, 0, partner_core)
        g_copy.start()
        host.run(*tail[1])
        g_own[...] = mm_tn(dj[...], a1[:, mine_cols]).astype(BF16).reshape(g_own.shape)
        g_save = pltpu.make_async_copy(g_own, gjoint_out.at[:, core], save_sems.at[1])
        g_save.start()
        host.run(*tail[2])

        for d in range(1, half):
            far_copy(d).wait_recv()
            acc[...] += far_recv[d - 1].astype(F32)
        d_normed = acc[...]
        normal, inverse = norm_stats(x_own[...].astype(F32))
        sums_one_ref[0:1, :] = jnp.sum(d_normed * normal, axis=0, keepdims=True)
        sums_one_ref[1:2, :] = jnp.sum(d_normed, axis=0, keepdims=True)
        d_normal = d_normed * vec_ref[0, LN1_GAIN : LN1_GAIN + 1, :]
        d_in = (
            dh[...]
            + inverse
            * (
                d_normal
                - jnp.mean(d_normal, axis=-1, keepdims=True)
                - normal * jnp.mean(d_normal * normal, axis=-1, keepdims=True)
            )
        ).astype(BF16)
        dx_own[...] = d_in
        dx_copy = send(dx_own, dx_recv, pair_sems, 1, partner_core)
        dx_copy.start()
        dx_save = pltpu.make_async_copy(dx_own, dx_out.at[0], save_sems.at[2])
        dx_save.start()
        host.run(*tail[3])
        g_copy.wait()
        g_save_other = pltpu.make_async_copy(g_recv, gjoint_out.at[:, 1 - core], save_sems.at[3])
        g_save_other.start()
        dx_copy.wait()
        dx_save_other = pltpu.make_async_copy(dx_recv, dx_out.at[1], save_sems.at[4])
        dx_save_other.start()
        for d in range(half):
            core_copy(d).wait_send()
        for d in range(1, half):
            far_copy(d).wait_send()
        for save in (gout_save, g_save, dx_save, g_save_other, dx_save_other):
            save.wait()
        rows_copy.wait()
        host.finish()


def back_call(layer, dy, hidden, wos, vec, upper, a2, ups, downs, given, late, mask, host, arrays):
    rows = dy.shape[1]
    ranks = host.count
    width = D // ranks
    half = ranks // 2
    shards = host.dp_count * ranks
    per = shards // NCH
    unit = FF // shards // 2
    heads = width // DH
    now = lambda i: (0, jnp.minimum(i, NCH - 1))
    whole = lambda i: (0, 0)
    anywhere = pl.BlockSpec(memory_space=pl.ANY)
    times = []
    for i in range(NCH):
        times += [2.9 * i + 1.6, 2.9 * i + 2.9]
    times += [29.0, 33.0, 36.0]
    for i in range(LEN // BQ * heads):
        times.append(36.0 + 28.0 / (LEN // BQ * heads) * (i + 1))
    times += [69.0, 73.0, 76.0, 84.0]
    ranges = host.slots(times)
    piece = pltpu.VMEM((NCH, rows, FC // 2), BF16)
    tokens = pltpu.VMEM((LEN, width), BF16)
    own = pltpu.VMEM((rows, D), BF16)
    view = host.view_shape(host.arrays - 1)
    return pl.pallas_call(
        functools.partial(back_kernel, layer, host, ranges),
        grid=(NCH + 1,),
        in_specs=[
            pl.BlockSpec((rows, FC), now),
            pl.BlockSpec((1, LEN), whole),
            pl.BlockSpec((1, VEC_ROWS, D), lambda i: (layer, 0, 0)),
        ]
        + [anywhere] * (10 + len(late) + len(arrays)),
        out_specs=[
            pl.BlockSpec((1, FC), now),
            pl.BlockSpec((8, D), whole),
            pl.BlockSpec((8, D), whole),
            pl.BlockSpec((8, width), whole),
        ]
        + [anywhere] * 5
        + host.out_specs(),
        out_shape=[
            jax.ShapeDtypeStruct((1, FF), F32),
            jax.ShapeDtypeStruct((8, D), F32),
            jax.ShapeDtypeStruct((8, D), F32),
            jax.ShapeDtypeStruct((8, width), F32),
            jax.ShapeDtypeStruct(view, BF16),
            jax.ShapeDtypeStruct((2, rows, D), BF16),
            jax.ShapeDtypeStruct((3, 2, width, D // 2), BF16),
            jax.ShapeDtypeStruct((D, D // 2), BF16),
            jax.ShapeDtypeStruct((2, rows, D), BF16),
        ]
        + host.out_shapes(),
        scratch_shapes=[
            own,
            pltpu.VMEM((rows, D), F32),
            pltpu.VMEM((2, rows, D), BF16),
            pltpu.VMEM((D, D), BF16),
            pltpu.VMEM((2, D, FC), BF16),
            pltpu.VMEM((2, FC, D), BF16),
            pltpu.SemaphoreType.DMA((4,)),
            pltpu.SemaphoreType.DMA((2, 2)),
            pltpu.VMEM((rows, D), F32),
            piece,
            piece,
            piece,
            pltpu.VMEM((2, per, unit, D), BF16),
            pltpu.VMEM((2, rows, D), BF16),
            pltpu.VMEM((rows, D), F32),
            pltpu.VMEM((ranks, rows, width), BF16),
            tokens,
        ]
        + dma_pair(NCH)
        + dma_pair(ranks + 1)
        + [pltpu.SemaphoreType.DMA((2,)), pltpu.SemaphoreType.DMA((5,))]
        + [pltpu.VMEM(t.shape[1:] if i == 5 else t.shape, t.dtype) for i, t in enumerate(late)]
        + [pltpu.SemaphoreType.DMA((len(late),))]
        + [
            pltpu.VMEM((LEN, width), F32),
            pltpu.VMEM((LEN, width), F32),
            pltpu.VMEM((LEN, 3 * width), BF16),
            pltpu.VMEM((half, rows, D), BF16),
            pltpu.VMEM((half - 1, rows, D), BF16),
            pltpu.VMEM((half - 1, rows, D), BF16),
        ]
        + ([] if ranks == 4 else [pltpu.VMEM((half, rows, D), BF16)])
        + [
            pltpu.VMEM((3, width, D // 2), BF16),
            pltpu.VMEM((3, width, D // 2), BF16),
            pltpu.VMEM((3, width, D // 2), BF16),
            pltpu.VMEM((D, D // 2), BF16),
            own,
        ]
        + dma_pair(half)
        + dma_pair(half - 1)
        + dma_pair(2)
        + deliver_sems()
        + host.scratch(),
        compiler_params=pltpu.CompilerParams(
            vmem_limit_bytes=BACK_LIMIT, collective_id=layer, has_side_effects=True
        ),
        cost_estimate=pl.CostEstimate(
            flops=100 * 10**9, bytes_accessed=60 * 2**20, transcendentals=rows * FF
        ),
    )(
        upper,
        mask,
        vec,
        dy,
        hidden,
        a2,
        wos[0],
        wos[1],
        ups[0],
        ups[1],
        downs[0],
        downs[1],
        given,
        *late,
        *[host.view(i, array) for i, array in enumerate(arrays)],
    )


def final_kernel(host, *refs):
    n = host.arrays
    srcs, rows_src = refs[:n], refs[n]
    outs, rows_out = refs[n + 1 : 2 * n + 1], refs[2 * n + 1]
    rows_sems = refs[2 * n + 2 : 2 * n + 5]
    rows_mine, rows_sem = refs[2 * n + 5 : 2 * n + 7]
    host.bind(srcs, outs, refs[2 * n + 7 :])
    rows_load = pltpu.make_async_copy(rows_src.at[0], rows_mine, rows_sem)
    rows_load.start()
    group = Group()
    group.greet(host.dp_count)
    host.begin()
    rows_copy = Deliver(group, 0, rows_mine, rows_out, rows_sems)
    rows_load.wait()
    rows_copy.start()
    host.run(0, len(host.events))
    host.finish()
    rows_copy.wait()


def final_call(host, arrays, rows_src, collective_id):
    anywhere = pl.BlockSpec(memory_space=pl.ANY)
    return pl.pallas_call(
        functools.partial(final_kernel, host),
        in_specs=[anywhere] * (host.arrays + 1),
        out_specs=[anywhere] * (host.arrays + 1),
        out_shape=host.out_shapes() + [jax.ShapeDtypeStruct(rows_src.shape, BF16)],
        scratch_shapes=deliver_sems()
        + [pltpu.VMEM(rows_src.shape[1:], BF16), pltpu.SemaphoreType.DMA]
        + host.scratch(),
        compiler_params=pltpu.CompilerParams(
            vmem_limit_bytes=VMEM_LIMIT, collective_id=collective_id, has_side_effects=True
        ),
    )(*host.views(arrays), rows_src)


def assemble_kernel(count, *refs):
    refs = list(refs)

    def pop(number):
        taken = refs[:number]
        del refs[:number]
        return taken

    sources = [pop(2) for _ in range(7)]
    row_outs = pop(2)
    up_out, down_out, out_out, joint_out = pop(4)
    vec_outs = pop(9)
    up, down, mixed, joint, little = pop(5)
    sems = pop(1)[0]
    core = lax.axis_index("section")
    half_ranks = count // 2
    compact = half_ranks == 2
    low = lax.rem(lax.axis_index("seq"), half_ranks)
    loads = []
    for i, (pair, target) in enumerate(zip(sources, [up, down, mixed, joint, little] + row_outs)):
        if i == 4:
            lines = little.shape[1]
            pair = [one.at[:, at * lines : (at + 1) * lines] for at, one in enumerate(pair)]
        first = pltpu.make_async_copy(pair[0], target, sems.at[i])
        second = pltpu.make_async_copy(pair[1], target, sems.at[i])
        pl.when(core == 0)(first.start)
        pl.when(core == 1)(second.start)
        loads.append(first)
    unit = up.shape[1]
    half_cols = D // 2
    loads[1].wait()
    for half in range(2):
        for g in range(FF // 2 // unit):
            at = (2 * g + half) * unit
            down_out[:, at : at + unit] = down[half, :, g * unit : (g + 1) * unit]
    loads[0].wait()
    for half in range(2):
        up_out[:, half * unit : (half + 1) * unit] = up[half].T
    for load in loads[2:5]:
        load.wait()
    for half in range(2):
        cols = slice(half * half_cols, (half + 1) * half_cols)
        value = mixed[half]
        if compact:
            heads = half_cols // DH // 2
            pieces = []
            for i in range(heads):
                for j in range(2):
                    at = (j * heads + i) * DH
                    pieces.append(value[:, at : at + DH])
            value = jnp.concatenate(pieces, axis=1)
        out_out[:, cols] = value
        value = joint[half]
        if compact:
            pieces = [value[i * DH : (i + 1) * DH, :] for i in range(4)]
            joint_out[0:DH, cols] = jnp.where(low == 0, pieces[0], pieces[1])
            joint_out[DH : 2 * DH, cols] = pieces[3]
            joint_out[2 * DH : 3 * DH, cols] = jnp.where(low == 0, pieces[1], pieces[2])
        else:
            joint_out[:, cols] = value
    total = little[0] + little[1]
    at = 0
    for out in vec_outs:
        size = out.shape[1]
        for start in range(0, size, 128):
            wide = min(128, size - start)
            row, lane = (at + start) // 128, (at + start) % 128
            out[:, start : start + wide] = total[row : row + 1, lane : lane + wide]
        at += size
    for load in loads[5:]:
        load.wait()


def assemble_call(count, groups, pairs):
    unit = D // groups
    anywhere = pl.BlockSpec(memory_space=pl.ANY)
    vmem = pl.BlockSpec(memory_space=pltpu.VMEM)
    sizes = [unit] * 8 + [FF // groups]
    flat = [array for pair in pairs for array in pair]
    return pl.pallas_call(
        functools.partial(assemble_kernel, count),
        in_specs=[anywhere] * len(flat),
        out_specs=[vmem] * 15,
        out_shape=[jax.ShapeDtypeStruct(pair[0].shape, BF16) for pair in pairs[5:]]
        + [
            jax.ShapeDtypeStruct((D, FF // groups), F32),
            jax.ShapeDtypeStruct((unit, FF), F32),
            jax.ShapeDtypeStruct((unit, D), F32),
            jax.ShapeDtypeStruct((3 * unit, D), F32),
        ]
        + [jax.ShapeDtypeStruct((1, size), F32) for size in sizes],
        scratch_shapes=[pltpu.VMEM(pair[0].shape, F32) for pair in pairs[:4]]
        + [pltpu.VMEM((2, pairs[4][0].shape[1] // 2, 128), F32)]
        + [pltpu.SemaphoreType.DMA((7,))],
        compiler_params=params(),
    )(*flat)


def swap(value, axis, mask):
    count = lax.axis_size(axis)
    return lax.ppermute(value, axis, [(i, i ^ mask) for i in range(count)])


def take(value, index, dim):
    return lax.dynamic_index_in_dim(value, index, dim, keepdims=False)


def ordered(bit, mine, other, dim):
    return jnp.where(
        bit == 0,
        jnp.stack([mine, other], axis=dim),
        jnp.stack([other, mine], axis=dim),
    )


def key_bias(counts, rotate):
    places = jnp.arange(LEN, dtype=jnp.int32)
    places = jnp.where(rotate, (places + LEN // 2) % LEN, places)
    offset = jnp.maximum(places - TRI, 0)
    view_index = offset // VSLOT
    inside = offset - view_index * VSLOT
    match = view_index[:, None] == jnp.arange(VIEWS, dtype=jnp.int32)[None, :]
    limits = jnp.sum(jnp.where(match, counts[None, :], 0), axis=1)
    valid = (places < TRI) | (inside < limits)
    return jnp.where(valid, 0.0, -1e30).astype(F32)[None, :]


def shards(
    inputs,
    cotangent,
    view_tokens,
    ln1_gain,
    ln1_bias,
    w_qkv,
    b_query,
    b_value,
    w_out,
    b_out,
    ln2_gain,
    ln2_bias,
    w_up,
    b_up,
    w_down,
    b_down,
):
    core = lax.axis_index("section")
    place = lax.axis_index("seq")
    dp_index = lax.axis_index("dp")
    count = lax.axis_size("seq")
    dp_count = lax.axis_size("dp")
    groups = dp_count * count
    half = count // 2
    micro = place // half
    low = place % half
    low_bits = half.bit_length() - 1
    rows = inputs.shape[2]
    width = D // count
    rank = core * half + low

    def swap_core(value):
        return swap(value, "section", 1)

    def swap_seq(value, bit):
        return swap(value, "seq", 1 << bit)

    def low_bit(bit):
        return (place >> bit) & 1

    def own_rows(local):
        chunks = local[:, 0]
        far = lax.ppermute(
            take(chunks, 1 - micro, 0),
            ("section", "seq"),
            [(count + z, count + (z ^ half)) for z in range(count)],
        )
        return jnp.where(core == 0, take(chunks, micro, 0), far)

    def gather_rows(own):
        value = own[None]
        for bit in range(low_bits):
            other = swap_seq(value, bit)
            value = ordered(low_bit(bit), value, other, 0).reshape((-1,) + own.shape)
        value = ordered(core, value, swap_core(value), 0)
        return value.reshape((-1,) + own.shape[1:])

    def exchange(value):
        tail = value.shape[1:]
        value = value.reshape((2,) * (low_bits + 1) + tail)
        for bit in range(low_bits):
            dim = low_bits - bit
            mine = take(value, low_bit(bit), dim)
            other = swap_seq(take(value, 1 - low_bit(bit), dim), bit)
            value = ordered(low_bit(bit), mine, other, dim)
        mine = take(value, core, 0)
        other = swap_core(take(value, 1 - core, 0))
        return ordered(core, mine, other, 0).reshape((count,) + tail)

    compact = half == 2
    span = half * width

    def vector_to(value):
        if compact:
            wide = jnp.stack(
                [jnp.where(low == i, value.reshape(len(value), -1, DH), 0.0) for i in range(2)], axis=2
            )
        else:
            wide = jnp.stack([jnp.where(low == i, value, 0.0) for i in range(half)], axis=1)
        wide = wide.reshape(len(value), span)
        return jnp.concatenate([jnp.where(core == i, wide, 0.0) for i in range(2)], axis=1)

    out_mine = w_out[0]
    ups = (w_up[0], swap_core(w_up[0]))
    downs = (w_down[0], swap_core(w_down[0]))
    bias_mask = key_bias(take(view_tokens[:, 0], micro, 0), micro == 1)

    saved = []
    acts = []
    for layer in range(2):
        if layer == 0:
            o_own, lse, a1, q, k, v, layer_in, joint_pair, out_other, vec = attend_call(
                True,
                0,
                bias_mask,
                count,
                dp_count,
                inputs,
                w_qkv,
                w_out,
                ln1_gain,
                ln1_bias,
                b_query,
                b_value,
                b_out,
                ln2_gain,
                ln2_bias,
                b_down,
                b_up,
            )
            outs_pair = (out_mine, out_other)
        else:
            o_own, lse, a1, q, k, v, d_out_all = attend_call(
                False, 1, bias_mask, count, dp_count, layer_in, joint_pair, vec, cotangent
            )
        hidden, upper, output, a2_all, o_all, gated_all, first_rows = mlp_call(
            layer, dp_count, o_own, layer_in, outs_pair, vec, ups, downs
        )
        acts.append(output)
        saved.append((layer_in, a1, q, k, v, lse, hidden, upper, a2_all, o_all, gated_all))
        layer_in = output

    def hosted(arrays, spans=None, shares=STAGE_SHARES, even=False):
        shapes = []
        for array in arrays:
            shapes.append((array.shape[1], array.shape[2], array.shape[0] != groups, array.dtype))
        return Hosted(dp_count, count, tuple(shapes), spans, shares, even)

    results = [{}, {}]
    pending = None
    sums = []
    for layer in (1, 0):
        x_own, a1, q, k, v, lse, hidden, upper, a2_all, o_all, gated_all = saved[layer]
        g_down = mm_tn(d_out_all.reshape(2 * rows, D), gated_all.reshape(2 * rows, FF // 2))
        g_down = g_down.astype(BF16).reshape(groups, D // groups, FF // 2)
        up_like = jax.ShapeDtypeStruct((groups, FF // groups // 2, D), BF16)
        if pending is None:
            arrays = [g_down]
            host = hosted(
                arrays + [up_like],
                ((0, 0.0, 48.0), (1, 28.0, 78.0)),
                (0.4, 0.6, 0.8, 1.0),
                True,
            )
        else:
            arrays = list(pending) + [g_down]
            host = hosted(
                arrays + [up_like],
                ((0, 0.0, 36.0), (0, 0.0, 36.0), (0, 12.0, 80.0), (1, 40.0, 120.0)),
            )
        (g_bup, sums_two, sums_one, sums_qv, g_up, d_in, g_joint, g_out, given, *reduced) = back_call(
            layer,
            d_out_all,
            hidden,
            outs_pair,
            vec,
            upper,
            a2_all,
            ups,
            downs,
            acts[1][None] if pending is None else d_out_all,
            (q, k, v, lse, a1, joint_pair, x_own, o_all),
            bias_mask,
            host,
            arrays,
        )
        if pending is None:
            second_rows = given
        else:
            second_grads = given
            for name in ("out", "joint"):
                results[1][name] = reduced.pop(0)
        results[layer]["down"], results[layer]["up"] = reduced
        g_out = g_out.reshape(groups, D // groups, D // 2)
        if compact:
            g_joint = g_joint.reshape(groups // 2, 3 * D // groups, D // 2)
        else:
            spread = jnp.stack(
                [jnp.where(low == i, g_joint, jnp.zeros_like(g_joint)) for i in range(half)], axis=2
            )
            g_joint = spread.reshape(groups, 3 * D // groups, D // 2)
        sums.append((sums_one, sums_qv, sums_two, g_bup))
        if pending is None:
            pending = (g_out, g_joint)
        else:
            one, qv, two, bup = (jnp.stack([sums[1][i], sums[0][i]]) for i in range(4))
            lines_of = jnp.concatenate(
                [
                    one[:, 0:2],
                    vector_to(qv[:, 0:2].reshape(4, width)).reshape(2, 2, D),
                    two[:, 2:3],
                    two[:, 0:2],
                    two[:, 3:4],
                ],
                axis=1,
            )
            small = jnp.concatenate(
                [
                    jnp.transpose(
                        lines_of.reshape(2, 8, groups, D // groups), (2, 0, 1, 3)
                    ).reshape(groups, 2, -1),
                    jnp.swapaxes(bup.reshape(2, groups, FF // groups), 0, 1),
                ],
                axis=2,
            )
            lines = -(-small.shape[2] // 128)
            lines += -lines % 8
            small = jnp.pad(small, ((0, 0), (0, 0), (0, lines * 128 - small.shape[2])))
            arrays = (g_out, g_joint, small.reshape(groups, 2 * lines, 128))
            out_0, joint_0, small_both, first_grads = final_call(hosted(arrays), arrays, d_in, 4)
            results[0]["out"], results[0]["joint"] = out_0, joint_0
            results[0]["small"] = results[1]["small"] = small_both
        d_out_all = d_in

    pairs = [
        (results[0][name], results[1][name]) for name in ("up", "down", "out", "joint", "small")
    ]
    pairs += [(first_rows, second_rows), (first_grads, second_grads)]
    acts_rows, grad_rows, g_w_up, g_w_down, g_w_out, g_w_qkv, *pieces = assemble_call(
        count, groups, pairs
    )
    g_ln1g, g_ln1b, g_bq, g_bv, g_bo, g_ln2g, g_ln2b, g_bd, g_bup = pieces
    return (
        acts_rows[None, :, None],
        grad_rows[None, :, None],
        g_ln1g,
        g_ln1b,
        g_w_qkv.T[None],
        g_bq,
        g_bv,
        g_w_out.T[None],
        g_bo,
        g_ln2g,
        g_ln2b,
        g_w_up[None],
        g_bup,
        g_w_down.T[None],
        g_bd,
    )


def solution(mesh):
    rows = P(None, "dp", "seq", None)
    vector = P("section", None)
    matrix = P("section", None, None)
    placed = (
        rows,
        rows,
        P(None, "dp", None),
        vector,
        vector,
        matrix,
        vector,
        vector,
        matrix,
        vector,
        vector,
        vector,
        matrix,
        vector,
        matrix,
        vector,
    )
    both = P("section", None, "dp", "seq", None)
    line = P("section", ("dp", "seq"))
    table = P("section", None, ("dp", "seq"))
    return jax.shard_map(
        shards,
        mesh=mesh,
        in_specs=placed,
        out_specs=(
            both,
            both,
            line,
            line,
            table,
            line,
            line,
            table,
            line,
            line,
            line,
            table,
            line,
            table,
            line,
        ),
        check_vma=False,
    )
```
